128 devices in a mesh: seq: 8 (over x, core), wshard: 16 (over z, y).
Axes of the slice: x: 4, y: 4, z: 4, core: 2. Of those that a mesh axis runs over, the one named last changes fastest.
Arguments:
- tokens: bfloat16 [16, 1024, 1024], P('wshard', 'seq'), may hold values from -6 to 6
- weight_qkv: bfloat16 [1024, 2048], P(('seq', 'wshard')), may hold values from -0.5 to 0.5
- weight_out: bfloat16 [1024, 1024], P(('seq', 'wshard')), may hold values from -2 to 2
- router: bfloat16 [1024, 32], P(('seq', 'wshard')), may hold values from -0.09375 to 0.09375
- gain_attn: bfloat16 [1024], P(('seq', 'wshard')), may hold values from 0.5 to 1.5
- gain_ffn: bfloat16 [1024], P(('seq', 'wshard')), may hold values from 0.5 to 1.5
- expert_gate: bfloat16 [32, 1024, 512], P('wshard', 'seq'), may hold values from -0.1875 to 0.1875
- expert_up: bfloat16 [32, 1024, 512], P('wshard', 'seq'), may hold values from -0.1875 to 0.1875
- expert_down: bfloat16 [32, 512, 1024], P('wshard', 'seq'), may hold values from -2 to 2
- expert_ids: int32 [16, 1024, 8], P('wshard', 'seq'), may hold values from 0 to 31, all different within a row; in each aligned block of 128 rows (0 to 127, 128 to 255, ..., all dimensions but the last counted through in order) at most 64 rows name the same one
- cotangent: bfloat16 [16, 1024, 1024], P('wshard', 'seq'), may hold values from -6 to 6
Outputs:
- output: bfloat16 [16, 1024, 1024], P('wshard', 'seq')
- grad_tokens: bfloat16 [16, 1024, 1024], P('wshard', 'seq')
- grad_qkv: float32 [1024, 2048], P(('seq', 'wshard'))
- grad_out: float32 [1024, 1024], P(('seq', 'wshard'))
- grad_router: float32 [1024, 32], P(('seq', 'wshard'))
- grad_gain_attn: float32 [1024], P(('seq', 'wshard'))
- grad_gain_ffn: float32 [1024], P(('seq', 'wshard'))
- grad_gate: float32 [32, 1024, 512], P('wshard', 'seq')
- grad_up: float32 [32, 1024, 512], P('wshard', 'seq')
- grad_down: float32 [32, 512, 1024], P('wshard', 'seq')
The draws below stay inside these ranges and needn't reach their ends.
Inputs may be any that keep to these rules, and one draw needn't show every extreme that they name: `expert_ids`: each row names 8 different experts. In the 128 rows of one device (aligned blocks of each sequence) no expert is named more than 64 times, and in every draw some expert is named exactly 64 times in some block.
All inputs are finite; a program needn't handle non-finite values.
Results may differ from the reference program's by a relative error of at most 0.02.
Values may be sent and summed in bfloat16 or wider, within the bound.
A program may use at most 128 MiB of HBM per device.

```python
import math
import jax
import jax.numpy as jnp
import numpy as np
from jax import lax

D = 1024
HEADS = 16
KV_HEADS = 8
HEAD_DIM = 64
FF = 512
EXPERTS = 32
TOPK = 8
TOK_DEV = 128
LENGTH = 1024
SEQS = 16
Q_WIDTH = 1024
KV_WIDTH = 512
CAP = 64
N_SEQ = 8


def block_levels(key, shape, pieces, low, largest):
    def one(dim, blocks):
        draws = jax.random.uniform(jax.random.fold_in(jax.random.fold_in(key, 6), dim), (blocks,), jnp.float32, low / len(pieces), largest / len(pieces))
        return jnp.repeat(jnp.exp(draws), shape[dim] // blocks).reshape((-1,) + (1,) * (len(shape) - dim - 1))

    loudness = one(*pieces[0])
    for cut in pieces[1:]:
        loudness = loudness * one(*cut)
    return loudness


def shared_out(key, own, number, rows, count, top, limit, lean):
    ranking = jax.random.permutation(key, count)
    crowded, ordinary = portions_of(count, rows * top, limit, lean, True), portions_of(count, rows * top, limit, lean, False)
    places = jnp.arange(count)

    def named(sizes, turn):
        used = int((sizes > 0).sum())
        fixed = max(1, used // 4)
        moved = fixed + (places - fixed + turn * (used - fixed)) % max(1, count - fixed)
        return jnp.zeros((count,), jnp.int32).at[ranking[jnp.where(places < fixed, places, moved)]].set(jnp.asarray(sizes, jnp.int32))

    sizes = jnp.where(number % 4 == 0, named(crowded, number // 4), named(ordinary, number - number // 4 - 1))
    mixed = jax.random.permutation(jax.random.fold_in(own, 3), count)
    source_of, receiver = mixed[0:count // 2 * 2:2], mixed[1:count // 2 * 2:2]
    margin = jnp.minimum(sizes[source_of] - 1, limit - sizes[receiver]) // 2
    margin = jnp.where((source_of == ranking[0]) | (receiver == ranking[0]) | (sizes[receiver] == 0), 0, jnp.maximum(margin, 0))
    moved = jax.random.randint(jax.random.fold_in(own, 4), (count // 2,), 0, 1 << 20) % (margin + 1)
    sizes = sizes.at[source_of].add(-moved).at[receiver].add(moved)
    items = jnp.searchsorted(jnp.cumsum(sizes), jnp.arange(rows * top), side="right").astype(jnp.int32)
    grid = items.reshape(top, rows).T
    grid = grid[jax.random.permutation(jax.random.fold_in(own, 1), rows)]
    turn = jax.random.randint(jax.random.fold_in(own, 2), (rows, 1), 0, top)
    return jnp.take_along_axis(grid, (jnp.arange(top)[None, :] + turn) % top, axis=1)


def portions_of(amount, total, most, skew, full):
    loads = [(1 << 20) // math.isqrt(rank ** skew) + 1 for rank in range(1, amount + 1)]
    largest = most if full else min(most, max(-(-total // amount), total * loads[0] // sum(loads)))
    least = 1 if total - largest >= amount - 1 else 0
    counts, spare = [largest] + [least] * (amount - 1), total - largest - least * (amount - 1)
    while spare > 0:
        free = [i for i in range(1, amount) if counts[i] < largest] or [i for i in range(1, amount) if counts[i] < most]
        whole, left = sum([loads[i] for i in free]), spare
        for i in free:
            more = min(most - counts[i], max(1, left * loads[i] // whole), spare)
            counts[i] = counts[i] + more
            spare = spare - more
    return np.array(counts)


def centred(key, extent, deviation, most, shards=(), held_as=jnp.bfloat16):
    values = deviation * jax.random.normal(key, extent, jnp.float32)
    if shards:
        values = values * block_levels(key, extent, shards, -0.22, 0.18)
    return jnp.clip(values, -most, most).astype(held_as)


def setup_inputs(seed: int = 0) -> dict:
    keys = jax.random.split(jax.random.key(seed), 12)
    tokens = centred(keys[0], (SEQS, LENGTH, D), 1.0, 6.0, ((0, 16), (1, 8)))
    weight_qkv = centred(keys[1], (D, Q_WIDTH + 2 * KV_WIDTH), (max(D // 9, 1)) ** -0.5, 0.5, ((0, 128),))
    weight_out = centred(keys[2], (Q_WIDTH, D), 8 ** -0.5, 2.0, ((0, 128),))
    router = centred(keys[3], (D, EXPERTS), (4 * D) ** -0.5, 0.09375, ((0, 128),))
    gain_attn = jnp.clip(1.0 + 0.1 * jax.random.normal(keys[4], (D,), jnp.float32), 0.5, 1.5).astype(jnp.bfloat16)
    gain_ffn = jnp.clip(1.0 + 0.1 * jax.random.normal(keys[5], (D,), jnp.float32), 0.5, 1.5).astype(jnp.bfloat16)
    expert_gate = centred(keys[6], (EXPERTS, D, FF), D ** -0.5, 0.1875, ((0, 16), (1, 8)))
    expert_up = centred(keys[7], (EXPERTS, D, FF), D ** -0.5, 0.1875, ((0, 16), (1, 8)))
    expert_down = centred(keys[8], (EXPERTS, FF, D), 8 ** -0.5, 2.0, ((0, 16), (1, 8)))
    expert_ids_keys = jax.random.split(jax.random.fold_in(keys[9], 1), SEQS * LENGTH // TOK_DEV)
    expert_ids_turns = jax.random.permutation(jax.random.fold_in(keys[9], 3), SEQS * LENGTH // TOK_DEV)
    expert_ids = jax.vmap(lambda own, number: shared_out(jax.random.fold_in(keys[9], 2), own, number, TOK_DEV, EXPERTS, TOPK, CAP, 1))(expert_ids_keys, expert_ids_turns).reshape((SEQS, LENGTH, TOPK))
    cotangent = centred(keys[10], (SEQS, LENGTH, D), 1.0, 6.0, ((0, 16), (1, 8)))
    return {"tokens": tokens, "weight_qkv": weight_qkv, "weight_out": weight_out, "router": router, "gain_attn": gain_attn, "gain_ffn": gain_ffn, "expert_gate": expert_gate, "expert_up": expert_up, "expert_down": expert_down, "expert_ids": expert_ids, "cotangent": cotangent}


epsilon = 1e-06
attention_multiplier = 0.015625
residual_multiplier = 0.22
rope_theta = 10000.0
highest = lax.Precision.HIGHEST

@jax.custom_vjp
def low(v):
    return lax.optimization_barrier(v.astype(jnp.bfloat16)).astype(jnp.float32)

@jax.custom_vjp
def low_back(v):
    return v

def low_keep(v):
    return (low(v), None)

def low_pass(kept, grad):
    return (grad,)

def back_keep(v):
    return (v, None)

def back_low(kept, grad):
    return (low(grad),)
low.defvjp(low_keep, low_pass)
low_back.defvjp(back_keep, back_low)

def rms_scale(values):
    return lax.rsqrt(lax.optimization_barrier(jnp.mean(values * values, axis=-1, keepdims=True)) + epsilon)

def rotate(heads_in, positions):
    half_dim = heads_in.shape[-1] // 2
    frequency = rope_theta ** (-jnp.arange(half_dim, dtype=jnp.float32) / half_dim)
    angles = positions.astype(jnp.float32)[:, None] * frequency[None, :]
    cosine = jnp.cos(angles)[:, None, :]
    sine_of = jnp.sin(angles)[:, None, :]
    leading = heads_in[..., :half_dim]
    second = heads_in[..., half_dim:]
    return jnp.concatenate([leading * cosine - second * sine_of, second * cosine + leading * sine_of], axis=-1)

def route_table(chosen_ids):
    flat_ids = chosen_ids.reshape(N_SEQ, TOK_DEV * TOPK)
    onehot = (flat_ids[:, :, None] == jnp.arange(EXPERTS, dtype=jnp.int32)[None, None, :]).astype(jnp.int32)
    places = jnp.cumsum(onehot, axis=1) - 1
    slot_of = lax.optimization_barrier(jnp.sum(places * onehot, axis=-1))
    blocks = jnp.arange(N_SEQ, dtype=jnp.int32)[:, None]
    targets = (flat_ids * (N_SEQ * CAP) + blocks * CAP + slot_of).reshape(-1).astype(jnp.int32)
    sources = jnp.full((EXPERTS * N_SEQ * CAP,), LENGTH * TOPK, dtype=jnp.int32)
    sources = sources.at[targets].set(jnp.arange(LENGTH * TOPK, dtype=jnp.int32))
    return (targets, sources)

def attention(queries, keys_all, values_all):
    group_size = HEADS // KV_HEADS
    block_rows = min(512, LENGTH)
    grouped = queries.reshape(LENGTH // block_rows, block_rows, KV_HEADS, group_size, HEAD_DIM)
    starts = jnp.arange(LENGTH // block_rows, dtype=jnp.int32) * block_rows
    key_pos = jnp.arange(LENGTH, dtype=jnp.int32)

    def one_block(operands):
        rows_in, offset = operands
        scores = jnp.einsum('qhrd,khd->hrqk', rows_in, keys_all, precision=highest)
        scores = low_back(attention_multiplier * scores)
        query_pos = offset + jnp.arange(block_rows, dtype=jnp.int32)
        allowed = key_pos[None, :] <= query_pos[:, None]
        scores = jnp.where(allowed, scores, -1e+30)
        peak_score = lax.optimization_barrier(jnp.max(scores, axis=-1, keepdims=True))
        exponent = jnp.exp(scores - peak_score)
        weights = exponent / lax.optimization_barrier(jnp.sum(exponent, axis=-1, keepdims=True))
        blended = jnp.einsum('hrqk,khd->qhrd', low(weights), values_all, precision=highest)
        return blended.reshape(block_rows, HEADS * HEAD_DIM)
    return lax.map(jax.checkpoint(one_block), (grouped, starts)).reshape(LENGTH, HEADS * HEAD_DIM)

def expert_block(operands):
    rows_in, gate_weight, up_weight, down_weight = operands
    gate_val = low_back(jnp.dot(rows_in, gate_weight, precision=highest))
    up_val = low_back(jnp.dot(rows_in, up_weight, precision=highest))
    inner_act = low(gate_val * jax.nn.sigmoid(gate_val) * up_val)
    return low_back(low(jnp.dot(inner_act, down_weight, precision=highest)))

def layer_sequence(inputs, chosen_ids, targets, sources, params):
    weight_qkv, weight_out, router, gain_attn, gain_ffn, expert_gate, expert_up, expert_down = params
    scale_one = rms_scale(inputs)
    normed_one = low(inputs * scale_one * gain_attn)
    projected = low_back(jnp.dot(normed_one, weight_qkv, precision=highest))
    positions = jnp.arange(LENGTH, dtype=jnp.int32)
    queries = low(rotate(projected[:, :Q_WIDTH].reshape(LENGTH, HEADS, HEAD_DIM), positions))
    keys_all = low(rotate(projected[:, Q_WIDTH:Q_WIDTH + KV_WIDTH].reshape(LENGTH, KV_HEADS, HEAD_DIM), positions))
    values_all = low(projected[:, Q_WIDTH + KV_WIDTH:].reshape(LENGTH, KV_HEADS, HEAD_DIM))
    attended = low_back(low(attention(queries, keys_all, values_all)))
    branch = low_back(jnp.dot(attended, weight_out, precision=highest))
    hidden = inputs + residual_multiplier * branch
    scale_two = rms_scale(hidden)
    normed_two = low(hidden * scale_two * gain_ffn)
    logits = low_back(jnp.dot(normed_two, router, precision=highest))
    chosen = jnp.take_along_axis(logits, chosen_ids, axis=1)
    peak_logit = lax.optimization_barrier(jnp.max(chosen, axis=1, keepdims=True))
    exponent = jnp.exp(chosen - peak_logit)
    gate_share = exponent / lax.optimization_barrier(jnp.sum(exponent, axis=1, keepdims=True))
    is_used = sources < LENGTH * TOPK
    token_of = jnp.minimum(sources // TOPK, LENGTH - 1)
    gathered = jnp.where(is_used[:, None], normed_two[token_of], 0.0)
    gathered = low_back(gathered).reshape(EXPERTS, N_SEQ * CAP, D)
    produced = lax.map(jax.checkpoint(expert_block), (gathered, expert_gate, expert_up, expert_down))
    routed = produced.reshape(EXPERTS * N_SEQ * CAP, D)[targets].reshape(LENGTH, TOPK, D)
    mixture = lax.optimization_barrier(jnp.sum(gate_share[:, :, None] * routed, axis=1))
    return hidden + residual_multiplier * mixture

def reference(tokens, weight_qkv, weight_out, router, gain_attn, gain_ffn, expert_gate, expert_up, expert_down, expert_ids, cotangent):
    params = (weight_qkv.astype(jnp.float32), weight_out.astype(jnp.float32), router.astype(jnp.float32), gain_attn.astype(jnp.float32), gain_ffn.astype(jnp.float32), expert_gate.astype(jnp.float32), expert_up.astype(jnp.float32), expert_down.astype(jnp.float32))
    targets, sources = jax.vmap(route_table)(expert_ids)

    def forward(inputs, weights):

        def per_sequence(operands):
            seq_in, seq_ids, seq_targets, seq_sources = operands
            return layer_sequence(seq_in, seq_ids, seq_targets, seq_sources, weights)
        return lax.map(jax.checkpoint(per_sequence), (inputs, expert_ids, targets, sources))
    output, pullback = jax.vjp(forward, tokens.astype(jnp.float32), params)
    grad_in, grads = pullback(cotangent.astype(jnp.float32))
    return (output.astype(jnp.bfloat16), grad_in.astype(jnp.bfloat16), grads[0], grads[1], grads[2], grads[3], grads[4], grads[5], grads[6], grads[7])
```

```python
import jax
import jax.numpy as jnp
from jax import lax
from jax.sharding import PartitionSpec as P

HEADS = 16
KV_HEADS = 8
HEAD_DIM = 64


epsilon = 1e-06
attention_multiplier = 0.015625
residual_multiplier = 0.22
rope_theta = 10000.0


def rms_scale(values):
    return lax.rsqrt(jnp.mean(values * values, axis=-1, keepdims=True) + epsilon)


def rotate(heads_in, positions, direction):
    half_dim = heads_in.shape[-1] // 2
    frequency = rope_theta ** (-jnp.arange(half_dim, dtype=jnp.float32) / half_dim)
    angles = positions.astype(jnp.float32)[:, None] * frequency[None, :]
    cosine = jnp.cos(angles)[:, None, :]
    sine_of = direction * jnp.sin(angles)[:, None, :]
    leading = heads_in[..., :half_dim]
    second = heads_in[..., half_dim:]
    return jnp.concatenate(
        [leading * cosine - second * sine_of, second * cosine + leading * sine_of], axis=-1
    )


def attend_forward(queries, keys_all, values_all):
    length, heads_dev, head_size = queries.shape
    key_heads = keys_all.shape[1]
    group_size = heads_dev // key_heads
    block_rows = min(512, length)
    block_count = length // block_rows
    grouped = queries.reshape(block_count, block_rows, key_heads, group_size, head_size)
    starts = jnp.arange(block_count, dtype=jnp.int32) * block_rows
    key_pos = jnp.arange(length, dtype=jnp.int32)

    def one_block(operands):
        rows_in, offset = operands
        scores = attention_multiplier * jnp.einsum(
            "qhrd,khd->hrqk", rows_in, keys_all, preferred_element_type=jnp.float32
        )
        allowed = key_pos[None, :] <= (offset + jnp.arange(block_rows, dtype=jnp.int32))[:, None]
        scores = jnp.where(allowed, scores, -1e30)
        peak_score = jnp.max(scores, axis=-1, keepdims=True)
        exponent = jnp.exp(scores - peak_score)
        total = jnp.sum(exponent, axis=-1, keepdims=True)
        weights = (exponent / total).astype(jnp.bfloat16)
        blended = jnp.einsum(
            "hrqk,khd->qhrd", weights, values_all, preferred_element_type=jnp.float32
        )
        return (
            blended.reshape(block_rows, heads_dev * head_size),
            (peak_score + jnp.log(total))[..., 0],
        )

    blended, logsum = lax.map(one_block, (grouped, starts))
    return (blended.reshape(length, heads_dev * head_size), logsum)


def attend_backward(queries, keys_all, values_all, grads_out, logsum):
    length, heads_dev, head_size = queries.shape
    key_heads = keys_all.shape[1]
    group_size = heads_dev // key_heads
    block_rows = min(512, length)
    block_count = length // block_rows
    grouped = queries.reshape(block_count, block_rows, key_heads, group_size, head_size)
    grads_grouped = grads_out.reshape(block_count, block_rows, key_heads, group_size, head_size)
    starts = jnp.arange(block_count, dtype=jnp.int32) * block_rows
    key_pos = jnp.arange(length, dtype=jnp.int32)

    def one_block(carry, operands):
        rows_in, grads_in, block_lse, offset = operands
        scores = attention_multiplier * jnp.einsum(
            "qhrd,khd->hrqk", rows_in, keys_all, preferred_element_type=jnp.float32
        )
        allowed = key_pos[None, :] <= (offset + jnp.arange(block_rows, dtype=jnp.int32))[:, None]
        weights = jnp.where(allowed, jnp.exp(scores - block_lse[..., None]), 0.0)
        grad_weights = jnp.einsum(
            "qhrd,khd->hrqk", grads_in, values_all, preferred_element_type=jnp.float32
        )
        center = jnp.sum(weights * grad_weights, axis=-1, keepdims=True)
        grad_scores = (weights * (grad_weights - center)).astype(jnp.bfloat16)
        grad_rows = attention_multiplier * jnp.einsum(
            "hrqk,khd->qhrd", grad_scores, keys_all, preferred_element_type=jnp.float32
        )
        grad_keys = carry[0] + attention_multiplier * jnp.einsum(
            "hrqk,qhrd->khd", grad_scores, rows_in, preferred_element_type=jnp.float32
        )
        grad_values = carry[1] + jnp.einsum(
            "hrqk,qhrd->khd",
            weights.astype(jnp.bfloat16),
            grads_in,
            preferred_element_type=jnp.float32,
        )
        return ((grad_keys, grad_values), grad_rows.reshape(block_rows, heads_dev, head_size))

    zeros_kv = jnp.zeros((length, key_heads, head_size), jnp.float32)
    totals, grad_queries = lax.scan(
        one_block, (zeros_kv, zeros_kv), (grouped, grads_grouped, logsum, starts)
    )
    return (grad_queries.reshape(length, heads_dev, head_size), totals[0], totals[1])


def dense_gates(logits, chosen_ids, experts_all):
    named = jnp.any(
        chosen_ids[..., None] == jnp.arange(experts_all, dtype=jnp.int32), axis=-2
    )
    peak = jnp.max(jnp.where(named, logits, -jnp.inf), axis=-1, keepdims=True)
    exponent = jnp.where(named, jnp.exp(logits - peak), 0.0)
    return (named, exponent / jnp.sum(exponent, axis=-1, keepdims=True))


def norm_backward(grad_normed, values, scale, gain_full):
    grad_gain = jnp.sum(grad_normed * values * scale, axis=0)
    grad_hat = grad_normed * gain_full
    grad_values = scale * grad_hat - values * (scale * scale * scale) * jnp.mean(
        grad_hat * values, axis=1, keepdims=True
    )
    return (grad_values, grad_gain)


def local(
    tokens,
    weight_qkv,
    weight_out,
    router,
    gain_attn,
    gain_ffn,
    expert_gate,
    expert_up,
    expert_down,
    expert_ids,
    cotangent,
):
    tok_dev = tokens.shape[1]
    features = tokens.shape[2]
    seq_parts = lax.axis_size("seq")
    owners = lax.axis_size("wshard")
    local_experts = expert_gate.shape[0]
    experts_all = local_experts * owners
    top_count = expert_ids.shape[2]
    capacity = 2 * tok_dev * top_count // experts_all
    heads_dev = HEADS // seq_parts
    key_heads = KV_HEADS // seq_parts
    query_cols = heads_dev * HEAD_DIM
    key_cols = key_heads * HEAD_DIM
    query_width = HEADS * HEAD_DIM
    key_width = KV_HEADS * HEAD_DIM
    length = tok_dev * seq_parts
    smalls = jnp.concatenate(
        [
            weight_out,
            router,
            gain_attn[:, None],
            gain_ffn[:, None],
            jnp.zeros((router.shape[0], 128 - experts_all - 2), jnp.bfloat16),
        ],
        axis=1,
    )
    gains = lax.all_gather(gain_attn, ("seq", "wshard"), axis=0, tiled=True)
    qkv_full = lax.all_gather(weight_qkv, ("seq", "wshard"), axis=0, tiled=True)
    smalls_full = lax.all_gather(smalls, ("seq", "wshard"), axis=0, tiled=True)
    out_full = smalls_full[:, :features]
    router_full = smalls_full[:, features : features + experts_all]
    gain_one = gains.astype(jnp.float32)
    gain_two = smalls_full[:, features + experts_all + 1].astype(jnp.float32)
    ids_all = lax.all_gather(expert_ids[0], "wshard", axis=0)
    cot_all = lax.all_gather(cotangent[0], "wshard", axis=0)
    owned = (
        lax.all_gather(expert_gate, "seq", axis=1, tiled=True),
        lax.all_gather(expert_up, "seq", axis=1, tiled=True),
        lax.all_gather(expert_down, "seq", axis=1, tiled=True),
    )
    gate_full, up_full, down_full = (owned[0], owned[1], owned[2])
    inputs = tokens[0].astype(jnp.float32)
    chosen_ids = expert_ids[0]
    scale_one = rms_scale(inputs)
    normed_one = (inputs * scale_one * gain_one).astype(jnp.bfloat16)
    projected = jnp.dot(normed_one, qkv_full, preferred_element_type=jnp.float32)
    positions = lax.axis_index("seq") * tok_dev + jnp.arange(tok_dev, dtype=jnp.int32)
    queries = rotate(projected[:, :query_width].reshape(tok_dev, HEADS, HEAD_DIM), positions, 1.0)
    keys_tok = rotate(
        projected[:, query_width : query_width + key_width].reshape(tok_dev, KV_HEADS, HEAD_DIM),
        positions,
        1.0,
    )
    values_tok = projected[:, query_width + key_width :]
    packed = jnp.concatenate(
        [
            queries.reshape(tok_dev, seq_parts, query_cols),
            keys_tok,
            values_tok.reshape(tok_dev, seq_parts, key_cols),
        ],
        axis=2,
    ).astype(jnp.bfloat16)
    heads_all = lax.all_to_all(packed, "seq", split_axis=1, concat_axis=0, tiled=True)
    head_queries = heads_all[:, 0, :query_cols].reshape(length, heads_dev, HEAD_DIM)
    head_keys = heads_all[:, 0, query_cols : query_cols + key_cols].reshape(
        length, key_heads, HEAD_DIM
    )
    head_values = heads_all[:, 0, query_cols + key_cols :].reshape(length, key_heads, HEAD_DIM)
    blended, logsum = attend_forward(head_queries, head_keys, head_values)
    returned_heads = lax.all_to_all(
        blended.astype(jnp.bfloat16).reshape(length, 1, query_cols),
        "seq",
        split_axis=0,
        concat_axis=1,
        tiled=True,
    )
    attended = returned_heads.reshape(tok_dev, query_width)
    branch = jnp.dot(attended, out_full, preferred_element_type=jnp.float32)
    hidden = inputs + residual_multiplier * branch
    scale_two = rms_scale(hidden)
    normed_two = (hidden * scale_two * gain_two).astype(jnp.bfloat16)
    logits = jnp.dot(normed_two, router_full, preferred_element_type=jnp.float32)
    _, gates_own = dense_gates(logits, chosen_ids, experts_all)
    normed_all = lax.all_gather(normed_two, "wshard", axis=0)
    logits_all = jnp.einsum(
        "std,de->ste", normed_all, router_full, preferred_element_type=jnp.float32
    )
    named_all, gates_all = dense_gates(logits_all, ids_all, experts_all)
    first_expert = lax.axis_index("wshard") * local_experts
    named = lax.dynamic_slice_in_dim(named_all, first_expert, local_experts, axis=2)
    gates_mine = lax.dynamic_slice_in_dim(gates_all, first_expert, local_experts, axis=2)
    lower = jnp.tril(jnp.ones((tok_dev, tok_dev), jnp.bfloat16))
    places = jnp.einsum(
        "ut,ste->seu", lower, named.astype(jnp.bfloat16), preferred_element_type=jnp.float32
    ).astype(jnp.int32) - 1
    picks = (
        places[:, :, None, :] == jnp.arange(capacity, dtype=jnp.int32)[None, None, :, None]
    ) & jnp.transpose(named, (0, 2, 1))[:, :, None, :]
    picks = jnp.transpose(picks, (1, 0, 2, 3))
    pick = picks.astype(jnp.bfloat16)
    row_gate = jnp.sum(
        jnp.where(picks, jnp.transpose(gates_mine, (2, 0, 1))[:, :, None, :], 0.0), axis=-1
    ).reshape(local_experts, owners * capacity)
    received = (
        jnp.einsum("esct,std->escd", pick, normed_all, preferred_element_type=jnp.float32)
        .astype(jnp.bfloat16)
        .reshape(local_experts, owners * capacity, features)
    )
    cot_rows = (
        jnp.einsum("esct,std->escd", pick, cot_all, preferred_element_type=jnp.float32)
        .astype(jnp.bfloat16)
        .reshape(local_experts, owners * capacity, features)
    )
    gate_val = jnp.einsum("erd,edf->erf", received, gate_full, preferred_element_type=jnp.float32)
    up_val = jnp.einsum("erd,edf->erf", received, up_full, preferred_element_type=jnp.float32)
    sigma = jax.nn.sigmoid(gate_val)
    activated = gate_val * sigma
    inner_act = (activated * up_val).astype(jnp.bfloat16)
    produced = jnp.einsum(
        "erf,efd->erd", inner_act, down_full, preferred_element_type=jnp.float32
    ).astype(jnp.bfloat16)
    grad_mix_rows = residual_multiplier * cot_rows.astype(jnp.float32)
    weighted = (row_gate[:, :, None] * produced).astype(jnp.bfloat16)
    mix_part = jnp.einsum(
        "esct,escd->std",
        pick,
        weighted.reshape(local_experts, owners, capacity, features),
        preferred_element_type=jnp.float32,
    ).astype(jnp.bfloat16)
    grad_gate_rows = jnp.sum(produced * grad_mix_rows, axis=-1).reshape(
        local_experts, owners, capacity
    )
    gate_part = jnp.sum(
        jnp.where(picks, grad_gate_rows[:, :, :, None], 0.0), axis=2
    )
    gate_part = jnp.transpose(gate_part, (1, 2, 0))
    grad_gates = lax.all_to_all(gate_part, "wshard", split_axis=0, concat_axis=0, tiled=True)
    grad_gates = jnp.transpose(grad_gates, (1, 0, 2)).reshape(tok_dev, experts_all)
    mixture = lax.psum_scatter(mix_part, "wshard", scatter_dimension=0, tiled=True)[0]
    output = hidden + residual_multiplier * mixture.astype(jnp.float32)
    grad_output = cotangent[0].astype(jnp.float32)
    grad_logits = (
        gates_own
        * (grad_gates - jnp.sum(gates_own * grad_gates, axis=1, keepdims=True))
    ).astype(jnp.bfloat16)
    grad_router = jnp.dot(normed_two.T, grad_logits, preferred_element_type=jnp.float32)
    grad_normed_two = jnp.dot(grad_logits, router_full.T, preferred_element_type=jnp.float32)
    grad_received = (row_gate[:, :, None] * grad_mix_rows).astype(jnp.bfloat16)
    grad_inner = jnp.einsum(
        "erd,efd->erf", grad_received, down_full, preferred_element_type=jnp.float32
    )
    grad_down = jnp.einsum(
        "erf,erd->efd", inner_act, grad_received, preferred_element_type=jnp.float32
    )
    grad_gate_val = (grad_inner * up_val * (sigma * (1.0 + gate_val * (1.0 - sigma)))).astype(
        jnp.bfloat16
    )
    grad_up_val = (grad_inner * activated).astype(jnp.bfloat16)
    grad_rows = (
        jnp.einsum("erf,edf->erd", grad_gate_val, gate_full, preferred_element_type=jnp.float32)
        + jnp.einsum("erf,edf->erd", grad_up_val, up_full, preferred_element_type=jnp.float32)
    ).astype(jnp.bfloat16)
    rows_part = jnp.einsum(
        "esct,escd->std",
        pick,
        grad_rows.reshape(local_experts, owners, capacity, features),
        preferred_element_type=jnp.float32,
    ).astype(jnp.bfloat16)
    grad_back = lax.psum_scatter(rows_part, "wshard", scatter_dimension=0, tiled=True)[0]
    grad_gate = jnp.einsum(
        "erd,erf->edf", received, grad_gate_val, preferred_element_type=jnp.float32
    )
    grad_up = jnp.einsum("erd,erf->edf", received, grad_up_val, preferred_element_type=jnp.float32)
    expert_shares = (
        lax.psum_scatter(
            grad_gate.astype(jnp.bfloat16), "seq", scatter_dimension=1, tiled=True
        ).astype(jnp.float32),
        lax.psum_scatter(
            grad_up.astype(jnp.bfloat16), "seq", scatter_dimension=1, tiled=True
        ).astype(jnp.float32),
        lax.psum_scatter(
            grad_down.astype(jnp.bfloat16), "seq", scatter_dimension=1, tiled=True
        ).astype(jnp.float32),
    )
    grad_normed_two = grad_normed_two + grad_back.astype(jnp.float32)
    grad_hidden_norm, grad_gain_ffn = norm_backward(grad_normed_two, hidden, scale_two, gain_two)
    grad_hidden = grad_output + grad_hidden_norm
    grad_branch = (residual_multiplier * grad_hidden).astype(jnp.bfloat16)
    grad_out = jnp.dot(attended.T, grad_branch, preferred_element_type=jnp.float32)
    grad_attended = jnp.dot(grad_branch, out_full.T, preferred_element_type=jnp.float32).astype(
        jnp.bfloat16
    )
    grad_heads = lax.all_to_all(
        grad_attended.reshape(tok_dev, seq_parts, query_cols),
        "seq",
        split_axis=1,
        concat_axis=0,
        tiled=True,
    )
    grad_heads = grad_heads.reshape(length, heads_dev, HEAD_DIM)
    grad_queries, grad_keys, grad_values = attend_backward(
        head_queries, head_keys, head_values, grad_heads, logsum
    )
    head_pos = jnp.arange(length, dtype=jnp.int32)
    grad_queries = rotate(grad_queries, head_pos, -1.0)
    grad_keys = rotate(grad_keys, head_pos, -1.0)
    grad_packed = jnp.concatenate(
        [
            grad_queries.reshape(length, query_cols),
            grad_keys.reshape(length, key_cols),
            grad_values.reshape(length, key_cols),
        ],
        axis=1,
    ).astype(jnp.bfloat16)
    grad_parts = lax.all_to_all(
        grad_packed.reshape(length, 1, query_cols + 2 * key_cols),
        "seq",
        split_axis=0,
        concat_axis=1,
        tiled=True,
    )
    grad_proj = jnp.concatenate(
        [
            grad_parts[:, :, :query_cols].reshape(tok_dev, query_width),
            grad_parts[:, :, query_cols : query_cols + key_cols].reshape(tok_dev, key_width),
            grad_parts[:, :, query_cols + key_cols :].reshape(tok_dev, key_width),
        ],
        axis=1,
    )
    grad_qkv = jnp.dot(normed_one.T, grad_proj, preferred_element_type=jnp.float32)
    grad_normed_one = jnp.dot(grad_proj, qkv_full.T, preferred_element_type=jnp.float32)
    grad_input_norm, grad_gain_attn = norm_backward(grad_normed_one, inputs, scale_one, gain_one)
    grad_input = grad_hidden + grad_input_norm
    packed_grads = jnp.concatenate(
        [
            grad_qkv,
            grad_out,
            grad_router,
            grad_gain_attn[:, None],
            grad_gain_ffn[:, None],
            jnp.zeros((features, 128 - experts_all - 2), jnp.float32),
        ],
        axis=1,
    ).astype(jnp.bfloat16)
    width = packed_grads.shape[1]
    by_owner = jnp.transpose(
        packed_grads.reshape(seq_parts, owners, features // (seq_parts * owners), width),
        (1, 0, 2, 3),
    ).reshape(owners, features // owners, width)
    by_seq = lax.psum_scatter(by_owner, "wshard", scatter_dimension=0, tiled=True)
    by_seq = by_seq.reshape(seq_parts, features // (seq_parts * owners), width)
    own = lax.psum_scatter(by_seq, "seq", scatter_dimension=0, tiled=True)[0].astype(jnp.float32)
    qkv_cols = grad_qkv.shape[1]
    shares = (
        own[:, :qkv_cols],
        own[:, qkv_cols : qkv_cols + features],
        own[:, qkv_cols + features : qkv_cols + features + experts_all],
        own[:, qkv_cols + features + experts_all],
        own[:, qkv_cols + features + experts_all + 1],
    )
    return (
        output.astype(jnp.bfloat16)[None],
        grad_input.astype(jnp.bfloat16)[None],
        shares[0],
        shares[1],
        shares[2],
        shares[3],
        shares[4],
        expert_shares[0],
        expert_shares[1],
        expert_shares[2],
    )


def solution(mesh):
    placed = (
        P("wshard", "seq", None),
        P(("seq", "wshard"), None),
        P(("seq", "wshard"), None),
        P(("seq", "wshard"), None),
        P(("seq", "wshard")),
        P(("seq", "wshard")),
        P("wshard", "seq", None),
        P("wshard", "seq", None),
        P("wshard", "seq", None),
        P("wshard", "seq", None),
        P("wshard", "seq", None),
    )
    return jax.shard_map(
        local,
        mesh=mesh,
        in_specs=placed,
        out_specs=(
            P("wshard", "seq", None),
            P("wshard", "seq", None),
            P(("seq", "wshard"), None),
            P(("seq", "wshard"), None),
            P(("seq", "wshard"), None),
            P(("seq", "wshard")),
            P(("seq", "wshard")),
            P("wshard", "seq", None),
            P("wshard", "seq", None),
            P("wshard", "seq", None),
        ),
        check_vma=False,
    )
```

```python
import jax
import jax.numpy as jnp
from jax import lax
from jax.experimental import pallas as pl
from jax.experimental.pallas import tpu as pltpu
from jax.sharding import PartitionSpec as P

HEADS = 16
KV_HEADS = 8
HEAD_DIM = 64


epsilon = 1e-06
attention_multiplier = 0.015625
residual_multiplier = 0.22
rope_theta = 10000.0


MESH = pl.DeviceIdType.MESH
SIDE = 4


def plane_place(first, offset_first, offset_second):
    mine = lax.axis_index("wshard")
    z, y = mine // SIDE, mine % SIDE
    if first == "y":
        return ((z + offset_second + SIDE) % SIDE, (y + offset_first + SIDE) % SIDE)
    return ((z + offset_first + SIDE) % SIDE, (y + offset_second + SIDE) % SIDE)


def plane_peer(first, offset_first, offset_second):
    z, y = plane_place(first, offset_first, offset_second)
    return {"wshard": z * SIDE + y}


def plane_neighbours():
    return [plane_peer("y", step, 0) for step in (1, -1)] + [
        plane_peer("y", 0, step) for step in (1, -1)
    ]


def seq_peer(offset_x, flip):
    mine = lax.axis_index("seq")
    x, core = mine // 2, mine % 2
    if flip:
        core = 1 - core
    return {"seq": ((x + offset_x) % SIDE) * 2 + core}


def greet(peers):
    barrier = pltpu.get_barrier_semaphore()
    for peer in peers:
        pl.semaphore_signal(barrier, inc=1, device_id=peer, device_id_type=MESH)
    pl.semaphore_wait(barrier, len(peers))


HALVES = (("y", 0), ("z", 2))
ORDER = (0, -1, 1, 2)


def plane_gather(own, view, send, recv, after_row):
    started = []

    def copy(half, kind, source, target, peer):
        return pltpu.make_async_remote_copy(
            src_ref=source,
            dst_ref=target,
            send_sem=send.at[half, kind],
            recv_sem=recv.at[half, kind],
            device_id=peer,
            device_id_type=MESH,
        )

    def push(half, kind, source, target, peer):
        item = copy(half, kind, source, target, peer)
        item.start()
        started.append(item)

    def arrived(half, kind, target):
        first, _ = HALVES[half]
        copy(half, kind, target, target, plane_peer(first, 1, 0)).wait_recv()

    def block(half, along_first, along_second, low, count):
        first, base = HALVES[half]
        z, y = plane_place(first, along_first, along_second)
        return view(z, y, base + low, count)

    def ring(half, slot, axis, along, source):
        first, base = HALVES[half]
        for kind, step in ((0, 1), (1, -1)):
            peer = plane_peer(first, step, 0) if axis == 0 else plane_peer(first, 0, step)
            push(half, 4 * slot + kind, source, block(half, along, 0, 0, 2), peer)

    def ring_relay(half, slot, axis, along):
        first, base = HALVES[half]
        for kind, step in ((0, 1), (1, -1)):
            where = (-step, 0) if axis == 0 else (along, -step)
            arrived(half, 4 * slot + kind, block(half, where[0], where[1], 0, 2))
            part = block(half, where[0], where[1], kind, 1)
            peer = plane_peer(first, step, 0) if axis == 0 else plane_peer(first, 0, step)
            push(half, 4 * slot + 2 + kind, part, part, peer)

    def ring_end(half, slot, axis, along):
        where = (2, 0) if axis == 0 else (along, 2)
        for kind in (0, 1):
            arrived(half, 4 * slot + 2 + kind, block(half, where[0], where[1], kind, 1))

    for half in (0, 1):
        ring(half, 0, 0, 0, own(HALVES[half][1], 2))
    for half in (0, 1):
        ring(half, 1, 1, 0, own(HALVES[half][1], 2))
    for half in (0, 1):
        ring_relay(half, 0, 0, 0)
        for slot in (1, 2):
            ring(half, 1 + slot, 1, ORDER[slot], block(half, ORDER[slot], 0, 0, 2))
    for half in (0, 1):
        ring_end(half, 0, 0, 0)
        ring(half, 4, 1, 2, block(half, 2, 0, 0, 2))
        after_row(half, 0)
    for slot in (0, 1, 2, 3):
        for half in (0, 1):
            ring_relay(half, 1 + slot, 1, ORDER[slot])
    for half in (0, 1):
        after_row(half, -1)
        after_row(half, 1)
    for half in (0, 1):
        for slot in (0, 1, 2, 3):
            ring_end(half, 1 + slot, 1, ORDER[slot])
        after_row(half, 2)
    for item in started:
        item.wait_send()


def plane_reduce(parts, far, near, far_last, near_last, send, recv, store):
    started = []

    def copy(half, kind, source, target, peer):
        return pltpu.make_async_remote_copy(
            src_ref=source,
            dst_ref=target,
            send_sem=send.at[half, kind],
            recv_sem=recv.at[half, kind],
            device_id=peer,
            device_id_type=MESH,
        )

    def push(half, kind, source, target, peer):
        item = copy(half, kind, source, target, peer)
        item.start()
        started.append(item)

    def arrived(half, kind, target):
        first, _ = HALVES[half]
        copy(half, kind, target, target, plane_peer(first, 1, 0)).wait_recv()

    def rows(half, offset, low, count):
        first, base = HALVES[half]
        z, y = plane_place(first, 0, offset)
        if first == "y":
            return parts.at[z, :, pl.ds(base + low, count)]
        return parts.at[:, y, pl.ds(base + low, count)]

    def one(half, offset, low, count):
        first, base = HALVES[half]
        z, y = plane_place(first, offset, 0)
        return parts.at[z, y, pl.ds(base + low, count)]

    def add(target, *others):
        total = target[...].astype(jnp.float32)
        for other in others:
            total = total + other[...].astype(jnp.float32)
        target[...] = total.astype(target.dtype)

    def add_rows(half, offset, low, count, *others):
        target = rows(half, offset, low, count)
        def step(at, carry):
            add(target.at[at], *[other.at[at] for other in others])
            return carry
        lax.fori_loop(0, SIDE, step, 0)

    def peer(half, axis, step):
        first, _ = HALVES[half]
        return plane_peer(first, 0, step) if axis == 1 else plane_peer(first, step, 0)

    for half in (0, 1):
        push(half, 0, rows(half, 2, 0, 1), far.at[half, 0], peer(half, 1, 1))
        push(half, 1, rows(half, 2, 1, 1), far.at[half, 1], peer(half, 1, -1))
    for half in (0, 1):
        push(half, 2, rows(half, 1, 1, 1), near.at[half, 0, :, pl.ds(1, 1)], peer(half, 1, 1))
        push(half, 3, rows(half, -1, 0, 1), near.at[half, 1, :, pl.ds(0, 1)], peer(half, 1, -1))
    for half in (0, 1):
        arrived(half, 0, far.at[half, 0])
        add_rows(half, 1, 0, 1, far.at[half, 0])
        push(half, 4, rows(half, 1, 0, 1), near.at[half, 0, :, pl.ds(0, 1)], peer(half, 1, 1))
        arrived(half, 1, far.at[half, 1])
        add_rows(half, -1, 1, 1, far.at[half, 1])
        push(half, 5, rows(half, -1, 1, 1), near.at[half, 1, :, pl.ds(1, 1)], peer(half, 1, -1))
    for half in (0, 1):
        arrived(half, 2, near.at[half, 0, :, pl.ds(1, 1)])
        arrived(half, 3, near.at[half, 1, :, pl.ds(0, 1)])
        arrived(half, 4, near.at[half, 0, :, pl.ds(0, 1)])
        arrived(half, 5, near.at[half, 1, :, pl.ds(1, 1)])
        add_rows(half, 0, 0, 2, near.at[half, 0], near.at[half, 1])
        push(half, 6, one(half, 2, 0, 1), far_last.at[half, 0], peer(half, 0, 1))
        push(half, 7, one(half, 2, 1, 1), far_last.at[half, 1], peer(half, 0, -1))
        push(half, 8, one(half, 1, 1, 1), near_last.at[half, 0, pl.ds(1, 1)], peer(half, 0, 1))
        push(half, 9, one(half, -1, 0, 1), near_last.at[half, 1, pl.ds(0, 1)], peer(half, 0, -1))
    for half in (0, 1):
        arrived(half, 6, far_last.at[half, 0])
        add(one(half, 1, 0, 1), far_last.at[half, 0])
        push(half, 10, one(half, 1, 0, 1), near_last.at[half, 0, pl.ds(0, 1)], peer(half, 0, 1))
        arrived(half, 7, far_last.at[half, 1])
        add(one(half, -1, 1, 1), far_last.at[half, 1])
        push(half, 11, one(half, -1, 1, 1), near_last.at[half, 1, pl.ds(1, 1)], peer(half, 0, -1))
    for half in (0, 1):
        arrived(half, 8, near_last.at[half, 0, pl.ds(1, 1)])
        arrived(half, 9, near_last.at[half, 1, pl.ds(0, 1)])
        arrived(half, 10, near_last.at[half, 0, pl.ds(0, 1)])
        arrived(half, 11, near_last.at[half, 1, pl.ds(1, 1)])
        total = one(half, 0, 0, 2)[...].astype(jnp.float32)
        for side in (0, 1):
            total = total + near_last[half, side].astype(jnp.float32)
        store(HALVES[half][1], total)
    for item in started:
        item.wait_send()


def reduce_scratch(quarter_rows, width):
    unit = (quarter_rows, width)
    return [
        pltpu.VMEM((SIDE, SIDE, 4) + unit, jnp.bfloat16),
        pltpu.VMEM((2, 2, SIDE, 1) + unit, jnp.bfloat16),
        pltpu.VMEM((2, 2, SIDE, 2) + unit, jnp.bfloat16),
        pltpu.VMEM((2, 2, 1) + unit, jnp.bfloat16),
        pltpu.VMEM((2, 2, 2) + unit, jnp.bfloat16),
        pltpu.SemaphoreType.DMA((2, 12)),
        pltpu.SemaphoreType.DMA((2, 12)),
    ]


def comm_params(number, limit_mb):
    return pltpu.CompilerParams(
        collective_id=number, has_side_effects=True, vmem_limit_bytes=limit_mb * 1024 * 1024
    )


def nothing(half, offset):
    return None


def token_gather(block, number):
    rows, width = block.shape

    def kernel(own_ref, out_ref, send, recv, local_sem):
        greet(plane_neighbours())
        z, y = plane_place("y", 0, 0)
        keep = pltpu.make_async_copy(own_ref, out_ref.at[z, y], local_sem)
        keep.start()
        plane_gather(
            lambda low, count: own_ref.at[pl.ds(low, count)],
            lambda z, y, low, count: out_ref.at[z, y, pl.ds(low, count)],
            send,
            recv,
            nothing,
        )
        keep.wait()

    out = pl.pallas_call(
        kernel,
        out_shape=jax.ShapeDtypeStruct((SIDE, SIDE, 4, rows // 4, width), block.dtype),
        in_specs=[pl.BlockSpec(memory_space=pl.ANY)],
        out_specs=pl.BlockSpec(memory_space=pl.ANY),
        scratch_shapes=[
            pltpu.SemaphoreType.DMA((2, 20)),
            pltpu.SemaphoreType.DMA((2, 20)),
            pltpu.SemaphoreType.DMA,
        ],
        compiler_params=comm_params(number, 8),
        name="token_gather",
    )(block.reshape(4, rows // 4, width))
    return out.reshape(SIDE * SIDE, rows, width)


def token_reduce(pieces, number):
    owners, rows, _ = pieces[0].shape
    widths = [piece.shape[2] for piece in pieces]
    width = sum(widths)
    quarter = rows // 4

    def kernel(*refs):
        ins, out_ref, rest = refs[: len(widths)], refs[len(widths)], refs[len(widths) + 1 :]
        parts, far, near, far_last, near_last, send, recv, load = rest
        loads, at = [], 0
        for i, one_width in enumerate(widths):
            loads.append(
                pltpu.make_async_copy(
                    ins[i], parts.at[:, :, :, :, pl.ds(at, one_width)], load.at[i]
                )
            )
            loads[-1].start()
            at += one_width
        greet(plane_neighbours())
        for item in loads:
            item.wait()

        def store(low, total):
            out_ref[pl.ds(low, 2)] = total

        plane_reduce(parts, far, near, far_last, near_last, send, recv, store)

    out = pl.pallas_call(
        kernel,
        out_shape=jax.ShapeDtypeStruct((4, quarter, width), jnp.float32),
        in_specs=[pl.BlockSpec(memory_space=pl.ANY)] * len(widths),
        out_specs=pl.BlockSpec(memory_space=pltpu.VMEM),
        scratch_shapes=reduce_scratch(quarter, width) + [pltpu.SemaphoreType.DMA((len(widths),))],
        compiler_params=comm_params(number, 32),
        name="token_reduce",
    )(*[piece.reshape(SIDE, SIDE, 4, quarter, piece.shape[2]) for piece in pieces])
    return out.reshape(rows, width)


def weights_gather(piece, number):
    rows, width = piece.shape

    def kernel(own_ref, out_ref, send, recv, x_send, x_recv, core_send, core_recv, local_sem):
        seq = lax.axis_index("seq")
        x, core = seq // 2, seq % 2
        x_peers = [seq_peer(step, False) for step in (1, 3, 2)]
        other = seq_peer(0, True)
        greet(plane_neighbours() + x_peers + [other])
        z, y = plane_place("y", 0, 0)
        keep = pltpu.make_async_copy(own_ref, out_ref.at[x, core, z, y], local_sem)
        keep.start()
        sends = []
        for i, step in enumerate((1, 3, 2)):
            item = pltpu.make_async_remote_copy(
                src_ref=own_ref,
                dst_ref=out_ref.at[x, core, z, y],
                send_sem=x_send.at[i],
                recv_sem=x_recv.at[i],
                device_id=x_peers[i],
                device_id_type=MESH,
            )
            item.start()
            sends.append(item)
        keep.wait()
        for i, step in enumerate((1, 3, 2)):
            came = out_ref.at[(x + SIDE - step) % SIDE, core, z, y]
            pltpu.make_async_remote_copy(
                src_ref=came,
                dst_ref=came,
                send_sem=x_send.at[i],
                recv_sem=x_recv.at[i],
                device_id=x_peers[i],
                device_id_type=MESH,
            ).wait_recv()

        swaps = []

        def swap(half, offset):
            first, base = HALVES[half]
            z, y = plane_place(first, 0, offset)
            mine = (
                out_ref.at[pl.ds(base, 2), core, z]
                if first == "y"
                else out_ref.at[pl.ds(base, 2), core, :, y]
            )
            theirs = (
                out_ref.at[pl.ds(base, 2), 1 - core, z]
                if first == "y"
                else out_ref.at[pl.ds(base, 2), 1 - core, :, y]
            )
            kind = ORDER.index(offset)
            item = pltpu.make_async_remote_copy(
                src_ref=mine,
                dst_ref=mine,
                send_sem=core_send.at[half, kind],
                recv_sem=core_recv.at[half, kind],
                device_id=other,
                device_id_type=MESH,
            )
            item.start()
            sends.append(item)
            swaps.append(
                pltpu.make_async_remote_copy(
                    src_ref=theirs,
                    dst_ref=theirs,
                    send_sem=core_send.at[half, kind],
                    recv_sem=core_recv.at[half, kind],
                    device_id=other,
                    device_id_type=MESH,
                )
            )

        plane_gather(
            lambda low, count: out_ref.at[pl.ds(low, count), core, z, y],
            lambda z, y, low, count: out_ref.at[pl.ds(low, count), core, z, y],
            send,
            recv,
            swap,
        )
        for item in swaps:
            item.wait_recv()
        for item in sends:
            item.wait_send()

    out = pl.pallas_call(
        kernel,
        out_shape=jax.ShapeDtypeStruct((4, 2, SIDE, SIDE, rows, width), piece.dtype),
        in_specs=[pl.BlockSpec(memory_space=pl.ANY)],
        out_specs=pl.BlockSpec(memory_space=pl.ANY),
        scratch_shapes=[
            pltpu.SemaphoreType.DMA((2, 20)),
            pltpu.SemaphoreType.DMA((2, 20)),
            pltpu.SemaphoreType.DMA((3,)),
            pltpu.SemaphoreType.DMA((3,)),
            pltpu.SemaphoreType.DMA((2, 4)),
            pltpu.SemaphoreType.DMA((2, 4)),
            pltpu.SemaphoreType.DMA,
        ],
        compiler_params=comm_params(number, 8),
        name="weights_gather",
    )(piece)
    return out.reshape(4 * 2 * SIDE * SIDE * rows, width)


def weights_reduce(pieces, number):
    widths = [piece.shape[1] for piece in pieces]
    width = sum(widths)
    rows = pieces[0].shape[0] // (4 * 2 * SIDE * SIDE)

    def kernel(*refs):
        ins, out_ref, rest = refs[: len(widths)], refs[len(widths)], refs[len(widths) + 1 :]
        (parts, far, near, far_last, near_last, send, recv, twin, mine, from_x, load, core_send,
         core_recv, x_send, x_recv) = rest
        seq = lax.axis_index("seq")
        x, core = seq // 2, seq % 2
        x_peers = [seq_peer(step, False) for step in (1, 3, 2)]
        other = seq_peer(0, True)
        loads = []
        for quarter in range(4):
            at = 0
            for i, one_width in enumerate(widths):
                item = pltpu.make_async_copy(
                    ins[i].at[quarter, core],
                    parts.at[:, :, quarter, :, pl.ds(at, one_width)],
                    load.at[quarter, i],
                )
                item.start()
                loads.append(item)
                at += one_width
        greet(plane_neighbours() + x_peers + [other])
        swaps = []
        for quarter in range(4):
            at = 0
            for i, one_width in enumerate(widths):
                item = pltpu.make_async_remote_copy(
                    src_ref=ins[i].at[quarter, 1 - core],
                    dst_ref=twin.at[quarter, :, :, :, pl.ds(at, one_width)],
                    send_sem=core_send.at[quarter, i],
                    recv_sem=core_recv.at[quarter, i],
                    device_id=other,
                    device_id_type=MESH,
                )
                item.start()
                swaps.append(item)
                at += one_width
        for quarter in range(4):
            for i in range(len(widths)):
                loads[quarter * len(widths) + i].wait()
                swaps[quarter * len(widths) + i].wait_recv()

            def add(at, carry):
                z, y = at // SIDE, at % SIDE
                parts[z, y, quarter] = (
                    parts[z, y, quarter].astype(jnp.float32)
                    + twin[quarter, z, y].astype(jnp.float32)
                ).astype(parts.dtype)
                return carry

            lax.fori_loop(0, SIDE * SIDE, add, 0)

        def store(low, total):
            mine[pl.ds(low, 2)] = total.astype(mine.dtype)

        plane_reduce(parts, far, near, far_last, near_last, send, recv, store)
        sends = []
        for i, step in enumerate((1, 3, 2)):
            item = pltpu.make_async_remote_copy(
                src_ref=mine.at[(x + step) % SIDE],
                dst_ref=from_x.at[i],
                send_sem=x_send.at[i],
                recv_sem=x_recv.at[i],
                device_id=x_peers[i],
                device_id_type=MESH,
            )
            item.start()
            sends.append(item)
        total = mine[x].astype(jnp.float32)
        for i in range(3):
            sends[i].wait_recv()
            total = total + from_x[i].astype(jnp.float32)
        out_ref[...] = total
        for item in sends + swaps:
            item.wait_send()

    unit = (rows, width)
    pairs = (4, len(widths))
    return pl.pallas_call(
        kernel,
        out_shape=jax.ShapeDtypeStruct(unit, jnp.float32),
        in_specs=[pl.BlockSpec(memory_space=pl.ANY)] * len(widths),
        out_specs=pl.BlockSpec(memory_space=pltpu.VMEM),
        scratch_shapes=reduce_scratch(rows, width)
        + [
            pltpu.VMEM((4, SIDE, SIDE) + unit, jnp.bfloat16),
            pltpu.VMEM((4,) + unit, jnp.bfloat16),
            pltpu.VMEM((3,) + unit, jnp.bfloat16),
            pltpu.SemaphoreType.DMA(pairs),
            pltpu.SemaphoreType.DMA(pairs),
            pltpu.SemaphoreType.DMA(pairs),
            pltpu.SemaphoreType.DMA((3,)),
            pltpu.SemaphoreType.DMA((3,)),
        ],
        compiler_params=comm_params(number, 40),
        name="weights_reduce",
    )(*[piece.reshape(4, 2, SIDE, SIDE, rows, piece.shape[1]) for piece in pieces])


def rms_scale(values):
    return lax.rsqrt(jnp.mean(values * values, axis=-1, keepdims=True) + epsilon)


def rotate(heads_in, positions, direction):
    half_dim = heads_in.shape[-1] // 2
    frequency = rope_theta ** (-jnp.arange(half_dim, dtype=jnp.float32) / half_dim)
    angles = positions.astype(jnp.float32)[:, None] * frequency[None, :]
    cosine = jnp.cos(angles)[:, None, :]
    sine_of = direction * jnp.sin(angles)[:, None, :]
    leading = heads_in[..., :half_dim]
    second = heads_in[..., half_dim:]
    return jnp.concatenate(
        [leading * cosine - second * sine_of, second * cosine + leading * sine_of], axis=-1
    )


def attend_forward(queries, keys_all, values_all):
    length, heads_dev, head_size = queries.shape
    key_heads = keys_all.shape[1]
    group_size = heads_dev // key_heads
    block_rows = min(512, length)
    block_count = length // block_rows
    grouped = queries.reshape(block_count, block_rows, key_heads, group_size, head_size)
    starts = jnp.arange(block_count, dtype=jnp.int32) * block_rows
    key_pos = jnp.arange(length, dtype=jnp.int32)

    def one_block(operands):
        rows_in, offset = operands
        scores = attention_multiplier * jnp.einsum(
            "qhrd,khd->hrqk", rows_in, keys_all, preferred_element_type=jnp.float32
        )
        allowed = key_pos[None, :] <= (offset + jnp.arange(block_rows, dtype=jnp.int32))[:, None]
        scores = jnp.where(allowed, scores, -1e30)
        peak_score = jnp.max(scores, axis=-1, keepdims=True)
        exponent = jnp.exp(scores - peak_score)
        total = jnp.sum(exponent, axis=-1, keepdims=True)
        weights = (exponent / total).astype(jnp.bfloat16)
        blended = jnp.einsum(
            "hrqk,khd->qhrd", weights, values_all, preferred_element_type=jnp.float32
        )
        return (
            blended.reshape(block_rows, heads_dev * head_size),
            (peak_score + jnp.log(total))[..., 0],
        )

    blended, logsum = lax.map(one_block, (grouped, starts))
    return (blended.reshape(length, heads_dev * head_size), logsum)


def attend_backward(queries, keys_all, values_all, grads_out, logsum):
    length, heads_dev, head_size = queries.shape
    key_heads = keys_all.shape[1]
    group_size = heads_dev // key_heads
    block_rows = min(512, length)
    block_count = length // block_rows
    grouped = queries.reshape(block_count, block_rows, key_heads, group_size, head_size)
    grads_grouped = grads_out.reshape(block_count, block_rows, key_heads, group_size, head_size)
    starts = jnp.arange(block_count, dtype=jnp.int32) * block_rows
    key_pos = jnp.arange(length, dtype=jnp.int32)

    def one_block(carry, operands):
        rows_in, grads_in, block_lse, offset = operands
        scores = attention_multiplier * jnp.einsum(
            "qhrd,khd->hrqk", rows_in, keys_all, preferred_element_type=jnp.float32
        )
        allowed = key_pos[None, :] <= (offset + jnp.arange(block_rows, dtype=jnp.int32))[:, None]
        weights = jnp.where(allowed, jnp.exp(scores - block_lse[..., None]), 0.0)
        grad_weights = jnp.einsum(
            "qhrd,khd->hrqk", grads_in, values_all, preferred_element_type=jnp.float32
        )
        center = jnp.sum(weights * grad_weights, axis=-1, keepdims=True)
        grad_scores = (weights * (grad_weights - center)).astype(jnp.bfloat16)
        grad_rows = attention_multiplier * jnp.einsum(
            "hrqk,khd->qhrd", grad_scores, keys_all, preferred_element_type=jnp.float32
        )
        grad_keys = carry[0] + attention_multiplier * jnp.einsum(
            "hrqk,qhrd->khd", grad_scores, rows_in, preferred_element_type=jnp.float32
        )
        grad_values = carry[1] + jnp.einsum(
            "hrqk,qhrd->khd",
            weights.astype(jnp.bfloat16),
            grads_in,
            preferred_element_type=jnp.float32,
        )
        return ((grad_keys, grad_values), grad_rows.reshape(block_rows, heads_dev, head_size))

    zeros_kv = jnp.zeros((length, key_heads, head_size), jnp.float32)
    totals, grad_queries = lax.scan(
        one_block, (zeros_kv, zeros_kv), (grouped, grads_grouped, logsum, starts)
    )
    return (grad_queries.reshape(length, heads_dev, head_size), totals[0], totals[1])


def dense_gates(logits, chosen_ids, experts_all):
    named = jnp.any(
        chosen_ids[..., None] == jnp.arange(experts_all, dtype=jnp.int32), axis=-2
    )
    peak = jnp.max(jnp.where(named, logits, -jnp.inf), axis=-1, keepdims=True)
    exponent = jnp.where(named, jnp.exp(logits - peak), 0.0)
    return (named, exponent / jnp.sum(exponent, axis=-1, keepdims=True))


def norm_backward(grad_normed, values, scale, gain_full):
    grad_gain = jnp.sum(grad_normed * values * scale, axis=0)
    grad_hat = grad_normed * gain_full
    grad_values = scale * grad_hat - values * (scale * scale * scale) * jnp.mean(
        grad_hat * values, axis=1, keepdims=True
    )
    return (grad_values, grad_gain)


def local(
    tokens,
    weight_qkv,
    weight_out,
    router,
    gain_attn,
    gain_ffn,
    expert_gate,
    expert_up,
    expert_down,
    expert_ids,
    cotangent,
):
    tok_dev = tokens.shape[1]
    features = tokens.shape[2]
    seq_parts = lax.axis_size("seq")
    owners = lax.axis_size("wshard")
    local_experts = expert_gate.shape[0]
    experts_all = local_experts * owners
    top_count = expert_ids.shape[2]
    capacity = 2 * tok_dev * top_count // experts_all
    heads_dev = HEADS // seq_parts
    key_heads = KV_HEADS // seq_parts
    query_cols = heads_dev * HEAD_DIM
    key_cols = key_heads * HEAD_DIM
    query_width = HEADS * HEAD_DIM
    key_width = KV_HEADS * HEAD_DIM
    length = tok_dev * seq_parts
    weights_own = jnp.concatenate(
        [
            weight_qkv,
            weight_out,
            router,
            gain_attn[:, None],
            gain_ffn[:, None],
            jnp.zeros((router.shape[0], 128 - experts_all - 2), jnp.bfloat16),
        ],
        axis=1,
    )
    weights_full = weights_gather(weights_own, 0)
    qkv_width = weight_qkv.shape[1]
    qkv_full = weights_full[:, :qkv_width]
    out_full = weights_full[:, qkv_width : qkv_width + features]
    smalls_full = weights_full[:, qkv_width + features :]
    router_full = smalls_full[:, :experts_all]
    gain_one = smalls_full[:, experts_all].astype(jnp.float32)
    gain_two = smalls_full[:, experts_all + 1].astype(jnp.float32)
    ids_all = lax.all_gather(expert_ids[0], "wshard", axis=0)
    cot_all = lax.all_gather(cotangent[0], "wshard", axis=0)
    owned = (
        lax.all_gather(expert_gate, "seq", axis=1, tiled=True),
        lax.all_gather(expert_up, "seq", axis=1, tiled=True),
        lax.all_gather(expert_down, "seq", axis=1, tiled=True),
    )
    gate_full, up_full, down_full = (owned[0], owned[1], owned[2])
    inputs = tokens[0].astype(jnp.float32)
    chosen_ids = expert_ids[0]
    scale_one = rms_scale(inputs)
    normed_one = (inputs * scale_one * gain_one).astype(jnp.bfloat16)
    projected = jnp.dot(normed_one, qkv_full, preferred_element_type=jnp.float32)
    positions = lax.axis_index("seq") * tok_dev + jnp.arange(tok_dev, dtype=jnp.int32)
    queries = rotate(projected[:, :query_width].reshape(tok_dev, HEADS, HEAD_DIM), positions, 1.0)
    keys_tok = rotate(
        projected[:, query_width : query_width + key_width].reshape(tok_dev, KV_HEADS, HEAD_DIM),
        positions,
        1.0,
    )
    values_tok = projected[:, query_width + key_width :]
    packed = jnp.concatenate(
        [
            queries.reshape(tok_dev, seq_parts, query_cols),
            keys_tok,
            values_tok.reshape(tok_dev, seq_parts, key_cols),
        ],
        axis=2,
    ).astype(jnp.bfloat16)
    heads_all = lax.all_to_all(packed, "seq", split_axis=1, concat_axis=0, tiled=True)
    head_queries = heads_all[:, 0, :query_cols].reshape(length, heads_dev, HEAD_DIM)
    head_keys = heads_all[:, 0, query_cols : query_cols + key_cols].reshape(
        length, key_heads, HEAD_DIM
    )
    head_values = heads_all[:, 0, query_cols + key_cols :].reshape(length, key_heads, HEAD_DIM)
    blended, logsum = attend_forward(head_queries, head_keys, head_values)
    returned_heads = lax.all_to_all(
        blended.astype(jnp.bfloat16).reshape(length, 1, query_cols),
        "seq",
        split_axis=0,
        concat_axis=1,
        tiled=True,
    )
    attended = returned_heads.reshape(tok_dev, query_width)
    branch = jnp.dot(attended, out_full, preferred_element_type=jnp.float32)
    hidden = inputs + residual_multiplier * branch
    scale_two = rms_scale(hidden)
    normed_two = (hidden * scale_two * gain_two).astype(jnp.bfloat16)
    logits = jnp.dot(normed_two, router_full, preferred_element_type=jnp.float32)
    _, gates_own = dense_gates(logits, chosen_ids, experts_all)
    normed_all = token_gather(normed_two, 1)
    logits_all = jnp.einsum(
        "std,de->ste", normed_all, router_full, preferred_element_type=jnp.float32
    )
    named_all, gates_all = dense_gates(logits_all, ids_all, experts_all)
    first_expert = lax.axis_index("wshard") * local_experts
    named = lax.dynamic_slice_in_dim(named_all, first_expert, local_experts, axis=2)
    gates_mine = lax.dynamic_slice_in_dim(gates_all, first_expert, local_experts, axis=2)
    lower = jnp.tril(jnp.ones((tok_dev, tok_dev), jnp.bfloat16))
    places = jnp.einsum(
        "ut,ste->seu", lower, named.astype(jnp.bfloat16), preferred_element_type=jnp.float32
    ).astype(jnp.int32) - 1
    picks = (
        places[:, :, None, :] == jnp.arange(capacity, dtype=jnp.int32)[None, None, :, None]
    ) & jnp.transpose(named, (0, 2, 1))[:, :, None, :]
    picks = jnp.transpose(picks, (1, 0, 2, 3))
    pick = picks.astype(jnp.bfloat16)
    row_gate = jnp.sum(
        jnp.where(picks, jnp.transpose(gates_mine, (2, 0, 1))[:, :, None, :], 0.0), axis=-1
    ).reshape(local_experts, owners * capacity)
    received = (
        jnp.einsum("esct,std->escd", pick, normed_all, preferred_element_type=jnp.float32)
        .astype(jnp.bfloat16)
        .reshape(local_experts, owners * capacity, features)
    )
    cot_rows = (
        jnp.einsum("esct,std->escd", pick, cot_all, preferred_element_type=jnp.float32)
        .astype(jnp.bfloat16)
        .reshape(local_experts, owners * capacity, features)
    )
    gate_val = jnp.einsum("erd,edf->erf", received, gate_full, preferred_element_type=jnp.float32)
    up_val = jnp.einsum("erd,edf->erf", received, up_full, preferred_element_type=jnp.float32)
    sigma = jax.nn.sigmoid(gate_val)
    activated = gate_val * sigma
    inner_act = (activated * up_val).astype(jnp.bfloat16)
    produced = jnp.einsum(
        "erf,efd->erd", inner_act, down_full, preferred_element_type=jnp.float32
    ).astype(jnp.bfloat16)
    grad_mix_rows = residual_multiplier * cot_rows.astype(jnp.float32)
    weighted = (row_gate[:, :, None] * produced).astype(jnp.bfloat16)
    mix_part = jnp.einsum(
        "esct,escd->std",
        pick,
        weighted.reshape(local_experts, owners, capacity, features),
        preferred_element_type=jnp.float32,
    ).astype(jnp.bfloat16)
    grad_gate_rows = jnp.sum(produced * grad_mix_rows, axis=-1).reshape(
        local_experts, owners, capacity
    )
    gate_part = jnp.sum(
        jnp.where(picks, grad_gate_rows[:, :, :, None], 0.0), axis=2
    )
    gate_part = jnp.transpose(gate_part, (1, 2, 0))
    coarse = lax.reduce_precision(gate_part, 8, 7)
    fine = gate_part - coarse
    column = jnp.arange(128, dtype=jnp.int32)
    gate_cols = sum(
        jnp.where(column == first_expert + j, coarse[:, :, j : j + 1], 0.0)
        + jnp.where(column == experts_all + first_expert + j, fine[:, :, j : j + 1], 0.0)
        for j in range(local_experts)
    ).astype(jnp.bfloat16)
    mixture = token_reduce([mix_part], 2)
    output = hidden + residual_multiplier * mixture
    grad_output = cotangent[0].astype(jnp.float32)
    grad_received = (row_gate[:, :, None] * grad_mix_rows).astype(jnp.bfloat16)
    grad_inner = jnp.einsum(
        "erd,efd->erf", grad_received, down_full, preferred_element_type=jnp.float32
    )
    grad_down = jnp.einsum(
        "erf,erd->efd", inner_act, grad_received, preferred_element_type=jnp.float32
    )
    grad_gate_val = (grad_inner * up_val * (sigma * (1.0 + gate_val * (1.0 - sigma)))).astype(
        jnp.bfloat16
    )
    grad_up_val = (grad_inner * activated).astype(jnp.bfloat16)
    grad_rows = (
        jnp.einsum("erf,edf->erd", grad_gate_val, gate_full, preferred_element_type=jnp.float32)
        + jnp.einsum("erf,edf->erd", grad_up_val, up_full, preferred_element_type=jnp.float32)
    ).astype(jnp.bfloat16)
    rows_part = jnp.einsum(
        "esct,escd->std",
        pick,
        grad_rows.reshape(local_experts, owners, capacity, features),
        preferred_element_type=jnp.float32,
    ).astype(jnp.bfloat16)
    back = token_reduce([rows_part, gate_cols], 3)
    grad_back = back[:, :features]
    grad_gates = (
        back[:, features : features + experts_all]
        + back[:, features + experts_all : features + 2 * experts_all]
    )
    grad_logits = (
        gates_own
        * (grad_gates - jnp.sum(gates_own * grad_gates, axis=1, keepdims=True))
    ).astype(jnp.bfloat16)
    grad_router = jnp.dot(normed_two.T, grad_logits, preferred_element_type=jnp.float32)
    grad_normed_two = jnp.dot(grad_logits, router_full.T, preferred_element_type=jnp.float32)
    grad_gate = jnp.einsum(
        "erd,erf->edf", received, grad_gate_val, preferred_element_type=jnp.float32
    )
    grad_up = jnp.einsum("erd,erf->edf", received, grad_up_val, preferred_element_type=jnp.float32)
    expert_shares = (
        lax.psum_scatter(
            grad_gate.astype(jnp.bfloat16), "seq", scatter_dimension=1, tiled=True
        ).astype(jnp.float32),
        lax.psum_scatter(
            grad_up.astype(jnp.bfloat16), "seq", scatter_dimension=1, tiled=True
        ).astype(jnp.float32),
        lax.psum_scatter(
            grad_down.astype(jnp.bfloat16), "seq", scatter_dimension=1, tiled=True
        ).astype(jnp.float32),
    )
    grad_normed_two = grad_normed_two + grad_back
    grad_hidden_norm, grad_gain_ffn = norm_backward(grad_normed_two, hidden, scale_two, gain_two)
    grad_hidden = grad_output + grad_hidden_norm
    grad_branch = (residual_multiplier * grad_hidden).astype(jnp.bfloat16)
    grad_out = jnp.dot(attended.T, grad_branch, preferred_element_type=jnp.float32)
    grad_attended = jnp.dot(grad_branch, out_full.T, preferred_element_type=jnp.float32).astype(
        jnp.bfloat16
    )
    grad_heads = lax.all_to_all(
        grad_attended.reshape(tok_dev, seq_parts, query_cols),
        "seq",
        split_axis=1,
        concat_axis=0,
        tiled=True,
    )
    grad_heads = grad_heads.reshape(length, heads_dev, HEAD_DIM)
    grad_queries, grad_keys, grad_values = attend_backward(
        head_queries, head_keys, head_values, grad_heads, logsum
    )
    head_pos = jnp.arange(length, dtype=jnp.int32)
    grad_queries = rotate(grad_queries, head_pos, -1.0)
    grad_keys = rotate(grad_keys, head_pos, -1.0)
    grad_packed = jnp.concatenate(
        [
            grad_queries.reshape(length, query_cols),
            grad_keys.reshape(length, key_cols),
            grad_values.reshape(length, key_cols),
        ],
        axis=1,
    ).astype(jnp.bfloat16)
    grad_parts = lax.all_to_all(
        grad_packed.reshape(length, 1, query_cols + 2 * key_cols),
        "seq",
        split_axis=0,
        concat_axis=1,
        tiled=True,
    )
    grad_proj = jnp.concatenate(
        [
            grad_parts[:, :, :query_cols].reshape(tok_dev, query_width),
            grad_parts[:, :, query_cols : query_cols + key_cols].reshape(tok_dev, key_width),
            grad_parts[:, :, query_cols + key_cols :].reshape(tok_dev, key_width),
        ],
        axis=1,
    )
    grad_qkv = jnp.dot(normed_one.T, grad_proj, preferred_element_type=jnp.float32)
    grad_normed_one = jnp.dot(grad_proj, qkv_full.T, preferred_element_type=jnp.float32)
    grad_input_norm, grad_gain_attn = norm_backward(grad_normed_one, inputs, scale_one, gain_one)
    grad_input = grad_hidden + grad_input_norm
    packed_grads = jnp.concatenate(
        [
            grad_out,
            grad_router,
            grad_gain_attn[:, None],
            grad_gain_ffn[:, None],
            jnp.zeros((features, 128 - experts_all - 2), jnp.float32),
        ],
        axis=1,
    ).astype(jnp.bfloat16)
    own = weights_reduce([grad_qkv.astype(jnp.bfloat16), packed_grads], 4)
    qkv_cols = grad_qkv.shape[1]
    shares = (
        own[:, :qkv_cols],
        own[:, qkv_cols : qkv_cols + features],
        own[:, qkv_cols + features : qkv_cols + features + experts_all],
        own[:, qkv_cols + features + experts_all],
        own[:, qkv_cols + features + experts_all + 1],
    )
    return (
        output.astype(jnp.bfloat16)[None],
        grad_input.astype(jnp.bfloat16)[None],
        shares[0],
        shares[1],
        shares[2],
        shares[3],
        shares[4],
        expert_shares[0],
        expert_shares[1],
        expert_shares[2],
    )


def solution(mesh):
    placed = (
        P("wshard", "seq", None),
        P(("seq", "wshard"), None),
        P(("seq", "wshard"), None),
        P(("seq", "wshard"), None),
        P(("seq", "wshard")),
        P(("seq", "wshard")),
        P("wshard", "seq", None),
        P("wshard", "seq", None),
        P("wshard", "seq", None),
        P("wshard", "seq", None),
        P("wshard", "seq", None),
    )
    return jax.shard_map(
        local,
        mesh=mesh,
        in_specs=placed,
        out_specs=(
            P("wshard", "seq", None),
            P("wshard", "seq", None),
            P(("seq", "wshard"), None),
            P(("seq", "wshard"), None),
            P(("seq", "wshard"), None),
            P(("seq", "wshard")),
            P(("seq", "wshard")),
            P("wshard", "seq", None),
            P("wshard", "seq", None),
            P("wshard", "seq", None),
        ),
        check_vma=False,
    )
```

```python
import jax
import jax.numpy as jnp
import numpy as np
from jax import lax
from jax.experimental import pallas as pl
from jax.experimental.pallas import tpu as pltpu
from jax.sharding import PartitionSpec as P

HEADS = 16
KV_HEADS = 8
HEAD_DIM = 64


epsilon = 1e-06
attention_multiplier = 0.015625
residual_multiplier = 0.22
rope_theta = 10000.0


MESH = pl.DeviceIdType.MESH
SIDE = 4


def plane_place(first, offset_first, offset_second):
    mine = lax.axis_index("wshard")
    z, y = mine // SIDE, mine % SIDE
    if first == "y":
        return ((z + offset_second + SIDE) % SIDE, (y + offset_first + SIDE) % SIDE)
    return ((z + offset_first + SIDE) % SIDE, (y + offset_second + SIDE) % SIDE)


def plane_peer(first, offset_first, offset_second):
    z, y = plane_place(first, offset_first, offset_second)
    return {"wshard": z * SIDE + y}


def plane_neighbours():
    return [plane_peer("y", step, 0) for step in (1, -1)] + [
        plane_peer("y", 0, step) for step in (1, -1)
    ]


def seq_peer(offset_x, flip):
    mine = lax.axis_index("seq")
    x, core = mine // 2, mine % 2
    if flip:
        core = 1 - core
    return {"seq": ((x + offset_x) % SIDE) * 2 + core}


def greet(peers):
    barrier = pltpu.get_barrier_semaphore()
    for peer in peers:
        pl.semaphore_signal(barrier, inc=1, device_id=peer, device_id_type=MESH)
    pl.semaphore_wait(barrier, len(peers))


HALVES = (("y", 0), ("z", 2))
ORDER = (0, -1, 1, 2)


def plane_gather(own, view, send, recv, after_row):
    started = []

    def copy(half, kind, source, target, peer):
        return pltpu.make_async_remote_copy(
            src_ref=source,
            dst_ref=target,
            send_sem=send.at[half, kind],
            recv_sem=recv.at[half, kind],
            device_id=peer,
            device_id_type=MESH,
        )

    def push(half, kind, source, target, peer):
        item = copy(half, kind, source, target, peer)
        item.start()
        started.append(item)

    def arrived(half, kind, target):
        first, _ = HALVES[half]
        copy(half, kind, target, target, plane_peer(first, 1, 0)).wait_recv()

    def block(half, along_first, along_second, low, count):
        first, base = HALVES[half]
        z, y = plane_place(first, along_first, along_second)
        return view(z, y, base + low, count)

    def ring(half, slot, axis, along, source):
        first, base = HALVES[half]
        for kind, step in ((0, 1), (1, -1)):
            peer = plane_peer(first, step, 0) if axis == 0 else plane_peer(first, 0, step)
            push(half, 4 * slot + kind, source, block(half, along, 0, 0, 2), peer)

    def ring_relay(half, slot, axis, along):
        first, base = HALVES[half]
        for kind, step in ((0, 1), (1, -1)):
            where = (-step, 0) if axis == 0 else (along, -step)
            arrived(half, 4 * slot + kind, block(half, where[0], where[1], 0, 2))
            part = block(half, where[0], where[1], kind, 1)
            peer = plane_peer(first, step, 0) if axis == 0 else plane_peer(first, 0, step)
            push(half, 4 * slot + 2 + kind, part, part, peer)

    def ring_end(half, slot, axis, along):
        where = (2, 0) if axis == 0 else (along, 2)
        for kind in (0, 1):
            arrived(half, 4 * slot + 2 + kind, block(half, where[0], where[1], kind, 1))

    for half in (0, 1):
        ring(half, 0, 0, 0, own(HALVES[half][1], 2))
    for half in (0, 1):
        ring(half, 1, 1, 0, own(HALVES[half][1], 2))
    yield
    for half in (0, 1):
        ring_relay(half, 0, 0, 0)
        for slot in (1, 2):
            ring(half, 1 + slot, 1, ORDER[slot], block(half, ORDER[slot], 0, 0, 2))
    yield
    for half in (0, 1):
        ring_end(half, 0, 0, 0)
        ring(half, 4, 1, 2, block(half, 2, 0, 0, 2))
        after_row(half, 0)
    for slot in (0, 1, 2, 3):
        for half in (0, 1):
            ring_relay(half, 1 + slot, 1, ORDER[slot])
        yield
    for half in (0, 1):
        after_row(half, -1)
        after_row(half, 1)
    for half in (0, 1):
        for slot in (0, 1, 2, 3):
            ring_end(half, 1 + slot, 1, ORDER[slot])
        after_row(half, 2)
    for item in started:
        item.wait_send()


def plane_reduce(parts, far, near, far_last, near_last, send, recv, store):
    started = []

    def copy(half, kind, source, target, peer):
        return pltpu.make_async_remote_copy(
            src_ref=source,
            dst_ref=target,
            send_sem=send.at[half, kind],
            recv_sem=recv.at[half, kind],
            device_id=peer,
            device_id_type=MESH,
        )

    def push(half, kind, source, target, peer):
        item = copy(half, kind, source, target, peer)
        item.start()
        started.append(item)

    def arrived(half, kind, target):
        first, _ = HALVES[half]
        copy(half, kind, target, target, plane_peer(first, 1, 0)).wait_recv()

    def rows(half, offset, low, count):
        first, base = HALVES[half]
        z, y = plane_place(first, 0, offset)
        if first == "y":
            return parts.at[z, :, pl.ds(base + low, count)]
        return parts.at[:, y, pl.ds(base + low, count)]

    def one(half, offset, low, count):
        first, base = HALVES[half]
        z, y = plane_place(first, offset, 0)
        return parts.at[z, y, pl.ds(base + low, count)]

    def add(target, *others):
        total = target[...].astype(jnp.float32)
        for other in others:
            total = total + other[...].astype(jnp.float32)
        target[...] = total.astype(target.dtype)

    def add_rows(half, offset, low, count, *others):
        target = rows(half, offset, low, count)
        def step(at, carry):
            add(target.at[at], *[other.at[at] for other in others])
            return carry
        lax.fori_loop(0, SIDE, step, 0)

    def peer(half, axis, step):
        first, _ = HALVES[half]
        return plane_peer(first, 0, step) if axis == 1 else plane_peer(first, step, 0)

    for half in (0, 1):
        push(half, 0, rows(half, 2, 0, 1), far.at[half, 0], peer(half, 1, 1))
        push(half, 1, rows(half, 2, 1, 1), far.at[half, 1], peer(half, 1, -1))
    for half in (0, 1):
        push(half, 2, rows(half, 1, 1, 1), near.at[half, 0, :, pl.ds(1, 1)], peer(half, 1, 1))
        push(half, 3, rows(half, -1, 0, 1), near.at[half, 1, :, pl.ds(0, 1)], peer(half, 1, -1))
    yield
    for half in (0, 1):
        arrived(half, 0, far.at[half, 0])
        add_rows(half, 1, 0, 1, far.at[half, 0])
        push(half, 4, rows(half, 1, 0, 1), near.at[half, 0, :, pl.ds(0, 1)], peer(half, 1, 1))
        arrived(half, 1, far.at[half, 1])
        add_rows(half, -1, 1, 1, far.at[half, 1])
        push(half, 5, rows(half, -1, 1, 1), near.at[half, 1, :, pl.ds(1, 1)], peer(half, 1, -1))
    yield
    for half in (0, 1):
        arrived(half, 2, near.at[half, 0, :, pl.ds(1, 1)])
        arrived(half, 3, near.at[half, 1, :, pl.ds(0, 1)])
        arrived(half, 4, near.at[half, 0, :, pl.ds(0, 1)])
        arrived(half, 5, near.at[half, 1, :, pl.ds(1, 1)])
        add_rows(half, 0, 0, 2, near.at[half, 0], near.at[half, 1])
        push(half, 6, one(half, 2, 0, 1), far_last.at[half, 0], peer(half, 0, 1))
        push(half, 7, one(half, 2, 1, 1), far_last.at[half, 1], peer(half, 0, -1))
        push(half, 8, one(half, 1, 1, 1), near_last.at[half, 0, pl.ds(1, 1)], peer(half, 0, 1))
        push(half, 9, one(half, -1, 0, 1), near_last.at[half, 1, pl.ds(0, 1)], peer(half, 0, -1))
    yield
    for half in (0, 1):
        arrived(half, 6, far_last.at[half, 0])
        add(one(half, 1, 0, 1), far_last.at[half, 0])
        push(half, 10, one(half, 1, 0, 1), near_last.at[half, 0, pl.ds(0, 1)], peer(half, 0, 1))
        arrived(half, 7, far_last.at[half, 1])
        add(one(half, -1, 1, 1), far_last.at[half, 1])
        push(half, 11, one(half, -1, 1, 1), near_last.at[half, 1, pl.ds(1, 1)], peer(half, 0, -1))
    yield
    for half in (0, 1):
        arrived(half, 8, near_last.at[half, 0, pl.ds(1, 1)])
        arrived(half, 9, near_last.at[half, 1, pl.ds(0, 1)])
        arrived(half, 10, near_last.at[half, 0, pl.ds(0, 1)])
        arrived(half, 11, near_last.at[half, 1, pl.ds(1, 1)])
        total = one(half, 0, 0, 2)[...].astype(jnp.float32)
        for side in (0, 1):
            total = total + near_last[half, side].astype(jnp.float32)
        store(HALVES[half][1], total)
    for item in started:
        item.wait_send()


def reduce_scratch(quarter_rows, width):
    unit = (quarter_rows, width)
    return [
        pltpu.VMEM((SIDE, SIDE, 4) + unit, jnp.bfloat16),
        pltpu.VMEM((2, 2, SIDE, 1) + unit, jnp.bfloat16),
        pltpu.VMEM((2, 2, SIDE, 2) + unit, jnp.bfloat16),
        pltpu.VMEM((2, 2, 1) + unit, jnp.bfloat16),
        pltpu.VMEM((2, 2, 2) + unit, jnp.bfloat16),
        pltpu.SemaphoreType.DMA((2, 12)),
        pltpu.SemaphoreType.DMA((2, 12)),
    ]


def comm_params(number, limit_mb):
    return pltpu.CompilerParams(
        collective_id=number, has_side_effects=True, vmem_limit_bytes=limit_mb * 1024 * 1024
    )


def nothing(half, offset):
    return None


def advance(steps):
    next(steps, None)


def finish(steps):
    for _ in steps:
        pass


def token_gather(block, number):
    rows, width = block.shape

    def kernel(own_ref, out_ref, send, recv, local_sem):
        greet(plane_neighbours())
        z, y = plane_place("y", 0, 0)
        keep = pltpu.make_async_copy(own_ref, out_ref.at[z, y], local_sem)
        keep.start()
        finish(
            plane_gather(
                lambda low, count: own_ref.at[pl.ds(low, count)],
                lambda z, y, low, count: out_ref.at[z, y, pl.ds(low, count)],
                send,
                recv,
                nothing,
            )
        )
        keep.wait()

    out = pl.pallas_call(
        kernel,
        out_shape=jax.ShapeDtypeStruct((SIDE, SIDE, 4, rows // 4, width), block.dtype),
        in_specs=[pl.BlockSpec(memory_space=pl.ANY)],
        out_specs=pl.BlockSpec(memory_space=pl.ANY),
        scratch_shapes=[
            pltpu.SemaphoreType.DMA((2, 20)),
            pltpu.SemaphoreType.DMA((2, 20)),
            pltpu.SemaphoreType.DMA,
        ],
        compiler_params=comm_params(number, 8),
        name="token_gather",
    )(block.reshape(4, rows // 4, width))
    return out.reshape(SIDE * SIDE, rows, width)


def token_reduce(pieces, number):
    owners, rows, _ = pieces[0].shape
    widths = [piece.shape[2] for piece in pieces]
    width = sum(widths)
    quarter = rows // 4

    def kernel(*refs):
        ins, out_ref, rest = refs[: len(widths)], refs[len(widths)], refs[len(widths) + 1 :]
        parts, far, near, far_last, near_last, send, recv, load = rest
        loads, at = [], 0
        for i, one_width in enumerate(widths):
            loads.append(
                pltpu.make_async_copy(
                    ins[i], parts.at[:, :, :, :, pl.ds(at, one_width)], load.at[i]
                )
            )
            loads[-1].start()
            at += one_width
        greet(plane_neighbours())
        for item in loads:
            item.wait()

        def store(low, total):
            out_ref[pl.ds(low, 2)] = total

        finish(plane_reduce(parts, far, near, far_last, near_last, send, recv, store))

    out = pl.pallas_call(
        kernel,
        out_shape=jax.ShapeDtypeStruct((4, quarter, width), jnp.float32),
        in_specs=[pl.BlockSpec(memory_space=pl.ANY)] * len(widths),
        out_specs=pl.BlockSpec(memory_space=pltpu.VMEM),
        scratch_shapes=reduce_scratch(quarter, width) + [pltpu.SemaphoreType.DMA((len(widths),))],
        compiler_params=comm_params(number, 32),
        name="token_reduce",
    )(*[piece.reshape(SIDE, SIDE, 4, quarter, piece.shape[2]) for piece in pieces])
    return out.reshape(rows, width)


def weights_gather(piece, number):
    rows, width = piece.shape

    def kernel(own_ref, out_ref, send, recv, x_send, x_recv, core_send, core_recv, local_sem):
        seq = lax.axis_index("seq")
        x, core = seq // 2, seq % 2
        x_peers = [seq_peer(step, False) for step in (1, 3, 2)]
        other = seq_peer(0, True)
        greet(plane_neighbours() + x_peers + [other])
        z, y = plane_place("y", 0, 0)
        keep = pltpu.make_async_copy(own_ref, out_ref.at[x, core, z, y], local_sem)
        keep.start()
        sends = []
        for i, step in enumerate((1, 3, 2)):
            item = pltpu.make_async_remote_copy(
                src_ref=own_ref,
                dst_ref=out_ref.at[x, core, z, y],
                send_sem=x_send.at[i],
                recv_sem=x_recv.at[i],
                device_id=x_peers[i],
                device_id_type=MESH,
            )
            item.start()
            sends.append(item)
        keep.wait()
        for i, step in enumerate((1, 3, 2)):
            came = out_ref.at[(x + SIDE - step) % SIDE, core, z, y]
            pltpu.make_async_remote_copy(
                src_ref=came,
                dst_ref=came,
                send_sem=x_send.at[i],
                recv_sem=x_recv.at[i],
                device_id=x_peers[i],
                device_id_type=MESH,
            ).wait_recv()

        swaps = []

        def swap(half, offset):
            first, base = HALVES[half]
            z, y = plane_place(first, 0, offset)
            mine = (
                out_ref.at[pl.ds(base, 2), core, z]
                if first == "y"
                else out_ref.at[pl.ds(base, 2), core, :, y]
            )
            theirs = (
                out_ref.at[pl.ds(base, 2), 1 - core, z]
                if first == "y"
                else out_ref.at[pl.ds(base, 2), 1 - core, :, y]
            )
            kind = ORDER.index(offset)
            item = pltpu.make_async_remote_copy(
                src_ref=mine,
                dst_ref=mine,
                send_sem=core_send.at[half, kind],
                recv_sem=core_recv.at[half, kind],
                device_id=other,
                device_id_type=MESH,
            )
            item.start()
            sends.append(item)
            swaps.append(
                pltpu.make_async_remote_copy(
                    src_ref=theirs,
                    dst_ref=theirs,
                    send_sem=core_send.at[half, kind],
                    recv_sem=core_recv.at[half, kind],
                    device_id=other,
                    device_id_type=MESH,
                )
            )

        finish(
            plane_gather(
                lambda low, count: out_ref.at[pl.ds(low, count), core, z, y],
                lambda z, y, low, count: out_ref.at[pl.ds(low, count), core, z, y],
                send,
                recv,
                swap,
            )
        )
        for item in swaps:
            item.wait_recv()
        for item in sends:
            item.wait_send()

    out = pl.pallas_call(
        kernel,
        out_shape=jax.ShapeDtypeStruct((4, 2, SIDE, SIDE, rows, width), piece.dtype),
        in_specs=[pl.BlockSpec(memory_space=pl.ANY)],
        out_specs=pl.BlockSpec(memory_space=pl.ANY),
        scratch_shapes=[
            pltpu.SemaphoreType.DMA((2, 20)),
            pltpu.SemaphoreType.DMA((2, 20)),
            pltpu.SemaphoreType.DMA((3,)),
            pltpu.SemaphoreType.DMA((3,)),
            pltpu.SemaphoreType.DMA((2, 4)),
            pltpu.SemaphoreType.DMA((2, 4)),
            pltpu.SemaphoreType.DMA,
        ],
        compiler_params=comm_params(number, 8),
        name="weights_gather",
    )(piece)
    return out.reshape(4 * 2 * SIDE * SIDE * rows, width)


def weights_reduce(pieces, number):
    widths = [piece.shape[1] for piece in pieces]
    width = sum(widths)
    rows = pieces[0].shape[0] // (4 * 2 * SIDE * SIDE)

    def kernel(*refs):
        ins, out_ref, rest = refs[: len(widths)], refs[len(widths)], refs[len(widths) + 1 :]
        (parts, far, near, far_last, near_last, send, recv, twin, mine, from_x, load, core_send,
         core_recv, x_send, x_recv) = rest
        seq = lax.axis_index("seq")
        x, core = seq // 2, seq % 2
        x_peers = [seq_peer(step, False) for step in (1, 3, 2)]
        other = seq_peer(0, True)
        loads = []
        for quarter in range(4):
            at = 0
            for i, one_width in enumerate(widths):
                item = pltpu.make_async_copy(
                    ins[i].at[quarter, core],
                    parts.at[:, :, quarter, :, pl.ds(at, one_width)],
                    load.at[quarter, i],
                )
                item.start()
                loads.append(item)
                at += one_width
        greet(plane_neighbours() + x_peers + [other])
        swaps = []
        for quarter in range(4):
            at = 0
            for i, one_width in enumerate(widths):
                item = pltpu.make_async_remote_copy(
                    src_ref=ins[i].at[quarter, 1 - core],
                    dst_ref=twin.at[quarter, :, :, :, pl.ds(at, one_width)],
                    send_sem=core_send.at[quarter, i],
                    recv_sem=core_recv.at[quarter, i],
                    device_id=other,
                    device_id_type=MESH,
                )
                item.start()
                swaps.append(item)
                at += one_width
        for quarter in range(4):
            for i in range(len(widths)):
                loads[quarter * len(widths) + i].wait()
                swaps[quarter * len(widths) + i].wait_recv()

            def add(at, carry):
                z, y = at // SIDE, at % SIDE
                parts[z, y, quarter] = (
                    parts[z, y, quarter].astype(jnp.float32)
                    + twin[quarter, z, y].astype(jnp.float32)
                ).astype(parts.dtype)
                return carry

            lax.fori_loop(0, SIDE * SIDE, add, 0)

        def store(low, total):
            mine[pl.ds(low, 2)] = total.astype(mine.dtype)

        finish(plane_reduce(parts, far, near, far_last, near_last, send, recv, store))
        sends = []
        for i, step in enumerate((1, 3, 2)):
            item = pltpu.make_async_remote_copy(
                src_ref=mine.at[(x + step) % SIDE],
                dst_ref=from_x.at[i],
                send_sem=x_send.at[i],
                recv_sem=x_recv.at[i],
                device_id=x_peers[i],
                device_id_type=MESH,
            )
            item.start()
            sends.append(item)
        total = mine[x].astype(jnp.float32)
        for i in range(3):
            sends[i].wait_recv()
            total = total + from_x[i].astype(jnp.float32)
        out_ref[...] = total
        for item in sends + swaps:
            item.wait_send()

    unit = (rows, width)
    pairs = (4, len(widths))
    return pl.pallas_call(
        kernel,
        out_shape=jax.ShapeDtypeStruct(unit, jnp.float32),
        in_specs=[pl.BlockSpec(memory_space=pl.ANY)] * len(widths),
        out_specs=pl.BlockSpec(memory_space=pltpu.VMEM),
        scratch_shapes=reduce_scratch(rows, width)
        + [
            pltpu.VMEM((4, SIDE, SIDE) + unit, jnp.bfloat16),
            pltpu.VMEM((4,) + unit, jnp.bfloat16),
            pltpu.VMEM((3,) + unit, jnp.bfloat16),
            pltpu.SemaphoreType.DMA(pairs),
            pltpu.SemaphoreType.DMA(pairs),
            pltpu.SemaphoreType.DMA(pairs),
            pltpu.SemaphoreType.DMA((3,)),
            pltpu.SemaphoreType.DMA((3,)),
        ],
        compiler_params=comm_params(number, 40),
        name="weights_reduce",
    )(*[piece.reshape(4, 2, SIDE, SIDE, rows, piece.shape[1]) for piece in pieces])


def rms_scale(values):
    return lax.rsqrt(jnp.mean(values * values, axis=-1, keepdims=True) + epsilon)


def rope_tables(length):
    half_dim = HEAD_DIM // 2
    frequency = np.float32(rope_theta) ** (
        -np.arange(half_dim, dtype=np.float32) / np.float32(half_dim)
    )
    angles = np.arange(length, dtype=np.float32)[:, None] * frequency[None, :].astype(np.float32)
    cosine = np.cos(angles.astype(np.float64)).astype(np.float32)
    sine = np.sin(angles.astype(np.float64)).astype(np.float32)
    one_cos = np.concatenate([cosine, cosine], axis=1)
    one_sin = np.concatenate([-sine, sine], axis=1)
    flat = np.ones_like(one_cos)
    return (
        np.concatenate([one_cos, one_cos, one_cos, flat], axis=1),
        np.concatenate([one_sin, one_sin, one_sin, 0.0 * flat], axis=1),
    )


def turn(values, cosine, sine):
    half_dim = HEAD_DIM // 2
    width = values.shape[1]
    lane = lax.broadcasted_iota(jnp.int32, values.shape, 1)
    ahead = pltpu.roll(values, width - half_dim, 1)
    behind = pltpu.roll(values, half_dim, 1)
    return values * cosine + jnp.where(lane % HEAD_DIM < half_dim, ahead, behind) * sine


SEQ_STEPS = (4, 5, 3, 2, 6, 1, 7)


def seq_exchange(source, target, send, recv):
    me = lax.axis_index("seq")
    count = 8

    def copy(step, peer, out_of, into):
        return pltpu.make_async_remote_copy(
            src_ref=out_of,
            dst_ref=into,
            send_sem=send.at[step - 1],
            recv_sem=recv.at[step - 1],
            device_id={"seq": peer},
            device_id_type=MESH,
        )

    def start(steps):
        items = []
        for step in steps:
            peer = (me + step) % count
            item = copy(step, peer, source(peer), target(me))
            item.start()
            items.append(item)
        return items

    def wait(step):
        peer = (me + count - step) % count
        copy(step, peer, target(peer), target(peer)).wait_recv()

    return (start, wait)


def seq_plane_greet():
    me = lax.axis_index("seq")
    greet(plane_neighbours() + [{"seq": (me + step) % 8} for step in range(1, 8)])


def twice(pair, lane):
    swapped = pltpu.roll(pair.astype(jnp.float32), HEAD_DIM, 1).astype(pair.dtype)
    return (
        jnp.where(lane < HEAD_DIM, pair, swapped),
        jnp.where(lane < HEAD_DIM, swapped, pair),
    )


def apart(pair, lane):
    zero = jnp.zeros_like(pair)
    return jnp.concatenate(
        [jnp.where(lane < HEAD_DIM, pair, zero), jnp.where(lane < HEAD_DIM, zero, pair)], axis=0
    )


def matmul(a, b, dims):
    return lax.dot_general(a, b, (dims, ((), ())), preferred_element_type=jnp.float32)


BLOCK = 256


def block_probs(queries, keys, at):
    scores = matmul(queries, keys, ((1,), (1,)))
    row = lax.broadcasted_iota(jnp.int32, scores.shape, 0) % BLOCK + at * BLOCK
    column = lax.broadcasted_iota(jnp.int32, scores.shape, 1)
    scores = jnp.where(column <= row, scores, -1e30)
    exponent = jnp.exp(scores - jnp.max(scores, axis=1, keepdims=True))
    return exponent * (1.0 / jnp.sum(exponent, axis=1, keepdims=True))


def attention_forward(projected, cosine, sine, beside, number):
    tok, width = projected.shape
    features = beside.shape[1]
    seq_parts = 8
    group = width // seq_parts
    pair = 2 * HEAD_DIM
    length = tok * seq_parts
    per_block = BLOCK // tok

    def kernel(
        proj_ref, cos_ref, sin_ref, beside_ref, out_ref, heads_ref, all_ref,
        packed, mixed, send, recv, o_send, o_recv, p_send, p_recv, local_sem,
    ):
        me = lax.axis_index("seq")
        z, y = plane_place("y", 0, 0)
        keep = pltpu.make_async_copy(beside_ref, all_ref.at[z, y], local_sem)
        keep.start()
        seq_plane_greet()
        steps = plane_gather(
            lambda low, count: beside_ref.at[pl.ds(low, count)],
            lambda z, y, low, count: all_ref.at[z, y, pl.ds(low, count)],
            p_send,
            p_recv,
            nothing,
        )
        advance(steps)
        for d in range(seq_parts):
            packed[d] = turn(
                proj_ref[:, d * group : (d + 1) * group], cos_ref[...], sin_ref[...]
            ).astype(packed.dtype)
        start, wait = seq_exchange(
            lambda d: packed.at[d], lambda d: heads_ref.at[d], send, recv
        )
        items = start(SEQ_STEPS)
        heads_ref[me] = packed[me]
        advance(steps)
        for step in SEQ_STEPS:
            wait(step)
        advance(steps)
        lane = lax.broadcasted_iota(jnp.int32, (length, pair), 1)
        heads = heads_ref[...].reshape(length, group)
        keys, values = twice(heads[:, pair:], lane)
        lane_block = lane[:BLOCK]
        back, back_wait = seq_exchange(
            lambda d: mixed.at[d],
            lambda d: out_ref.at[:, pl.ds(pl.multiple_of(d * pair, pair), pair)],
            o_send,
            o_recv,
        )
        for at in range(length // BLOCK):
            block = heads[at * BLOCK : (at + 1) * BLOCK, :pair]
            queries = apart(block * jnp.asarray(attention_multiplier, block.dtype), lane_block)
            upto = (at + 1) * BLOCK
            probs = block_probs(queries, keys[:upto], at).astype(jnp.bfloat16)
            both = matmul(probs, values[:upto], ((1,), (0,)))
            made = jnp.where(lane_block < HEAD_DIM, both[:BLOCK], both[BLOCK:]).astype(mixed.dtype)
            mixed[at * per_block : (at + 1) * per_block] = made.reshape(per_block, tok, pair)
            if at % 2:
                advance(steps)
        items += back(SEQ_STEPS)
        out_ref[:, pl.ds(pl.multiple_of(me * pair, pair), pair)] = mixed[me]
        advance(steps)
        for step in SEQ_STEPS:
            back_wait(step)
        finish(steps)
        keep.wait()
        for item in items:
            item.wait_send()

    vmem = pl.BlockSpec(memory_space=pltpu.VMEM)
    anywhere = pl.BlockSpec(memory_space=pl.ANY)
    attended, heads, gathered = pl.pallas_call(
        kernel,
        out_shape=(
            jax.ShapeDtypeStruct((tok, seq_parts * pair), jnp.bfloat16),
            jax.ShapeDtypeStruct((seq_parts, tok, group), jnp.bfloat16),
            jax.ShapeDtypeStruct((SIDE, SIDE, 4, tok // 4, features), beside.dtype),
        ),
        in_specs=[vmem] * 3 + [anywhere],
        out_specs=(vmem, vmem, anywhere),
        scratch_shapes=[
            pltpu.VMEM((seq_parts, tok, group), jnp.bfloat16),
            pltpu.VMEM((seq_parts, tok, pair), jnp.bfloat16),
        ]
        + [pltpu.SemaphoreType.DMA((7,))] * 4
        + [pltpu.SemaphoreType.DMA((2, 20))] * 2
        + [pltpu.SemaphoreType.DMA],
        compiler_params=comm_params(number, 48),
        name="attention_forward",
    )(projected, cosine, sine, beside.reshape(4, tok // 4, features))
    return (attended, heads, gathered.reshape(SIDE * SIDE, tok, features))


def attention_backward(grad_attended, heads_in, cosine, sine, beside, number):
    seq_parts, tok, group = heads_in.shape
    features = beside.shape[2]
    pair = 2 * HEAD_DIM
    length = tok * seq_parts
    per_block = BLOCK // tok

    def kernel(
        grad_ref, heads_ref, cos_ref, sin_ref, beside_ref, out_ref, sum_ref,
        came, packed, d_queries, d_keys, d_values, send, recv, o_send, o_recv,
        parts, far, near, far_last, near_last, p_send, p_recv, load,
    ):
        me = lax.axis_index("seq")
        loaded = pltpu.make_async_copy(beside_ref, parts, load)
        loaded.start()
        seq_plane_greet()

        def store(low, total):
            sum_ref[pl.ds(low, 2)] = total

        steps = plane_reduce(parts, far, near, far_last, near_last, p_send, p_recv, store)
        columns = lambda d: grad_ref.at[:, pl.ds(pl.multiple_of(d * pair, pair), pair)]
        start, wait = seq_exchange(columns, lambda d: came.at[d], send, recv)
        items = start(SEQ_STEPS)
        loaded.wait()
        advance(steps)
        came[me] = grad_ref[:, pl.ds(pl.multiple_of(me * pair, pair), pair)]
        lane = lax.broadcasted_iota(jnp.int32, (length, pair), 1)
        lane_block = lane[:BLOCK]
        heads = heads_ref[...].reshape(length, group)
        keys, values = twice(heads[:, pair:], lane)
        for step in SEQ_STEPS:
            wait(step)
        for at in range(length // BLOCK):
            upto = (at + 1) * BLOCK
            block = heads[at * BLOCK : upto, :pair]
            queries = apart(block * jnp.asarray(attention_multiplier, block.dtype), lane_block)
            grads = apart(
                came[at * per_block : (at + 1) * per_block].reshape(BLOCK, pair), lane_block
            )
            probs = block_probs(queries, keys[:upto], at)
            d_probs = matmul(grads, values[:upto], ((1,), (1,)))
            center = jnp.sum(probs * d_probs, axis=1, keepdims=True)
            d_scores = (probs * (d_probs - center)).astype(jnp.bfloat16)
            both = matmul(d_scores, keys[:upto], ((1,), (0,))) * attention_multiplier
            d_queries[at * BLOCK : upto] = jnp.where(
                lane_block < HEAD_DIM, both[:BLOCK], both[BLOCK:]
            )
            more_keys = matmul(d_scores, queries, ((0,), (0,)))
            more_values = matmul(probs.astype(jnp.bfloat16), grads, ((0,), (0,)))
            before = at * BLOCK
            if at:
                d_keys[:before] += more_keys[:before]
                d_values[:before] += more_values[:before]
            d_keys[before:upto] = more_keys[before:]
            d_values[before:upto] = more_values[before:]
            if at in (1, 2, 3):
                advance(steps)
        sum_keys = d_keys[...] + pltpu.roll(d_keys[...], HEAD_DIM, 1)
        sum_values = d_values[...] + pltpu.roll(d_values[...], HEAD_DIM, 1)
        rest = jnp.where(lane < HEAD_DIM, sum_keys, sum_values)
        whole = jnp.concatenate([d_queries[...], rest], axis=1)
        packed[...] = (
            turn(whole, cos_ref[...], -sin_ref[...])
            .astype(packed.dtype)
            .reshape(seq_parts, tok, group)
        )
        back, back_wait = seq_exchange(
            lambda d: packed.at[d],
            lambda d: out_ref.at[:, pl.ds(pl.multiple_of(d * group, group), group)],
            o_send,
            o_recv,
        )
        items += back(SEQ_STEPS)
        out_ref[:, pl.ds(pl.multiple_of(me * group, group), group)] = packed[me]
        advance(steps)
        for step in SEQ_STEPS:
            back_wait(step)
        finish(steps)
        for item in items:
            item.wait_send()

    vmem = pl.BlockSpec(memory_space=pltpu.VMEM)
    grads, summed = pl.pallas_call(
        kernel,
        out_shape=(
            jax.ShapeDtypeStruct((tok, seq_parts * group), jnp.bfloat16),
            jax.ShapeDtypeStruct((4, tok // 4, features), jnp.float32),
        ),
        in_specs=[vmem] * 4 + [pl.BlockSpec(memory_space=pl.ANY)],
        out_specs=(vmem, vmem),
        scratch_shapes=[
            pltpu.VMEM((seq_parts, tok, pair), jnp.bfloat16),
            pltpu.VMEM((seq_parts, tok, group), jnp.bfloat16),
            pltpu.VMEM((length, pair), jnp.float32),
            pltpu.VMEM((length, pair), jnp.float32),
            pltpu.VMEM((length, pair), jnp.float32),
        ]
        + [pltpu.SemaphoreType.DMA((7,))] * 4
        + reduce_scratch(tok // 4, features)
        + [pltpu.SemaphoreType.DMA],
        compiler_params=comm_params(number, 56),
        name="attention_backward",
    )(grad_attended, heads_in, cosine, sine, beside.reshape(SIDE, SIDE, 4, tok // 4, features))
    return (grads, summed.reshape(tok, features))


def gate_columns(logits, chosen_ids, experts_all):
    named = jnp.any(
        chosen_ids[..., None] == jnp.arange(experts_all, dtype=jnp.int32), axis=-2
    )
    peak = jnp.max(jnp.where(named, logits, -jnp.inf), axis=-1, keepdims=True)
    exponent = jnp.where(named, jnp.exp(logits - peak), 0.0)
    gates = exponent / jnp.sum(exponent, axis=-1, keepdims=True)
    coarse = lax.reduce_precision(gates, 8, 7)
    columns = jnp.concatenate(
        [named.astype(jnp.float32), coarse, gates - coarse, jnp.zeros_like(gates)], axis=-1
    ).astype(jnp.bfloat16)
    return (gates, columns)


def expert_layer(tokens_all, cot_all, gate_full, up_full, down_full, experts_all, capacity):
    sources, tok, wide = tokens_all.shape
    features = wide - 128
    hidden_units = gate_full.shape[2]
    group = 8
    chunks = sources // group
    chunk_rows = group * capacity
    f32, b16 = jnp.float32, jnp.bfloat16

    def matmul(a, b, dims):
        return lax.dot_general(a, b, (dims, ((), ())), preferred_element_type=f32)

    def kernel(
        tok_hbm, cot_hbm, gate_hbm, up_hbm, down_hbm,
        mix_hbm, rows_hbm, ggate_hbm, gup_hbm, gdown_hbm,
        tok_v, cot_v, gate_v, up_v, down_v, mix_v, rows_v, grad_v,
        x_v, deo_v, slope_v, act_v, inner_v, pick_v, pick_t, share_v, dgate_v,
        in_sem, out_sem,
    ):
        first = lax.axis_index("wshard") * 2
        loads = [
            pltpu.make_async_copy(source, target, in_sem.at[i])
            for i, (source, target) in enumerate(
                [(tok_hbm, tok_v), (cot_hbm, cot_v), (gate_hbm, gate_v), (up_hbm, up_v),
                 (down_hbm, down_v)]
            )
        ]
        for item in loads:
            item.start()
        lane = lax.broadcasted_iota(jnp.int32, (tok, 128), 1)
        down_rows = lax.broadcasted_iota(jnp.int32, (tok, 128), 0)
        lower = jnp.where(down_rows >= lane, 1.0, 0.0).astype(b16)
        loads[0].wait()
        loads[1].wait()

        def prepare(s, carry):
            info = tok_v[s, :, pl.ds(features, 128)]
            info32 = info.astype(f32)
            place = matmul(lower, info, ((1,), (0,))) - 1.0
            place = jnp.where(info32 > 0.5, place, -1.0)
            place_rows = place.T
            info_rows = info32.T
            row_picks, col_places = [], []
            shares = []
            for e in (0, 1):
                at = first + e
                row = jnp.sum(jnp.where(down_rows == at, place_rows, 0.0), axis=0, keepdims=True)
                gate = jnp.sum(
                    jnp.where(
                        (down_rows == experts_all + at) | (down_rows == 2 * experts_all + at),
                        info_rows,
                        0.0,
                    ),
                    axis=0,
                    keepdims=True,
                )
                slot = lax.broadcasted_iota(jnp.int32, (capacity, tok), 0).astype(f32)
                hit = slot == row
                row_picks.append(jnp.where(hit, 1.0, 0.0))
                shares.append(jnp.sum(jnp.where(hit, gate, 0.0), axis=1, keepdims=True))
                col_places.append(
                    jnp.sum(jnp.where(lane == at, place, 0.0), axis=1, keepdims=True)
                )
            pick = jnp.concatenate(row_picks, axis=0).astype(b16)
            pick_v[s] = pick
            lane_f = lane.astype(f32)
            pick_t[s] = (
                jnp.where(lane_f == col_places[0], 1.0, 0.0) * jnp.where(lane < capacity, 1.0, 0.0)
                + jnp.where(lane_f - float(capacity) == col_places[1], 1.0, 0.0)
                * jnp.where(lane >= capacity, 1.0, 0.0)
            ).astype(b16)
            share_v[s] = jnp.concatenate(shares, axis=0)
            rows = matmul(pick, tok_v[s, :, pl.ds(0, features)], ((1,), (0,))).astype(b16)
            c, i = s // group, s % group
            x_v[0, c, i] = rows[:capacity]
            x_v[1, c, i] = rows[capacity:]
            cots = matmul(pick, cot_v[s], ((1,), (0,))).astype(b16)
            deo_v[0, c, i] = cots[:capacity]
            deo_v[1, c, i] = cots[capacity:]
            return carry

        lax.fori_loop(0, sources, prepare, 0)
        for item in loads[2:]:
            item.wait()

        def forward(c, carry):
            weighted = []
            for e in (0, 1):
                x = x_v[e, c].reshape(chunk_rows, features)
                gate_val = matmul(x, gate_v[e], ((1,), (0,)))
                up_val = matmul(x, up_v[e], ((1,), (0,)))
                sigma = 1.0 / (1.0 + jnp.exp(-gate_val))
                act = gate_val * sigma
                inner = (act * up_val).astype(b16)
                inner_v[e, c] = inner
                act_v[e, c] = act.astype(b16)
                slope_v[e, c] = (up_val * (sigma * (1.0 + gate_val * (1.0 - sigma)))).astype(b16)
                made = matmul(inner, down_v[e], ((1,), (0,))).astype(b16).astype(f32)
                share = jnp.concatenate(
                    [share_v[c * group + i, pl.ds(e * capacity, capacity)] for i in range(group)],
                    axis=0,
                )
                mix_grad = residual_multiplier * deo_v[e, c].reshape(chunk_rows, features).astype(f32)
                dgate_v[e, c] = jnp.sum(made * mix_grad, axis=1, keepdims=True)
                deo_v[e, c] = (share * mix_grad).astype(b16).reshape(group, capacity, features)
                weighted.append((share * made).astype(b16))
            for i in range(group):
                both = jnp.concatenate(
                    [w[i * capacity : (i + 1) * capacity] for w in weighted], axis=0
                )
                mix_v[c * group + i] = matmul(pick_t[c * group + i], both, ((1,), (0,))).astype(b16)
            return carry

        lax.fori_loop(0, chunks, forward, 0)
        stores = [pltpu.make_async_copy(mix_v, mix_hbm, out_sem.at[0])]
        stores[0].start()
        lane_rows = lax.broadcasted_iota(jnp.int32, (chunk_rows, 128), 1)

        def backward(c, carry):
            made = []
            for e in (0, 1):
                deo = deo_v[e, c].reshape(chunk_rows, features)
                d_inner = matmul(deo, down_v[e], ((1,), (1,)))
                d_gate = (d_inner * slope_v[e, c].astype(f32)).astype(b16)
                d_up = (d_inner * act_v[e, c].astype(f32)).astype(b16)
                slope_v[e, c] = d_gate
                act_v[e, c] = d_up
                d_rows = (
                    matmul(d_gate, gate_v[e], ((1,), (1,))) + matmul(d_up, up_v[e], ((1,), (1,)))
                ).astype(b16)
                coarse = dgate_v[e, c].astype(b16).astype(f32)
                fine = dgate_v[e, c] - coarse
                columns = jnp.where(lane_rows == first + e, coarse, 0.0) + jnp.where(
                    lane_rows == experts_all + first + e, fine, 0.0
                )
                made.append(jnp.concatenate([d_rows, columns.astype(b16)], axis=1))
            for i in range(group):
                both = jnp.concatenate(
                    [m[i * capacity : (i + 1) * capacity] for m in made], axis=0
                )
                rows_v[c * group + i] = matmul(pick_t[c * group + i], both, ((1,), (0,))).astype(b16)
            return carry

        lax.fori_loop(0, chunks, backward, 0)
        stores.append(pltpu.make_async_copy(rows_v, rows_hbm, out_sem.at[1]))
        stores[1].start()
        rows_all = chunks * chunk_rows

        def whole(ref, e, columns):
            return ref[e].reshape(rows_all, columns)

        for e in (0, 1):
            x = whole(x_v, e, features)
            grad_v[e] = matmul(x, whole(slope_v, e, hidden_units), ((0,), (0,))).astype(b16)
            grad_v[2 + e] = matmul(x, whole(act_v, e, hidden_units), ((0,), (0,))).astype(b16)
            for i, target in ((e, ggate_hbm), (2 + e, gup_hbm)):
                stores.append(
                    pltpu.make_async_copy(grad_v.at[i], target.at[e], out_sem.at[2 + i])
                )
                stores[-1].start()
        for e in (0, 1):
            grad = matmul(
                whole(inner_v, e, hidden_units), whole(deo_v, e, features), ((0,), (0,))
            ).astype(b16)
            tok_v[pl.ds(4 * e, 4), :, pl.ds(0, features)] = grad.reshape(4, 128, features)
            stores.append(
                pltpu.make_async_copy(
                    tok_v.at[pl.ds(4 * e, 4), :, pl.ds(0, features)],
                    gdown_hbm.at[e],
                    out_sem.at[6 + e],
                )
            )
            stores[-1].start()
        for item in stores:
            item.wait()

    anywhere = pl.BlockSpec(memory_space=pl.ANY)
    local = gate_full.shape[0]
    outs = pl.pallas_call(
        kernel,
        out_shape=(
            jax.ShapeDtypeStruct((sources, tok, features), b16),
            jax.ShapeDtypeStruct((sources, tok, wide), b16),
            jax.ShapeDtypeStruct((local, features, hidden_units), b16),
            jax.ShapeDtypeStruct((local, features, hidden_units), b16),
            jax.ShapeDtypeStruct((local, 4, hidden_units // 4, features), b16),
        ),
        in_specs=[anywhere] * 5,
        out_specs=(anywhere,) * 5,
        scratch_shapes=[
            pltpu.VMEM((sources, tok, wide), b16),
            pltpu.VMEM((sources, tok, features), b16),
            pltpu.VMEM(gate_full.shape, b16),
            pltpu.VMEM(up_full.shape, b16),
            pltpu.VMEM(down_full.shape, b16),
            pltpu.VMEM((sources, tok, features), b16),
            pltpu.VMEM((sources, tok, wide), b16),
            pltpu.VMEM((4, features, hidden_units), b16),
            pltpu.VMEM((2, chunks, group, capacity, features), b16),
            pltpu.VMEM((2, chunks, group, capacity, features), b16),
            pltpu.VMEM((2, chunks, chunk_rows, hidden_units), b16),
            pltpu.VMEM((2, chunks, chunk_rows, hidden_units), b16),
            pltpu.VMEM((2, chunks, chunk_rows, hidden_units), b16),
            pltpu.VMEM((sources, 2 * capacity, tok), b16),
            pltpu.VMEM((sources, tok, 2 * capacity), b16),
            pltpu.VMEM((sources, 2 * capacity, 1), f32),
            pltpu.VMEM((2, chunks, chunk_rows, 1), f32),
            pltpu.SemaphoreType.DMA((5,)),
            pltpu.SemaphoreType.DMA((8,)),
        ],
        compiler_params=pltpu.CompilerParams(vmem_limit_bytes=60 * 1024 * 1024),
        cost_estimate=pl.CostEstimate(
            flops=20 * 10**9, bytes_accessed=40 * 10**6, transcendentals=10**6
        ),
        name="expert_layer",
    )(tokens_all, cot_all, gate_full, up_full, down_full)
    return outs[:4] + (outs[4].reshape(local, hidden_units, features),)


def norm_backward(grad_normed, values, scale, gain_full):
    grad_gain = jnp.sum(grad_normed * values * scale, axis=0)
    grad_hat = grad_normed * gain_full
    grad_values = scale * grad_hat - values * (scale * scale * scale) * jnp.mean(
        grad_hat * values, axis=1, keepdims=True
    )
    return (grad_values, grad_gain)


def local(
    tokens,
    weight_qkv,
    weight_out,
    router,
    gain_attn,
    gain_ffn,
    expert_gate,
    expert_up,
    expert_down,
    expert_ids,
    cotangent,
):
    tok_dev = tokens.shape[1]
    features = tokens.shape[2]
    seq_parts = lax.axis_size("seq")
    owners = lax.axis_size("wshard")
    local_experts = expert_gate.shape[0]
    experts_all = local_experts * owners
    top_count = expert_ids.shape[2]
    capacity = 2 * tok_dev * top_count // experts_all
    heads_dev = HEADS // seq_parts
    key_heads = KV_HEADS // seq_parts
    query_cols = heads_dev * HEAD_DIM
    key_cols = key_heads * HEAD_DIM
    query_width = HEADS * HEAD_DIM
    key_width = KV_HEADS * HEAD_DIM
    length = tok_dev * seq_parts
    qkv_width = weight_qkv.shape[1]
    own_rows = weight_qkv.shape[0]
    weights_own = jnp.concatenate(
        [
            jnp.concatenate(
                [
                    weight_qkv[:, :query_width].reshape(own_rows, seq_parts, query_cols),
                    weight_qkv[:, query_width : query_width + key_width].reshape(
                        own_rows, seq_parts, key_cols
                    ),
                    weight_qkv[:, query_width + key_width :].reshape(
                        own_rows, seq_parts, key_cols
                    ),
                ],
                axis=2,
            ).reshape(own_rows, qkv_width),
            weight_out,
            router,
            gain_attn[:, None],
            gain_ffn[:, None],
            jnp.zeros((router.shape[0], 128 - experts_all - 2), jnp.bfloat16),
        ],
        axis=1,
    )
    weights_full = weights_gather(weights_own, 0)
    qkv_full = weights_full[:, :qkv_width]
    out_full = weights_full[:, qkv_width : qkv_width + features]
    smalls_full = weights_full[:, qkv_width + features :]
    router_full = smalls_full[:, :experts_all]
    gain_one = smalls_full[:, experts_all].astype(jnp.float32)
    gain_two = smalls_full[:, experts_all + 1].astype(jnp.float32)
    owned = (
        lax.all_gather(expert_gate, "seq", axis=1, tiled=True),
        lax.all_gather(expert_up, "seq", axis=1, tiled=True),
        lax.all_gather(expert_down, "seq", axis=1, tiled=True),
    )
    gate_full, up_full, down_full = (owned[0], owned[1], owned[2])
    inputs = tokens[0].astype(jnp.float32)
    chosen_ids = expert_ids[0]
    scale_one = rms_scale(inputs)
    normed_one = (inputs * scale_one * gain_one).astype(jnp.bfloat16)
    projected = jnp.dot(normed_one, qkv_full, preferred_element_type=jnp.float32)
    cosine, sine = (jnp.asarray(table) for table in rope_tables(length))
    offset = lax.axis_index("seq") * tok_dev
    attended, heads_all, cot_all = attention_forward(
        projected,
        lax.dynamic_slice_in_dim(cosine, offset, tok_dev),
        lax.dynamic_slice_in_dim(sine, offset, tok_dev),
        cotangent[0],
        5,
    )
    branch = jnp.dot(attended, out_full, preferred_element_type=jnp.float32)
    hidden = inputs + residual_multiplier * branch
    scale_two = rms_scale(hidden)
    normed_two = (hidden * scale_two * gain_two).astype(jnp.bfloat16)
    logits = jnp.dot(normed_two, router_full, preferred_element_type=jnp.float32)
    gates_own, gate_info = gate_columns(logits, chosen_ids, experts_all)
    tokens_all = token_gather(jnp.concatenate([normed_two, gate_info], axis=1), 1)
    mix_part, rows_part, grad_gate, grad_up, grad_down = expert_layer(
        tokens_all, cot_all, gate_full, up_full, down_full, experts_all, capacity
    )
    grad_output = cotangent[0].astype(jnp.float32)
    back = token_reduce([rows_part], 3)
    grad_back = back[:, :features]
    grad_gates = (
        back[:, features : features + experts_all]
        + back[:, features + experts_all : features + 2 * experts_all]
    )
    grad_logits = (
        gates_own
        * (grad_gates - jnp.sum(gates_own * grad_gates, axis=1, keepdims=True))
    ).astype(jnp.bfloat16)
    grad_router = jnp.dot(normed_two.T, grad_logits, preferred_element_type=jnp.float32)
    grad_normed_two = jnp.dot(grad_logits, router_full.T, preferred_element_type=jnp.float32)
    expert_shares = (
        lax.psum_scatter(
            grad_gate, "seq", scatter_dimension=1, tiled=True
        ).astype(jnp.float32),
        lax.psum_scatter(
            grad_up, "seq", scatter_dimension=1, tiled=True
        ).astype(jnp.float32),
        lax.psum_scatter(
            grad_down, "seq", scatter_dimension=1, tiled=True
        ).astype(jnp.float32),
    )
    grad_normed_two = grad_normed_two + grad_back
    grad_hidden_norm, grad_gain_ffn = norm_backward(grad_normed_two, hidden, scale_two, gain_two)
    grad_hidden = grad_output + grad_hidden_norm
    grad_branch = (residual_multiplier * grad_hidden).astype(jnp.bfloat16)
    grad_out = jnp.dot(attended.T, grad_branch, preferred_element_type=jnp.float32)
    grad_attended = jnp.dot(grad_branch, out_full.T, preferred_element_type=jnp.float32).astype(
        jnp.bfloat16
    )
    grad_proj, mixture = attention_backward(
        grad_attended, heads_all, cosine, sine, mix_part, 6
    )
    output = hidden + residual_multiplier * mixture
    grad_qkv = jnp.dot(normed_one.T, grad_proj, preferred_element_type=jnp.float32)
    grad_normed_one = jnp.dot(grad_proj, qkv_full.T, preferred_element_type=jnp.float32)
    grad_input_norm, grad_gain_attn = norm_backward(grad_normed_one, inputs, scale_one, gain_one)
    grad_input = grad_hidden + grad_input_norm
    packed_grads = jnp.concatenate(
        [
            grad_out,
            grad_router,
            grad_gain_attn[:, None],
            grad_gain_ffn[:, None],
            jnp.zeros((features, 128 - experts_all - 2), jnp.float32),
        ],
        axis=1,
    ).astype(jnp.bfloat16)
    own = weights_reduce([grad_qkv.astype(jnp.bfloat16), packed_grads], 4)
    qkv_cols = grad_qkv.shape[1]
    own_groups = own[:, :qkv_cols].reshape(own_rows, seq_parts, query_cols + 2 * key_cols)
    shares = (
        jnp.concatenate(
            [
                own_groups[:, :, :query_cols].reshape(own_rows, query_width),
                own_groups[:, :, query_cols : query_cols + key_cols].reshape(own_rows, key_width),
                own_groups[:, :, query_cols + key_cols :].reshape(own_rows, key_width),
            ],
            axis=1,
        ),
        own[:, qkv_cols : qkv_cols + features],
        own[:, qkv_cols + features : qkv_cols + features + experts_all],
        own[:, qkv_cols + features + experts_all],
        own[:, qkv_cols + features + experts_all + 1],
    )
    return (
        output.astype(jnp.bfloat16)[None],
        grad_input.astype(jnp.bfloat16)[None],
        shares[0],
        shares[1],
        shares[2],
        shares[3],
        shares[4],
        expert_shares[0],
        expert_shares[1],
        expert_shares[2],
    )


def solution(mesh):
    placed = (
        P("wshard", "seq", None),
        P(("seq", "wshard"), None),
        P(("seq", "wshard"), None),
        P(("seq", "wshard"), None),
        P(("seq", "wshard")),
        P(("seq", "wshard")),
        P("wshard", "seq", None),
        P("wshard", "seq", None),
        P("wshard", "seq", None),
        P("wshard", "seq", None),
        P("wshard", "seq", None),
    )
    return jax.shard_map(
        local,
        mesh=mesh,
        in_specs=placed,
        out_specs=(
            P("wshard", "seq", None),
            P("wshard", "seq", None),
            P(("seq", "wshard"), None),
            P(("seq", "wshard"), None),
            P(("seq", "wshard"), None),
            P(("seq", "wshard")),
            P(("seq", "wshard")),
            P("wshard", "seq", None),
            P("wshard", "seq", None),
            P("wshard", "seq", None),
        ),
        check_vma=False,
    )
```

```python
import jax
import jax.numpy as jnp
import numpy as np
from jax import lax
from jax.experimental import pallas as pl
from jax.experimental.pallas import tpu as pltpu
from jax.sharding import PartitionSpec as P

HEADS = 16
KV_HEADS = 8
HEAD_DIM = 64


epsilon = 1e-06
attention_multiplier = 0.015625
residual_multiplier = 0.22
rope_theta = 10000.0


MESH = pl.DeviceIdType.MESH
SIDE = 4


def plane_place(first, offset_first, offset_second):
    mine = lax.axis_index("wshard")
    z, y = mine // SIDE, mine % SIDE
    if first == "y":
        return ((z + offset_second + SIDE) % SIDE, (y + offset_first + SIDE) % SIDE)
    return ((z + offset_first + SIDE) % SIDE, (y + offset_second + SIDE) % SIDE)


def plane_peer(first, offset_first, offset_second):
    z, y = plane_place(first, offset_first, offset_second)
    return {"wshard": z * SIDE + y}


def plane_neighbours():
    return [plane_peer("y", step, 0) for step in (1, -1)] + [
        plane_peer("y", 0, step) for step in (1, -1)
    ]


def seq_peer(offset_x, flip):
    mine = lax.axis_index("seq")
    x, core = mine // 2, mine % 2
    if flip:
        core = 1 - core
    return {"seq": ((x + offset_x) % SIDE) * 2 + core}


def greet(peers):
    barrier = pltpu.get_barrier_semaphore()
    for peer in peers:
        pl.semaphore_signal(barrier, inc=1, device_id=peer, device_id_type=MESH)
    pl.semaphore_wait(barrier, len(peers))


HALVES = (("y", 0), ("z", 2))
ORDER = (0, -1, 1, 2)


def plane_gather(own, view, send, recv, after_row):
    started = []

    def copy(half, kind, source, target, peer):
        return pltpu.make_async_remote_copy(
            src_ref=source,
            dst_ref=target,
            send_sem=send.at[half, kind],
            recv_sem=recv.at[half, kind],
            device_id=peer,
            device_id_type=MESH,
        )

    def push(half, kind, source, target, peer):
        item = copy(half, kind, source, target, peer)
        item.start()
        started.append(item)

    def arrived(half, kind, target):
        first, _ = HALVES[half]
        copy(half, kind, target, target, plane_peer(first, 1, 0)).wait_recv()

    def block(half, along_first, along_second, low, count):
        first, base = HALVES[half]
        z, y = plane_place(first, along_first, along_second)
        return view(z, y, base + low, count)

    def ring(half, slot, axis, along, source):
        first, base = HALVES[half]
        for kind, step in ((0, 1), (1, -1)):
            peer = plane_peer(first, step, 0) if axis == 0 else plane_peer(first, 0, step)
            push(half, 4 * slot + kind, source, block(half, along, 0, 0, 2), peer)

    def ring_relay(half, slot, axis, along):
        first, base = HALVES[half]
        for kind, step in ((0, 1), (1, -1)):
            where = (-step, 0) if axis == 0 else (along, -step)
            arrived(half, 4 * slot + kind, block(half, where[0], where[1], 0, 2))
            part = block(half, where[0], where[1], kind, 1)
            peer = plane_peer(first, step, 0) if axis == 0 else plane_peer(first, 0, step)
            push(half, 4 * slot + 2 + kind, part, part, peer)

    def ring_end(half, slot, axis, along):
        where = (2, 0) if axis == 0 else (along, 2)
        for kind in (0, 1):
            arrived(half, 4 * slot + 2 + kind, block(half, where[0], where[1], kind, 1))

    for half in (0, 1):
        ring(half, 0, 0, 0, own(HALVES[half][1], 2))
    for half in (0, 1):
        ring(half, 1, 1, 0, own(HALVES[half][1], 2))
    yield
    for half in (0, 1):
        ring_relay(half, 0, 0, 0)
        for slot in (1, 2):
            ring(half, 1 + slot, 1, ORDER[slot], block(half, ORDER[slot], 0, 0, 2))
    yield
    for half in (0, 1):
        ring_end(half, 0, 0, 0)
        ring(half, 4, 1, 2, block(half, 2, 0, 0, 2))
        after_row(half, 0)
    for slot in (0, 1, 2, 3):
        for half in (0, 1):
            ring_relay(half, 1 + slot, 1, ORDER[slot])
        yield
    for half in (0, 1):
        after_row(half, -1)
        after_row(half, 1)
    for half in (0, 1):
        for slot in (0, 1, 2, 3):
            ring_end(half, 1 + slot, 1, ORDER[slot])
        after_row(half, 2)
    for item in started:
        item.wait_send()


def plane_reduce(parts, far, near, far_last, near_last, send, recv, store):
    started = []

    def copy(half, kind, source, target, peer):
        return pltpu.make_async_remote_copy(
            src_ref=source,
            dst_ref=target,
            send_sem=send.at[half, kind],
            recv_sem=recv.at[half, kind],
            device_id=peer,
            device_id_type=MESH,
        )

    def push(half, kind, source, target, peer):
        item = copy(half, kind, source, target, peer)
        item.start()
        started.append(item)

    def arrived(half, kind, target):
        first, _ = HALVES[half]
        copy(half, kind, target, target, plane_peer(first, 1, 0)).wait_recv()

    def rows(half, offset, low, count):
        first, base = HALVES[half]
        z, y = plane_place(first, 0, offset)
        if first == "y":
            return parts.at[z, :, pl.ds(base + low, count)]
        return parts.at[:, y, pl.ds(base + low, count)]

    def one(half, offset, low, count):
        first, base = HALVES[half]
        z, y = plane_place(first, offset, 0)
        return parts.at[z, y, pl.ds(base + low, count)]

    def add(target, *others):
        total = target[...].astype(jnp.float32)
        for other in others:
            total = total + other[...].astype(jnp.float32)
        target[...] = total.astype(target.dtype)

    def add_rows(half, offset, low, count, *others):
        target = rows(half, offset, low, count)
        def step(at, carry):
            add(target.at[at], *[other.at[at] for other in others])
            return carry
        lax.fori_loop(0, SIDE, step, 0)

    def peer(half, axis, step):
        first, _ = HALVES[half]
        return plane_peer(first, 0, step) if axis == 1 else plane_peer(first, step, 0)

    for half in (0, 1):
        push(half, 0, rows(half, 2, 0, 1), far.at[half, 0], peer(half, 1, 1))
        push(half, 1, rows(half, 2, 1, 1), far.at[half, 1], peer(half, 1, -1))
    yield
    for half in (0, 1):
        push(half, 2, rows(half, 1, 1, 1), near.at[half, 0, :, pl.ds(1, 1)], peer(half, 1, 1))
        push(half, 3, rows(half, -1, 0, 1), near.at[half, 1, :, pl.ds(0, 1)], peer(half, 1, -1))
    yield
    for half in (0, 1):
        arrived(half, 0, far.at[half, 0])
        add_rows(half, 1, 0, 1, far.at[half, 0])
        push(half, 4, rows(half, 1, 0, 1), near.at[half, 0, :, pl.ds(0, 1)], peer(half, 1, 1))
        arrived(half, 1, far.at[half, 1])
        add_rows(half, -1, 1, 1, far.at[half, 1])
        push(half, 5, rows(half, -1, 1, 1), near.at[half, 1, :, pl.ds(1, 1)], peer(half, 1, -1))
    yield
    for half in (0, 1):
        arrived(half, 2, near.at[half, 0, :, pl.ds(1, 1)])
        arrived(half, 3, near.at[half, 1, :, pl.ds(0, 1)])
        arrived(half, 4, near.at[half, 0, :, pl.ds(0, 1)])
        arrived(half, 5, near.at[half, 1, :, pl.ds(1, 1)])
        add_rows(half, 0, 0, 2, near.at[half, 0], near.at[half, 1])
        push(half, 6, one(half, 2, 0, 1), far_last.at[half, 0], peer(half, 0, 1))
        push(half, 7, one(half, 2, 1, 1), far_last.at[half, 1], peer(half, 0, -1))
        push(half, 8, one(half, 1, 1, 1), near_last.at[half, 0, pl.ds(1, 1)], peer(half, 0, 1))
        push(half, 9, one(half, -1, 0, 1), near_last.at[half, 1, pl.ds(0, 1)], peer(half, 0, -1))
    yield
    for half in (0, 1):
        arrived(half, 6, far_last.at[half, 0])
        add(one(half, 1, 0, 1), far_last.at[half, 0])
        push(half, 10, one(half, 1, 0, 1), near_last.at[half, 0, pl.ds(0, 1)], peer(half, 0, 1))
        arrived(half, 7, far_last.at[half, 1])
        add(one(half, -1, 1, 1), far_last.at[half, 1])
        push(half, 11, one(half, -1, 1, 1), near_last.at[half, 1, pl.ds(1, 1)], peer(half, 0, -1))
    yield
    for half in (0, 1):
        arrived(half, 8, near_last.at[half, 0, pl.ds(1, 1)])
        arrived(half, 9, near_last.at[half, 1, pl.ds(0, 1)])
        arrived(half, 10, near_last.at[half, 0, pl.ds(0, 1)])
        arrived(half, 11, near_last.at[half, 1, pl.ds(1, 1)])
        total = one(half, 0, 0, 2)[...].astype(jnp.float32)
        for side in (0, 1):
            total = total + near_last[half, side].astype(jnp.float32)
        store(HALVES[half][1], total)
    for item in started:
        item.wait_send()


def reduce_scratch(quarter_rows, width):
    unit = (quarter_rows, width)
    return [
        pltpu.VMEM((SIDE, SIDE, 4) + unit, jnp.bfloat16),
        pltpu.VMEM((2, 2, SIDE, 1) + unit, jnp.bfloat16),
        pltpu.VMEM((2, 2, SIDE, 2) + unit, jnp.bfloat16),
        pltpu.VMEM((2, 2, 1) + unit, jnp.bfloat16),
        pltpu.VMEM((2, 2, 2) + unit, jnp.bfloat16),
        pltpu.SemaphoreType.DMA((2, 12)),
        pltpu.SemaphoreType.DMA((2, 12)),
    ]


def comm_params(number, limit_mb):
    return pltpu.CompilerParams(
        collective_id=number, has_side_effects=True, vmem_limit_bytes=limit_mb * 1024 * 1024
    )


def nothing(half, offset):
    return None


def advance(steps):
    next(steps, None)


def finish(steps):
    for _ in steps:
        pass


def pair_up(low, high, lane):
    return (
        jnp.where(lane < HEAD_DIM, low, pltpu.roll(high, HEAD_DIM, 1)),
        jnp.where(lane < HEAD_DIM, pltpu.roll(low, HEAD_DIM, 1), high),
    )


def by_group(rows):
    lane = lax.broadcasted_iota(jnp.int32, (rows.shape[0], 128), 1)
    tile = lambda at: rows[:, at * 128 : (at + 1) * 128]
    parts = []
    for j in range(4):
        low, high = tile(8 + j), tile(12 + j)
        first, second = pair_up(low, high, lane)
        parts += [tile(2 * j), first, tile(2 * j + 1), second]
    return jnp.concatenate(parts, axis=1)


def by_kind(rows):
    lane = lax.broadcasted_iota(jnp.int32, (rows.shape[0], 128), 1)
    tile = lambda at: rows[:, at * 128 : (at + 1) * 128]
    queries, keys, values = [], [], []
    for j in range(4):
        queries += [tile(4 * j), tile(4 * j + 2)]
        key, value = pair_up(tile(4 * j + 1), tile(4 * j + 3), lane)
        keys.append(key)
        values.append(value)
    return jnp.concatenate(queries + keys + values, axis=1)


def weights_gather(qkv, others, number):
    rows, qkv_width = qkv.shape
    width = qkv_width + sum(other.shape[1] for other in others)

    def kernel(*refs):
        ins, out_ref, rest = refs[: 1 + len(others)], refs[1 + len(others)], refs[2 + len(others) :]
        own_ref, send, recv, x_send, x_recv, core_send, core_recv, local_sem = rest
        own_ref[:, pl.ds(0, qkv_width)] = by_group(ins[0][...].astype(jnp.float32)).astype(
            own_ref.dtype
        )
        at = qkv_width
        for other in ins[1:]:
            own_ref[:, pl.ds(at, other.shape[1])] = other[...]
            at += other.shape[1]
        seq = lax.axis_index("seq")
        x, core = seq // 2, seq % 2
        x_peers = [seq_peer(step, False) for step in (1, 3, 2)]
        other = seq_peer(0, True)
        greet(plane_neighbours() + x_peers + [other])
        z, y = plane_place("y", 0, 0)
        keep = pltpu.make_async_copy(own_ref, out_ref.at[x, core, z, y], local_sem)
        keep.start()
        sends = []
        for i, step in enumerate((1, 3, 2)):
            item = pltpu.make_async_remote_copy(
                src_ref=own_ref,
                dst_ref=out_ref.at[x, core, z, y],
                send_sem=x_send.at[i],
                recv_sem=x_recv.at[i],
                device_id=x_peers[i],
                device_id_type=MESH,
            )
            item.start()
            sends.append(item)
        keep.wait()
        for i, step in enumerate((1, 3, 2)):
            came = out_ref.at[(x + SIDE - step) % SIDE, core, z, y]
            pltpu.make_async_remote_copy(
                src_ref=came,
                dst_ref=came,
                send_sem=x_send.at[i],
                recv_sem=x_recv.at[i],
                device_id=x_peers[i],
                device_id_type=MESH,
            ).wait_recv()

        swaps = []

        def swap(half, offset):
            first, base = HALVES[half]
            z, y = plane_place(first, 0, offset)
            mine = (
                out_ref.at[pl.ds(base, 2), core, z]
                if first == "y"
                else out_ref.at[pl.ds(base, 2), core, :, y]
            )
            theirs = (
                out_ref.at[pl.ds(base, 2), 1 - core, z]
                if first == "y"
                else out_ref.at[pl.ds(base, 2), 1 - core, :, y]
            )
            kind = ORDER.index(offset)
            item = pltpu.make_async_remote_copy(
                src_ref=mine,
                dst_ref=mine,
                send_sem=core_send.at[half, kind],
                recv_sem=core_recv.at[half, kind],
                device_id=other,
                device_id_type=MESH,
            )
            item.start()
            sends.append(item)
            swaps.append(
                pltpu.make_async_remote_copy(
                    src_ref=theirs,
                    dst_ref=theirs,
                    send_sem=core_send.at[half, kind],
                    recv_sem=core_recv.at[half, kind],
                    device_id=other,
                    device_id_type=MESH,
                )
            )

        finish(
            plane_gather(
                lambda low, count: out_ref.at[pl.ds(low, count), core, z, y],
                lambda z, y, low, count: out_ref.at[pl.ds(low, count), core, z, y],
                send,
                recv,
                swap,
            )
        )
        for item in swaps:
            item.wait_recv()
        for item in sends:
            item.wait_send()

    out = pl.pallas_call(
        kernel,
        out_shape=jax.ShapeDtypeStruct((4, 2, SIDE, SIDE, rows, width), qkv.dtype),
        in_specs=[pl.BlockSpec(memory_space=pltpu.VMEM)] * (1 + len(others)),
        out_specs=pl.BlockSpec(memory_space=pl.ANY),
        scratch_shapes=[
            pltpu.VMEM((rows, width), qkv.dtype),
            pltpu.SemaphoreType.DMA((2, 20)),
            pltpu.SemaphoreType.DMA((2, 20)),
            pltpu.SemaphoreType.DMA((3,)),
            pltpu.SemaphoreType.DMA((3,)),
            pltpu.SemaphoreType.DMA((2, 4)),
            pltpu.SemaphoreType.DMA((2, 4)),
            pltpu.SemaphoreType.DMA,
        ],
        compiler_params=comm_params(number, 8),
        name="weights_gather",
    )(qkv, *others)
    return out.reshape(4 * 2 * SIDE * SIDE * rows, width)


def ring_reduce(sums, far, near, send, recv, outs):
    x = lax.axis_index("seq") // 2
    started = []

    def copy(m, kind, source, target, step):
        return pltpu.make_async_remote_copy(
            src_ref=source,
            dst_ref=target,
            send_sem=send.at[m, kind],
            recv_sem=recv.at[m, kind],
            device_id=seq_peer(step, False),
            device_id_type=MESH,
        )

    def push(m, kind, source, target, step):
        item = copy(m, kind, source, target, step)
        item.start()
        started.append(item)

    def arrived(m, kind, target):
        copy(m, kind, target, target, 1).wait_recv()

    def at(step):
        return (x + step) % SIDE

    count = len(sums)
    for m in range(count):
        push(m, 0, sums[m].at[0, at(2)], far[m].at[0], 1)
        push(m, 1, sums[m].at[1, at(2)], far[m].at[1], 3)
    for m in range(count):
        push(m, 2, sums[m].at[1, at(1)], near[m].at[0, 1], 1)
        push(m, 3, sums[m].at[0, at(3)], near[m].at[1, 0], 3)
    yield
    for m in range(count):
        for kind, expert, step in ((0, 0, 1), (1, 1, 3)):
            arrived(m, kind, far[m].at[kind])
            target = sums[m].at[expert, at(step)]
            target[...] = (
                target[...].astype(jnp.float32) + far[m][kind].astype(jnp.float32)
            ).astype(target.dtype)
            push(m, 4 + kind, target, near[m].at[kind, expert], step)
    yield
    for m in range(count):
        arrived(m, 2, near[m].at[0, 1])
        arrived(m, 3, near[m].at[1, 0])
        arrived(m, 4, near[m].at[0, 0])
        arrived(m, 5, near[m].at[1, 1])
        for expert in (0, 1):
            outs[m][expert] = (
                sums[m][expert, at(0)].astype(jnp.float32)
                + near[m][0, expert].astype(jnp.float32)
                + near[m][1, expert].astype(jnp.float32)
            )
    for item in started:
        item.wait_send()


def weights_reduce(pieces, experts, number):
    widths = [piece.shape[1] for piece in pieces]
    width = sum(widths)
    rows = pieces[0].shape[0] // (4 * 2 * SIDE * SIDE)
    kinds = len(experts)
    shares = [
        (2, 4, 2, expert.shape[1] // 8, expert.shape[2]) for expert in experts
    ]

    def kernel(*refs):
        refs = list(refs)
        take = lambda count: [refs.pop(0) for _ in range(count)]
        ins, ex_ins = take(len(widths)), take(kinds)
        qkv_ref, out_ref, small_ref = take(3)
        ex_outs = take(kinds)
        (parts, far, near, far_last, near_last, send, recv, twin, mine, from_x, load, core_send,
         core_recv, x_send, x_recv) = take(15)
        ex_sums, ex_twins, ex_far, ex_near = take(kinds), take(kinds), take(kinds), take(kinds)
        ex_load, ex_core_send, ex_core_recv, ring_send, ring_recv = take(5)
        seq = lax.axis_index("seq")
        x, core = seq // 2, seq % 2
        x_peers = [seq_peer(step, False) for step in (1, 3, 2)]
        other = seq_peer(0, True)
        loads = []
        for quarter in range(4):
            at = 0
            for i, one_width in enumerate(widths):
                item = pltpu.make_async_copy(
                    ins[i].at[quarter, core],
                    parts.at[:, :, quarter, :, pl.ds(at, one_width)],
                    load.at[quarter, i],
                )
                item.start()
                loads.append(item)
                at += one_width
        ex_loads = []
        for m in range(kinds):
            ex_loads.append(
                pltpu.make_async_copy(ex_ins[m].at[:, :, core], ex_sums[m], ex_load.at[m])
            )
            ex_loads[-1].start()
        greet(plane_neighbours() + x_peers + [other])
        swaps = []
        for quarter in range(4):
            at = 0
            for i, one_width in enumerate(widths):
                item = pltpu.make_async_remote_copy(
                    src_ref=ins[i].at[quarter, 1 - core],
                    dst_ref=twin.at[quarter, :, :, :, pl.ds(at, one_width)],
                    send_sem=core_send.at[quarter, i],
                    recv_sem=core_recv.at[quarter, i],
                    device_id=other,
                    device_id_type=MESH,
                )
                item.start()
                swaps.append(item)
                at += one_width
        ex_swaps = []
        for m in range(kinds):
            item = pltpu.make_async_remote_copy(
                src_ref=ex_ins[m].at[:, :, 1 - core],
                dst_ref=ex_twins[m],
                send_sem=ex_core_send.at[m],
                recv_sem=ex_core_recv.at[m],
                device_id=other,
                device_id_type=MESH,
            )
            item.start()
            ex_swaps.append(item)
        for quarter in range(4):
            for i in range(len(widths)):
                loads[quarter * len(widths) + i].wait()
                swaps[quarter * len(widths) + i].wait_recv()

            def add(at, carry):
                z, y = at // SIDE, at % SIDE
                parts[z, y, quarter] = (
                    parts[z, y, quarter].astype(jnp.float32)
                    + twin[quarter, z, y].astype(jnp.float32)
                ).astype(parts.dtype)
                return carry

            lax.fori_loop(0, SIDE * SIDE, add, 0)

        def store(low, total):
            mine[pl.ds(low, 2)] = total.astype(mine.dtype)

        plane = plane_reduce(parts, far, near, far_last, near_last, send, recv, store)
        advance(plane)
        advance(plane)
        for m in range(kinds):
            ex_loads[m].wait()
            ex_swaps[m].wait_recv()

            def add_pair(at, carry):
                ex_sums[m][at // 4, at % 4] = (
                    ex_sums[m][at // 4, at % 4].astype(jnp.float32)
                    + ex_twins[m][at // 4, at % 4].astype(jnp.float32)
                ).astype(jnp.bfloat16)
                return carry

            lax.fori_loop(0, 8, add_pair, 0)
        ring = ring_reduce(ex_sums, ex_far, ex_near, ring_send, ring_recv, ex_outs)
        advance(ring)
        advance(plane)
        advance(ring)
        advance(plane)
        advance(plane)
        finish(ring)
        finish(plane)
        sends = []
        for i, step in enumerate((1, 3, 2)):
            item = pltpu.make_async_remote_copy(
                src_ref=mine.at[(x + step) % SIDE],
                dst_ref=from_x.at[i],
                send_sem=x_send.at[i],
                recv_sem=x_recv.at[i],
                device_id=x_peers[i],
                device_id_type=MESH,
            )
            item.start()
            sends.append(item)
        total = mine[x].astype(jnp.float32)
        for i in range(3):
            sends[i].wait_recv()
            total = total + from_x[i].astype(jnp.float32)
        qkv_ref[...] = by_kind(total[:, : widths[0]])
        out_ref[...] = total[:, widths[0] : widths[0] + widths[1]]
        small_ref[...] = total[:, widths[0] + widths[1] :]
        for item in sends + swaps + ex_swaps:
            item.wait_send()

    unit = (rows, width)
    pairs = (4, len(widths))
    vmem = pl.BlockSpec(memory_space=pltpu.VMEM)
    return pl.pallas_call(
        kernel,
        out_shape=tuple(
            [jax.ShapeDtypeStruct((rows, one_width), jnp.float32) for one_width in widths]
            + [jax.ShapeDtypeStruct((2,) + share[3:], jnp.float32) for share in shares]
        ),
        in_specs=[pl.BlockSpec(memory_space=pl.ANY)] * (len(widths) + kinds),
        out_specs=(vmem,) * (len(widths) + kinds),
        scratch_shapes=reduce_scratch(rows, width)
        + [
            pltpu.VMEM((4, SIDE, SIDE) + unit, jnp.bfloat16),
            pltpu.VMEM((4,) + unit, jnp.bfloat16),
            pltpu.VMEM((3,) + unit, jnp.bfloat16),
            pltpu.SemaphoreType.DMA(pairs),
            pltpu.SemaphoreType.DMA(pairs),
            pltpu.SemaphoreType.DMA(pairs),
            pltpu.SemaphoreType.DMA((3,)),
            pltpu.SemaphoreType.DMA((3,)),
        ]
        + [pltpu.VMEM((2, 4) + share[3:], jnp.bfloat16) for share in shares]
        + [pltpu.VMEM((2, 4) + share[3:], jnp.bfloat16) for share in shares]
        + [pltpu.VMEM((2,) + share[3:], jnp.bfloat16) for share in shares]
        + [pltpu.VMEM((2, 2) + share[3:], jnp.bfloat16) for share in shares]
        + [pltpu.SemaphoreType.DMA((kinds,))] * 3
        + [pltpu.SemaphoreType.DMA((kinds, 6))] * 2,
        compiler_params=comm_params(number, 48),
        name="weights_reduce",
    )(
        *[piece.reshape(4, 2, SIDE, SIDE, rows, piece.shape[1]) for piece in pieces],
        *[expert.reshape(share) for expert, share in zip(experts, shares)],
    )


def rms_scale(values):
    return lax.rsqrt(jnp.mean(values * values, axis=-1, keepdims=True) + epsilon)


def rope_tables(length):
    half_dim = HEAD_DIM // 2
    frequency = np.float32(rope_theta) ** (
        -np.arange(half_dim, dtype=np.float32) / np.float32(half_dim)
    )
    angles = np.arange(length, dtype=np.float32)[:, None] * frequency[None, :].astype(np.float32)
    cosine = np.cos(angles.astype(np.float64)).astype(np.float32)
    sine = np.sin(angles.astype(np.float64)).astype(np.float32)
    one_cos = np.concatenate([cosine, cosine], axis=1)
    one_sin = np.concatenate([-sine, sine], axis=1)
    flat = np.ones_like(one_cos)
    return (
        np.concatenate([one_cos, one_cos, one_cos, flat], axis=1),
        np.concatenate([one_sin, one_sin, one_sin, 0.0 * flat], axis=1),
    )


def turn(values, cosine, sine):
    half_dim = HEAD_DIM // 2
    width = values.shape[1]
    lane = lax.broadcasted_iota(jnp.int32, values.shape, 1)
    ahead = pltpu.roll(values, width - half_dim, 1)
    behind = pltpu.roll(values, half_dim, 1)
    return values * cosine + jnp.where(lane % HEAD_DIM < half_dim, ahead, behind) * sine


SEQ_STEPS = (4, 5, 3, 2, 6, 1, 7)


def seq_exchange(source, target, send, recv):
    me = lax.axis_index("seq")
    count = 8

    def copy(step, peer, out_of, into):
        return pltpu.make_async_remote_copy(
            src_ref=out_of,
            dst_ref=into,
            send_sem=send.at[step - 1],
            recv_sem=recv.at[step - 1],
            device_id={"seq": peer},
            device_id_type=MESH,
        )

    def start(steps):
        items = []
        for step in steps:
            peer = (me + step) % count
            item = copy(step, peer, source(peer), target(me))
            item.start()
            items.append(item)
        return items

    def wait(step):
        peer = (me + count - step) % count
        copy(step, peer, target(peer), target(peer)).wait_recv()

    return (start, wait)


def seq_plane_greet():
    me = lax.axis_index("seq")
    greet(plane_neighbours() + [{"seq": (me + step) % 8} for step in range(1, 8)])


def twice(pair, lane):
    swapped = pltpu.roll(pair.astype(jnp.float32), HEAD_DIM, 1).astype(pair.dtype)
    return (
        jnp.where(lane < HEAD_DIM, pair, swapped),
        jnp.where(lane < HEAD_DIM, swapped, pair),
    )


def apart(pair, lane):
    zero = jnp.zeros_like(pair)
    return jnp.concatenate(
        [jnp.where(lane < HEAD_DIM, pair, zero), jnp.where(lane < HEAD_DIM, zero, pair)], axis=0
    )


def matmul(a, b, dims):
    return lax.dot_general(a, b, (dims, ((), ())), preferred_element_type=jnp.float32)


BLOCK = 256


def block_probs(queries, keys, at):
    scores = matmul(queries, keys, ((1,), (1,)))
    row = lax.broadcasted_iota(jnp.int32, scores.shape, 0) % BLOCK + at * BLOCK
    column = lax.broadcasted_iota(jnp.int32, scores.shape, 1)
    scores = jnp.where(column <= row, scores, -1e30)
    exponent = jnp.exp(scores - jnp.max(scores, axis=1, keepdims=True))
    return exponent * (1.0 / jnp.sum(exponent, axis=1, keepdims=True))


def attention_forward(projected, cosine, sine, beside, number):
    tok, width = projected.shape
    features = beside.shape[1]
    seq_parts = 8
    group = width // seq_parts
    pair = 2 * HEAD_DIM
    length = tok * seq_parts
    per_block = BLOCK // tok

    def kernel(
        proj_ref, cos_ref, sin_ref, beside_ref, out_ref, heads_ref, all_ref,
        packed, mixed, send, recv, o_send, o_recv, p_send, p_recv, local_sem,
    ):
        me = lax.axis_index("seq")
        z, y = plane_place("y", 0, 0)
        keep = pltpu.make_async_copy(beside_ref, all_ref.at[z, y], local_sem)
        keep.start()
        seq_plane_greet()
        steps = plane_gather(
            lambda low, count: beside_ref.at[pl.ds(low, count)],
            lambda z, y, low, count: all_ref.at[z, y, pl.ds(low, count)],
            p_send,
            p_recv,
            nothing,
        )
        advance(steps)
        for d in range(seq_parts):
            packed[d] = turn(
                proj_ref[:, d * group : (d + 1) * group], cos_ref[...], sin_ref[...]
            ).astype(packed.dtype)
        start, wait = seq_exchange(
            lambda d: packed.at[d], lambda d: heads_ref.at[d], send, recv
        )
        items = start(SEQ_STEPS)
        heads_ref[me] = packed[me]
        advance(steps)
        for step in SEQ_STEPS:
            wait(step)
        advance(steps)
        lane = lax.broadcasted_iota(jnp.int32, (length, pair), 1)
        heads = heads_ref[...].reshape(length, group)
        keys, values = twice(heads[:, pair:], lane)
        lane_block = lane[:BLOCK]
        back, back_wait = seq_exchange(
            lambda d: mixed.at[d],
            lambda d: out_ref.at[:, pl.ds(pl.multiple_of(d * pair, pair), pair)],
            o_send,
            o_recv,
        )
        for at in range(length // BLOCK):
            block = heads[at * BLOCK : (at + 1) * BLOCK, :pair]
            queries = apart(block * jnp.asarray(attention_multiplier, block.dtype), lane_block)
            upto = (at + 1) * BLOCK
            probs = block_probs(queries, keys[:upto], at).astype(jnp.bfloat16)
            both = matmul(probs, values[:upto], ((1,), (0,)))
            made = jnp.where(lane_block < HEAD_DIM, both[:BLOCK], both[BLOCK:]).astype(mixed.dtype)
            mixed[at * per_block : (at + 1) * per_block] = made.reshape(per_block, tok, pair)
            if at % 2:
                advance(steps)
        items += back(SEQ_STEPS)
        out_ref[:, pl.ds(pl.multiple_of(me * pair, pair), pair)] = mixed[me]
        advance(steps)
        for step in SEQ_STEPS:
            back_wait(step)
        finish(steps)
        keep.wait()
        for item in items:
            item.wait_send()

    vmem = pl.BlockSpec(memory_space=pltpu.VMEM)
    anywhere = pl.BlockSpec(memory_space=pl.ANY)
    attended, heads, gathered = pl.pallas_call(
        kernel,
        out_shape=(
            jax.ShapeDtypeStruct((tok, seq_parts * pair), jnp.bfloat16),
            jax.ShapeDtypeStruct((seq_parts, tok, group), jnp.bfloat16),
            jax.ShapeDtypeStruct((SIDE, SIDE, 4, tok // 4, features), beside.dtype),
        ),
        in_specs=[vmem] * 3 + [anywhere],
        out_specs=(vmem, vmem, anywhere),
        scratch_shapes=[
            pltpu.VMEM((seq_parts, tok, group), jnp.bfloat16),
            pltpu.VMEM((seq_parts, tok, pair), jnp.bfloat16),
        ]
        + [pltpu.SemaphoreType.DMA((7,))] * 4
        + [pltpu.SemaphoreType.DMA((2, 20))] * 2
        + [pltpu.SemaphoreType.DMA],
        compiler_params=comm_params(number, 48),
        name="attention_forward",
    )(projected, cosine, sine, beside.reshape(4, tok // 4, features))
    return (attended, heads, gathered.reshape(SIDE * SIDE, tok, features))


def attention_backward(grad_attended, heads_in, cosine, sine, beside, number):
    seq_parts, tok, group = heads_in.shape
    features = beside.shape[2]
    pair = 2 * HEAD_DIM
    length = tok * seq_parts
    per_block = BLOCK // tok

    def kernel(
        grad_ref, heads_ref, cos_ref, sin_ref, beside_ref, out_ref, sum_ref,
        came, packed, d_queries, d_keys, d_values, send, recv, o_send, o_recv,
        parts, far, near, far_last, near_last, p_send, p_recv, load,
    ):
        me = lax.axis_index("seq")
        loaded = pltpu.make_async_copy(beside_ref, parts, load)
        loaded.start()
        seq_plane_greet()

        def store(low, total):
            sum_ref[pl.ds(low, 2)] = total

        steps = plane_reduce(parts, far, near, far_last, near_last, p_send, p_recv, store)
        columns = lambda d: grad_ref.at[:, pl.ds(pl.multiple_of(d * pair, pair), pair)]
        start, wait = seq_exchange(columns, lambda d: came.at[d], send, recv)
        items = start(SEQ_STEPS)
        loaded.wait()
        advance(steps)
        advance(steps)
        came[me] = grad_ref[:, pl.ds(pl.multiple_of(me * pair, pair), pair)]
        lane = lax.broadcasted_iota(jnp.int32, (length, pair), 1)
        lane_block = lane[:BLOCK]
        heads = heads_ref[...].reshape(length, group)
        keys, values = twice(heads[:, pair:], lane)
        for step in SEQ_STEPS:
            wait(step)
        for at in range(length // BLOCK):
            upto = (at + 1) * BLOCK
            block = heads[at * BLOCK : upto, :pair]
            queries = apart(block * jnp.asarray(attention_multiplier, block.dtype), lane_block)
            grads = apart(
                came[at * per_block : (at + 1) * per_block].reshape(BLOCK, pair), lane_block
            )
            probs = block_probs(queries, keys[:upto], at)
            d_probs = matmul(grads, values[:upto], ((1,), (1,)))
            center = jnp.sum(probs * d_probs, axis=1, keepdims=True)
            d_scores = (probs * (d_probs - center)).astype(jnp.bfloat16)
            both = matmul(d_scores, keys[:upto], ((1,), (0,))) * attention_multiplier
            d_queries[at * BLOCK : upto] = jnp.where(
                lane_block < HEAD_DIM, both[:BLOCK], both[BLOCK:]
            )
            more_keys = matmul(d_scores, queries, ((0,), (0,)))
            more_values = matmul(probs.astype(jnp.bfloat16), grads, ((0,), (0,)))
            before = at * BLOCK
            if at:
                d_keys[:before] += more_keys[:before]
                d_values[:before] += more_values[:before]
            d_keys[before:upto] = more_keys[before:]
            d_values[before:upto] = more_values[before:]
            if at in (1, 2, 3):
                advance(steps)
        sum_keys = d_keys[...] + pltpu.roll(d_keys[...], HEAD_DIM, 1)
        sum_values = d_values[...] + pltpu.roll(d_values[...], HEAD_DIM, 1)
        rest = jnp.where(lane < HEAD_DIM, sum_keys, sum_values)
        whole = jnp.concatenate([d_queries[...], rest], axis=1)
        packed[...] = (
            turn(whole, cos_ref[...], -sin_ref[...])
            .astype(packed.dtype)
            .reshape(seq_parts, tok, group)
        )
        back, back_wait = seq_exchange(
            lambda d: packed.at[d],
            lambda d: out_ref.at[:, pl.ds(pl.multiple_of(d * group, group), group)],
            o_send,
            o_recv,
        )
        items += back(SEQ_STEPS)
        out_ref[:, pl.ds(pl.multiple_of(me * group, group), group)] = packed[me]
        advance(steps)
        for step in SEQ_STEPS:
            back_wait(step)
        finish(steps)
        for item in items:
            item.wait_send()

    vmem = pl.BlockSpec(memory_space=pltpu.VMEM)
    grads, summed = pl.pallas_call(
        kernel,
        out_shape=(
            jax.ShapeDtypeStruct((tok, seq_parts * group), jnp.bfloat16),
            jax.ShapeDtypeStruct((4, tok // 4, features), jnp.float32),
        ),
        in_specs=[vmem] * 4 + [pl.BlockSpec(memory_space=pl.ANY)],
        out_specs=(vmem, vmem),
        scratch_shapes=[
            pltpu.VMEM((seq_parts, tok, pair), jnp.bfloat16),
            pltpu.VMEM((seq_parts, tok, group), jnp.bfloat16),
            pltpu.VMEM((length, pair), jnp.float32),
            pltpu.VMEM((length, pair), jnp.float32),
            pltpu.VMEM((length, pair), jnp.float32),
        ]
        + [pltpu.SemaphoreType.DMA((7,))] * 4
        + reduce_scratch(tok // 4, features)
        + [pltpu.SemaphoreType.DMA],
        compiler_params=comm_params(number, 56),
        name="attention_backward",
    )(grad_attended, heads_in, cosine, sine, beside.reshape(SIDE, SIDE, 4, tok // 4, features))
    return (grads, summed.reshape(tok, features))


def gate_columns(logits, chosen_ids, experts_all):
    named = jnp.any(
        chosen_ids[..., None] == jnp.arange(experts_all, dtype=jnp.int32), axis=-2
    )
    peak = jnp.max(jnp.where(named, logits, -jnp.inf), axis=-1, keepdims=True)
    exponent = jnp.where(named, jnp.exp(logits - peak), 0.0)
    gates = exponent / jnp.sum(exponent, axis=-1, keepdims=True)
    coarse = lax.reduce_precision(gates, 8, 7)
    columns = jnp.concatenate(
        [named.astype(jnp.float32), coarse, gates - coarse, jnp.zeros_like(gates)], axis=-1
    ).astype(jnp.bfloat16)
    return (gates, columns)


def near_place(at):
    if isinstance(at, int) and at >= 9:
        return far_place(at)
    return (at // 3 - 1, at % 3 - 1)


def far_place(at):
    beyond = at - 9
    turn_over = beyond // 4
    return (
        2 * (1 - turn_over) + turn_over * (beyond - 5),
        (1 - turn_over) * (beyond - 1) + turn_over * 2,
    )


def expert_layer(
    tokens_own, cot_all, gate_full, up_full, down_full, experts_all, capacity, number
):
    tok, wide = tokens_own.shape
    sources = SIDE * SIDE
    quarter = tok // 4
    features = wide - 128
    hidden_units = gate_full.shape[2]
    group = 8
    chunks = sources // group
    chunk_rows = group * capacity
    f32, b16 = jnp.float32, jnp.bfloat16

    def kernel(
        tok_hbm, cot_hbm, gate_hbm, up_hbm, down_hbm,
        mix_hbm, back_ref, ggate_hbm, gup_hbm, gdown_hbm,
        tok_v, cot_v, gate_v, up_v, down_v, mix_v, grad_v,
        x_v, deo_v, slope_v, act_v, inner_v, pick_t, share_v, dgate_v,
        in_sem, out_sem, g_send, g_recv,
        rows_v, far, near, far_last, near_last, r_send, r_recv,
    ):
        first = lax.axis_index("wshard") * 2
        home_z, home_y = plane_place("y", 0, 0)
        loads = [
            pltpu.make_async_copy(source, target, in_sem.at[i])
            for i, (source, target) in enumerate(
                [(tok_hbm, tok_v.at[home_z, home_y]), (cot_hbm, cot_v), (gate_hbm, gate_v), (up_hbm, up_v),
                 (down_hbm, down_v)]
            )
        ]
        for item in loads:
            item.start()
        lane = lax.broadcasted_iota(jnp.int32, (tok, 128), 1)
        down_rows = lax.broadcasted_iota(jnp.int32, (tok, 128), 0)
        lower = jnp.where(down_rows >= lane, 1.0, 0.0).astype(b16)
        greet(plane_neighbours())
        gather = plane_gather(
            lambda low, count: tok_hbm.at[pl.ds(low, count)],
            lambda z, y, low, count: tok_v.at[z, y, pl.ds(low, count)],
            g_send,
            g_recv,
            nothing,
        )
        advance(gather)
        advance(gather)
        advance(gather)
        advance(gather)
        advance(gather)
        loads[0].wait()
        loads[1].wait()

        def prepare(s, place_of):
            off_z, off_y = place_of(s)
            z, y = plane_place("y", off_y, off_z)
            info = tok_v[z, y, :, :, pl.ds(features, 128)].reshape(tok, 128)
            info32 = info.astype(f32)
            place = matmul(lower, info, ((1,), (0,))) - 1.0
            place = jnp.where(info32 > 0.5, place, -1.0)
            place_rows = place.T
            info_rows = info32.T
            row_picks, col_places = [], []
            shares = []
            for e in (0, 1):
                at = first + e
                row = jnp.sum(jnp.where(down_rows == at, place_rows, 0.0), axis=0, keepdims=True)
                gate = jnp.sum(
                    jnp.where(
                        (down_rows == experts_all + at) | (down_rows == 2 * experts_all + at),
                        info_rows,
                        0.0,
                    ),
                    axis=0,
                    keepdims=True,
                )
                slot = lax.broadcasted_iota(jnp.int32, (capacity, tok), 0).astype(f32)
                hit = slot == row
                row_picks.append(jnp.where(hit, 1.0, 0.0))
                shares.append(jnp.sum(jnp.where(hit, gate, 0.0), axis=1, keepdims=True))
                col_places.append(
                    jnp.sum(jnp.where(lane == at, place, 0.0), axis=1, keepdims=True)
                )
            pick = jnp.concatenate(row_picks, axis=0).astype(b16)
            lane_f = lane.astype(f32)
            pick_t[s] = (
                jnp.where(lane_f == col_places[0], 1.0, 0.0) * jnp.where(lane < capacity, 1.0, 0.0)
                + jnp.where(lane_f - float(capacity) == col_places[1], 1.0, 0.0)
                * jnp.where(lane >= capacity, 1.0, 0.0)
            ).astype(b16)
            share_v[s] = jnp.concatenate(shares, axis=0)
            rows = matmul(
                pick, tok_v[z, y, :, :, pl.ds(0, features)].reshape(tok, features), ((1,), (0,))
            ).astype(b16)
            c, i = s // group, s % group
            x_v[0, c, i] = rows[:capacity]
            x_v[1, c, i] = rows[capacity:]
            cots = matmul(pick, cot_v[z, y], ((1,), (0,))).astype(b16)
            deo_v[0, c, i] = cots[:capacity]
            deo_v[1, c, i] = cots[capacity:]

        def prepare_all(low, high, place_of):
            def step(s, carry):
                prepare(s, place_of)
                return carry

            lax.fori_loop(low, high, step, 0)

        def forward(c):
            weighted = []
            for e in (0, 1):
                x = x_v[e, c].reshape(chunk_rows, features)
                gate_val = matmul(x, gate_v[e], ((1,), (0,)))
                up_val = matmul(x, up_v[e], ((1,), (0,)))
                sigma = 1.0 / (1.0 + jnp.exp(-gate_val))
                act = gate_val * sigma
                inner = (act * up_val).astype(b16)
                inner_v[e, c] = inner
                act_v[e, c] = act.astype(b16)
                slope_v[e, c] = (up_val * (sigma * (1.0 + gate_val * (1.0 - sigma)))).astype(b16)
                made = matmul(inner, down_v[e], ((1,), (0,))).astype(b16).astype(f32)
                share = jnp.concatenate(
                    [share_v[c * group + i, pl.ds(e * capacity, capacity)] for i in range(group)],
                    axis=0,
                )
                mix_grad = residual_multiplier * deo_v[e, c].reshape(chunk_rows, features).astype(f32)
                dgate_v[e, c] = jnp.sum(made * mix_grad, axis=1, keepdims=True)
                deo_v[e, c] = (share * mix_grad).astype(b16).reshape(group, capacity, features)
                weighted.append((share * made).astype(b16))
            for i in range(group):
                both = jnp.concatenate(
                    [w[i * capacity : (i + 1) * capacity] for w in weighted], axis=0
                )
                off_z, off_y = near_place(c * group + i)
                z, y = plane_place("y", off_y, off_z)
                mix_v[z, y] = matmul(pick_t[c * group + i], both, ((1,), (0,))).astype(b16)

        prepare_all(0, 9, near_place)
        advance(gather)
        for item in loads[2:]:
            item.wait()
        forward(0)
        finish(gather)
        prepare_all(9, sources, far_place)
        forward(1)
        stores = [pltpu.make_async_copy(mix_v, mix_hbm, out_sem.at[0])]
        stores[0].start()
        lane_rows = lax.broadcasted_iota(jnp.int32, (chunk_rows, 128), 1)

        def backward(c):
            made = []
            for e in (0, 1):
                deo = deo_v[e, c].reshape(chunk_rows, features)
                d_inner = matmul(deo, down_v[e], ((1,), (1,)))
                d_gate = (d_inner * slope_v[e, c].astype(f32)).astype(b16)
                d_up = (d_inner * act_v[e, c].astype(f32)).astype(b16)
                slope_v[e, c] = d_gate
                act_v[e, c] = d_up
                d_rows = (
                    matmul(d_gate, gate_v[e], ((1,), (1,))) + matmul(d_up, up_v[e], ((1,), (1,)))
                ).astype(b16)
                coarse = dgate_v[e, c].astype(b16).astype(f32)
                fine = dgate_v[e, c] - coarse
                columns = jnp.where(lane_rows == first + e, coarse, 0.0) + jnp.where(
                    lane_rows == experts_all + first + e, fine, 0.0
                )
                made.append(jnp.concatenate([d_rows, columns.astype(b16)], axis=1))
            for i in range(group):
                both = jnp.concatenate(
                    [m[i * capacity : (i + 1) * capacity] for m in made], axis=0
                )
                off_z, off_y = near_place(c * group + i)
                z, y = plane_place("y", off_y, off_z)
                rows_v[z, y] = (
                    matmul(pick_t[c * group + i], both, ((1,), (0,)))
                    .astype(b16)
                    .reshape(4, quarter, wide)
                )

        def store(low, total):
            back_ref[pl.ds(low, 2)] = total

        reduce = plane_reduce(
            rows_v, far, near, far_last, near_last, r_send, r_recv, store
        )
        backward(1)
        advance(reduce)
        backward(0)
        advance(reduce)
        rows_all = chunks * chunk_rows

        def whole(ref, e, columns):
            return ref[e].reshape(rows_all, columns)

        for e in (0, 1):
            x = whole(x_v, e, features)
            for i, source, target in (
                (e, slope_v, ggate_hbm),
                (2 + e, act_v, gup_hbm),
            ):
                grad_v[i] = matmul(x, whole(source, e, hidden_units), ((0,), (0,))).astype(b16)
                stores.append(
                    pltpu.make_async_copy(grad_v.at[i], target.at[e], out_sem.at[1 + i])
                )
                stores[-1].start()
            advance(reduce)
        for e in (0, 1):
            grad = matmul(
                whole(inner_v, e, hidden_units), whole(deo_v, e, features), ((0,), (0,))
            ).astype(b16)
            cot_v[e] = grad.reshape(4, 128, features)
            stores.append(
                pltpu.make_async_copy(cot_v.at[e], gdown_hbm.at[e], out_sem.at[5 + e])
            )
            stores[-1].start()
            if e == 0:
                advance(reduce)
        finish(reduce)
        for item in stores:
            item.wait()

    anywhere = pl.BlockSpec(memory_space=pl.ANY)
    local = gate_full.shape[0]
    outs = pl.pallas_call(
        kernel,
        out_shape=(
            jax.ShapeDtypeStruct((SIDE, SIDE, tok, features), b16),
            jax.ShapeDtypeStruct((4, quarter, wide), f32),
            jax.ShapeDtypeStruct((local, features, hidden_units), b16),
            jax.ShapeDtypeStruct((local, features, hidden_units), b16),
            jax.ShapeDtypeStruct((local, 4, hidden_units // 4, features), b16),
        ),
        in_specs=[anywhere] * 5,
        out_specs=(anywhere, pl.BlockSpec(memory_space=pltpu.VMEM)) + (anywhere,) * 3,
        scratch_shapes=[
            pltpu.VMEM((SIDE, SIDE, 4, quarter, wide), b16),
            pltpu.VMEM((SIDE, SIDE, tok, features), b16),
            pltpu.VMEM(gate_full.shape, b16),
            pltpu.VMEM(up_full.shape, b16),
            pltpu.VMEM(down_full.shape, b16),
            pltpu.VMEM((SIDE, SIDE, tok, features), b16),
            pltpu.VMEM((4, features, hidden_units), b16),
            pltpu.VMEM((2, chunks, group, capacity, features), b16),
            pltpu.VMEM((2, chunks, group, capacity, features), b16),
            pltpu.VMEM((2, chunks, chunk_rows, hidden_units), b16),
            pltpu.VMEM((2, chunks, chunk_rows, hidden_units), b16),
            pltpu.VMEM((2, chunks, chunk_rows, hidden_units), b16),
            pltpu.VMEM((sources, tok, 2 * capacity), b16),
            pltpu.VMEM((sources, 2 * capacity, 1), f32),
            pltpu.VMEM((2, chunks, chunk_rows, 1), f32),
            pltpu.SemaphoreType.DMA((5,)),
            pltpu.SemaphoreType.DMA((7,)),
            pltpu.SemaphoreType.DMA((2, 20)),
            pltpu.SemaphoreType.DMA((2, 20)),
        ]
        + reduce_scratch(quarter, wide),
        compiler_params=comm_params(number, 60),
        name="expert_layer",
    )(
        tokens_own.reshape(4, quarter, wide),
        cot_all.reshape(SIDE, SIDE, tok, features),
        gate_full,
        up_full,
        down_full,
    )
    return (
        outs[0].reshape(sources, tok, features),
        outs[1].reshape(tok, wide),
        outs[2],
        outs[3],
        outs[4].reshape(local, hidden_units, features),
    )


def norm_backward(grad_normed, values, scale, gain_full):
    grad_gain = jnp.sum(grad_normed * values * scale, axis=0)
    grad_hat = grad_normed * gain_full
    grad_values = scale * grad_hat - values * (scale * scale * scale) * jnp.mean(
        grad_hat * values, axis=1, keepdims=True
    )
    return (grad_values, grad_gain)


def local(
    tokens,
    weight_qkv,
    weight_out,
    router,
    gain_attn,
    gain_ffn,
    expert_gate,
    expert_up,
    expert_down,
    expert_ids,
    cotangent,
):
    tok_dev = tokens.shape[1]
    features = tokens.shape[2]
    seq_parts = lax.axis_size("seq")
    owners = lax.axis_size("wshard")
    local_experts = expert_gate.shape[0]
    experts_all = local_experts * owners
    top_count = expert_ids.shape[2]
    capacity = 2 * tok_dev * top_count // experts_all
    heads_dev = HEADS // seq_parts
    key_heads = KV_HEADS // seq_parts
    query_cols = heads_dev * HEAD_DIM
    key_cols = key_heads * HEAD_DIM
    query_width = HEADS * HEAD_DIM
    key_width = KV_HEADS * HEAD_DIM
    length = tok_dev * seq_parts
    qkv_width = weight_qkv.shape[1]
    smalls = jnp.concatenate(
        [
            router,
            gain_attn[:, None],
            gain_ffn[:, None],
            jnp.zeros((router.shape[0], 128 - experts_all - 2), jnp.bfloat16),
        ],
        axis=1,
    )
    weights_full = weights_gather(weight_qkv, [weight_out, smalls], 0)
    qkv_full = weights_full[:, :qkv_width]
    out_full = weights_full[:, qkv_width : qkv_width + features]
    smalls_full = weights_full[:, qkv_width + features :]
    router_full = smalls_full[:, :experts_all]
    gain_one = smalls_full[:, experts_all].astype(jnp.float32)
    gain_two = smalls_full[:, experts_all + 1].astype(jnp.float32)
    owned = (
        lax.all_gather(expert_gate, "seq", axis=1, tiled=True),
        lax.all_gather(expert_up, "seq", axis=1, tiled=True),
        lax.all_gather(expert_down, "seq", axis=1, tiled=True),
    )
    gate_full, up_full, down_full = (owned[0], owned[1], owned[2])
    inputs = tokens[0].astype(jnp.float32)
    chosen_ids = expert_ids[0]
    scale_one = rms_scale(inputs)
    normed_one = (inputs * scale_one * gain_one).astype(jnp.bfloat16)
    projected = jnp.dot(normed_one, qkv_full, preferred_element_type=jnp.float32)
    cosine, sine = (jnp.asarray(table) for table in rope_tables(length))
    offset = lax.axis_index("seq") * tok_dev
    attended, heads_all, cot_all = attention_forward(
        projected,
        lax.dynamic_slice_in_dim(cosine, offset, tok_dev),
        lax.dynamic_slice_in_dim(sine, offset, tok_dev),
        cotangent[0],
        5,
    )
    branch = jnp.dot(attended, out_full, preferred_element_type=jnp.float32)
    hidden = inputs + residual_multiplier * branch
    scale_two = rms_scale(hidden)
    normed_two = (hidden * scale_two * gain_two).astype(jnp.bfloat16)
    logits = jnp.dot(normed_two, router_full, preferred_element_type=jnp.float32)
    gates_own, gate_info = gate_columns(logits, chosen_ids, experts_all)
    mix_part, back, grad_gate, grad_up, grad_down = expert_layer(
        jnp.concatenate([normed_two, gate_info], axis=1),
        cot_all,
        gate_full,
        up_full,
        down_full,
        experts_all,
        capacity,
        1,
    )
    grad_output = cotangent[0].astype(jnp.float32)
    grad_back = back[:, :features]
    grad_gates = (
        back[:, features : features + experts_all]
        + back[:, features + experts_all : features + 2 * experts_all]
    )
    grad_logits = (
        gates_own
        * (grad_gates - jnp.sum(gates_own * grad_gates, axis=1, keepdims=True))
    ).astype(jnp.bfloat16)
    grad_normed_two = jnp.dot(grad_logits, router_full.T, preferred_element_type=jnp.float32)
    grad_normed_two = grad_normed_two + grad_back
    grad_hidden_norm, grad_gain_ffn = norm_backward(grad_normed_two, hidden, scale_two, gain_two)
    grad_hidden = grad_output + grad_hidden_norm
    grad_branch = (residual_multiplier * grad_hidden).astype(jnp.bfloat16)
    grad_out = jnp.dot(attended.T, grad_branch, preferred_element_type=jnp.float32)
    grad_attended = jnp.dot(grad_branch, out_full.T, preferred_element_type=jnp.float32).astype(
        jnp.bfloat16
    )
    grad_proj, mixture = attention_backward(
        grad_attended, heads_all, cosine, sine, mix_part, 6
    )
    output = hidden + residual_multiplier * mixture
    grad_qkv = jnp.dot(normed_one.T, grad_proj, preferred_element_type=jnp.float32)
    grad_normed_one = jnp.dot(grad_proj, qkv_full.T, preferred_element_type=jnp.float32)
    grad_input_norm, grad_gain_attn = norm_backward(grad_normed_one, inputs, scale_one, gain_one)
    grad_input = grad_hidden + grad_input_norm
    column = jnp.arange(128, dtype=jnp.int32)[None, :]
    grad_smalls = (
        jnp.dot(
            normed_two.T,
            jnp.pad(grad_logits, ((0, 0), (0, 128 - experts_all))),
            preferred_element_type=jnp.float32,
        )
        + jnp.where(column == experts_all, grad_gain_attn[:, None], 0.0)
        + jnp.where(column == experts_all + 1, grad_gain_ffn[:, None], 0.0)
    ).astype(jnp.bfloat16)
    own_qkv, own_out, own_smalls, own_gate, own_up, own_down = weights_reduce(
        [grad_qkv.astype(jnp.bfloat16), grad_out.astype(jnp.bfloat16), grad_smalls],
        [grad_gate, grad_up, grad_down],
        4,
    )
    shares = (
        own_qkv,
        own_out,
        own_smalls[:, :experts_all],
        own_smalls[:, experts_all],
        own_smalls[:, experts_all + 1],
    )
    expert_shares = (own_gate, own_up, own_down)
    return (
        output.astype(jnp.bfloat16)[None],
        grad_input.astype(jnp.bfloat16)[None],
        shares[0],
        shares[1],
        shares[2],
        shares[3],
        shares[4],
        expert_shares[0],
        expert_shares[1],
        expert_shares[2],
    )


def solution(mesh):
    placed = (
        P("wshard", "seq", None),
        P(("seq", "wshard"), None),
        P(("seq", "wshard"), None),
        P(("seq", "wshard"), None),
        P(("seq", "wshard")),
        P(("seq", "wshard")),
        P("wshard", "seq", None),
        P("wshard", "seq", None),
        P("wshard", "seq", None),
        P("wshard", "seq", None),
        P("wshard", "seq", None),
    )
    return jax.shard_map(
        local,
        mesh=mesh,
        in_specs=placed,
        out_specs=(
            P("wshard", "seq", None),
            P("wshard", "seq", None),
            P(("seq", "wshard"), None),
            P(("seq", "wshard"), None),
            P(("seq", "wshard"), None),
            P(("seq", "wshard")),
            P(("seq", "wshard")),
            P("wshard", "seq", None),
            P("wshard", "seq", None),
            P("wshard", "seq", None),
        ),
        check_vma=False,
    )
```

```python
import jax
import jax.numpy as jnp
import numpy as np
from jax import lax
from jax.experimental import pallas as pl
from jax.experimental.pallas import tpu as pltpu
from jax.sharding import PartitionSpec as P

HEADS = 16
KV_HEADS = 8
HEAD_DIM = 64


epsilon = 1e-06
attention_multiplier = 0.015625
residual_multiplier = 0.22
rope_theta = 10000.0


MESH = pl.DeviceIdType.MESH
SIDE = 4


def plane_place(first, offset_first, offset_second):
    mine = lax.axis_index("wshard")
    z, y = mine // SIDE, mine % SIDE
    if first == "y":
        return ((z + offset_second + SIDE) % SIDE, (y + offset_first + SIDE) % SIDE)
    return ((z + offset_first + SIDE) % SIDE, (y + offset_second + SIDE) % SIDE)


def plane_peer(first, offset_first, offset_second):
    z, y = plane_place(first, offset_first, offset_second)
    return {"wshard": z * SIDE + y}


def plane_neighbours():
    return [plane_peer("y", step, 0) for step in (1, -1)] + [
        plane_peer("y", 0, step) for step in (1, -1)
    ]


def seq_peer(offset_x, flip):
    mine = lax.axis_index("seq")
    x, core = mine // 2, mine % 2
    if flip:
        core = 1 - core
    return {"seq": ((x + offset_x) % SIDE) * 2 + core}


def greet(peers):
    barrier = pltpu.get_barrier_semaphore()
    for peer in peers:
        pl.semaphore_signal(barrier, inc=1, device_id=peer, device_id_type=MESH)
    pl.semaphore_wait(barrier, len(peers))


HALVES = (("y", 0), ("z", 2))
ORDER = (0, -1, 1, 2)


def plane_gather(own, view, send, recv, after_row):
    started = []

    def copy(half, kind, source, target, peer):
        return pltpu.make_async_remote_copy(
            src_ref=source,
            dst_ref=target,
            send_sem=send.at[half, kind],
            recv_sem=recv.at[half, kind],
            device_id=peer,
            device_id_type=MESH,
        )

    def push(half, kind, source, target, peer):
        item = copy(half, kind, source, target, peer)
        item.start()
        started.append(item)

    def arrived(half, kind, target):
        first, _ = HALVES[half]
        copy(half, kind, target, target, plane_peer(first, 1, 0)).wait_recv()

    def block(half, along_first, along_second, low, count):
        first, base = HALVES[half]
        z, y = plane_place(first, along_first, along_second)
        return view(z, y, base + low, count)

    def ring(half, slot, axis, along, source):
        first, base = HALVES[half]
        for kind, step in ((0, 1), (1, -1)):
            peer = plane_peer(first, step, 0) if axis == 0 else plane_peer(first, 0, step)
            push(half, 4 * slot + kind, source, block(half, along, 0, 0, 2), peer)

    def ring_relay(half, slot, axis, along):
        first, base = HALVES[half]
        for kind, step in ((0, 1), (1, -1)):
            where = (-step, 0) if axis == 0 else (along, -step)
            arrived(half, 4 * slot + kind, block(half, where[0], where[1], 0, 2))
            part = block(half, where[0], where[1], kind, 1)
            peer = plane_peer(first, step, 0) if axis == 0 else plane_peer(first, 0, step)
            push(half, 4 * slot + 2 + kind, part, part, peer)

    def ring_end(half, slot, axis, along):
        where = (2, 0) if axis == 0 else (along, 2)
        for kind in (0, 1):
            arrived(half, 4 * slot + 2 + kind, block(half, where[0], where[1], kind, 1))

    for half in (0, 1):
        ring(half, 0, 0, 0, own(HALVES[half][1], 2))
    for half in (0, 1):
        ring(half, 1, 1, 0, own(HALVES[half][1], 2))
    yield
    for half in (0, 1):
        ring_relay(half, 0, 0, 0)
        for slot in (1, 2):
            ring(half, 1 + slot, 1, ORDER[slot], block(half, ORDER[slot], 0, 0, 2))
    yield
    for half in (0, 1):
        ring_end(half, 0, 0, 0)
        ring(half, 4, 1, 2, block(half, 2, 0, 0, 2))
        after_row(half, 0)
    for slot in (0, 1, 2, 3):
        for half in (0, 1):
            ring_relay(half, 1 + slot, 1, ORDER[slot])
        yield
    for half in (0, 1):
        after_row(half, -1)
        after_row(half, 1)
    for half in (0, 1):
        for slot in (0, 1, 2, 3):
            ring_end(half, 1 + slot, 1, ORDER[slot])
        after_row(half, 2)
    for item in started:
        item.wait_send()


def plane_reduce(parts, far, near, far_last, near_last, send, recv, store):
    started = []

    def copy(half, kind, source, target, peer):
        return pltpu.make_async_remote_copy(
            src_ref=source,
            dst_ref=target,
            send_sem=send.at[half, kind],
            recv_sem=recv.at[half, kind],
            device_id=peer,
            device_id_type=MESH,
        )

    def push(half, kind, source, target, peer):
        item = copy(half, kind, source, target, peer)
        item.start()
        started.append(item)

    def arrived(half, kind, target):
        first, _ = HALVES[half]
        copy(half, kind, target, target, plane_peer(first, 1, 0)).wait_recv()

    def rows(half, offset, low, count):
        first, base = HALVES[half]
        z, y = plane_place(first, 0, offset)
        if first == "y":
            return parts.at[z, :, pl.ds(base + low, count)]
        return parts.at[:, y, pl.ds(base + low, count)]

    def one(half, offset, low, count):
        first, base = HALVES[half]
        z, y = plane_place(first, offset, 0)
        return parts.at[z, y, pl.ds(base + low, count)]

    def add(target, *others):
        if len(others) == 1:
            target[...] = target[...] + others[0][...]
            return
        total = target[...].astype(jnp.float32)
        for other in others:
            total = total + other[...].astype(jnp.float32)
        target[...] = total.astype(target.dtype)

    def add_rows(half, offset, low, count, *others):
        target = rows(half, offset, low, count)
        def step(at, carry):
            add(target.at[at], *[other.at[at] for other in others])
            return carry
        lax.fori_loop(0, SIDE, step, 0)

    def peer(half, axis, step):
        first, _ = HALVES[half]
        return plane_peer(first, 0, step) if axis == 1 else plane_peer(first, step, 0)

    for half in (0, 1):
        push(half, 0, rows(half, 2, 0, 1), far.at[half, 0], peer(half, 1, 1))
        push(half, 1, rows(half, 2, 1, 1), far.at[half, 1], peer(half, 1, -1))
    yield
    for half in (0, 1):
        push(half, 2, rows(half, 1, 1, 1), near.at[half, 0, :, pl.ds(1, 1)], peer(half, 1, 1))
        push(half, 3, rows(half, -1, 0, 1), near.at[half, 1, :, pl.ds(0, 1)], peer(half, 1, -1))
    yield
    for half in (0, 1):
        arrived(half, 0, far.at[half, 0])
        add_rows(half, 1, 0, 1, far.at[half, 0])
        push(half, 4, rows(half, 1, 0, 1), near.at[half, 0, :, pl.ds(0, 1)], peer(half, 1, 1))
        arrived(half, 1, far.at[half, 1])
        add_rows(half, -1, 1, 1, far.at[half, 1])
        push(half, 5, rows(half, -1, 1, 1), near.at[half, 1, :, pl.ds(1, 1)], peer(half, 1, -1))
    yield
    for half in (0, 1):
        arrived(half, 2, near.at[half, 0, :, pl.ds(1, 1)])
        arrived(half, 3, near.at[half, 1, :, pl.ds(0, 1)])
        arrived(half, 4, near.at[half, 0, :, pl.ds(0, 1)])
        arrived(half, 5, near.at[half, 1, :, pl.ds(1, 1)])
        add_rows(half, 0, 0, 2, near.at[half, 0], near.at[half, 1])
        push(half, 6, one(half, 2, 0, 1), far_last.at[half, 0], peer(half, 0, 1))
        push(half, 7, one(half, 2, 1, 1), far_last.at[half, 1], peer(half, 0, -1))
        push(half, 8, one(half, 1, 1, 1), near_last.at[half, 0, pl.ds(1, 1)], peer(half, 0, 1))
        push(half, 9, one(half, -1, 0, 1), near_last.at[half, 1, pl.ds(0, 1)], peer(half, 0, -1))
    yield
    for half in (0, 1):
        arrived(half, 6, far_last.at[half, 0])
        add(one(half, 1, 0, 1), far_last.at[half, 0])
        push(half, 10, one(half, 1, 0, 1), near_last.at[half, 0, pl.ds(0, 1)], peer(half, 0, 1))
        arrived(half, 7, far_last.at[half, 1])
        add(one(half, -1, 1, 1), far_last.at[half, 1])
        push(half, 11, one(half, -1, 1, 1), near_last.at[half, 1, pl.ds(1, 1)], peer(half, 0, -1))
    yield
    for half in (0, 1):
        arrived(half, 8, near_last.at[half, 0, pl.ds(1, 1)])
        arrived(half, 9, near_last.at[half, 1, pl.ds(0, 1)])
        arrived(half, 10, near_last.at[half, 0, pl.ds(0, 1)])
        arrived(half, 11, near_last.at[half, 1, pl.ds(1, 1)])
        total = one(half, 0, 0, 2)[...].astype(jnp.float32)
        for side in (0, 1):
            total = total + near_last[half, side].astype(jnp.float32)
        store(HALVES[half][1], total)
    for item in started:
        item.wait_send()


def reduce_scratch(quarter_rows, width):
    unit = (quarter_rows, width)
    return [
        pltpu.VMEM((SIDE, SIDE, 4) + unit, jnp.bfloat16),
        pltpu.VMEM((2, 2, SIDE, 1) + unit, jnp.bfloat16),
        pltpu.VMEM((2, 2, SIDE, 2) + unit, jnp.bfloat16),
        pltpu.VMEM((2, 2, 1) + unit, jnp.bfloat16),
        pltpu.VMEM((2, 2, 2) + unit, jnp.bfloat16),
        pltpu.SemaphoreType.DMA((2, 12)),
        pltpu.SemaphoreType.DMA((2, 12)),
    ]


def comm_params(number, limit_mb):
    return pltpu.CompilerParams(
        collective_id=number, has_side_effects=True, vmem_limit_bytes=limit_mb * 1024 * 1024
    )


def nothing(half, offset):
    return None


def advance(steps):
    next(steps, None)


def finish(steps):
    for _ in steps:
        pass


def pair_up(low, high, lane):
    return (
        jnp.where(lane < HEAD_DIM, low, pltpu.roll(high, HEAD_DIM, 1)),
        jnp.where(lane < HEAD_DIM, pltpu.roll(low, HEAD_DIM, 1), high),
    )


def by_group(rows):
    lane = lax.broadcasted_iota(jnp.int32, (rows.shape[0], 128), 1)
    tile = lambda at: rows[:, at * 128 : (at + 1) * 128]
    parts = []
    for j in range(4):
        low, high = tile(8 + j), tile(12 + j)
        first, second = pair_up(low, high, lane)
        parts += [tile(2 * j), first, tile(2 * j + 1), second]
    return jnp.concatenate(parts, axis=1)


def by_kind(rows):
    lane = lax.broadcasted_iota(jnp.int32, (rows.shape[0], 128), 1)
    tile = lambda at: rows[:, at * 128 : (at + 1) * 128]
    queries, keys, values = [], [], []
    for j in range(4):
        queries += [tile(4 * j), tile(4 * j + 2)]
        key, value = pair_up(tile(4 * j + 1), tile(4 * j + 3), lane)
        keys.append(key)
        values.append(value)
    return jnp.concatenate(queries + keys + values, axis=1)


def ring_gather(owns, outs, send, recv, core_send, core_recv, local):
    seq = lax.axis_index("seq")
    x, core = seq // 2, seq % 2
    other = seq_peer(0, True)
    started, swaps = [], []
    count = len(owns)

    def at(m, step, side):
        return outs[m].at[:, (x + step) % SIDE, side]

    def copy(m, kind, source, target, step):
        return pltpu.make_async_remote_copy(
            src_ref=source,
            dst_ref=target,
            send_sem=send.at[m, kind],
            recv_sem=recv.at[m, kind],
            device_id=seq_peer(step, False),
            device_id_type=MESH,
        )

    def push(m, kind, source, target, step):
        item = copy(m, kind, source, target, step)
        item.start()
        started.append(item)

    def arrived(m, kind, target):
        copy(m, kind, target, target, 1).wait_recv()

    def swap(m, kind, source, step):
        def across(out_of, into):
            return pltpu.make_async_remote_copy(
                src_ref=out_of,
                dst_ref=into,
                send_sem=core_send.at[m, kind],
                recv_sem=core_recv.at[m, kind],
                device_id=other,
                device_id_type=MESH,
            )

        item = across(source, at(m, step, core))
        item.start()
        started.append(item)
        swaps.append(across(at(m, step, 1 - core), at(m, step, 1 - core)))

    keeps = [pltpu.make_async_copy(owns[m], at(m, 0, core), local.at[m]) for m in range(count)]
    for m in range(count):
        push(m, 0, owns[m], at(m, 0, core), 1)
        push(m, 1, owns[m], at(m, 0, core), 3)
    for m in range(count):
        keeps[m].start()
        swap(m, 0, owns[m], 0)
    yield
    for m in range(count):
        for kind, expert, came, onward in ((0, 0, 3, 1), (1, 1, 1, 3)):
            arrived(m, kind, at(m, came, core))
            part = outs[m].at[expert, (x + came) % SIDE, core]
            push(m, 2 + kind, part, part, onward)
            swap(m, 1 + kind, at(m, came, core), came)
    yield
    for m in range(count):
        for kind in (0, 1):
            arrived(m, 2 + kind, outs[m].at[kind, (x + 2) % SIDE, core])
        swap(m, 3, at(m, 2, core), 2)
    for item in swaps:
        item.wait_recv()
    for item in keeps:
        item.wait()
    for item in started:
        item.wait_send()


def weights_gather(qkv, others, experts, number):
    rows, qkv_width = qkv.shape
    width = qkv_width + sum(other.shape[1] for other in others)
    kinds = len(experts)

    def kernel(*refs):
        refs = list(refs)
        take = lambda count: [refs.pop(0) for _ in range(count)]
        ins, ex_ins, (out_ref,), ex_outs = take(1 + len(others)), take(kinds), take(1), take(kinds)
        own_ref, send, recv, x_send, x_recv, core_send, core_recv, local_sem = take(8)
        ring_send, ring_recv, swap_send, swap_recv, ring_local = take(5)
        own_ref[:, pl.ds(0, qkv_width)] = by_group(ins[0][...].astype(jnp.float32)).astype(
            own_ref.dtype
        )
        at = qkv_width
        for other in ins[1:]:
            own_ref[:, pl.ds(at, other.shape[1])] = other[...]
            at += other.shape[1]
        seq = lax.axis_index("seq")
        x, core = seq // 2, seq % 2
        x_peers = [seq_peer(step, False) for step in (1, 3, 2)]
        other = seq_peer(0, True)
        greet(plane_neighbours() + x_peers + [other])
        z, y = plane_place("y", 0, 0)
        keep = pltpu.make_async_copy(own_ref, out_ref.at[x, core, z, y], local_sem)
        keep.start()
        sends = []
        for i, step in enumerate((1, 3, 2)):
            item = pltpu.make_async_remote_copy(
                src_ref=own_ref,
                dst_ref=out_ref.at[x, core, z, y],
                send_sem=x_send.at[i],
                recv_sem=x_recv.at[i],
                device_id=x_peers[i],
                device_id_type=MESH,
            )
            item.start()
            sends.append(item)
        keep.wait()
        for i, step in enumerate((1, 3, 2)):
            came = out_ref.at[(x + SIDE - step) % SIDE, core, z, y]
            pltpu.make_async_remote_copy(
                src_ref=came,
                dst_ref=came,
                send_sem=x_send.at[i],
                recv_sem=x_recv.at[i],
                device_id=x_peers[i],
                device_id_type=MESH,
            ).wait_recv()

        swaps = []

        def swap(half, offset):
            first, base = HALVES[half]
            z, y = plane_place(first, 0, offset)
            mine = (
                out_ref.at[pl.ds(base, 2), core, z]
                if first == "y"
                else out_ref.at[pl.ds(base, 2), core, :, y]
            )
            theirs = (
                out_ref.at[pl.ds(base, 2), 1 - core, z]
                if first == "y"
                else out_ref.at[pl.ds(base, 2), 1 - core, :, y]
            )
            kind = ORDER.index(offset)
            item = pltpu.make_async_remote_copy(
                src_ref=mine,
                dst_ref=mine,
                send_sem=core_send.at[half, kind],
                recv_sem=core_recv.at[half, kind],
                device_id=other,
                device_id_type=MESH,
            )
            item.start()
            sends.append(item)
            swaps.append(
                pltpu.make_async_remote_copy(
                    src_ref=theirs,
                    dst_ref=theirs,
                    send_sem=core_send.at[half, kind],
                    recv_sem=core_recv.at[half, kind],
                    device_id=other,
                    device_id_type=MESH,
                )
            )

        plane = plane_gather(
            lambda low, count: out_ref.at[pl.ds(low, count), core, z, y],
            lambda z, y, low, count: out_ref.at[pl.ds(low, count), core, z, y],
            send,
            recv,
            swap,
        )
        ring = ring_gather(
            ex_ins, ex_outs, ring_send, ring_recv, swap_send, swap_recv, ring_local
        )
        advance(plane)
        advance(ring)
        for _ in range(5):
            advance(plane)
        advance(ring)
        finish(plane)
        finish(ring)
        for item in swaps:
            item.wait_recv()
        for item in sends:
            item.wait_send()

    out = pl.pallas_call(
        kernel,
        out_shape=(jax.ShapeDtypeStruct((4, 2, SIDE, SIDE, rows, width), qkv.dtype),)
        + tuple(
            jax.ShapeDtypeStruct((2, 4, 2) + expert.shape[1:], expert.dtype) for expert in experts
        ),
        in_specs=[pl.BlockSpec(memory_space=pltpu.VMEM)] * (1 + len(others))
        + [pl.BlockSpec(memory_space=pl.ANY)] * kinds,
        out_specs=(pl.BlockSpec(memory_space=pl.ANY),) * (1 + kinds),
        scratch_shapes=[
            pltpu.VMEM((rows, width), qkv.dtype),
            pltpu.SemaphoreType.DMA((2, 20)),
            pltpu.SemaphoreType.DMA((2, 20)),
            pltpu.SemaphoreType.DMA((3,)),
            pltpu.SemaphoreType.DMA((3,)),
            pltpu.SemaphoreType.DMA((2, 4)),
            pltpu.SemaphoreType.DMA((2, 4)),
            pltpu.SemaphoreType.DMA,
        ]
        + [pltpu.SemaphoreType.DMA((kinds, 4))] * 4
        + [pltpu.SemaphoreType.DMA((kinds,))],
        compiler_params=comm_params(number, 8),
        name="weights_gather",
    )(qkv, *others, *experts)
    return (out[0].reshape(4 * 2 * SIDE * SIDE * rows, width),) + tuple(
        full.reshape(2, 8 * expert.shape[1], expert.shape[2])
        for full, expert in zip(out[1:], experts)
    )


def ring_reduce(sums, far, near, send, recv, outs):
    x = lax.axis_index("seq") // 2
    started = []

    def copy(m, kind, source, target, step):
        return pltpu.make_async_remote_copy(
            src_ref=source,
            dst_ref=target,
            send_sem=send.at[m, kind],
            recv_sem=recv.at[m, kind],
            device_id=seq_peer(step, False),
            device_id_type=MESH,
        )

    def push(m, kind, source, target, step):
        item = copy(m, kind, source, target, step)
        item.start()
        started.append(item)

    def arrived(m, kind, target):
        copy(m, kind, target, target, 1).wait_recv()

    def at(step):
        return (x + step) % SIDE

    count = len(sums)
    for m in range(count):
        push(m, 0, sums[m].at[0, at(2)], far[m].at[0], 1)
        push(m, 1, sums[m].at[1, at(2)], far[m].at[1], 3)
    for m in range(count):
        push(m, 2, sums[m].at[1, at(1)], near[m].at[0, 1], 1)
        push(m, 3, sums[m].at[0, at(3)], near[m].at[1, 0], 3)
    yield
    for m in range(count):
        for kind, expert, step in ((0, 0, 1), (1, 1, 3)):
            arrived(m, kind, far[m].at[kind])
            target = sums[m].at[expert, at(step)]
            target[...] = target[...] + far[m][kind]
            push(m, 4 + kind, target, near[m].at[kind, expert], step)
    yield
    for m in range(count):
        arrived(m, 2, near[m].at[0, 1])
        arrived(m, 3, near[m].at[1, 0])
        arrived(m, 4, near[m].at[0, 0])
        arrived(m, 5, near[m].at[1, 1])
        for expert in (0, 1):
            outs[m][expert] = (
                sums[m][expert, at(0)].astype(jnp.float32)
                + near[m][0, expert].astype(jnp.float32)
                + near[m][1, expert].astype(jnp.float32)
            )
    for item in started:
        item.wait_send()


def weights_reduce(pieces, experts, number):
    widths = [piece.shape[1] for piece in pieces]
    width = sum(widths)
    rows = pieces[0].shape[0] // (4 * 2 * SIDE * SIDE)
    kinds = len(experts)
    shares = [
        (2, 4, 2, expert.shape[1] // 8, expert.shape[2]) for expert in experts
    ]

    def kernel(*refs):
        refs = list(refs)
        take = lambda count: [refs.pop(0) for _ in range(count)]
        ins, ex_ins = take(len(widths)), take(kinds)
        qkv_ref, out_ref, small_ref = take(3)
        ex_outs = take(kinds)
        (parts, far, near, far_last, near_last, send, recv, twin, mine, from_x, load, core_send,
         core_recv, x_send, x_recv) = take(15)
        ex_sums, ex_twins, ex_far, ex_near = take(kinds), take(kinds), take(kinds), take(kinds)
        ex_load, ex_core_send, ex_core_recv, ring_send, ring_recv = take(5)
        seq = lax.axis_index("seq")
        x, core = seq // 2, seq % 2
        x_peers = [seq_peer(step, False) for step in (1, 3, 2)]
        other = seq_peer(0, True)
        loads = []
        for quarter in range(4):
            at = 0
            for i, one_width in enumerate(widths):
                item = pltpu.make_async_copy(
                    ins[i].at[quarter, core],
                    parts.at[:, :, quarter, :, pl.ds(at, one_width)],
                    load.at[quarter, i],
                )
                item.start()
                loads.append(item)
                at += one_width
        ex_loads = []
        for m in range(kinds):
            ex_loads.append(
                pltpu.make_async_copy(ex_ins[m].at[:, :, core], ex_sums[m], ex_load.at[m])
            )
            ex_loads[-1].start()
        greet(plane_neighbours() + x_peers + [other])
        swaps = []
        for quarter in range(4):
            at = 0
            for i, one_width in enumerate(widths):
                item = pltpu.make_async_remote_copy(
                    src_ref=ins[i].at[quarter, 1 - core],
                    dst_ref=twin.at[quarter, :, :, :, pl.ds(at, one_width)],
                    send_sem=core_send.at[quarter, i],
                    recv_sem=core_recv.at[quarter, i],
                    device_id=other,
                    device_id_type=MESH,
                )
                item.start()
                swaps.append(item)
                at += one_width
        ex_swaps = []
        for m in range(kinds):
            item = pltpu.make_async_remote_copy(
                src_ref=ex_ins[m].at[:, :, 1 - core],
                dst_ref=ex_twins[m],
                send_sem=ex_core_send.at[m],
                recv_sem=ex_core_recv.at[m],
                device_id=other,
                device_id_type=MESH,
            )
            item.start()
            ex_swaps.append(item)
        for quarter in range(4):
            for i in range(len(widths)):
                loads[quarter * len(widths) + i].wait()
                swaps[quarter * len(widths) + i].wait_recv()

            def add(at, carry):
                z, y = at // SIDE, at % SIDE
                parts[z, y, quarter] = parts[z, y, quarter] + twin[quarter, z, y]
                return carry

            lax.fori_loop(0, SIDE * SIDE, add, 0)

        def store(low, total):
            mine[pl.ds(low, 2)] = total.astype(mine.dtype)

        plane = plane_reduce(parts, far, near, far_last, near_last, send, recv, store)
        advance(plane)
        advance(plane)
        for m in range(kinds):
            ex_loads[m].wait()
            ex_swaps[m].wait_recv()

            def add_pair(at, carry):
                ex_sums[m][at // 4, at % 4] = (
                    ex_sums[m][at // 4, at % 4] + ex_twins[m][at // 4, at % 4]
                )
                return carry

            lax.fori_loop(0, 8, add_pair, 0)
        ring = ring_reduce(ex_sums, ex_far, ex_near, ring_send, ring_recv, ex_outs)
        advance(ring)
        advance(plane)
        advance(ring)
        advance(plane)
        advance(plane)
        finish(ring)
        finish(plane)
        sends = []
        for i, step in enumerate((1, 3, 2)):
            item = pltpu.make_async_remote_copy(
                src_ref=mine.at[(x + step) % SIDE],
                dst_ref=from_x.at[i],
                send_sem=x_send.at[i],
                recv_sem=x_recv.at[i],
                device_id=x_peers[i],
                device_id_type=MESH,
            )
            item.start()
            sends.append(item)
        total = mine[x].astype(jnp.float32)
        for i in range(3):
            sends[i].wait_recv()
            total = total + from_x[i].astype(jnp.float32)
        qkv_ref[...] = by_kind(total[:, : widths[0]])
        out_ref[...] = total[:, widths[0] : widths[0] + widths[1]]
        small_ref[...] = total[:, widths[0] + widths[1] :]
        for item in sends + swaps + ex_swaps:
            item.wait_send()

    unit = (rows, width)
    pairs = (4, len(widths))
    vmem = pl.BlockSpec(memory_space=pltpu.VMEM)
    return pl.pallas_call(
        kernel,
        out_shape=tuple(
            [jax.ShapeDtypeStruct((rows, one_width), jnp.float32) for one_width in widths]
            + [jax.ShapeDtypeStruct((2,) + share[3:], jnp.float32) for share in shares]
        ),
        in_specs=[pl.BlockSpec(memory_space=pl.ANY)] * (len(widths) + kinds),
        out_specs=(vmem,) * (len(widths) + kinds),
        scratch_shapes=reduce_scratch(rows, width)
        + [
            pltpu.VMEM((4, SIDE, SIDE) + unit, jnp.bfloat16),
            pltpu.VMEM((4,) + unit, jnp.bfloat16),
            pltpu.VMEM((3,) + unit, jnp.bfloat16),
            pltpu.SemaphoreType.DMA(pairs),
            pltpu.SemaphoreType.DMA(pairs),
            pltpu.SemaphoreType.DMA(pairs),
            pltpu.SemaphoreType.DMA((3,)),
            pltpu.SemaphoreType.DMA((3,)),
        ]
        + [pltpu.VMEM((2, 4) + share[3:], jnp.bfloat16) for share in shares]
        + [pltpu.VMEM((2, 4) + share[3:], jnp.bfloat16) for share in shares]
        + [pltpu.VMEM((2,) + share[3:], jnp.bfloat16) for share in shares]
        + [pltpu.VMEM((2, 2) + share[3:], jnp.bfloat16) for share in shares]
        + [pltpu.SemaphoreType.DMA((kinds,))] * 3
        + [pltpu.SemaphoreType.DMA((kinds, 6))] * 2,
        compiler_params=comm_params(number, 48),
        name="weights_reduce",
    )(
        *[piece.reshape(4, 2, SIDE, SIDE, rows, piece.shape[1]) for piece in pieces],
        *[expert.reshape(share) for expert, share in zip(experts, shares)],
    )


def rms_scale(values):
    return lax.rsqrt(jnp.mean(values * values, axis=-1, keepdims=True) + epsilon)


def rope_tables(length):
    half_dim = HEAD_DIM // 2
    frequency = np.float32(rope_theta) ** (
        -np.arange(half_dim, dtype=np.float32) / np.float32(half_dim)
    )
    angles = np.arange(length, dtype=np.float32)[:, None] * frequency[None, :].astype(np.float32)
    cosine = np.cos(angles.astype(np.float64)).astype(np.float32)
    sine = np.sin(angles.astype(np.float64)).astype(np.float32)
    one_cos = np.concatenate([cosine, cosine], axis=1)
    one_sin = np.concatenate([-sine, sine], axis=1)
    flat = np.ones_like(one_cos)
    return (
        np.concatenate([one_cos, one_cos, one_cos, flat], axis=1),
        np.concatenate([one_sin, one_sin, one_sin, 0.0 * flat], axis=1),
    )


def turn(values, cosine, sine):
    half_dim = HEAD_DIM // 2
    width = values.shape[1]
    lane = lax.broadcasted_iota(jnp.int32, values.shape, 1)
    ahead = pltpu.roll(values, width - half_dim, 1)
    behind = pltpu.roll(values, half_dim, 1)
    return values * cosine + jnp.where(lane % HEAD_DIM < half_dim, ahead, behind) * sine


SEQ_STEPS = (4, 5, 3, 2, 6, 1, 7)


def seq_exchange(source, target, send, recv):
    me = lax.axis_index("seq")
    count = 8

    def copy(step, peer, out_of, into):
        return pltpu.make_async_remote_copy(
            src_ref=out_of,
            dst_ref=into,
            send_sem=send.at[step - 1],
            recv_sem=recv.at[step - 1],
            device_id={"seq": peer},
            device_id_type=MESH,
        )

    def start(steps):
        items = []
        for step in steps:
            peer = (me + step) % count
            item = copy(step, peer, source(peer), target(me))
            item.start()
            items.append(item)
        return items

    def wait(step):
        peer = (me + count - step) % count
        copy(step, peer, target(peer), target(peer)).wait_recv()

    return (start, wait)


def seq_plane_greet():
    me = lax.axis_index("seq")
    greet(plane_neighbours() + [{"seq": (me + step) % 8} for step in range(1, 8)])


def twice(pair, lane):
    swapped = pltpu.roll(pair.astype(jnp.float32), HEAD_DIM, 1).astype(pair.dtype)
    return (
        jnp.where(lane < HEAD_DIM, pair, swapped),
        jnp.where(lane < HEAD_DIM, swapped, pair),
    )


def apart(pair, lane):
    zero = jnp.zeros_like(pair)
    return jnp.concatenate(
        [jnp.where(lane < HEAD_DIM, pair, zero), jnp.where(lane < HEAD_DIM, zero, pair)], axis=0
    )


def matmul(a, b, dims):
    return lax.dot_general(a, b, (dims, ((), ())), preferred_element_type=jnp.float32)


BLOCK = 256


def block_probs(queries, keys, at):
    scores = matmul(queries, keys, ((1,), (1,)))
    row = lax.broadcasted_iota(jnp.int32, scores.shape, 0) % BLOCK + at * BLOCK
    column = lax.broadcasted_iota(jnp.int32, scores.shape, 1)
    scores = jnp.where(column <= row, scores, -1e30)
    exponent = jnp.exp(scores - jnp.max(scores, axis=1, keepdims=True))
    return exponent * (1.0 / jnp.sum(exponent, axis=1, keepdims=True))


def attention_forward(normed, weights, width, cosine, sine, beside, number):
    tok, depth = normed.shape
    features = beside.shape[1]
    seq_parts = 8
    group = width // seq_parts
    pair = 2 * HEAD_DIM
    length = tok * seq_parts
    per_block = BLOCK // tok

    def kernel(
        normed_ref, weights_ref, cos_hbm, sin_hbm, beside_ref, out_ref, heads_ref, all_ref,
        packed, mixed, proj_w, cos_ref, sin_ref,
        send, recv, o_send, o_recv, p_send, p_recv, local_sem, load,
    ):
        me = lax.axis_index("seq")
        here = pl.ds(pl.multiple_of(me * tok, tok), tok)
        loads = [
            pltpu.make_async_copy(weights_ref.at[:, pl.ds(0, width)], proj_w, load.at[0]),
            pltpu.make_async_copy(cos_hbm.at[here], cos_ref, load.at[1]),
            pltpu.make_async_copy(sin_hbm.at[here], sin_ref, load.at[2]),
        ]
        for item in loads:
            item.start()
        z, y = plane_place("y", 0, 0)
        keep = pltpu.make_async_copy(beside_ref, all_ref.at[z, y], local_sem)
        keep.start()
        seq_plane_greet()
        steps = plane_gather(
            lambda low, count: beside_ref.at[pl.ds(low, count)],
            lambda z, y, low, count: all_ref.at[z, y, pl.ds(low, count)],
            p_send,
            p_recv,
            nothing,
        )
        advance(steps)
        for item in loads:
            item.wait()
        for d in range(seq_parts):
            projected = matmul(
                normed_ref[...], proj_w[:, d * group : (d + 1) * group], ((1,), (0,))
            )
            packed[d] = turn(projected, cos_ref[...], sin_ref[...]).astype(packed.dtype)
        start, wait = seq_exchange(
            lambda d: packed.at[d], lambda d: heads_ref.at[d], send, recv
        )
        items = start(SEQ_STEPS)
        heads_ref[me] = packed[me]
        advance(steps)
        for step in SEQ_STEPS:
            wait(step)
        advance(steps)
        lane = lax.broadcasted_iota(jnp.int32, (length, pair), 1)
        heads = heads_ref[...].reshape(length, group)
        keys, values = twice(heads[:, pair:], lane)
        lane_block = lane[:BLOCK]
        back, back_wait = seq_exchange(
            lambda d: mixed.at[d],
            lambda d: out_ref.at[:, pl.ds(pl.multiple_of(d * pair, pair), pair)],
            o_send,
            o_recv,
        )
        for at in range(length // BLOCK):
            block = heads[at * BLOCK : (at + 1) * BLOCK, :pair]
            queries = apart(block * jnp.asarray(attention_multiplier, block.dtype), lane_block)
            upto = (at + 1) * BLOCK
            probs = block_probs(queries, keys[:upto], at).astype(jnp.bfloat16)
            both = matmul(probs, values[:upto], ((1,), (0,)))
            made = jnp.where(lane_block < HEAD_DIM, both[:BLOCK], both[BLOCK:]).astype(mixed.dtype)
            mixed[at * per_block : (at + 1) * per_block] = made.reshape(per_block, tok, pair)
            if at % 2:
                advance(steps)
        items += back(SEQ_STEPS)
        out_ref[:, pl.ds(pl.multiple_of(me * pair, pair), pair)] = mixed[me]
        advance(steps)
        for step in SEQ_STEPS:
            back_wait(step)
        finish(steps)
        keep.wait()
        for item in items:
            item.wait_send()

    vmem = pl.BlockSpec(memory_space=pltpu.VMEM)
    anywhere = pl.BlockSpec(memory_space=pl.ANY)
    attended, heads, gathered = pl.pallas_call(
        kernel,
        out_shape=(
            jax.ShapeDtypeStruct((tok, seq_parts * pair), jnp.bfloat16),
            jax.ShapeDtypeStruct((seq_parts, tok, group), jnp.bfloat16),
            jax.ShapeDtypeStruct((SIDE, SIDE, 4, tok // 4, features), beside.dtype),
        ),
        in_specs=[vmem] + [anywhere] * 4,
        out_specs=(vmem, vmem, anywhere),
        scratch_shapes=[
            pltpu.VMEM((seq_parts, tok, group), jnp.bfloat16),
            pltpu.VMEM((seq_parts, tok, pair), jnp.bfloat16),
            pltpu.VMEM((depth, width), jnp.bfloat16),
            pltpu.VMEM((tok, group), jnp.float32),
            pltpu.VMEM((tok, group), jnp.float32),
        ]
        + [pltpu.SemaphoreType.DMA((7,))] * 4
        + [pltpu.SemaphoreType.DMA((2, 20))] * 2
        + [pltpu.SemaphoreType.DMA, pltpu.SemaphoreType.DMA((3,))],
        compiler_params=comm_params(number, 48),
        name="attention_forward",
    )(normed, weights, cosine, sine, beside.reshape(4, tok // 4, features))
    return (attended, heads, gathered.reshape(SIDE * SIDE, tok, features))


def attention_backward(grad_attended, heads_in, cosine, sine, beside, number):
    seq_parts, tok, group = heads_in.shape
    features = beside.shape[2]
    pair = 2 * HEAD_DIM
    length = tok * seq_parts
    per_block = BLOCK // tok

    def kernel(
        grad_ref, heads_ref, cos_ref, sin_ref, beside_ref, out_ref, sum_ref,
        came, packed, d_queries, d_keys, d_values, send, recv, o_send, o_recv,
        parts, far, near, far_last, near_last, p_send, p_recv, load,
    ):
        me = lax.axis_index("seq")
        loaded = pltpu.make_async_copy(beside_ref, parts, load)
        loaded.start()
        seq_plane_greet()

        def store(low, total):
            sum_ref[pl.ds(low, 2)] = total

        steps = plane_reduce(parts, far, near, far_last, near_last, p_send, p_recv, store)
        columns = lambda d: grad_ref.at[:, pl.ds(pl.multiple_of(d * pair, pair), pair)]
        start, wait = seq_exchange(columns, lambda d: came.at[d], send, recv)
        items = start(SEQ_STEPS)
        loaded.wait()
        advance(steps)
        advance(steps)
        came[me] = grad_ref[:, pl.ds(pl.multiple_of(me * pair, pair), pair)]
        lane = lax.broadcasted_iota(jnp.int32, (length, pair), 1)
        lane_block = lane[:BLOCK]
        heads = heads_ref[...].reshape(length, group)
        keys, values = twice(heads[:, pair:], lane)
        for step in SEQ_STEPS:
            wait(step)
        for at in range(length // BLOCK):
            upto = (at + 1) * BLOCK
            block = heads[at * BLOCK : upto, :pair]
            queries = apart(block * jnp.asarray(attention_multiplier, block.dtype), lane_block)
            grads = apart(
                came[at * per_block : (at + 1) * per_block].reshape(BLOCK, pair), lane_block
            )
            probs = block_probs(queries, keys[:upto], at)
            d_probs = matmul(grads, values[:upto], ((1,), (1,)))
            center = jnp.sum(probs * d_probs, axis=1, keepdims=True)
            d_scores = (probs * (d_probs - center)).astype(jnp.bfloat16)
            both = matmul(d_scores, keys[:upto], ((1,), (0,))) * attention_multiplier
            d_queries[at * BLOCK : upto] = jnp.where(
                lane_block < HEAD_DIM, both[:BLOCK], both[BLOCK:]
            )
            more_keys = matmul(d_scores, queries, ((0,), (0,)))
            more_values = matmul(probs.astype(jnp.bfloat16), grads, ((0,), (0,)))
            before = at * BLOCK
            if at:
                d_keys[:before] += more_keys[:before]
                d_values[:before] += more_values[:before]
            d_keys[before:upto] = more_keys[before:]
            d_values[before:upto] = more_values[before:]
            if at in (1, 3):
                advance(steps)
        sum_keys = d_keys[...] + pltpu.roll(d_keys[...], HEAD_DIM, 1)
        sum_values = d_values[...] + pltpu.roll(d_values[...], HEAD_DIM, 1)
        rest = jnp.where(lane < HEAD_DIM, sum_keys, sum_values)
        whole = jnp.concatenate([d_queries[...], rest], axis=1)
        packed[...] = (
            turn(whole, cos_ref[...], -sin_ref[...])
            .astype(packed.dtype)
            .reshape(seq_parts, tok, group)
        )
        back, back_wait = seq_exchange(
            lambda d: packed.at[d],
            lambda d: out_ref.at[:, pl.ds(pl.multiple_of(d * group, group), group)],
            o_send,
            o_recv,
        )
        items += back(SEQ_STEPS)
        out_ref[:, pl.ds(pl.multiple_of(me * group, group), group)] = packed[me]
        advance(steps)
        for step in SEQ_STEPS:
            back_wait(step)
        finish(steps)
        for item in items:
            item.wait_send()

    vmem = pl.BlockSpec(memory_space=pltpu.VMEM)
    grads, summed = pl.pallas_call(
        kernel,
        out_shape=(
            jax.ShapeDtypeStruct((tok, seq_parts * group), jnp.bfloat16),
            jax.ShapeDtypeStruct((4, tok // 4, features), jnp.float32),
        ),
        in_specs=[vmem] * 4 + [pl.BlockSpec(memory_space=pl.ANY)],
        out_specs=(vmem, vmem),
        scratch_shapes=[
            pltpu.VMEM((seq_parts, tok, pair), jnp.bfloat16),
            pltpu.VMEM((seq_parts, tok, group), jnp.bfloat16),
            pltpu.VMEM((length, pair), jnp.float32),
            pltpu.VMEM((length, pair), jnp.float32),
            pltpu.VMEM((length, pair), jnp.float32),
        ]
        + [pltpu.SemaphoreType.DMA((7,))] * 4
        + reduce_scratch(tok // 4, features)
        + [pltpu.SemaphoreType.DMA],
        compiler_params=comm_params(number, 56),
        name="attention_backward",
    )(grad_attended, heads_in, cosine, sine, beside.reshape(SIDE, SIDE, 4, tok // 4, features))
    return (grads, summed.reshape(tok, features))


def gate_columns(logits, chosen_ids, experts_all):
    named = jnp.any(
        chosen_ids[..., None] == jnp.arange(experts_all, dtype=jnp.int32), axis=-2
    )
    peak = jnp.max(jnp.where(named, logits, -jnp.inf), axis=-1, keepdims=True)
    exponent = jnp.where(named, jnp.exp(logits - peak), 0.0)
    gates = exponent / jnp.sum(exponent, axis=-1, keepdims=True)
    coarse = lax.reduce_precision(gates, 8, 7)
    columns = jnp.concatenate(
        [named.astype(jnp.float32), coarse, gates - coarse, jnp.zeros_like(gates)], axis=-1
    ).astype(jnp.bfloat16)
    return (gates, columns)


def near_place(at):
    if isinstance(at, int) and at >= 9:
        return far_place(at)
    return (at // 3 - 1, at % 3 - 1)


def far_place(at):
    beyond = at - 9
    turn_over = beyond // 4
    return (
        2 * (1 - turn_over) + turn_over * (beyond - 5),
        (1 - turn_over) * (beyond - 1) + turn_over * 2,
    )


def expert_layer(
    tokens_own, cot_all, gate_full, up_full, down_full, experts_all, capacity, number
):
    tok, wide = tokens_own.shape
    sources = SIDE * SIDE
    quarter = tok // 4
    features = wide - 128
    hidden_units = gate_full.shape[2]
    group = 8
    chunks = sources // group
    chunk_rows = group * capacity
    f32, b16 = jnp.float32, jnp.bfloat16

    def kernel(
        tok_hbm, cot_hbm, gate_hbm, up_hbm, down_hbm,
        mix_hbm, back_ref, ggate_hbm, gup_hbm, gdown_hbm,
        tok_v, cot_v, gate_v, up_v, down_v, mix_v, grad_v,
        x_v, deo_v, slope_v, act_v, inner_v, pick_t, share_v, dgate_v,
        in_sem, out_sem, g_send, g_recv,
        rows_v, far, near, far_last, near_last, r_send, r_recv,
    ):
        first = lax.axis_index("wshard") * 2
        home_z, home_y = plane_place("y", 0, 0)
        loads = [
            pltpu.make_async_copy(source, target, in_sem.at[i])
            for i, (source, target) in enumerate(
                [(tok_hbm, tok_v.at[home_z, home_y]), (cot_hbm, cot_v), (gate_hbm, gate_v), (up_hbm, up_v),
                 (down_hbm, down_v)]
            )
        ]
        for item in loads:
            item.start()
        lane = lax.broadcasted_iota(jnp.int32, (tok, 128), 1)
        down_rows = lax.broadcasted_iota(jnp.int32, (tok, 128), 0)
        lower = jnp.where(down_rows >= lane, 1.0, 0.0).astype(b16)
        greet(plane_neighbours())
        gather = plane_gather(
            lambda low, count: tok_hbm.at[pl.ds(low, count)],
            lambda z, y, low, count: tok_v.at[z, y, pl.ds(low, count)],
            g_send,
            g_recv,
            nothing,
        )
        advance(gather)
        advance(gather)
        advance(gather)
        advance(gather)
        advance(gather)
        loads[0].wait()
        loads[1].wait()

        def prepare(s, place_of):
            off_z, off_y = place_of(s)
            z, y = plane_place("y", off_y, off_z)
            info = tok_v[z, y, :, :, pl.ds(features, 128)].reshape(tok, 128)
            info32 = info.astype(f32)
            place = matmul(lower, info, ((1,), (0,))) - 1.0
            place = jnp.where(info32 > 0.5, place, -1.0)
            place_rows = place.T
            info_rows = info32.T
            row_picks, col_places = [], []
            shares = []
            for e in (0, 1):
                at = first + e
                row = jnp.sum(jnp.where(down_rows == at, place_rows, 0.0), axis=0, keepdims=True)
                gate = jnp.sum(
                    jnp.where(
                        (down_rows == experts_all + at) | (down_rows == 2 * experts_all + at),
                        info_rows,
                        0.0,
                    ),
                    axis=0,
                    keepdims=True,
                )
                slot = lax.broadcasted_iota(jnp.int32, (capacity, tok), 0).astype(f32)
                hit = slot == row
                row_picks.append(jnp.where(hit, 1.0, 0.0))
                shares.append(jnp.sum(jnp.where(hit, gate, 0.0), axis=1, keepdims=True))
                col_places.append(
                    jnp.sum(jnp.where(lane == at, place, 0.0), axis=1, keepdims=True)
                )
            pick = jnp.concatenate(row_picks, axis=0).astype(b16)
            lane_f = lane.astype(f32)
            pick_t[s] = (
                jnp.where(lane_f == col_places[0], 1.0, 0.0) * jnp.where(lane < capacity, 1.0, 0.0)
                + jnp.where(lane_f - float(capacity) == col_places[1], 1.0, 0.0)
                * jnp.where(lane >= capacity, 1.0, 0.0)
            ).astype(b16)
            share_v[s] = jnp.concatenate(shares, axis=0)
            rows = matmul(
                pick, tok_v[z, y, :, :, pl.ds(0, features)].reshape(tok, features), ((1,), (0,))
            ).astype(b16)
            c, i = s // group, s % group
            x_v[0, c, i] = rows[:capacity]
            x_v[1, c, i] = rows[capacity:]
            cots = matmul(pick, cot_v[z, y], ((1,), (0,))).astype(b16)
            deo_v[0, c, i] = cots[:capacity]
            deo_v[1, c, i] = cots[capacity:]

        def prepare_all(low, high, place_of):
            def step(s, carry):
                prepare(s, place_of)
                return carry

            lax.fori_loop(low, high, step, 0)

        def forward(c):
            weighted = []
            for e in (0, 1):
                x = x_v[e, c].reshape(chunk_rows, features)
                gate_val = matmul(x, gate_v[e], ((1,), (0,)))
                up_val = matmul(x, up_v[e], ((1,), (0,)))
                sigma = 1.0 / (1.0 + jnp.exp(-gate_val))
                act = gate_val * sigma
                inner = (act * up_val).astype(b16)
                inner_v[e, c] = inner
                act_v[e, c] = act.astype(b16)
                slope_v[e, c] = (up_val * (sigma * (1.0 + gate_val * (1.0 - sigma)))).astype(b16)
                made = matmul(inner, down_v[e], ((1,), (0,))).astype(b16).astype(f32)
                share = jnp.concatenate(
                    [share_v[c * group + i, pl.ds(e * capacity, capacity)] for i in range(group)],
                    axis=0,
                )
                mix_grad = residual_multiplier * deo_v[e, c].reshape(chunk_rows, features).astype(f32)
                dgate_v[e, c] = jnp.sum(made * mix_grad, axis=1, keepdims=True)
                deo_v[e, c] = (share * mix_grad).astype(b16).reshape(group, capacity, features)
                weighted.append((share * made).astype(b16))
            for i in range(group):
                both = jnp.concatenate(
                    [w[i * capacity : (i + 1) * capacity] for w in weighted], axis=0
                )
                off_z, off_y = near_place(c * group + i)
                z, y = plane_place("y", off_y, off_z)
                mix_v[z, y] = matmul(pick_t[c * group + i], both, ((1,), (0,))).astype(b16)

        prepare_all(0, 9, near_place)
        advance(gather)
        for item in loads[2:]:
            item.wait()
        forward(0)
        finish(gather)
        prepare_all(9, sources, far_place)
        forward(1)
        stores = [pltpu.make_async_copy(mix_v, mix_hbm, out_sem.at[0])]
        stores[0].start()
        lane_rows = lax.broadcasted_iota(jnp.int32, (chunk_rows, 128), 1)

        def backward(c):
            made = []
            for e in (0, 1):
                deo = deo_v[e, c].reshape(chunk_rows, features)
                d_inner = matmul(deo, down_v[e], ((1,), (1,)))
                d_gate = (d_inner * slope_v[e, c].astype(f32)).astype(b16)
                d_up = (d_inner * act_v[e, c].astype(f32)).astype(b16)
                slope_v[e, c] = d_gate
                act_v[e, c] = d_up
                d_rows = (
                    matmul(d_gate, gate_v[e], ((1,), (1,))) + matmul(d_up, up_v[e], ((1,), (1,)))
                ).astype(b16)
                coarse = dgate_v[e, c].astype(b16).astype(f32)
                fine = dgate_v[e, c] - coarse
                columns = jnp.where(lane_rows == first + e, coarse, 0.0) + jnp.where(
                    lane_rows == experts_all + first + e, fine, 0.0
                )
                made.append(jnp.concatenate([d_rows, columns.astype(b16)], axis=1))
            for i in range(group):
                both = jnp.concatenate(
                    [m[i * capacity : (i + 1) * capacity] for m in made], axis=0
                )
                off_z, off_y = near_place(c * group + i)
                z, y = plane_place("y", off_y, off_z)
                rows_v[z, y] = (
                    matmul(pick_t[c * group + i], both, ((1,), (0,)))
                    .astype(b16)
                    .reshape(4, quarter, wide)
                )

        def store(low, total):
            back_ref[pl.ds(low, 2)] = total

        reduce = plane_reduce(
            rows_v, far, near, far_last, near_last, r_send, r_recv, store
        )
        backward(1)
        advance(reduce)
        backward(0)
        advance(reduce)
        rows_all = chunks * chunk_rows

        def whole(ref, e, columns):
            return ref[e].reshape(rows_all, columns)

        for e in (0, 1):
            x = whole(x_v, e, features)
            for i, source, target in (
                (e, slope_v, ggate_hbm),
                (2 + e, act_v, gup_hbm),
            ):
                grad_v[i] = matmul(x, whole(source, e, hidden_units), ((0,), (0,))).astype(b16)
                stores.append(
                    pltpu.make_async_copy(grad_v.at[i], target.at[e], out_sem.at[1 + i])
                )
                stores[-1].start()
            advance(reduce)
        for e in (0, 1):
            grad = matmul(
                whole(inner_v, e, hidden_units), whole(deo_v, e, features), ((0,), (0,))
            ).astype(b16)
            cot_v[e] = grad.reshape(4, 128, features)
            stores.append(
                pltpu.make_async_copy(cot_v.at[e], gdown_hbm.at[e], out_sem.at[5 + e])
            )
            stores[-1].start()
            if e == 0:
                advance(reduce)
        finish(reduce)
        for item in stores:
            item.wait()

    anywhere = pl.BlockSpec(memory_space=pl.ANY)
    local = gate_full.shape[0]
    outs = pl.pallas_call(
        kernel,
        out_shape=(
            jax.ShapeDtypeStruct((SIDE, SIDE, tok, features), b16),
            jax.ShapeDtypeStruct((4, quarter, wide), f32),
            jax.ShapeDtypeStruct((local, features, hidden_units), b16),
            jax.ShapeDtypeStruct((local, features, hidden_units), b16),
            jax.ShapeDtypeStruct((local, 4, hidden_units // 4, features), b16),
        ),
        in_specs=[anywhere] * 5,
        out_specs=(anywhere, pl.BlockSpec(memory_space=pltpu.VMEM)) + (anywhere,) * 3,
        scratch_shapes=[
            pltpu.VMEM((SIDE, SIDE, 4, quarter, wide), b16),
            pltpu.VMEM((SIDE, SIDE, tok, features), b16),
            pltpu.VMEM(gate_full.shape, b16),
            pltpu.VMEM(up_full.shape, b16),
            pltpu.VMEM(down_full.shape, b16),
            pltpu.VMEM((SIDE, SIDE, tok, features), b16),
            pltpu.VMEM((4, features, hidden_units), b16),
            pltpu.VMEM((2, chunks, group, capacity, features), b16),
            pltpu.VMEM((2, chunks, group, capacity, features), b16),
            pltpu.VMEM((2, chunks, chunk_rows, hidden_units), b16),
            pltpu.VMEM((2, chunks, chunk_rows, hidden_units), b16),
            pltpu.VMEM((2, chunks, chunk_rows, hidden_units), b16),
            pltpu.VMEM((sources, tok, 2 * capacity), b16),
            pltpu.VMEM((sources, 2 * capacity, 1), f32),
            pltpu.VMEM((2, chunks, chunk_rows, 1), f32),
            pltpu.SemaphoreType.DMA((5,)),
            pltpu.SemaphoreType.DMA((7,)),
            pltpu.SemaphoreType.DMA((2, 20)),
            pltpu.SemaphoreType.DMA((2, 20)),
        ]
        + reduce_scratch(quarter, wide),
        compiler_params=comm_params(number, 60),
        name="expert_layer",
    )(
        tokens_own.reshape(4, quarter, wide),
        cot_all.reshape(SIDE, SIDE, tok, features),
        gate_full,
        up_full,
        down_full,
    )
    return (
        outs[0].reshape(sources, tok, features),
        outs[1].reshape(tok, wide),
        outs[2],
        outs[3],
        outs[4].reshape(local, hidden_units, features),
    )


def norm_backward(grad_normed, values, scale, gain_full):
    grad_gain = jnp.sum(grad_normed * values * scale, axis=0)
    grad_hat = grad_normed * gain_full
    grad_values = scale * grad_hat - values * (scale * scale * scale) * jnp.mean(
        grad_hat * values, axis=1, keepdims=True
    )
    return (grad_values, grad_gain)


def local(
    tokens,
    weight_qkv,
    weight_out,
    router,
    gain_attn,
    gain_ffn,
    expert_gate,
    expert_up,
    expert_down,
    expert_ids,
    cotangent,
):
    tok_dev = tokens.shape[1]
    features = tokens.shape[2]
    seq_parts = lax.axis_size("seq")
    owners = lax.axis_size("wshard")
    local_experts = expert_gate.shape[0]
    experts_all = local_experts * owners
    top_count = expert_ids.shape[2]
    capacity = 2 * tok_dev * top_count // experts_all
    heads_dev = HEADS // seq_parts
    key_heads = KV_HEADS // seq_parts
    query_cols = heads_dev * HEAD_DIM
    key_cols = key_heads * HEAD_DIM
    query_width = HEADS * HEAD_DIM
    key_width = KV_HEADS * HEAD_DIM
    length = tok_dev * seq_parts
    qkv_width = weight_qkv.shape[1]
    smalls = jnp.concatenate(
        [
            router,
            gain_attn[:, None],
            gain_ffn[:, None],
            jnp.zeros((router.shape[0], 128 - experts_all - 2), jnp.bfloat16),
        ],
        axis=1,
    )
    weights_full, gate_full, up_full, down_full = weights_gather(
        weight_qkv, [weight_out, smalls], [expert_gate, expert_up, expert_down], 0
    )
    qkv_full = weights_full[:, :qkv_width]
    out_full = weights_full[:, qkv_width : qkv_width + features]
    smalls_full = weights_full[:, qkv_width + features :]
    router_full = smalls_full[:, :experts_all]
    gain_one = smalls_full[:, experts_all].astype(jnp.float32)
    gain_two = smalls_full[:, experts_all + 1].astype(jnp.float32)
    inputs = tokens[0].astype(jnp.float32)
    chosen_ids = expert_ids[0]
    scale_one = rms_scale(inputs)
    normed_one = (inputs * scale_one * gain_one).astype(jnp.bfloat16)
    cosine, sine = (jnp.asarray(table) for table in rope_tables(length))
    attended, heads_all, cot_all = attention_forward(
        normed_one, weights_full, qkv_width, cosine, sine, cotangent[0], 5
    )
    branch = jnp.dot(attended, out_full, preferred_element_type=jnp.float32)
    hidden = inputs + residual_multiplier * branch
    scale_two = rms_scale(hidden)
    normed_two = (hidden * scale_two * gain_two).astype(jnp.bfloat16)
    logits = jnp.dot(normed_two, router_full, preferred_element_type=jnp.float32)
    gates_own, gate_info = gate_columns(logits, chosen_ids, experts_all)
    mix_part, back, grad_gate, grad_up, grad_down = expert_layer(
        jnp.concatenate([normed_two, gate_info], axis=1),
        cot_all,
        gate_full,
        up_full,
        down_full,
        experts_all,
        capacity,
        1,
    )
    grad_output = cotangent[0].astype(jnp.float32)
    grad_back = back[:, :features]
    grad_gates = (
        back[:, features : features + experts_all]
        + back[:, features + experts_all : features + 2 * experts_all]
    )
    grad_logits = (
        gates_own
        * (grad_gates - jnp.sum(gates_own * grad_gates, axis=1, keepdims=True))
    ).astype(jnp.bfloat16)
    grad_normed_two = jnp.dot(grad_logits, router_full.T, preferred_element_type=jnp.float32)
    grad_normed_two = grad_normed_two + grad_back
    grad_hidden_norm, grad_gain_ffn = norm_backward(grad_normed_two, hidden, scale_two, gain_two)
    grad_hidden = grad_output + grad_hidden_norm
    grad_branch = (residual_multiplier * grad_hidden).astype(jnp.bfloat16)
    grad_out = jnp.dot(attended.T, grad_branch, preferred_element_type=jnp.float32)
    grad_attended = jnp.dot(grad_branch, out_full.T, preferred_element_type=jnp.float32).astype(
        jnp.bfloat16
    )
    grad_proj, mixture = attention_backward(
        grad_attended, heads_all, cosine, sine, mix_part, 6
    )
    output = hidden + residual_multiplier * mixture
    grad_qkv = jnp.dot(normed_one.T, grad_proj, preferred_element_type=jnp.float32)
    grad_normed_one = jnp.dot(grad_proj, qkv_full.T, preferred_element_type=jnp.float32)
    grad_input_norm, grad_gain_attn = norm_backward(grad_normed_one, inputs, scale_one, gain_one)
    grad_input = grad_hidden + grad_input_norm
    column = jnp.arange(128, dtype=jnp.int32)[None, :]
    grad_smalls = (
        jnp.dot(
            normed_two.T,
            jnp.pad(grad_logits, ((0, 0), (0, 128 - experts_all))),
            preferred_element_type=jnp.float32,
        )
        + jnp.where(column == experts_all, grad_gain_attn[:, None], 0.0)
        + jnp.where(column == experts_all + 1, grad_gain_ffn[:, None], 0.0)
    ).astype(jnp.bfloat16)
    own_qkv, own_out, own_smalls, own_gate, own_up, own_down = weights_reduce(
        [grad_qkv.astype(jnp.bfloat16), grad_out.astype(jnp.bfloat16), grad_smalls],
        [grad_gate, grad_up, grad_down],
        4,
    )
    shares = (
        own_qkv,
        own_out,
        own_smalls[:, :experts_all],
        own_smalls[:, experts_all],
        own_smalls[:, experts_all + 1],
    )
    expert_shares = (own_gate, own_up, own_down)
    return (
        output.astype(jnp.bfloat16)[None],
        grad_input.astype(jnp.bfloat16)[None],
        shares[0],
        shares[1],
        shares[2],
        shares[3],
        shares[4],
        expert_shares[0],
        expert_shares[1],
        expert_shares[2],
    )


def solution(mesh):
    placed = (
        P("wshard", "seq", None),
        P(("seq", "wshard"), None),
        P(("seq", "wshard"), None),
        P(("seq", "wshard"), None),
        P(("seq", "wshard")),
        P(("seq", "wshard")),
        P("wshard", "seq", None),
        P("wshard", "seq", None),
        P("wshard", "seq", None),
        P("wshard", "seq", None),
        P("wshard", "seq", None),
    )
    return jax.shard_map(
        local,
        mesh=mesh,
        in_specs=placed,
        out_specs=(
            P("wshard", "seq", None),
            P("wshard", "seq", None),
            P(("seq", "wshard"), None),
            P(("seq", "wshard"), None),
            P(("seq", "wshard"), None),
            P(("seq", "wshard")),
            P(("seq", "wshard")),
            P("wshard", "seq", None),
            P("wshard", "seq", None),
            P("wshard", "seq", None),
        ),
        check_vma=False,
    )
```

```python
import jax
import jax.numpy as jnp
import numpy as np
from jax import lax
from jax.experimental import pallas as pl
from jax.experimental.pallas import tpu as pltpu
from jax.sharding import PartitionSpec as P

HEADS = 16
KV_HEADS = 8
HEAD_DIM = 64


epsilon = 1e-06
attention_multiplier = 0.015625
residual_multiplier = 0.22
rope_theta = 10000.0


MESH = pl.DeviceIdType.MESH
SIDE = 4


def plane_place(first, offset_first, offset_second):
    mine = lax.axis_index("wshard")
    z, y = mine // SIDE, mine % SIDE
    if first == "y":
        return ((z + offset_second + SIDE) % SIDE, (y + offset_first + SIDE) % SIDE)
    return ((z + offset_first + SIDE) % SIDE, (y + offset_second + SIDE) % SIDE)


def plane_peer(first, offset_first, offset_second):
    z, y = plane_place(first, offset_first, offset_second)
    return {"wshard": z * SIDE + y}


def plane_neighbours():
    return [plane_peer("y", step, 0) for step in (1, -1)] + [
        plane_peer("y", 0, step) for step in (1, -1)
    ]


def seq_peer(offset_x, flip):
    mine = lax.axis_index("seq")
    x, core = mine // 2, mine % 2
    if flip:
        core = 1 - core
    return {"seq": ((x + offset_x) % SIDE) * 2 + core}


def greet(peers):
    barrier = pltpu.get_barrier_semaphore()
    for peer in peers:
        pl.semaphore_signal(barrier, inc=1, device_id=peer, device_id_type=MESH)
    pl.semaphore_wait(barrier, len(peers))


HALVES = (("y", 0), ("z", 2))
ORDER = (0, -1, 1, 2)


def plane_gather(own, view, send, recv, after_row):
    started = []

    def copy(half, kind, source, target, peer):
        return pltpu.make_async_remote_copy(
            src_ref=source,
            dst_ref=target,
            send_sem=send.at[half, kind],
            recv_sem=recv.at[half, kind],
            device_id=peer,
            device_id_type=MESH,
        )

    def push(half, kind, source, target, peer):
        item = copy(half, kind, source, target, peer)
        item.start()
        started.append(item)

    def arrived(half, kind, target):
        first, _ = HALVES[half]
        copy(half, kind, target, target, plane_peer(first, 1, 0)).wait_recv()

    def block(half, along_first, along_second, low, count):
        first, base = HALVES[half]
        z, y = plane_place(first, along_first, along_second)
        return view(z, y, base + low, count)

    def ring(half, slot, axis, along, source):
        first, base = HALVES[half]
        for kind, step in ((0, 1), (1, -1)):
            peer = plane_peer(first, step, 0) if axis == 0 else plane_peer(first, 0, step)
            push(half, 4 * slot + kind, source, block(half, along, 0, 0, 2), peer)

    def ring_relay(half, slot, axis, along):
        first, base = HALVES[half]
        for kind, step in ((0, 1), (1, -1)):
            where = (-step, 0) if axis == 0 else (along, -step)
            arrived(half, 4 * slot + kind, block(half, where[0], where[1], 0, 2))
            part = block(half, where[0], where[1], kind, 1)
            peer = plane_peer(first, step, 0) if axis == 0 else plane_peer(first, 0, step)
            push(half, 4 * slot + 2 + kind, part, part, peer)

    def ring_end(half, slot, axis, along):
        where = (2, 0) if axis == 0 else (along, 2)
        for kind in (0, 1):
            arrived(half, 4 * slot + 2 + kind, block(half, where[0], where[1], kind, 1))

    for half in (0, 1):
        ring(half, 0, 0, 0, own(HALVES[half][1], 2))
    for half in (0, 1):
        ring(half, 1, 1, 0, own(HALVES[half][1], 2))
    yield
    for half in (0, 1):
        ring_relay(half, 0, 0, 0)
        for slot in (1, 2):
            ring(half, 1 + slot, 1, ORDER[slot], block(half, ORDER[slot], 0, 0, 2))
    yield
    for half in (0, 1):
        ring_end(half, 0, 0, 0)
        ring(half, 4, 1, 2, block(half, 2, 0, 0, 2))
        after_row(half, 0)
    for slot in (0, 1, 2, 3):
        for half in (0, 1):
            ring_relay(half, 1 + slot, 1, ORDER[slot])
        yield
    for half in (0, 1):
        after_row(half, -1)
        after_row(half, 1)
    for half in (0, 1):
        for slot in (0, 1, 2, 3):
            ring_end(half, 1 + slot, 1, ORDER[slot])
        after_row(half, 2)
    for item in started:
        item.wait_send()


def plane_reduce(parts, far, near, far_last, near_last, send, recv, store):
    started = []

    def copy(half, kind, source, target, peer):
        return pltpu.make_async_remote_copy(
            src_ref=source,
            dst_ref=target,
            send_sem=send.at[half, kind],
            recv_sem=recv.at[half, kind],
            device_id=peer,
            device_id_type=MESH,
        )

    def push(half, kind, source, target, peer):
        item = copy(half, kind, source, target, peer)
        item.start()
        started.append(item)

    def arrived(half, kind, target):
        first, _ = HALVES[half]
        copy(half, kind, target, target, plane_peer(first, 1, 0)).wait_recv()

    def rows(half, offset, low, count):
        first, base = HALVES[half]
        z, y = plane_place(first, 0, offset)
        if first == "y":
            return parts.at[z, :, pl.ds(base + low, count)]
        return parts.at[:, y, pl.ds(base + low, count)]

    def one(half, offset, low, count):
        first, base = HALVES[half]
        z, y = plane_place(first, offset, 0)
        return parts.at[z, y, pl.ds(base + low, count)]

    def add(target, *others):
        if len(others) == 1:
            target[...] = target[...] + others[0][...]
            return
        total = target[...].astype(jnp.float32)
        for other in others:
            total = total + other[...].astype(jnp.float32)
        target[...] = total.astype(target.dtype)

    def add_rows(half, offset, low, count, *others):
        target = rows(half, offset, low, count)
        def step(at, carry):
            add(target.at[at], *[other.at[at] for other in others])
            return carry
        lax.fori_loop(0, SIDE, step, 0)

    def peer(half, axis, step):
        first, _ = HALVES[half]
        return plane_peer(first, 0, step) if axis == 1 else plane_peer(first, step, 0)

    for half in (0, 1):
        push(half, 0, rows(half, 2, 0, 1), far.at[half, 0], peer(half, 1, 1))
        push(half, 1, rows(half, 2, 1, 1), far.at[half, 1], peer(half, 1, -1))
    yield
    for half in (0, 1):
        push(half, 2, rows(half, 1, 1, 1), near.at[half, 0, :, pl.ds(1, 1)], peer(half, 1, 1))
        push(half, 3, rows(half, -1, 0, 1), near.at[half, 1, :, pl.ds(0, 1)], peer(half, 1, -1))
    yield
    for half in (0, 1):
        arrived(half, 0, far.at[half, 0])
        add_rows(half, 1, 0, 1, far.at[half, 0])
        push(half, 4, rows(half, 1, 0, 1), near.at[half, 0, :, pl.ds(0, 1)], peer(half, 1, 1))
        arrived(half, 1, far.at[half, 1])
        add_rows(half, -1, 1, 1, far.at[half, 1])
        push(half, 5, rows(half, -1, 1, 1), near.at[half, 1, :, pl.ds(1, 1)], peer(half, 1, -1))
    yield
    for half in (0, 1):
        arrived(half, 2, near.at[half, 0, :, pl.ds(1, 1)])
        arrived(half, 3, near.at[half, 1, :, pl.ds(0, 1)])
        arrived(half, 4, near.at[half, 0, :, pl.ds(0, 1)])
        arrived(half, 5, near.at[half, 1, :, pl.ds(1, 1)])
        add_rows(half, 0, 0, 2, near.at[half, 0], near.at[half, 1])
        push(half, 6, one(half, 2, 0, 1), far_last.at[half, 0], peer(half, 0, 1))
        push(half, 7, one(half, 2, 1, 1), far_last.at[half, 1], peer(half, 0, -1))
        push(half, 8, one(half, 1, 1, 1), near_last.at[half, 0, pl.ds(1, 1)], peer(half, 0, 1))
        push(half, 9, one(half, -1, 0, 1), near_last.at[half, 1, pl.ds(0, 1)], peer(half, 0, -1))
    yield
    for half in (0, 1):
        arrived(half, 6, far_last.at[half, 0])
        add(one(half, 1, 0, 1), far_last.at[half, 0])
        push(half, 10, one(half, 1, 0, 1), near_last.at[half, 0, pl.ds(0, 1)], peer(half, 0, 1))
        arrived(half, 7, far_last.at[half, 1])
        add(one(half, -1, 1, 1), far_last.at[half, 1])
        push(half, 11, one(half, -1, 1, 1), near_last.at[half, 1, pl.ds(1, 1)], peer(half, 0, -1))
    yield
    for half in (0, 1):
        arrived(half, 8, near_last.at[half, 0, pl.ds(1, 1)])
        arrived(half, 9, near_last.at[half, 1, pl.ds(0, 1)])
        arrived(half, 10, near_last.at[half, 0, pl.ds(0, 1)])
        arrived(half, 11, near_last.at[half, 1, pl.ds(1, 1)])
        total = one(half, 0, 0, 2)[...].astype(jnp.float32)
        for side in (0, 1):
            total = total + near_last[half, side].astype(jnp.float32)
        store(HALVES[half][1], total)
    for item in started:
        item.wait_send()


def reduce_scratch(quarter_rows, width):
    unit = (quarter_rows, width)
    return [
        pltpu.VMEM((SIDE, SIDE, 4) + unit, jnp.bfloat16),
        pltpu.VMEM((2, 2, SIDE, 1) + unit, jnp.bfloat16),
        pltpu.VMEM((2, 2, SIDE, 2) + unit, jnp.bfloat16),
        pltpu.VMEM((2, 2, 1) + unit, jnp.bfloat16),
        pltpu.VMEM((2, 2, 2) + unit, jnp.bfloat16),
        pltpu.SemaphoreType.DMA((2, 12)),
        pltpu.SemaphoreType.DMA((2, 12)),
    ]


def comm_params(number):
    return pltpu.CompilerParams(
        collective_id=number, has_side_effects=True, vmem_limit_bytes=62 * 1024 * 1024
    )


def nothing(half, offset):
    return None


def advance(steps):
    next(steps, None)


def finish(steps):
    for _ in steps:
        pass


def pair_up(low, high, lane):
    return (
        jnp.where(lane < HEAD_DIM, low, pltpu.roll(high, HEAD_DIM, 1)),
        jnp.where(lane < HEAD_DIM, pltpu.roll(low, HEAD_DIM, 1), high),
    )


def by_group(rows):
    lane = lax.broadcasted_iota(jnp.int32, (rows.shape[0], 128), 1)
    tile = lambda at: rows[:, at * 128 : (at + 1) * 128]
    parts = []
    for j in range(4):
        low, high = tile(8 + j), tile(12 + j)
        first, second = pair_up(low, high, lane)
        parts += [tile(2 * j), first, tile(2 * j + 1), second]
    return jnp.concatenate(parts, axis=1)


def by_kind(rows):
    lane = lax.broadcasted_iota(jnp.int32, (rows.shape[0], 128), 1)
    tile = lambda at: rows[:, at * 128 : (at + 1) * 128]
    queries, keys, values = [], [], []
    for j in range(4):
        queries += [tile(4 * j), tile(4 * j + 2)]
        key, value = pair_up(tile(4 * j + 1), tile(4 * j + 3), lane)
        keys.append(key)
        values.append(value)
    return jnp.concatenate(queries + keys + values, axis=1)


def ring_gather(owns, outs, send, recv, core_send, core_recv, local):
    seq = lax.axis_index("seq")
    x, core = seq // 2, seq % 2
    other = seq_peer(0, True)
    started, swaps = [], []
    count = len(owns)

    def at(m, step, side):
        return outs[m].at[:, (x + step) % SIDE, side]

    def copy(m, kind, source, target, step):
        return pltpu.make_async_remote_copy(
            src_ref=source,
            dst_ref=target,
            send_sem=send.at[m, kind],
            recv_sem=recv.at[m, kind],
            device_id=seq_peer(step, False),
            device_id_type=MESH,
        )

    def push(m, kind, source, target, step):
        item = copy(m, kind, source, target, step)
        item.start()
        started.append(item)

    def arrived(m, kind, target):
        copy(m, kind, target, target, 1).wait_recv()

    def swap(m, kind, source, step):
        def across(out_of, into):
            return pltpu.make_async_remote_copy(
                src_ref=out_of,
                dst_ref=into,
                send_sem=core_send.at[m, kind],
                recv_sem=core_recv.at[m, kind],
                device_id=other,
                device_id_type=MESH,
            )

        item = across(source, at(m, step, core))
        item.start()
        started.append(item)
        swaps.append(across(at(m, step, 1 - core), at(m, step, 1 - core)))

    keeps = [pltpu.make_async_copy(owns[m], at(m, 0, core), local.at[m]) for m in range(count)]
    for m in range(count):
        push(m, 0, owns[m], at(m, 0, core), 1)
        push(m, 1, owns[m], at(m, 0, core), 3)
    for m in range(count):
        keeps[m].start()
        swap(m, 0, owns[m], 0)
    yield
    for m in range(count):
        for kind, expert, came, onward in ((0, 0, 3, 1), (1, 1, 1, 3)):
            arrived(m, kind, at(m, came, core))
            part = outs[m].at[expert, (x + came) % SIDE, core]
            push(m, 2 + kind, part, part, onward)
            swap(m, 1 + kind, at(m, came, core), came)
    yield
    for m in range(count):
        for kind in (0, 1):
            arrived(m, 2 + kind, outs[m].at[kind, (x + 2) % SIDE, core])
        swap(m, 3, at(m, 2, core), 2)
    for item in swaps:
        item.wait_recv()
    for item in keeps:
        item.wait()
    for item in started:
        item.wait_send()


def weights_gather(qkv, others, experts, number):
    rows, qkv_width = qkv.shape
    width = qkv_width + sum(other.shape[1] for other in others)
    kinds = len(experts)

    def kernel(*refs):
        refs = list(refs)
        take = lambda count: [refs.pop(0) for _ in range(count)]
        ins, ex_ins, (out_ref,), ex_outs = take(1 + len(others)), take(kinds), take(1), take(kinds)
        own_ref, send, recv, x_send, x_recv, core_send, core_recv, local_sem = take(8)
        ring_send, ring_recv, swap_send, swap_recv, ring_local = take(5)
        own_ref[:, pl.ds(0, qkv_width)] = by_group(ins[0][...].astype(jnp.float32)).astype(
            own_ref.dtype
        )
        at = qkv_width
        for other in ins[1:]:
            own_ref[:, pl.ds(at, other.shape[1])] = other[...]
            at += other.shape[1]
        seq = lax.axis_index("seq")
        x, core = seq // 2, seq % 2
        x_peers = [seq_peer(step, False) for step in (1, 3, 2)]
        other = seq_peer(0, True)
        greet(plane_neighbours() + x_peers + [other])
        z, y = plane_place("y", 0, 0)
        keep = pltpu.make_async_copy(own_ref, out_ref.at[x, core, z, y], local_sem)
        keep.start()
        sends = []
        for i, step in enumerate((1, 3, 2)):
            item = pltpu.make_async_remote_copy(
                src_ref=own_ref,
                dst_ref=out_ref.at[x, core, z, y],
                send_sem=x_send.at[i],
                recv_sem=x_recv.at[i],
                device_id=x_peers[i],
                device_id_type=MESH,
            )
            item.start()
            sends.append(item)
        keep.wait()
        for i, step in enumerate((1, 3, 2)):
            came = out_ref.at[(x + SIDE - step) % SIDE, core, z, y]
            pltpu.make_async_remote_copy(
                src_ref=came,
                dst_ref=came,
                send_sem=x_send.at[i],
                recv_sem=x_recv.at[i],
                device_id=x_peers[i],
                device_id_type=MESH,
            ).wait_recv()

        swaps = []

        def swap(half, offset):
            first, base = HALVES[half]
            z, y = plane_place(first, 0, offset)
            mine = (
                out_ref.at[pl.ds(base, 2), core, z]
                if first == "y"
                else out_ref.at[pl.ds(base, 2), core, :, y]
            )
            theirs = (
                out_ref.at[pl.ds(base, 2), 1 - core, z]
                if first == "y"
                else out_ref.at[pl.ds(base, 2), 1 - core, :, y]
            )
            kind = ORDER.index(offset)
            item = pltpu.make_async_remote_copy(
                src_ref=mine,
                dst_ref=mine,
                send_sem=core_send.at[half, kind],
                recv_sem=core_recv.at[half, kind],
                device_id=other,
                device_id_type=MESH,
            )
            item.start()
            sends.append(item)
            swaps.append(
                pltpu.make_async_remote_copy(
                    src_ref=theirs,
                    dst_ref=theirs,
                    send_sem=core_send.at[half, kind],
                    recv_sem=core_recv.at[half, kind],
                    device_id=other,
                    device_id_type=MESH,
                )
            )

        plane = plane_gather(
            lambda low, count: out_ref.at[pl.ds(low, count), core, z, y],
            lambda z, y, low, count: out_ref.at[pl.ds(low, count), core, z, y],
            send,
            recv,
            swap,
        )
        ring = ring_gather(
            ex_ins, ex_outs, ring_send, ring_recv, swap_send, swap_recv, ring_local
        )
        advance(plane)
        advance(ring)
        for _ in range(5):
            advance(plane)
        advance(ring)
        finish(plane)
        finish(ring)
        for item in swaps:
            item.wait_recv()
        for item in sends:
            item.wait_send()

    out = pl.pallas_call(
        kernel,
        out_shape=(jax.ShapeDtypeStruct((4, 2, SIDE, SIDE, rows, width), qkv.dtype),)
        + tuple(
            jax.ShapeDtypeStruct((2, 4, 2) + expert.shape[1:], expert.dtype) for expert in experts
        ),
        in_specs=[pl.BlockSpec(memory_space=pltpu.VMEM)] * (1 + len(others))
        + [pl.BlockSpec(memory_space=pl.ANY)] * kinds,
        out_specs=(pl.BlockSpec(memory_space=pl.ANY),) * (1 + kinds),
        scratch_shapes=[
            pltpu.VMEM((rows, width), qkv.dtype),
            pltpu.SemaphoreType.DMA((2, 20)),
            pltpu.SemaphoreType.DMA((2, 20)),
            pltpu.SemaphoreType.DMA((3,)),
            pltpu.SemaphoreType.DMA((3,)),
            pltpu.SemaphoreType.DMA((2, 4)),
            pltpu.SemaphoreType.DMA((2, 4)),
            pltpu.SemaphoreType.DMA,
        ]
        + [pltpu.SemaphoreType.DMA((kinds, 4))] * 4
        + [pltpu.SemaphoreType.DMA((kinds,))],
        compiler_params=comm_params(number),
        name="weights_gather",
    )(qkv, *others, *experts)
    return (out[0].reshape(4 * 2 * SIDE * SIDE * rows, width),) + tuple(
        full.reshape(2, 8 * expert.shape[1], expert.shape[2])
        for full, expert in zip(out[1:], experts)
    )


def expert_shares_of(experts):
    return [(2, 4, 2, expert.shape[1] // 8, expert.shape[2]) for expert in experts]


def ring_reduce_scratch(experts):
    units = [share[3:] for share in expert_shares_of(experts)]
    count = len(units)
    return (
        [pltpu.VMEM((2, 4) + unit, jnp.bfloat16) for unit in units]
        + [pltpu.VMEM((2, 4) + unit, jnp.bfloat16) for unit in units]
        + [pltpu.VMEM((2,) + unit, jnp.bfloat16) for unit in units]
        + [pltpu.VMEM((2, 2) + unit, jnp.bfloat16) for unit in units]
        + [pltpu.SemaphoreType.DMA((count,))] * 3
        + [pltpu.SemaphoreType.DMA((count, 6))] * 2
    )


def ring_reduce(ins, outs, refs):
    count = len(ins)
    sums, twins = refs[:count], refs[count : 2 * count]
    far, near = refs[2 * count : 3 * count], refs[3 * count : 4 * count]
    load, core_send, core_recv, send, recv = refs[4 * count :]
    core = lax.axis_index("seq") % 2
    loads, swaps = [], []
    for m in range(count):
        loads.append(pltpu.make_async_copy(ins[m].at[:, :, core], sums[m], load.at[m]))
        loads[m].start()
        swaps.append(
            pltpu.make_async_remote_copy(
                src_ref=ins[m].at[:, :, 1 - core],
                dst_ref=twins[m],
                send_sem=core_send.at[m],
                recv_sem=core_recv.at[m],
                device_id=seq_peer(0, True),
                device_id_type=MESH,
            )
        )
        swaps[m].start()
    yield
    x = lax.axis_index("seq") // 2
    started = []

    def copy(m, kind, source, target, step):
        return pltpu.make_async_remote_copy(
            src_ref=source,
            dst_ref=target,
            send_sem=send.at[m, kind],
            recv_sem=recv.at[m, kind],
            device_id=seq_peer(step, False),
            device_id_type=MESH,
        )

    def push(m, kind, source, target, step):
        item = copy(m, kind, source, target, step)
        item.start()
        started.append(item)

    def arrived(m, kind, target):
        copy(m, kind, target, target, 1).wait_recv()

    def at(step):
        return (x + step) % SIDE

    for m in range(count):
        loads[m].wait()
        swaps[m].wait_recv()
        started.append(swaps[m])

        def add_pair(at, carry):
            sums[m][at // 4, at % 4] = sums[m][at // 4, at % 4] + twins[m][at // 4, at % 4]
            return carry

        lax.fori_loop(0, 8, add_pair, 0)
        push(m, 0, sums[m].at[0, at(2)], far[m].at[0], 1)
        push(m, 1, sums[m].at[1, at(2)], far[m].at[1], 3)
    for m in range(count):
        push(m, 2, sums[m].at[1, at(1)], near[m].at[0, 1], 1)
        push(m, 3, sums[m].at[0, at(3)], near[m].at[1, 0], 3)
    yield
    for m in range(count):
        for kind, expert, step in ((0, 0, 1), (1, 1, 3)):
            arrived(m, kind, far[m].at[kind])
            target = sums[m].at[expert, at(step)]
            target[...] = target[...] + far[m][kind]
            push(m, 4 + kind, target, near[m].at[kind, expert], step)
    yield
    for m in range(count):
        arrived(m, 2, near[m].at[0, 1])
        arrived(m, 3, near[m].at[1, 0])
        arrived(m, 4, near[m].at[0, 0])
        arrived(m, 5, near[m].at[1, 1])
        for expert in (0, 1):
            outs[m][expert] = (
                sums[m][expert, at(0)].astype(jnp.float32)
                + near[m][0, expert].astype(jnp.float32)
                + near[m][1, expert].astype(jnp.float32)
            )
    for item in started:
        item.wait_send()


def weights_reduce(pieces, experts, number):
    widths = [piece.shape[1] for piece in pieces]
    width = sum(widths)
    rows = pieces[0].shape[0] // (4 * 2 * SIDE * SIDE)
    kinds = len(experts)
    shares = expert_shares_of(experts)

    def kernel(*refs):
        refs = list(refs)
        take = lambda count: [refs.pop(0) for _ in range(count)]
        ins, ex_ins = take(len(widths)), take(kinds)
        qkv_ref, out_ref, small_ref = take(3)
        ex_outs = take(kinds)
        (parts, far, near, far_last, near_last, send, recv, twin, mine, from_x, load, core_send,
         core_recv, x_send, x_recv) = take(15)
        ring = ring_reduce(ex_ins, ex_outs, refs)
        seq = lax.axis_index("seq")
        x, core = seq // 2, seq % 2
        x_peers = [seq_peer(step, False) for step in (1, 3, 2)]
        other = seq_peer(0, True)
        loads = []
        for quarter in range(4):
            at = 0
            for i, one_width in enumerate(widths):
                item = pltpu.make_async_copy(
                    ins[i].at[quarter, core],
                    parts.at[:, :, quarter, :, pl.ds(at, one_width)],
                    load.at[quarter, i],
                )
                item.start()
                loads.append(item)
                at += one_width
        greet(plane_neighbours() + x_peers + [other])
        swaps = []
        for quarter in range(4):
            at = 0
            for i, one_width in enumerate(widths):
                item = pltpu.make_async_remote_copy(
                    src_ref=ins[i].at[quarter, 1 - core],
                    dst_ref=twin.at[quarter, :, :, :, pl.ds(at, one_width)],
                    send_sem=core_send.at[quarter, i],
                    recv_sem=core_recv.at[quarter, i],
                    device_id=other,
                    device_id_type=MESH,
                )
                item.start()
                swaps.append(item)
                at += one_width
        for quarter in range(4):
            for i in range(len(widths)):
                loads[quarter * len(widths) + i].wait()
                swaps[quarter * len(widths) + i].wait_recv()

            def add(at, carry):
                z, y = at // SIDE, at % SIDE
                parts[z, y, quarter] = parts[z, y, quarter] + twin[quarter, z, y]
                return carry

            lax.fori_loop(0, SIDE * SIDE, add, 0)

        def store(low, total):
            mine[pl.ds(low, 2)] = total.astype(mine.dtype)

        plane = plane_reduce(parts, far, near, far_last, near_last, send, recv, store)
        advance(plane)
        advance(plane)
        advance(ring)
        advance(plane)
        advance(ring)
        advance(plane)
        advance(ring)
        advance(plane)
        finish(ring)
        finish(plane)
        sends = []
        for i, step in enumerate((1, 3, 2)):
            item = pltpu.make_async_remote_copy(
                src_ref=mine.at[(x + step) % SIDE],
                dst_ref=from_x.at[i],
                send_sem=x_send.at[i],
                recv_sem=x_recv.at[i],
                device_id=x_peers[i],
                device_id_type=MESH,
            )
            item.start()
            sends.append(item)
        total = mine[x].astype(jnp.float32)
        for i in range(3):
            sends[i].wait_recv()
            total = total + from_x[i].astype(jnp.float32)
        qkv_ref[...] = by_kind(total[:, : widths[0]])
        out_ref[...] = total[:, widths[0] : widths[0] + widths[1]]
        small_ref[...] = total[:, widths[0] + widths[1] :]
        for item in sends + swaps:
            item.wait_send()

    unit = (rows, width)
    pairs = (4, len(widths))
    vmem = pl.BlockSpec(memory_space=pltpu.VMEM)
    return pl.pallas_call(
        kernel,
        out_shape=tuple(
            [jax.ShapeDtypeStruct((rows, one_width), jnp.float32) for one_width in widths]
            + [jax.ShapeDtypeStruct((2,) + share[3:], jnp.float32) for share in shares]
        ),
        in_specs=[pl.BlockSpec(memory_space=pl.ANY)] * (len(widths) + kinds),
        out_specs=(vmem,) * (len(widths) + kinds),
        scratch_shapes=reduce_scratch(rows, width)
        + [
            pltpu.VMEM((4, SIDE, SIDE) + unit, jnp.bfloat16),
            pltpu.VMEM((4,) + unit, jnp.bfloat16),
            pltpu.VMEM((3,) + unit, jnp.bfloat16),
            pltpu.SemaphoreType.DMA(pairs),
            pltpu.SemaphoreType.DMA(pairs),
            pltpu.SemaphoreType.DMA(pairs),
            pltpu.SemaphoreType.DMA((3,)),
            pltpu.SemaphoreType.DMA((3,)),
        ]
        + ring_reduce_scratch(experts),
        compiler_params=comm_params(number),
        name="weights_reduce",
    )(
        *[piece.reshape(4, 2, SIDE, SIDE, rows, piece.shape[1]) for piece in pieces],
        *[expert.reshape(share) for expert, share in zip(experts, shares)],
    )


def rms_scale(values):
    return lax.rsqrt(jnp.mean(values * values, axis=-1, keepdims=True) + epsilon)


def rope_tables(length):
    half_dim = HEAD_DIM // 2
    frequency = np.float32(rope_theta) ** (
        -np.arange(half_dim, dtype=np.float32) / np.float32(half_dim)
    )
    angles = np.arange(length, dtype=np.float32)[:, None] * frequency[None, :].astype(np.float32)
    cosine = np.cos(angles.astype(np.float64)).astype(np.float32)
    sine = np.sin(angles.astype(np.float64)).astype(np.float32)
    one_cos = np.concatenate([cosine, cosine], axis=1)
    one_sin = np.concatenate([-sine, sine], axis=1)
    flat = np.ones_like(one_cos)
    return (
        np.concatenate([one_cos, one_cos, one_cos, flat], axis=1),
        np.concatenate([one_sin, one_sin, one_sin, 0.0 * flat], axis=1),
    )


def turn(values, cosine, sine):
    half_dim = HEAD_DIM // 2
    width = values.shape[1]
    lane = lax.broadcasted_iota(jnp.int32, values.shape, 1)
    ahead = pltpu.roll(values, width - half_dim, 1)
    behind = pltpu.roll(values, half_dim, 1)
    return values * cosine + jnp.where(lane % HEAD_DIM < half_dim, ahead, behind) * sine


SEQ_STEPS = (4, 5, 3, 2, 6, 1, 7)


def seq_exchange(source, target, send, recv):
    me = lax.axis_index("seq")
    count = 8

    def copy(step, peer, out_of, into):
        return pltpu.make_async_remote_copy(
            src_ref=out_of,
            dst_ref=into,
            send_sem=send.at[step - 1],
            recv_sem=recv.at[step - 1],
            device_id={"seq": peer},
            device_id_type=MESH,
        )

    def start(steps):
        items = []
        for step in steps:
            peer = (me + step) % count
            item = copy(step, peer, source(peer), target(me))
            item.start()
            items.append(item)
        return items

    def wait(step):
        peer = (me + count - step) % count
        copy(step, peer, target(peer), target(peer)).wait_recv()

    return (start, wait)


def seq_plane_greet():
    me = lax.axis_index("seq")
    greet(plane_neighbours() + [{"seq": (me + step) % 8} for step in range(1, 8)])


def twice(pair, lane):
    swapped = pltpu.roll(pair.astype(jnp.float32), HEAD_DIM, 1).astype(pair.dtype)
    return (
        jnp.where(lane < HEAD_DIM, pair, swapped),
        jnp.where(lane < HEAD_DIM, swapped, pair),
    )


def apart(pair, lane):
    zero = jnp.zeros_like(pair)
    return jnp.concatenate(
        [jnp.where(lane < HEAD_DIM, pair, zero), jnp.where(lane < HEAD_DIM, zero, pair)], axis=0
    )


def matmul(a, b, dims):
    return lax.dot_general(a, b, (dims, ((), ())), preferred_element_type=jnp.float32)


BLOCK = 256


def block_probs(queries, keys, at):
    scores = matmul(queries, keys, ((1,), (1,)))
    row = lax.broadcasted_iota(jnp.int32, scores.shape, 0) % BLOCK + at * BLOCK
    column = lax.broadcasted_iota(jnp.int32, scores.shape, 1)
    scores = jnp.where(column <= row, scores, -1e30)
    exponent = jnp.exp(scores - jnp.max(scores, axis=1, keepdims=True))
    return exponent * (1.0 / jnp.sum(exponent, axis=1, keepdims=True))


def attention_forward(normed, weights, width, cosine, sine, beside, expert, number):
    tok, depth = normed.shape
    features = beside.shape[1]
    seq_parts = 8
    group = width // seq_parts
    pair = 2 * HEAD_DIM
    length = tok * seq_parts
    per_block = BLOCK // tok

    def kernel(
        normed_ref, weights_ref, cos_hbm, sin_hbm, beside_ref, expert_ref,
        out_ref, heads_ref, all_ref, expert_all,
        packed, mixed, proj_w, cos_ref, sin_ref,
        send, recv, o_send, o_recv, p_send, p_recv, local_sem, load,
        ring_send, ring_recv, swap_send, swap_recv, ring_local,
    ):
        me = lax.axis_index("seq")
        here = pl.ds(pl.multiple_of(me * tok, tok), tok)
        loads = [
            pltpu.make_async_copy(weights_ref.at[:, pl.ds(0, width)], proj_w, load.at[0]),
            pltpu.make_async_copy(cos_hbm.at[here], cos_ref, load.at[1]),
            pltpu.make_async_copy(sin_hbm.at[here], sin_ref, load.at[2]),
        ]
        for item in loads:
            item.start()
        z, y = plane_place("y", 0, 0)
        keep = pltpu.make_async_copy(beside_ref, all_ref.at[z, y], local_sem)
        keep.start()
        seq_plane_greet()
        steps = plane_gather(
            lambda low, count: beside_ref.at[pl.ds(low, count)],
            lambda z, y, low, count: all_ref.at[z, y, pl.ds(low, count)],
            p_send,
            p_recv,
            nothing,
        )
        advance(steps)
        for item in loads:
            item.wait()
        for d in range(seq_parts):
            projected = matmul(
                normed_ref[...], proj_w[:, d * group : (d + 1) * group], ((1,), (0,))
            )
            packed[d] = turn(projected, cos_ref[...], sin_ref[...]).astype(packed.dtype)
        start, wait = seq_exchange(
            lambda d: packed.at[d], lambda d: heads_ref.at[d], send, recv
        )
        items = start(SEQ_STEPS)
        heads_ref[me] = packed[me]
        advance(steps)
        for step in SEQ_STEPS:
            wait(step)
        ring = ring_gather(
            [expert_ref], [expert_all], ring_send, ring_recv, swap_send, swap_recv, ring_local
        )
        advance(ring)
        advance(steps)
        lane = lax.broadcasted_iota(jnp.int32, (length, pair), 1)
        heads = heads_ref[...].reshape(length, group)
        keys, values = twice(heads[:, pair:], lane)
        lane_block = lane[:BLOCK]
        back, back_wait = seq_exchange(
            lambda d: mixed.at[d],
            lambda d: out_ref.at[:, pl.ds(pl.multiple_of(d * pair, pair), pair)],
            o_send,
            o_recv,
        )
        for at in range(length // BLOCK):
            block = heads[at * BLOCK : (at + 1) * BLOCK, :pair]
            queries = apart(block * jnp.asarray(attention_multiplier, block.dtype), lane_block)
            upto = (at + 1) * BLOCK
            probs = block_probs(queries, keys[:upto], at).astype(jnp.bfloat16)
            both = matmul(probs, values[:upto], ((1,), (0,)))
            made = jnp.where(lane_block < HEAD_DIM, both[:BLOCK], both[BLOCK:]).astype(mixed.dtype)
            mixed[at * per_block : (at + 1) * per_block] = made.reshape(per_block, tok, pair)
            if at % 2:
                advance(steps)
        items += back(SEQ_STEPS)
        advance(ring)
        out_ref[:, pl.ds(pl.multiple_of(me * pair, pair), pair)] = mixed[me]
        advance(steps)
        for step in SEQ_STEPS:
            back_wait(step)
        finish(steps)
        finish(ring)
        keep.wait()
        for item in items:
            item.wait_send()

    vmem = pl.BlockSpec(memory_space=pltpu.VMEM)
    anywhere = pl.BlockSpec(memory_space=pl.ANY)
    attended, heads, gathered, expert_full = pl.pallas_call(
        kernel,
        out_shape=(
            jax.ShapeDtypeStruct((tok, seq_parts * pair), jnp.bfloat16),
            jax.ShapeDtypeStruct((seq_parts, tok, group), jnp.bfloat16),
            jax.ShapeDtypeStruct((SIDE, SIDE, 4, tok // 4, features), beside.dtype),
            jax.ShapeDtypeStruct((2, 4, 2) + expert.shape[1:], expert.dtype),
        ),
        in_specs=[vmem] + [anywhere] * 5,
        out_specs=(vmem, vmem, anywhere, anywhere),
        scratch_shapes=[
            pltpu.VMEM((seq_parts, tok, group), jnp.bfloat16),
            pltpu.VMEM((seq_parts, tok, pair), jnp.bfloat16),
            pltpu.VMEM((depth, width), jnp.bfloat16),
            pltpu.VMEM((tok, group), jnp.float32),
            pltpu.VMEM((tok, group), jnp.float32),
        ]
        + [pltpu.SemaphoreType.DMA((7,))] * 4
        + [pltpu.SemaphoreType.DMA((2, 20))] * 2
        + [pltpu.SemaphoreType.DMA, pltpu.SemaphoreType.DMA((3,))]
        + [pltpu.SemaphoreType.DMA((1, 4))] * 4
        + [pltpu.SemaphoreType.DMA((1,))],
        compiler_params=comm_params(number),
        name="attention_forward",
    )(normed, weights, cosine, sine, beside.reshape(4, tok // 4, features), expert)
    return (
        attended,
        heads,
        gathered.reshape(SIDE * SIDE, tok, features),
        expert_full.reshape(2, 8 * expert.shape[1], expert.shape[2]),
    )


def attention_backward(grad_attended, heads_in, cosine, sine, beside, experts, number):
    kinds = len(experts)
    shares = expert_shares_of(experts)
    seq_parts, tok, group = heads_in.shape
    features = beside.shape[2]
    pair = 2 * HEAD_DIM
    length = tok * seq_parts
    per_block = BLOCK // tok

    def kernel(*refs):
        refs = list(refs)
        take = lambda count: [refs.pop(0) for _ in range(count)]
        grad_ref, heads_ref, cos_ref, sin_ref, beside_ref = take(5)
        ex_ins = take(kinds)
        out_ref, sum_ref = take(2)
        ex_outs = take(kinds)
        came, packed, d_queries, d_keys, d_values, send, recv, o_send, o_recv = take(9)
        parts, far, near, far_last, near_last, p_send, p_recv, load = take(8)
        ring = ring_reduce(ex_ins, ex_outs, refs)
        me = lax.axis_index("seq")
        loaded = pltpu.make_async_copy(beside_ref, parts, load)
        loaded.start()
        seq_plane_greet()

        def store(low, total):
            sum_ref[pl.ds(low, 2)] = total

        steps = plane_reduce(parts, far, near, far_last, near_last, p_send, p_recv, store)
        columns = lambda d: grad_ref.at[:, pl.ds(pl.multiple_of(d * pair, pair), pair)]
        start, wait = seq_exchange(columns, lambda d: came.at[d], send, recv)
        items = start(SEQ_STEPS)
        loaded.wait()
        advance(steps)
        advance(steps)
        advance(ring)
        came[me] = grad_ref[:, pl.ds(pl.multiple_of(me * pair, pair), pair)]
        lane = lax.broadcasted_iota(jnp.int32, (length, pair), 1)
        lane_block = lane[:BLOCK]
        heads = heads_ref[...].reshape(length, group)
        keys, values = twice(heads[:, pair:], lane)
        for step in SEQ_STEPS:
            wait(step)
        for at in range(length // BLOCK):
            if at == 1:
                advance(ring)
            if at == 3:
                advance(ring)
            upto = (at + 1) * BLOCK
            block = heads[at * BLOCK : upto, :pair]
            queries = apart(block * jnp.asarray(attention_multiplier, block.dtype), lane_block)
            grads = apart(
                came[at * per_block : (at + 1) * per_block].reshape(BLOCK, pair), lane_block
            )
            probs = block_probs(queries, keys[:upto], at)
            d_probs = matmul(grads, values[:upto], ((1,), (1,)))
            center = jnp.sum(probs * d_probs, axis=1, keepdims=True)
            d_scores = (probs * (d_probs - center)).astype(jnp.bfloat16)
            both = matmul(d_scores, keys[:upto], ((1,), (0,))) * attention_multiplier
            d_queries[at * BLOCK : upto] = jnp.where(
                lane_block < HEAD_DIM, both[:BLOCK], both[BLOCK:]
            )
            more_keys = matmul(d_scores, queries, ((0,), (0,)))
            more_values = matmul(probs.astype(jnp.bfloat16), grads, ((0,), (0,)))
            before = at * BLOCK
            if at:
                d_keys[:before] += more_keys[:before]
                d_values[:before] += more_values[:before]
            d_keys[before:upto] = more_keys[before:]
            d_values[before:upto] = more_values[before:]
            if at in (1, 3):
                advance(steps)
        sum_keys = d_keys[...] + pltpu.roll(d_keys[...], HEAD_DIM, 1)
        sum_values = d_values[...] + pltpu.roll(d_values[...], HEAD_DIM, 1)
        rest = jnp.where(lane < HEAD_DIM, sum_keys, sum_values)
        whole = jnp.concatenate([d_queries[...], rest], axis=1)
        packed[...] = (
            turn(whole, cos_ref[...], -sin_ref[...])
            .astype(packed.dtype)
            .reshape(seq_parts, tok, group)
        )
        back, back_wait = seq_exchange(
            lambda d: packed.at[d],
            lambda d: out_ref.at[:, pl.ds(pl.multiple_of(d * group, group), group)],
            o_send,
            o_recv,
        )
        items += back(SEQ_STEPS)
        out_ref[:, pl.ds(pl.multiple_of(me * group, group), group)] = packed[me]
        advance(steps)
        for step in SEQ_STEPS:
            back_wait(step)
        finish(ring)
        finish(steps)
        for item in items:
            item.wait_send()

    vmem = pl.BlockSpec(memory_space=pltpu.VMEM)
    outs = pl.pallas_call(
        kernel,
        out_shape=(
            jax.ShapeDtypeStruct((tok, seq_parts * group), jnp.bfloat16),
            jax.ShapeDtypeStruct((4, tok // 4, features), jnp.float32),
        )
        + tuple(jax.ShapeDtypeStruct((2,) + share[3:], jnp.float32) for share in shares),
        in_specs=[vmem] * 4 + [pl.BlockSpec(memory_space=pl.ANY)] * (1 + kinds),
        out_specs=(vmem,) * (2 + kinds),
        scratch_shapes=[
            pltpu.VMEM((seq_parts, tok, pair), jnp.bfloat16),
            pltpu.VMEM((seq_parts, tok, group), jnp.bfloat16),
            pltpu.VMEM((length, pair), jnp.float32),
            pltpu.VMEM((length, pair), jnp.float32),
            pltpu.VMEM((length, pair), jnp.float32),
        ]
        + [pltpu.SemaphoreType.DMA((7,))] * 4
        + reduce_scratch(tok // 4, features)
        + [pltpu.SemaphoreType.DMA]
        + ring_reduce_scratch(experts),
        compiler_params=comm_params(number),
        name="attention_backward",
    )(
        grad_attended,
        heads_in,
        cosine,
        sine,
        beside.reshape(SIDE, SIDE, 4, tok // 4, features),
        *[expert.reshape(share) for expert, share in zip(experts, shares)],
    )
    return (outs[0], outs[1].reshape(tok, features)) + tuple(outs[2:])


def gate_columns(logits, chosen_ids, experts_all):
    named = jnp.any(
        chosen_ids[..., None] == jnp.arange(experts_all, dtype=jnp.int32), axis=-2
    )
    peak = jnp.max(jnp.where(named, logits, -jnp.inf), axis=-1, keepdims=True)
    exponent = jnp.where(named, jnp.exp(logits - peak), 0.0)
    gates = exponent / jnp.sum(exponent, axis=-1, keepdims=True)
    coarse = lax.reduce_precision(gates, 8, 7)
    columns = jnp.concatenate(
        [named.astype(jnp.float32), coarse, gates - coarse, jnp.zeros_like(gates)], axis=-1
    ).astype(jnp.bfloat16)
    return (gates, columns)


def near_place(at):
    if isinstance(at, int) and at >= 9:
        return far_place(at)
    return (at // 3 - 1, at % 3 - 1)


def far_place(at):
    beyond = at - 9
    turn_over = beyond // 4
    return (
        2 * (1 - turn_over) + turn_over * (beyond - 5),
        (1 - turn_over) * (beyond - 1) + turn_over * 2,
    )


def expert_layer(
    tokens_own, cot_all, gate_full, up_full, down_full, experts_all, capacity, number
):
    tok, wide = tokens_own.shape
    sources = SIDE * SIDE
    quarter = tok // 4
    features = wide - 128
    hidden_units = gate_full.shape[2]
    group = 8
    chunks = sources // group
    chunk_rows = group * capacity
    f32, b16 = jnp.float32, jnp.bfloat16

    def kernel(
        tok_hbm, cot_hbm, gate_hbm, up_hbm, down_hbm,
        mix_hbm, back_ref, ggate_hbm, gup_hbm, gdown_hbm,
        tok_v, cot_v, gate_v, up_v, down_v, mix_v, grad_v,
        x_v, deo_v, slope_v, act_v, inner_v, pick_t, share_v, dgate_v,
        in_sem, out_sem, g_send, g_recv,
        rows_v, far, near, far_last, near_last, r_send, r_recv,
    ):
        first = lax.axis_index("wshard") * 2
        home_z, home_y = plane_place("y", 0, 0)
        loads = [
            pltpu.make_async_copy(source, target, in_sem.at[i])
            for i, (source, target) in enumerate(
                [(tok_hbm, tok_v.at[home_z, home_y]), (cot_hbm, cot_v), (gate_hbm, gate_v), (up_hbm, up_v),
                 (down_hbm, down_v)]
            )
        ]
        for item in loads:
            item.start()
        lane = lax.broadcasted_iota(jnp.int32, (tok, 128), 1)
        down_rows = lax.broadcasted_iota(jnp.int32, (tok, 128), 0)
        lower = jnp.where(down_rows >= lane, 1.0, 0.0).astype(b16)
        greet(plane_neighbours())
        gather = plane_gather(
            lambda low, count: tok_hbm.at[pl.ds(low, count)],
            lambda z, y, low, count: tok_v.at[z, y, pl.ds(low, count)],
            g_send,
            g_recv,
            nothing,
        )
        advance(gather)
        advance(gather)
        advance(gather)
        advance(gather)
        advance(gather)
        loads[0].wait()
        loads[1].wait()

        def prepare(s, place_of):
            off_z, off_y = place_of(s)
            z, y = plane_place("y", off_y, off_z)
            info = tok_v[z, y, :, :, pl.ds(features, 128)].reshape(tok, 128)
            info32 = info.astype(f32)
            place = matmul(lower, info, ((1,), (0,))) - 1.0
            place = jnp.where(info32 > 0.5, place, -1.0)
            place_rows = place.T
            info_rows = info32.T
            row_picks, col_places = [], []
            shares = []
            for e in (0, 1):
                at = first + e
                row = jnp.sum(jnp.where(down_rows == at, place_rows, 0.0), axis=0, keepdims=True)
                gate = jnp.sum(
                    jnp.where(
                        (down_rows == experts_all + at) | (down_rows == 2 * experts_all + at),
                        info_rows,
                        0.0,
                    ),
                    axis=0,
                    keepdims=True,
                )
                slot = lax.broadcasted_iota(jnp.int32, (capacity, tok), 0).astype(f32)
                hit = slot == row
                row_picks.append(jnp.where(hit, 1.0, 0.0))
                shares.append(jnp.sum(jnp.where(hit, gate, 0.0), axis=1, keepdims=True))
                col_places.append(
                    jnp.sum(jnp.where(lane == at, place, 0.0), axis=1, keepdims=True)
                )
            pick = jnp.concatenate(row_picks, axis=0).astype(b16)
            lane_f = lane.astype(f32)
            pick_t[s] = (
                jnp.where(lane_f == col_places[0], 1.0, 0.0) * jnp.where(lane < capacity, 1.0, 0.0)
                + jnp.where(lane_f - float(capacity) == col_places[1], 1.0, 0.0)
                * jnp.where(lane >= capacity, 1.0, 0.0)
            ).astype(b16)
            share_v[s] = jnp.concatenate(shares, axis=0)
            rows = matmul(
                pick, tok_v[z, y, :, :, pl.ds(0, features)].reshape(tok, features), ((1,), (0,))
            ).astype(b16)
            c, i = s // group, s % group
            x_v[0, c, i] = rows[:capacity]
            x_v[1, c, i] = rows[capacity:]
            cots = matmul(pick, cot_v[z, y], ((1,), (0,))).astype(b16)
            deo_v[0, c, i] = cots[:capacity]
            deo_v[1, c, i] = cots[capacity:]

        def prepare_all(low, high, place_of):
            def step(s, carry):
                prepare(s, place_of)
                return carry

            lax.fori_loop(low, high, step, 0)

        def forward(c):
            weighted = []
            for e in (0, 1):
                x = x_v[e, c].reshape(chunk_rows, features)
                gate_val = matmul(x, gate_v[e], ((1,), (0,)))
                up_val = matmul(x, up_v[e], ((1,), (0,)))
                sigma = 1.0 / (1.0 + jnp.exp(-gate_val))
                act = gate_val * sigma
                inner = (act * up_val).astype(b16)
                inner_v[e, c] = inner
                act_v[e, c] = act.astype(b16)
                slope_v[e, c] = (up_val * (sigma * (1.0 + gate_val * (1.0 - sigma)))).astype(b16)
                made = matmul(inner, down_v[e], ((1,), (0,))).astype(b16).astype(f32)
                share = jnp.concatenate(
                    [share_v[c * group + i, pl.ds(e * capacity, capacity)] for i in range(group)],
                    axis=0,
                )
                mix_grad = residual_multiplier * deo_v[e, c].reshape(chunk_rows, features).astype(f32)
                dgate_v[e, c] = jnp.sum(made * mix_grad, axis=1, keepdims=True)
                deo_v[e, c] = (share * mix_grad).astype(b16).reshape(group, capacity, features)
                weighted.append((share * made).astype(b16))
            for i in range(group):
                both = jnp.concatenate(
                    [w[i * capacity : (i + 1) * capacity] for w in weighted], axis=0
                )
                off_z, off_y = near_place(c * group + i)
                z, y = plane_place("y", off_y, off_z)
                mix_v[z, y] = matmul(pick_t[c * group + i], both, ((1,), (0,))).astype(b16)

        prepare_all(0, 9, near_place)
        advance(gather)
        for item in loads[2:]:
            item.wait()
        forward(0)
        finish(gather)
        prepare_all(9, sources, far_place)
        forward(1)
        stores = [pltpu.make_async_copy(mix_v, mix_hbm, out_sem.at[0])]
        stores[0].start()
        lane_rows = lax.broadcasted_iota(jnp.int32, (chunk_rows, 128), 1)

        def backward(c):
            made = []
            for e in (0, 1):
                deo = deo_v[e, c].reshape(chunk_rows, features)
                d_inner = matmul(deo, down_v[e], ((1,), (1,)))
                d_gate = (d_inner * slope_v[e, c].astype(f32)).astype(b16)
                d_up = (d_inner * act_v[e, c].astype(f32)).astype(b16)
                slope_v[e, c] = d_gate
                act_v[e, c] = d_up
                d_rows = (
                    matmul(d_gate, gate_v[e], ((1,), (1,))) + matmul(d_up, up_v[e], ((1,), (1,)))
                ).astype(b16)
                coarse = dgate_v[e, c].astype(b16).astype(f32)
                fine = dgate_v[e, c] - coarse
                columns = jnp.where(lane_rows == first + e, coarse, 0.0) + jnp.where(
                    lane_rows == experts_all + first + e, fine, 0.0
                )
                made.append(jnp.concatenate([d_rows, columns.astype(b16)], axis=1))
            for i in range(group):
                both = jnp.concatenate(
                    [m[i * capacity : (i + 1) * capacity] for m in made], axis=0
                )
                off_z, off_y = near_place(c * group + i)
                z, y = plane_place("y", off_y, off_z)
                rows_v[z, y] = (
                    matmul(pick_t[c * group + i], both, ((1,), (0,)))
                    .astype(b16)
                    .reshape(4, quarter, wide)
                )

        def store(low, total):
            back_ref[pl.ds(low, 2)] = total

        reduce = plane_reduce(
            rows_v, far, near, far_last, near_last, r_send, r_recv, store
        )
        backward(1)
        advance(reduce)
        backward(0)
        advance(reduce)
        rows_all = chunks * chunk_rows

        def whole(ref, e, columns):
            return ref[e].reshape(rows_all, columns)

        for e in (0, 1):
            x = whole(x_v, e, features)
            for i, source, target in (
                (e, slope_v, ggate_hbm),
                (2 + e, act_v, gup_hbm),
            ):
                grad_v[i] = matmul(x, whole(source, e, hidden_units), ((0,), (0,))).astype(b16)
                stores.append(
                    pltpu.make_async_copy(grad_v.at[i], target.at[e], out_sem.at[1 + i])
                )
                stores[-1].start()
            advance(reduce)
        for e in (0, 1):
            grad = matmul(
                whole(inner_v, e, hidden_units), whole(deo_v, e, features), ((0,), (0,))
            ).astype(b16)
            cot_v[e] = grad.reshape(4, 128, features)
            stores.append(
                pltpu.make_async_copy(cot_v.at[e], gdown_hbm.at[e], out_sem.at[5 + e])
            )
            stores[-1].start()
            if e == 0:
                advance(reduce)
        finish(reduce)
        for item in stores:
            item.wait()

    anywhere = pl.BlockSpec(memory_space=pl.ANY)
    local = gate_full.shape[0]
    outs = pl.pallas_call(
        kernel,
        out_shape=(
            jax.ShapeDtypeStruct((SIDE, SIDE, tok, features), b16),
            jax.ShapeDtypeStruct((4, quarter, wide), f32),
            jax.ShapeDtypeStruct((local, features, hidden_units), b16),
            jax.ShapeDtypeStruct((local, features, hidden_units), b16),
            jax.ShapeDtypeStruct((local, 4, hidden_units // 4, features), b16),
        ),
        in_specs=[anywhere] * 5,
        out_specs=(anywhere, pl.BlockSpec(memory_space=pltpu.VMEM)) + (anywhere,) * 3,
        scratch_shapes=[
            pltpu.VMEM((SIDE, SIDE, 4, quarter, wide), b16),
            pltpu.VMEM((SIDE, SIDE, tok, features), b16),
            pltpu.VMEM(gate_full.shape, b16),
            pltpu.VMEM(up_full.shape, b16),
            pltpu.VMEM(down_full.shape, b16),
            pltpu.VMEM((SIDE, SIDE, tok, features), b16),
            pltpu.VMEM((4, features, hidden_units), b16),
            pltpu.VMEM((2, chunks, group, capacity, features), b16),
            pltpu.VMEM((2, chunks, group, capacity, features), b16),
            pltpu.VMEM((2, chunks, chunk_rows, hidden_units), b16),
            pltpu.VMEM((2, chunks, chunk_rows, hidden_units), b16),
            pltpu.VMEM((2, chunks, chunk_rows, hidden_units), b16),
            pltpu.VMEM((sources, tok, 2 * capacity), b16),
            pltpu.VMEM((sources, 2 * capacity, 1), f32),
            pltpu.VMEM((2, chunks, chunk_rows, 1), f32),
            pltpu.SemaphoreType.DMA((5,)),
            pltpu.SemaphoreType.DMA((7,)),
            pltpu.SemaphoreType.DMA((2, 20)),
            pltpu.SemaphoreType.DMA((2, 20)),
        ]
        + reduce_scratch(quarter, wide),
        compiler_params=comm_params(number),
        name="expert_layer",
    )(
        tokens_own.reshape(4, quarter, wide),
        cot_all.reshape(SIDE, SIDE, tok, features),
        gate_full,
        up_full,
        down_full,
    )
    return (
        outs[0].reshape(sources, tok, features),
        outs[1].reshape(tok, wide),
        outs[2],
        outs[3],
        outs[4].reshape(local, hidden_units, features),
    )


def norm_backward(grad_normed, values, scale, gain_full):
    grad_gain = jnp.sum(grad_normed * values * scale, axis=0)
    grad_hat = grad_normed * gain_full
    grad_values = scale * grad_hat - values * (scale * scale * scale) * jnp.mean(
        grad_hat * values, axis=1, keepdims=True
    )
    return (grad_values, grad_gain)


def local(
    tokens,
    weight_qkv,
    weight_out,
    router,
    gain_attn,
    gain_ffn,
    expert_gate,
    expert_up,
    expert_down,
    expert_ids,
    cotangent,
):
    tok_dev = tokens.shape[1]
    features = tokens.shape[2]
    seq_parts = lax.axis_size("seq")
    owners = lax.axis_size("wshard")
    local_experts = expert_gate.shape[0]
    experts_all = local_experts * owners
    top_count = expert_ids.shape[2]
    capacity = 2 * tok_dev * top_count // experts_all
    heads_dev = HEADS // seq_parts
    key_heads = KV_HEADS // seq_parts
    query_cols = heads_dev * HEAD_DIM
    key_cols = key_heads * HEAD_DIM
    query_width = HEADS * HEAD_DIM
    key_width = KV_HEADS * HEAD_DIM
    length = tok_dev * seq_parts
    qkv_width = weight_qkv.shape[1]
    smalls = jnp.concatenate(
        [
            router,
            gain_attn[:, None],
            gain_ffn[:, None],
            jnp.zeros((router.shape[0], 128 - experts_all - 2), jnp.bfloat16),
        ],
        axis=1,
    )
    weights_full, gate_full, up_full = weights_gather(
        weight_qkv, [weight_out, smalls], [expert_gate, expert_up], 0
    )
    qkv_full = weights_full[:, :qkv_width]
    out_full = weights_full[:, qkv_width : qkv_width + features]
    smalls_full = weights_full[:, qkv_width + features :]
    router_full = smalls_full[:, :experts_all]
    gain_one = smalls_full[:, experts_all].astype(jnp.float32)
    gain_two = smalls_full[:, experts_all + 1].astype(jnp.float32)
    inputs = tokens[0].astype(jnp.float32)
    chosen_ids = expert_ids[0]
    scale_one = rms_scale(inputs)
    normed_one = (inputs * scale_one * gain_one).astype(jnp.bfloat16)
    cosine, sine = (jnp.asarray(table) for table in rope_tables(length))
    attended, heads_all, cot_all, down_full = attention_forward(
        normed_one, weights_full, qkv_width, cosine, sine, cotangent[0], expert_down, 5
    )
    branch = jnp.dot(attended, out_full, preferred_element_type=jnp.float32)
    hidden = inputs + residual_multiplier * branch
    scale_two = rms_scale(hidden)
    normed_two = (hidden * scale_two * gain_two).astype(jnp.bfloat16)
    logits = jnp.dot(normed_two, router_full, preferred_element_type=jnp.float32)
    gates_own, gate_info = gate_columns(logits, chosen_ids, experts_all)
    mix_part, back, grad_gate, grad_up, grad_down = expert_layer(
        jnp.concatenate([normed_two, gate_info], axis=1),
        cot_all,
        gate_full,
        up_full,
        down_full,
        experts_all,
        capacity,
        1,
    )
    grad_output = cotangent[0].astype(jnp.float32)
    grad_back = back[:, :features]
    grad_gates = (
        back[:, features : features + experts_all]
        + back[:, features + experts_all : features + 2 * experts_all]
    )
    grad_logits = (
        gates_own
        * (grad_gates - jnp.sum(gates_own * grad_gates, axis=1, keepdims=True))
    ).astype(jnp.bfloat16)
    grad_normed_two = jnp.dot(grad_logits, router_full.T, preferred_element_type=jnp.float32)
    grad_normed_two = grad_normed_two + grad_back
    grad_hidden_norm, grad_gain_ffn = norm_backward(grad_normed_two, hidden, scale_two, gain_two)
    grad_hidden = grad_output + grad_hidden_norm
    grad_branch = (residual_multiplier * grad_hidden).astype(jnp.bfloat16)
    grad_out = jnp.dot(attended.T, grad_branch, preferred_element_type=jnp.float32)
    grad_attended = jnp.dot(grad_branch, out_full.T, preferred_element_type=jnp.float32).astype(
        jnp.bfloat16
    )
    grad_proj, mixture, own_gate, own_up = attention_backward(
        grad_attended, heads_all, cosine, sine, mix_part, [grad_gate, grad_up], 6
    )
    output = hidden + residual_multiplier * mixture
    grad_qkv = jnp.dot(normed_one.T, grad_proj, preferred_element_type=jnp.float32)
    grad_normed_one = jnp.dot(grad_proj, qkv_full.T, preferred_element_type=jnp.float32)
    grad_input_norm, grad_gain_attn = norm_backward(grad_normed_one, inputs, scale_one, gain_one)
    grad_input = grad_hidden + grad_input_norm
    column = jnp.arange(128, dtype=jnp.int32)[None, :]
    grad_smalls = (
        jnp.dot(
            normed_two.T,
            jnp.pad(grad_logits, ((0, 0), (0, 128 - experts_all))),
            preferred_element_type=jnp.float32,
        )
        + jnp.where(column == experts_all, grad_gain_attn[:, None], 0.0)
        + jnp.where(column == experts_all + 1, grad_gain_ffn[:, None], 0.0)
    ).astype(jnp.bfloat16)
    own_qkv, own_out, own_smalls, own_down = weights_reduce(
        [grad_qkv.astype(jnp.bfloat16), grad_out.astype(jnp.bfloat16), grad_smalls],
        [grad_down],
        4,
    )
    shares = (
        own_qkv,
        own_out,
        own_smalls[:, :experts_all],
        own_smalls[:, experts_all],
        own_smalls[:, experts_all + 1],
    )
    expert_shares = (own_gate, own_up, own_down)
    return (
        output.astype(jnp.bfloat16)[None],
        grad_input.astype(jnp.bfloat16)[None],
        shares[0],
        shares[1],
        shares[2],
        shares[3],
        shares[4],
        expert_shares[0],
        expert_shares[1],
        expert_shares[2],
    )


def solution(mesh):
    placed = (
        P("wshard", "seq", None),
        P(("seq", "wshard"), None),
        P(("seq", "wshard"), None),
        P(("seq", "wshard"), None),
        P(("seq", "wshard")),
        P(("seq", "wshard")),
        P("wshard", "seq", None),
        P("wshard", "seq", None),
        P("wshard", "seq", None),
        P("wshard", "seq", None),
        P("wshard", "seq", None),
    )
    return jax.shard_map(
        local,
        mesh=mesh,
        in_specs=placed,
        out_specs=(
            P("wshard", "seq", None),
            P("wshard", "seq", None),
            P(("seq", "wshard"), None),
            P(("seq", "wshard"), None),
            P(("seq", "wshard"), None),
            P(("seq", "wshard")),
            P(("seq", "wshard")),
            P("wshard", "seq", None),
            P("wshard", "seq", None),
            P("wshard", "seq", None),
        ),
        check_vma=False,
    )
```

```python
import jax
import jax.numpy as jnp
import numpy as np
from jax import lax
from jax.experimental import pallas as pl
from jax.experimental.pallas import tpu as pltpu
from jax.sharding import PartitionSpec as P

HEADS = 16
KV_HEADS = 8
HEAD_DIM = 64


epsilon = 1e-06
attention_multiplier = 0.015625
residual_multiplier = 0.22
rope_theta = 10000.0


MESH = pl.DeviceIdType.MESH
SIDE = 4


def plane_place(first, offset_first, offset_second):
    mine = lax.axis_index("wshard")
    z, y = mine // SIDE, mine % SIDE
    if first == "y":
        return ((z + offset_second + SIDE) % SIDE, (y + offset_first + SIDE) % SIDE)
    return ((z + offset_first + SIDE) % SIDE, (y + offset_second + SIDE) % SIDE)


def plane_peer(first, offset_first, offset_second):
    z, y = plane_place(first, offset_first, offset_second)
    return {"wshard": z * SIDE + y}


def plane_neighbours():
    return [plane_peer("y", step, 0) for step in (1, -1)] + [
        plane_peer("y", 0, step) for step in (1, -1)
    ]


def seq_peer(offset_x, flip):
    mine = lax.axis_index("seq")
    x, core = mine // 2, mine % 2
    if flip:
        core = 1 - core
    return {"seq": ((x + offset_x) % SIDE) * 2 + core}


def greet(peers):
    barrier = pltpu.get_barrier_semaphore()
    for peer in peers:
        pl.semaphore_signal(barrier, inc=1, device_id=peer, device_id_type=MESH)
    pl.semaphore_wait(barrier, len(peers))


HALVES = (("y", 0), ("z", 2))
ORDER = (0, -1, 1, 2)


def plane_gather(own, view, send, recv, after_row):
    started = []

    def copy(half, kind, source, target, peer):
        return pltpu.make_async_remote_copy(
            src_ref=source,
            dst_ref=target,
            send_sem=send.at[half, kind],
            recv_sem=recv.at[half, kind],
            device_id=peer,
            device_id_type=MESH,
        )

    def push(half, kind, source, target, peer):
        item = copy(half, kind, source, target, peer)
        item.start()
        started.append(item)

    def arrived(half, kind, target):
        first, _ = HALVES[half]
        copy(half, kind, target, target, plane_peer(first, 1, 0)).wait_recv()

    def block(half, along_first, along_second, low, count):
        first, base = HALVES[half]
        z, y = plane_place(first, along_first, along_second)
        return view(z, y, base + low, count)

    def ring(half, slot, axis, along, source):
        first, base = HALVES[half]
        for kind, step in ((0, 1), (1, -1)):
            peer = plane_peer(first, step, 0) if axis == 0 else plane_peer(first, 0, step)
            push(half, 4 * slot + kind, source, block(half, along, 0, 0, 2), peer)

    def ring_relay(half, slot, axis, along):
        first, base = HALVES[half]
        for kind, step in ((0, 1), (1, -1)):
            where = (-step, 0) if axis == 0 else (along, -step)
            arrived(half, 4 * slot + kind, block(half, where[0], where[1], 0, 2))
            part = block(half, where[0], where[1], kind, 1)
            peer = plane_peer(first, step, 0) if axis == 0 else plane_peer(first, 0, step)
            push(half, 4 * slot + 2 + kind, part, part, peer)

    def ring_end(half, slot, axis, along):
        where = (2, 0) if axis == 0 else (along, 2)
        for kind in (0, 1):
            arrived(half, 4 * slot + 2 + kind, block(half, where[0], where[1], kind, 1))

    for half in (0, 1):
        ring(half, 0, 0, 0, own(HALVES[half][1], 2))
    for half in (0, 1):
        ring(half, 1, 1, 0, own(HALVES[half][1], 2))
    yield
    for half in (0, 1):
        ring_relay(half, 0, 0, 0)
        for slot in (1, 2):
            ring(half, 1 + slot, 1, ORDER[slot], block(half, ORDER[slot], 0, 0, 2))
    yield
    for half in (0, 1):
        ring_end(half, 0, 0, 0)
        ring(half, 4, 1, 2, block(half, 2, 0, 0, 2))
        after_row(half, 0)
    for slot in (0, 1, 2, 3):
        for half in (0, 1):
            ring_relay(half, 1 + slot, 1, ORDER[slot])
        yield
    for half in (0, 1):
        after_row(half, -1)
        after_row(half, 1)
    for half in (0, 1):
        for slot in (0, 1, 2, 3):
            ring_end(half, 1 + slot, 1, ORDER[slot])
        after_row(half, 2)
    for item in started:
        item.wait_send()


def plane_reduce(parts, far, near, far_last, near_last, send, recv, store):
    started = []

    def copy(half, kind, source, target, peer):
        return pltpu.make_async_remote_copy(
            src_ref=source,
            dst_ref=target,
            send_sem=send.at[half, kind],
            recv_sem=recv.at[half, kind],
            device_id=peer,
            device_id_type=MESH,
        )

    def push(half, kind, source, target, peer):
        item = copy(half, kind, source, target, peer)
        item.start()
        started.append(item)

    def arrived(half, kind, target):
        first, _ = HALVES[half]
        copy(half, kind, target, target, plane_peer(first, 1, 0)).wait_recv()

    def rows(half, offset, low, count):
        first, base = HALVES[half]
        z, y = plane_place(first, 0, offset)
        if first == "y":
            return parts.at[z, :, pl.ds(base + low, count)]
        return parts.at[:, y, pl.ds(base + low, count)]

    def one(half, offset, low, count):
        first, base = HALVES[half]
        z, y = plane_place(first, offset, 0)
        return parts.at[z, y, pl.ds(base + low, count)]

    def add(target, *others):
        if len(others) == 1:
            target[...] = target[...] + others[0][...]
            return
        total = target[...].astype(jnp.float32)
        for other in others:
            total = total + other[...].astype(jnp.float32)
        target[...] = total.astype(target.dtype)

    def add_rows(half, offset, low, count, *others):
        target = rows(half, offset, low, count)
        def step(at, carry):
            add(target.at[at], *[other.at[at] for other in others])
            return carry
        lax.fori_loop(0, SIDE, step, 0)

    def peer(half, axis, step):
        first, _ = HALVES[half]
        return plane_peer(first, 0, step) if axis == 1 else plane_peer(first, step, 0)

    for half in (0, 1):
        push(half, 0, rows(half, 2, 0, 1), far.at[half, 0], peer(half, 1, 1))
        push(half, 1, rows(half, 2, 1, 1), far.at[half, 1], peer(half, 1, -1))
    yield
    for half in (0, 1):
        push(half, 2, rows(half, 1, 1, 1), near.at[half, 0, :, pl.ds(1, 1)], peer(half, 1, 1))
        push(half, 3, rows(half, -1, 0, 1), near.at[half, 1, :, pl.ds(0, 1)], peer(half, 1, -1))
    yield
    for half in (0, 1):
        arrived(half, 0, far.at[half, 0])
        add_rows(half, 1, 0, 1, far.at[half, 0])
        push(half, 4, rows(half, 1, 0, 1), near.at[half, 0, :, pl.ds(0, 1)], peer(half, 1, 1))
        arrived(half, 1, far.at[half, 1])
        add_rows(half, -1, 1, 1, far.at[half, 1])
        push(half, 5, rows(half, -1, 1, 1), near.at[half, 1, :, pl.ds(1, 1)], peer(half, 1, -1))
    yield
    for half in (0, 1):
        arrived(half, 2, near.at[half, 0, :, pl.ds(1, 1)])
        arrived(half, 3, near.at[half, 1, :, pl.ds(0, 1)])
        arrived(half, 4, near.at[half, 0, :, pl.ds(0, 1)])
        arrived(half, 5, near.at[half, 1, :, pl.ds(1, 1)])
        add_rows(half, 0, 0, 2, near.at[half, 0], near.at[half, 1])
        push(half, 6, one(half, 2, 0, 1), far_last.at[half, 0], peer(half, 0, 1))
        push(half, 7, one(half, 2, 1, 1), far_last.at[half, 1], peer(half, 0, -1))
        push(half, 8, one(half, 1, 1, 1), near_last.at[half, 0, pl.ds(1, 1)], peer(half, 0, 1))
        push(half, 9, one(half, -1, 0, 1), near_last.at[half, 1, pl.ds(0, 1)], peer(half, 0, -1))
    yield
    for half in (0, 1):
        arrived(half, 6, far_last.at[half, 0])
        add(one(half, 1, 0, 1), far_last.at[half, 0])
        push(half, 10, one(half, 1, 0, 1), near_last.at[half, 0, pl.ds(0, 1)], peer(half, 0, 1))
        arrived(half, 7, far_last.at[half, 1])
        add(one(half, -1, 1, 1), far_last.at[half, 1])
        push(half, 11, one(half, -1, 1, 1), near_last.at[half, 1, pl.ds(1, 1)], peer(half, 0, -1))
    yield
    for half in (0, 1):
        arrived(half, 8, near_last.at[half, 0, pl.ds(1, 1)])
        arrived(half, 9, near_last.at[half, 1, pl.ds(0, 1)])
        arrived(half, 10, near_last.at[half, 0, pl.ds(0, 1)])
        arrived(half, 11, near_last.at[half, 1, pl.ds(1, 1)])
        total = one(half, 0, 0, 2)[...].astype(jnp.float32)
        for side in (0, 1):
            total = total + near_last[half, side].astype(jnp.float32)
        store(HALVES[half][1], total)
    for item in started:
        item.wait_send()


def reduce_scratch(quarter_rows, width):
    unit = (quarter_rows, width)
    return [
        pltpu.VMEM((SIDE, SIDE, 4) + unit, jnp.bfloat16),
        pltpu.VMEM((2, 2, SIDE, 1) + unit, jnp.bfloat16),
        pltpu.VMEM((2, 2, SIDE, 2) + unit, jnp.bfloat16),
        pltpu.VMEM((2, 2, 1) + unit, jnp.bfloat16),
        pltpu.VMEM((2, 2, 2) + unit, jnp.bfloat16),
        pltpu.SemaphoreType.DMA((2, 12)),
        pltpu.SemaphoreType.DMA((2, 12)),
    ]


def comm_params(number, limit_mb):
    return pltpu.CompilerParams(
        collective_id=number, has_side_effects=True, vmem_limit_bytes=limit_mb * 1024 * 1024
    )


def nothing(half, offset):
    return None


def advance(steps):
    next(steps, None)


def finish(steps):
    for _ in steps:
        pass


def pair_up(low, high, lane):
    return (
        jnp.where(lane < HEAD_DIM, low, pltpu.roll(high, HEAD_DIM, 1)),
        jnp.where(lane < HEAD_DIM, pltpu.roll(low, HEAD_DIM, 1), high),
    )


def by_group(rows):
    lane = lax.broadcasted_iota(jnp.int32, (rows.shape[0], 128), 1)
    tile = lambda at: rows[:, at * 128 : (at + 1) * 128]
    parts = []
    for j in range(4):
        low, high = tile(8 + j), tile(12 + j)
        first, second = pair_up(low, high, lane)
        parts += [tile(2 * j), first, tile(2 * j + 1), second]
    return jnp.concatenate(parts, axis=1)


def by_kind(rows):
    lane = lax.broadcasted_iota(jnp.int32, (rows.shape[0], 128), 1)
    tile = lambda at: rows[:, at * 128 : (at + 1) * 128]
    queries, keys, values = [], [], []
    for j in range(4):
        queries += [tile(4 * j), tile(4 * j + 2)]
        key, value = pair_up(tile(4 * j + 1), tile(4 * j + 3), lane)
        keys.append(key)
        values.append(value)
    return jnp.concatenate(queries + keys + values, axis=1)


def ring_gather(owns, outs, send, recv, core_send, core_recv, local):
    seq = lax.axis_index("seq")
    x, core = seq // 2, seq % 2
    other = seq_peer(0, True)
    started, swaps = [], []
    count = len(owns)

    def at(m, step, side):
        return outs[m].at[:, (x + step) % SIDE, side]

    def copy(m, kind, source, target, step):
        return pltpu.make_async_remote_copy(
            src_ref=source,
            dst_ref=target,
            send_sem=send.at[m, kind],
            recv_sem=recv.at[m, kind],
            device_id=seq_peer(step, False),
            device_id_type=MESH,
        )

    def push(m, kind, source, target, step):
        item = copy(m, kind, source, target, step)
        item.start()
        started.append(item)

    def arrived(m, kind, target):
        copy(m, kind, target, target, 1).wait_recv()

    def swap(m, kind, source, step):
        def across(out_of, into):
            return pltpu.make_async_remote_copy(
                src_ref=out_of,
                dst_ref=into,
                send_sem=core_send.at[m, kind],
                recv_sem=core_recv.at[m, kind],
                device_id=other,
                device_id_type=MESH,
            )

        item = across(source, at(m, step, core))
        item.start()
        started.append(item)
        swaps.append(across(at(m, step, 1 - core), at(m, step, 1 - core)))

    keeps = [pltpu.make_async_copy(owns[m], at(m, 0, core), local.at[m]) for m in range(count)]
    for m in range(count):
        push(m, 0, owns[m], at(m, 0, core), 1)
        push(m, 1, owns[m], at(m, 0, core), 3)
    for m in range(count):
        keeps[m].start()
        swap(m, 0, owns[m], 0)
    yield
    for m in range(count):
        for kind, expert, came, onward in ((0, 0, 3, 1), (1, 1, 1, 3)):
            arrived(m, kind, at(m, came, core))
            part = outs[m].at[expert, (x + came) % SIDE, core]
            push(m, 2 + kind, part, part, onward)
            swap(m, 1 + kind, at(m, came, core), came)
    yield
    for m in range(count):
        for kind in (0, 1):
            arrived(m, 2 + kind, outs[m].at[kind, (x + 2) % SIDE, core])
        swap(m, 3, at(m, 2, core), 2)
    for item in swaps:
        item.wait_recv()
    for item in keeps:
        item.wait()
    for item in started:
        item.wait_send()


def weights_gather(qkv, others, experts, number):
    rows, qkv_width = qkv.shape
    width = qkv_width + sum(other.shape[1] for other in others)
    kinds = len(experts)

    def kernel(*refs):
        refs = list(refs)
        take = lambda count: [refs.pop(0) for _ in range(count)]
        ins, ex_ins, (out_ref,), ex_outs = take(1 + len(others)), take(kinds), take(1), take(kinds)
        own_ref, send, recv, x_send, x_recv, core_send, core_recv, local_sem = take(8)
        ring_send, ring_recv, swap_send, swap_recv, ring_local = take(5)
        own_ref[:, pl.ds(0, qkv_width)] = by_group(ins[0][...].astype(jnp.float32)).astype(
            own_ref.dtype
        )
        at = qkv_width
        for other in ins[1:]:
            own_ref[:, pl.ds(at, other.shape[1])] = other[...]
            at += other.shape[1]
        seq = lax.axis_index("seq")
        x, core = seq // 2, seq % 2
        x_peers = [seq_peer(step, False) for step in (1, 3, 2)]
        other = seq_peer(0, True)
        greet(plane_neighbours() + x_peers + [other])
        z, y = plane_place("y", 0, 0)
        keep = pltpu.make_async_copy(own_ref, out_ref.at[x, core, z, y], local_sem)
        keep.start()
        sends = []
        for i, step in enumerate((1, 3, 2)):
            item = pltpu.make_async_remote_copy(
                src_ref=own_ref,
                dst_ref=out_ref.at[x, core, z, y],
                send_sem=x_send.at[i],
                recv_sem=x_recv.at[i],
                device_id=x_peers[i],
                device_id_type=MESH,
            )
            item.start()
            sends.append(item)
        keep.wait()
        for i, step in enumerate((1, 3, 2)):
            came = out_ref.at[(x + SIDE - step) % SIDE, core, z, y]
            pltpu.make_async_remote_copy(
                src_ref=came,
                dst_ref=came,
                send_sem=x_send.at[i],
                recv_sem=x_recv.at[i],
                device_id=x_peers[i],
                device_id_type=MESH,
            ).wait_recv()

        swaps = []

        def swap(half, offset):
            first, base = HALVES[half]
            z, y = plane_place(first, 0, offset)
            mine = (
                out_ref.at[pl.ds(base, 2), core, z]
                if first == "y"
                else out_ref.at[pl.ds(base, 2), core, :, y]
            )
            theirs = (
                out_ref.at[pl.ds(base, 2), 1 - core, z]
                if first == "y"
                else out_ref.at[pl.ds(base, 2), 1 - core, :, y]
            )
            kind = ORDER.index(offset)
            item = pltpu.make_async_remote_copy(
                src_ref=mine,
                dst_ref=mine,
                send_sem=core_send.at[half, kind],
                recv_sem=core_recv.at[half, kind],
                device_id=other,
                device_id_type=MESH,
            )
            item.start()
            sends.append(item)
            swaps.append(
                pltpu.make_async_remote_copy(
                    src_ref=theirs,
                    dst_ref=theirs,
                    send_sem=core_send.at[half, kind],
                    recv_sem=core_recv.at[half, kind],
                    device_id=other,
                    device_id_type=MESH,
                )
            )

        plane = plane_gather(
            lambda low, count: out_ref.at[pl.ds(low, count), core, z, y],
            lambda z, y, low, count: out_ref.at[pl.ds(low, count), core, z, y],
            send,
            recv,
            swap,
        )
        ring = ring_gather(
            ex_ins, ex_outs, ring_send, ring_recv, swap_send, swap_recv, ring_local
        )
        advance(plane)
        advance(ring)
        for _ in range(5):
            advance(plane)
        advance(ring)
        finish(plane)
        finish(ring)
        for item in swaps:
            item.wait_recv()
        for item in sends:
            item.wait_send()

    out = pl.pallas_call(
        kernel,
        out_shape=(jax.ShapeDtypeStruct((4, 2, SIDE, SIDE, rows, width), qkv.dtype),)
        + tuple(
            jax.ShapeDtypeStruct((2, 4, 2) + expert.shape[1:], expert.dtype) for expert in experts
        ),
        in_specs=[pl.BlockSpec(memory_space=pltpu.VMEM)] * (1 + len(others))
        + [pl.BlockSpec(memory_space=pl.ANY)] * kinds,
        out_specs=(pl.BlockSpec(memory_space=pl.ANY),) * (1 + kinds),
        scratch_shapes=[
            pltpu.VMEM((rows, width), qkv.dtype),
            pltpu.SemaphoreType.DMA((2, 20)),
            pltpu.SemaphoreType.DMA((2, 20)),
            pltpu.SemaphoreType.DMA((3,)),
            pltpu.SemaphoreType.DMA((3,)),
            pltpu.SemaphoreType.DMA((2, 4)),
            pltpu.SemaphoreType.DMA((2, 4)),
            pltpu.SemaphoreType.DMA,
        ]
        + [pltpu.SemaphoreType.DMA((kinds, 4))] * 4
        + [pltpu.SemaphoreType.DMA((kinds,))],
        compiler_params=comm_params(number, 8),
        name="weights_gather",
    )(qkv, *others, *experts)
    return (out[0].reshape(4 * 2 * SIDE * SIDE * rows, width),) + tuple(
        full.reshape(2, 8 * expert.shape[1], expert.shape[2])
        for full, expert in zip(out[1:], experts)
    )


def expert_shares_of(experts):
    return [(2, 4, 2, expert.shape[1] // 8, expert.shape[2]) for expert in experts]


def ring_reduce_scratch(experts):
    units = [share[3:] for share in expert_shares_of(experts)]
    count = len(units)
    return (
        [pltpu.VMEM((2, 4) + unit, jnp.bfloat16) for unit in units]
        + [pltpu.VMEM((2, 4) + unit, jnp.bfloat16) for unit in units]
        + [pltpu.VMEM((2,) + unit, jnp.bfloat16) for unit in units]
        + [pltpu.VMEM((2, 2) + unit, jnp.bfloat16) for unit in units]
        + [pltpu.SemaphoreType.DMA((count,))] * 3
        + [pltpu.SemaphoreType.DMA((count, 6))] * 2
    )


def ring_reduce(ins, outs, refs):
    count = len(ins)
    sums, twins = refs[:count], refs[count : 2 * count]
    far, near = refs[2 * count : 3 * count], refs[3 * count : 4 * count]
    load, core_send, core_recv, send, recv = refs[4 * count :]
    core = lax.axis_index("seq") % 2
    loads, swaps = [], []
    for m in range(count):
        loads.append(pltpu.make_async_copy(ins[m].at[:, :, core], sums[m], load.at[m]))
        loads[m].start()
        swaps.append(
            pltpu.make_async_remote_copy(
                src_ref=ins[m].at[:, :, 1 - core],
                dst_ref=twins[m],
                send_sem=core_send.at[m],
                recv_sem=core_recv.at[m],
                device_id=seq_peer(0, True),
                device_id_type=MESH,
            )
        )
        swaps[m].start()
    yield
    x = lax.axis_index("seq") // 2
    started = []

    def copy(m, kind, source, target, step):
        return pltpu.make_async_remote_copy(
            src_ref=source,
            dst_ref=target,
            send_sem=send.at[m, kind],
            recv_sem=recv.at[m, kind],
            device_id=seq_peer(step, False),
            device_id_type=MESH,
        )

    def push(m, kind, source, target, step):
        item = copy(m, kind, source, target, step)
        item.start()
        started.append(item)

    def arrived(m, kind, target):
        copy(m, kind, target, target, 1).wait_recv()

    def at(step):
        return (x + step) % SIDE

    for m in range(count):
        loads[m].wait()
        swaps[m].wait_recv()
        started.append(swaps[m])

        def add_pair(at, carry):
            sums[m][at // 4, at % 4] = sums[m][at // 4, at % 4] + twins[m][at // 4, at % 4]
            return carry

        lax.fori_loop(0, 8, add_pair, 0)
        push(m, 0, sums[m].at[0, at(2)], far[m].at[0], 1)
        push(m, 1, sums[m].at[1, at(2)], far[m].at[1], 3)
    for m in range(count):
        push(m, 2, sums[m].at[1, at(1)], near[m].at[0, 1], 1)
        push(m, 3, sums[m].at[0, at(3)], near[m].at[1, 0], 3)
    yield
    for m in range(count):
        for kind, expert, step in ((0, 0, 1), (1, 1, 3)):
            arrived(m, kind, far[m].at[kind])
            target = sums[m].at[expert, at(step)]
            target[...] = target[...] + far[m][kind]
            push(m, 4 + kind, target, near[m].at[kind, expert], step)
    yield
    for m in range(count):
        arrived(m, 2, near[m].at[0, 1])
        arrived(m, 3, near[m].at[1, 0])
        arrived(m, 4, near[m].at[0, 0])
        arrived(m, 5, near[m].at[1, 1])
        for expert in (0, 1):
            outs[m][expert] = (
                sums[m][expert, at(0)].astype(jnp.float32)
                + near[m][0, expert].astype(jnp.float32)
                + near[m][1, expert].astype(jnp.float32)
            )
    for item in started:
        item.wait_send()


def weights_reduce(pieces, experts, number):
    widths = [piece.shape[1] for piece in pieces]
    width = sum(widths)
    rows = pieces[0].shape[0] // (4 * 2 * SIDE * SIDE)
    kinds = len(experts)
    shares = expert_shares_of(experts)

    def kernel(*refs):
        refs = list(refs)
        take = lambda count: [refs.pop(0) for _ in range(count)]
        ins, ex_ins = take(len(widths)), take(kinds)
        qkv_ref, out_ref, small_ref = take(3)
        ex_outs = take(kinds)
        (parts, far, near, far_last, near_last, send, recv, twin, mine, from_x, load, core_send,
         core_recv, x_send, x_recv) = take(15)
        ring = ring_reduce(ex_ins, ex_outs, refs)
        seq = lax.axis_index("seq")
        x, core = seq // 2, seq % 2
        x_peers = [seq_peer(step, False) for step in (1, 3, 2)]
        other = seq_peer(0, True)
        loads = []
        for quarter in range(4):
            at = 0
            for i, one_width in enumerate(widths):
                item = pltpu.make_async_copy(
                    ins[i].at[quarter, core],
                    parts.at[:, :, quarter, :, pl.ds(at, one_width)],
                    load.at[quarter, i],
                )
                item.start()
                loads.append(item)
                at += one_width
        greet(plane_neighbours() + x_peers + [other])
        swaps = []
        for quarter in range(4):
            at = 0
            for i, one_width in enumerate(widths):
                item = pltpu.make_async_remote_copy(
                    src_ref=ins[i].at[quarter, 1 - core],
                    dst_ref=twin.at[quarter, :, :, :, pl.ds(at, one_width)],
                    send_sem=core_send.at[quarter, i],
                    recv_sem=core_recv.at[quarter, i],
                    device_id=other,
                    device_id_type=MESH,
                )
                item.start()
                swaps.append(item)
                at += one_width
        for quarter in range(4):
            for i in range(len(widths)):
                loads[quarter * len(widths) + i].wait()
                swaps[quarter * len(widths) + i].wait_recv()

            def add(at, carry):
                z, y = at // SIDE, at % SIDE
                parts[z, y, quarter] = parts[z, y, quarter] + twin[quarter, z, y]
                return carry

            lax.fori_loop(0, SIDE * SIDE, add, 0)

        def store(low, total):
            mine[pl.ds(low, 2)] = total.astype(mine.dtype)

        plane = plane_reduce(parts, far, near, far_last, near_last, send, recv, store)
        advance(plane)
        advance(plane)
        advance(ring)
        advance(plane)
        advance(ring)
        advance(plane)
        advance(ring)
        advance(plane)
        finish(ring)
        finish(plane)
        sends = []
        for i, step in enumerate((1, 3, 2)):
            item = pltpu.make_async_remote_copy(
                src_ref=mine.at[(x + step) % SIDE],
                dst_ref=from_x.at[i],
                send_sem=x_send.at[i],
                recv_sem=x_recv.at[i],
                device_id=x_peers[i],
                device_id_type=MESH,
            )
            item.start()
            sends.append(item)
        total = mine[x].astype(jnp.float32)
        for i in range(3):
            sends[i].wait_recv()
            total = total + from_x[i].astype(jnp.float32)
        qkv_ref[...] = by_kind(total[:, : widths[0]])
        out_ref[...] = total[:, widths[0] : widths[0] + widths[1]]
        small_ref[...] = total[:, widths[0] + widths[1] :]
        for item in sends + swaps:
            item.wait_send()

    unit = (rows, width)
    pairs = (4, len(widths))
    vmem = pl.BlockSpec(memory_space=pltpu.VMEM)
    return pl.pallas_call(
        kernel,
        out_shape=tuple(
            [jax.ShapeDtypeStruct((rows, one_width), jnp.float32) for one_width in widths]
            + [jax.ShapeDtypeStruct((2,) + share[3:], jnp.float32) for share in shares]
        ),
        in_specs=[pl.BlockSpec(memory_space=pl.ANY)] * (len(widths) + kinds),
        out_specs=(vmem,) * (len(widths) + kinds),
        scratch_shapes=reduce_scratch(rows, width)
        + [
            pltpu.VMEM((4, SIDE, SIDE) + unit, jnp.bfloat16),
            pltpu.VMEM((4,) + unit, jnp.bfloat16),
            pltpu.VMEM((3,) + unit, jnp.bfloat16),
            pltpu.SemaphoreType.DMA(pairs),
            pltpu.SemaphoreType.DMA(pairs),
            pltpu.SemaphoreType.DMA(pairs),
            pltpu.SemaphoreType.DMA((3,)),
            pltpu.SemaphoreType.DMA((3,)),
        ]
        + ring_reduce_scratch(experts),
        compiler_params=comm_params(number, 48),
        name="weights_reduce",
    )(
        *[piece.reshape(4, 2, SIDE, SIDE, rows, piece.shape[1]) for piece in pieces],
        *[expert.reshape(share) for expert, share in zip(experts, shares)],
    )


def rms_scale(values):
    return lax.rsqrt(jnp.mean(values * values, axis=-1, keepdims=True) + epsilon)


def rope_tables(length):
    half_dim = HEAD_DIM // 2
    frequency = np.float32(rope_theta) ** (
        -np.arange(half_dim, dtype=np.float32) / np.float32(half_dim)
    )
    angles = np.arange(length, dtype=np.float32)[:, None] * frequency[None, :].astype(np.float32)
    cosine = np.cos(angles.astype(np.float64)).astype(np.float32)
    sine = np.sin(angles.astype(np.float64)).astype(np.float32)
    one_cos = np.concatenate([cosine, cosine], axis=1)
    one_sin = np.concatenate([-sine, sine], axis=1)
    return (
        np.concatenate([one_cos, one_cos], axis=1),
        np.concatenate([one_sin, one_sin], axis=1),
    )


def group_tables(cosine, sine):
    lane = lax.broadcasted_iota(jnp.int32, cosine.shape, 1)
    return (
        jnp.concatenate([cosine, jnp.where(lane < HEAD_DIM, cosine, 1.0)], axis=1),
        jnp.concatenate([sine, jnp.where(lane < HEAD_DIM, sine, 0.0)], axis=1),
    )


def turn(values, cosine, sine):
    half_dim = HEAD_DIM // 2
    width = values.shape[1]
    lane = lax.broadcasted_iota(jnp.int32, values.shape, 1)
    ahead = pltpu.roll(values, width - half_dim, 1)
    behind = pltpu.roll(values, half_dim, 1)
    return values * cosine + jnp.where(lane % HEAD_DIM < half_dim, ahead, behind) * sine


SEQ_STEPS = (4, 5, 3, 2, 6, 1, 7)


def seq_exchange(source, target, send, recv):
    me = lax.axis_index("seq")
    count = 8

    def copy(step, peer, out_of, into):
        return pltpu.make_async_remote_copy(
            src_ref=out_of,
            dst_ref=into,
            send_sem=send.at[step - 1],
            recv_sem=recv.at[step - 1],
            device_id={"seq": peer},
            device_id_type=MESH,
        )

    def start(steps):
        items = []
        for step in steps:
            peer = (me + step) % count
            item = copy(step, peer, source(peer), target(me))
            item.start()
            items.append(item)
        return items

    def wait(step):
        peer = (me + count - step) % count
        copy(step, peer, target(peer), target(peer)).wait_recv()

    return (start, wait)


def seq_plane_greet():
    me = lax.axis_index("seq")
    greet(plane_neighbours() + [{"seq": (me + step) % 8} for step in range(1, 8)])


def twice(pair, lane):
    swapped = pltpu.roll(pair.astype(jnp.float32), HEAD_DIM, 1).astype(pair.dtype)
    return (
        jnp.where(lane < HEAD_DIM, pair, swapped),
        jnp.where(lane < HEAD_DIM, swapped, pair),
    )


def apart(pair, lane):
    zero = jnp.zeros_like(pair)
    return jnp.concatenate(
        [jnp.where(lane < HEAD_DIM, pair, zero), jnp.where(lane < HEAD_DIM, zero, pair)], axis=0
    )


def matmul(a, b, dims):
    return lax.dot_general(a, b, (dims, ((), ())), preferred_element_type=jnp.float32)


BLOCK = 256


def block_probs(queries, keys, at):
    scores = matmul(queries, keys, ((1,), (1,)))
    row = lax.broadcasted_iota(jnp.int32, scores.shape, 0) % BLOCK + at * BLOCK
    column = lax.broadcasted_iota(jnp.int32, scores.shape, 1)
    scores = jnp.where(column <= row, scores, -1e30)
    exponent = jnp.exp(scores - jnp.max(scores, axis=1, keepdims=True))
    return exponent * (1.0 / jnp.sum(exponent, axis=1, keepdims=True))


def attention_forward(normed, weights, width, cosine, sine, beside, number):
    tok, depth = normed.shape
    features = beside.shape[1]
    seq_parts = 8
    group = width // seq_parts
    pair = 2 * HEAD_DIM
    length = tok * seq_parts
    per_block = BLOCK // tok

    def kernel(
        normed_ref, weights_ref, cos_hbm, sin_hbm, beside_ref, out_ref, heads_ref, all_ref,
        packed, mixed, proj_w, cos_ref, sin_ref,
        send, recv, o_send, o_recv, p_send, p_recv, local_sem, load,
    ):
        me = lax.axis_index("seq")
        here = pl.ds(pl.multiple_of(me * tok, tok), tok)
        loads = [
            pltpu.make_async_copy(weights_ref.at[:, pl.ds(0, width)], proj_w, load.at[0]),
            pltpu.make_async_copy(cos_hbm.at[here], cos_ref, load.at[1]),
            pltpu.make_async_copy(sin_hbm.at[here], sin_ref, load.at[2]),
        ]
        for item in loads:
            item.start()
        z, y = plane_place("y", 0, 0)
        keep = pltpu.make_async_copy(beside_ref, all_ref.at[z, y], local_sem)
        keep.start()
        seq_plane_greet()
        steps = plane_gather(
            lambda low, count: beside_ref.at[pl.ds(low, count)],
            lambda z, y, low, count: all_ref.at[z, y, pl.ds(low, count)],
            p_send,
            p_recv,
            nothing,
        )
        advance(steps)
        for item in loads:
            item.wait()
        cosines, sines = group_tables(cos_ref[...], sin_ref[...])
        for d in range(seq_parts):
            projected = matmul(
                normed_ref[...], proj_w[:, d * group : (d + 1) * group], ((1,), (0,))
            )
            packed[d] = turn(projected, cosines, sines).astype(packed.dtype)
        start, wait = seq_exchange(
            lambda d: packed.at[d], lambda d: heads_ref.at[d], send, recv
        )
        items = start(SEQ_STEPS)
        heads_ref[me] = packed[me]
        advance(steps)
        for step in SEQ_STEPS:
            wait(step)
        advance(steps)
        lane = lax.broadcasted_iota(jnp.int32, (length, pair), 1)
        heads = heads_ref[...].reshape(length, group)
        keys, values = twice(heads[:, pair:], lane)
        lane_block = lane[:BLOCK]
        back, back_wait = seq_exchange(
            lambda d: mixed.at[d],
            lambda d: out_ref.at[:, pl.ds(pl.multiple_of(d * pair, pair), pair)],
            o_send,
            o_recv,
        )
        for at in range(length // BLOCK):
            block = heads[at * BLOCK : (at + 1) * BLOCK, :pair]
            queries = apart(block * jnp.asarray(attention_multiplier, block.dtype), lane_block)
            upto = (at + 1) * BLOCK
            probs = block_probs(queries, keys[:upto], at).astype(jnp.bfloat16)
            both = matmul(probs, values[:upto], ((1,), (0,)))
            made = jnp.where(lane_block < HEAD_DIM, both[:BLOCK], both[BLOCK:]).astype(mixed.dtype)
            mixed[at * per_block : (at + 1) * per_block] = made.reshape(per_block, tok, pair)
            if at % 2:
                advance(steps)
        items += back(SEQ_STEPS)
        out_ref[:, pl.ds(pl.multiple_of(me * pair, pair), pair)] = mixed[me]
        advance(steps)
        for step in SEQ_STEPS:
            back_wait(step)
        finish(steps)
        keep.wait()
        for item in items:
            item.wait_send()

    vmem = pl.BlockSpec(memory_space=pltpu.VMEM)
    anywhere = pl.BlockSpec(memory_space=pl.ANY)
    attended, heads, gathered = pl.pallas_call(
        kernel,
        out_shape=(
            jax.ShapeDtypeStruct((tok, seq_parts * pair), jnp.bfloat16),
            jax.ShapeDtypeStruct((seq_parts, tok, group), jnp.bfloat16),
            jax.ShapeDtypeStruct((SIDE, SIDE, 4, tok // 4, features), beside.dtype),
        ),
        in_specs=[vmem] + [anywhere] * 4,
        out_specs=(vmem, vmem, anywhere),
        scratch_shapes=[
            pltpu.VMEM((seq_parts, tok, group), jnp.bfloat16),
            pltpu.VMEM((seq_parts, tok, pair), jnp.bfloat16),
            pltpu.VMEM((depth, width), jnp.bfloat16),
            pltpu.VMEM((tok, pair), jnp.float32),
            pltpu.VMEM((tok, pair), jnp.float32),
        ]
        + [pltpu.SemaphoreType.DMA((7,))] * 4
        + [pltpu.SemaphoreType.DMA((2, 20))] * 2
        + [pltpu.SemaphoreType.DMA, pltpu.SemaphoreType.DMA((3,))],
        compiler_params=comm_params(number, 48),
        name="attention_forward",
    )(normed, weights, cosine, sine, beside.reshape(4, tok // 4, features))
    return (attended, heads, gathered.reshape(SIDE * SIDE, tok, features))


def attention_backward(grad_attended, heads_in, cosine, sine, beside, experts, number):
    kinds = len(experts)
    shares = expert_shares_of(experts)
    seq_parts, tok, group = heads_in.shape
    features = beside.shape[2]
    pair = 2 * HEAD_DIM
    length = tok * seq_parts
    per_block = BLOCK // tok

    def kernel(*refs):
        refs = list(refs)
        take = lambda count: [refs.pop(0) for _ in range(count)]
        grad_ref, heads_ref, cos_ref, sin_ref, beside_ref = take(5)
        ex_ins = take(kinds)
        out_ref, sum_ref = take(2)
        ex_outs = take(kinds)
        came, packed, d_queries, d_keys, d_values, send, recv, o_send, o_recv = take(9)
        parts, far, near, far_last, near_last, p_send, p_recv, load = take(8)
        ring = ring_reduce(ex_ins, ex_outs, refs)
        me = lax.axis_index("seq")
        loaded = pltpu.make_async_copy(beside_ref, parts, load)
        loaded.start()
        seq_plane_greet()

        def store(low, total):
            sum_ref[pl.ds(low, 2)] = total

        steps = plane_reduce(parts, far, near, far_last, near_last, p_send, p_recv, store)
        columns = lambda d: grad_ref.at[:, pl.ds(pl.multiple_of(d * pair, pair), pair)]
        start, wait = seq_exchange(columns, lambda d: came.at[d], send, recv)
        items = start(SEQ_STEPS)
        loaded.wait()
        advance(steps)
        advance(steps)
        advance(ring)
        came[me] = grad_ref[:, pl.ds(pl.multiple_of(me * pair, pair), pair)]
        lane = lax.broadcasted_iota(jnp.int32, (length, pair), 1)
        lane_block = lane[:BLOCK]
        heads = heads_ref[...].reshape(length, group)
        keys, values = twice(heads[:, pair:], lane)
        for step in SEQ_STEPS:
            wait(step)
        for at in range(length // BLOCK):
            if at == 1:
                advance(ring)
            if at == 3:
                advance(ring)
            upto = (at + 1) * BLOCK
            block = heads[at * BLOCK : upto, :pair]
            queries = apart(block * jnp.asarray(attention_multiplier, block.dtype), lane_block)
            grads = apart(
                came[at * per_block : (at + 1) * per_block].reshape(BLOCK, pair), lane_block
            )
            probs = block_probs(queries, keys[:upto], at)
            d_probs = matmul(grads, values[:upto], ((1,), (1,)))
            center = jnp.sum(probs * d_probs, axis=1, keepdims=True)
            d_scores = (probs * (d_probs - center)).astype(jnp.bfloat16)
            both = matmul(d_scores, keys[:upto], ((1,), (0,))) * attention_multiplier
            d_queries[at * BLOCK : upto] = jnp.where(
                lane_block < HEAD_DIM, both[:BLOCK], both[BLOCK:]
            )
            more_keys = matmul(d_scores, queries, ((0,), (0,)))
            more_values = matmul(probs.astype(jnp.bfloat16), grads, ((0,), (0,)))
            before = at * BLOCK
            if at:
                d_keys[:before] += more_keys[:before]
                d_values[:before] += more_values[:before]
            d_keys[before:upto] = more_keys[before:]
            d_values[before:upto] = more_values[before:]
            if at in (1, 3):
                advance(steps)
        sum_keys = d_keys[...] + pltpu.roll(d_keys[...], HEAD_DIM, 1)
        sum_values = d_values[...] + pltpu.roll(d_values[...], HEAD_DIM, 1)
        rest = jnp.where(lane < HEAD_DIM, sum_keys, sum_values)
        whole = jnp.concatenate([d_queries[...], rest], axis=1)
        cosines, sines = group_tables(cos_ref[...], sin_ref[...])
        packed[...] = (
            turn(whole, cosines, -sines)
            .astype(packed.dtype)
            .reshape(seq_parts, tok, group)
        )
        back, back_wait = seq_exchange(
            lambda d: packed.at[d],
            lambda d: out_ref.at[:, pl.ds(pl.multiple_of(d * group, group), group)],
            o_send,
            o_recv,
        )
        items += back(SEQ_STEPS)
        out_ref[:, pl.ds(pl.multiple_of(me * group, group), group)] = packed[me]
        advance(steps)
        for step in SEQ_STEPS:
            back_wait(step)
        finish(ring)
        finish(steps)
        for item in items:
            item.wait_send()

    vmem = pl.BlockSpec(memory_space=pltpu.VMEM)
    outs = pl.pallas_call(
        kernel,
        out_shape=(
            jax.ShapeDtypeStruct((tok, seq_parts * group), jnp.bfloat16),
            jax.ShapeDtypeStruct((4, tok // 4, features), jnp.float32),
        )
        + tuple(jax.ShapeDtypeStruct((2,) + share[3:], jnp.float32) for share in shares),
        in_specs=[vmem] * 4 + [pl.BlockSpec(memory_space=pl.ANY)] * (1 + kinds),
        out_specs=(vmem,) * (2 + kinds),
        scratch_shapes=[
            pltpu.VMEM((seq_parts, tok, pair), jnp.bfloat16),
            pltpu.VMEM((seq_parts, tok, group), jnp.bfloat16),
            pltpu.VMEM((length, pair), jnp.float32),
            pltpu.VMEM((length, pair), jnp.float32),
            pltpu.VMEM((length, pair), jnp.float32),
        ]
        + [pltpu.SemaphoreType.DMA((7,))] * 4
        + reduce_scratch(tok // 4, features)
        + [pltpu.SemaphoreType.DMA]
        + ring_reduce_scratch(experts),
        compiler_params=comm_params(number, 56),
        name="attention_backward",
    )(
        grad_attended,
        heads_in,
        cosine,
        sine,
        beside.reshape(SIDE, SIDE, 4, tok // 4, features),
        *[expert.reshape(share) for expert, share in zip(experts, shares)],
    )
    return (outs[0], outs[1].reshape(tok, features)) + tuple(outs[2:])


def gate_columns(logits, chosen_ids, experts_all):
    named = jnp.any(
        chosen_ids[..., None] == jnp.arange(experts_all, dtype=jnp.int32), axis=-2
    )
    peak = jnp.max(jnp.where(named, logits, -jnp.inf), axis=-1, keepdims=True)
    exponent = jnp.where(named, jnp.exp(logits - peak), 0.0)
    gates = exponent / jnp.sum(exponent, axis=-1, keepdims=True)
    coarse = lax.reduce_precision(gates, 8, 7)
    columns = jnp.concatenate(
        [named.astype(jnp.float32), coarse, gates - coarse, jnp.zeros_like(gates)], axis=-1
    ).astype(jnp.bfloat16)
    return (gates, columns)


def near_place(at):
    if isinstance(at, int) and at >= 9:
        return far_place(at)
    return (at // 3 - 1, at % 3 - 1)


def far_place(at):
    beyond = at - 9
    turn_over = beyond // 4
    return (
        2 * (1 - turn_over) + turn_over * (beyond - 5),
        (1 - turn_over) * (beyond - 1) + turn_over * 2,
    )


def expert_layer(
    tokens_own, cot_all, gate_full, up_full, down_full, experts_all, capacity, number
):
    tok, wide = tokens_own.shape
    sources = SIDE * SIDE
    quarter = tok // 4
    features = wide - 128
    hidden_units = gate_full.shape[2]
    group = 8
    chunks = sources // group
    chunk_rows = group * capacity
    f32, b16 = jnp.float32, jnp.bfloat16

    def kernel(
        tok_hbm, cot_hbm, gate_hbm, up_hbm, down_hbm,
        mix_hbm, back_ref, ggate_hbm, gup_hbm, gdown_hbm,
        tok_v, cot_v, gate_v, up_v, down_v, mix_v, grad_v,
        x_v, deo_v, slope_v, act_v, inner_v, pick_t, share_v, dgate_v,
        in_sem, out_sem, g_send, g_recv,
        rows_v, far, near, far_last, near_last, r_send, r_recv,
    ):
        first = lax.axis_index("wshard") * 2
        home_z, home_y = plane_place("y", 0, 0)
        loads = [
            pltpu.make_async_copy(source, target, in_sem.at[i])
            for i, (source, target) in enumerate(
                [(tok_hbm, tok_v.at[home_z, home_y]), (cot_hbm, cot_v), (gate_hbm, gate_v), (up_hbm, up_v),
                 (down_hbm, down_v)]
            )
        ]
        for item in loads:
            item.start()
        lane = lax.broadcasted_iota(jnp.int32, (tok, 128), 1)
        down_rows = lax.broadcasted_iota(jnp.int32, (tok, 128), 0)
        lower = jnp.where(down_rows >= lane, 1.0, 0.0).astype(b16)
        greet(plane_neighbours())
        gather = plane_gather(
            lambda low, count: tok_hbm.at[pl.ds(low, count)],
            lambda z, y, low, count: tok_v.at[z, y, pl.ds(low, count)],
            g_send,
            g_recv,
            nothing,
        )
        advance(gather)
        advance(gather)
        advance(gather)
        advance(gather)
        advance(gather)
        loads[0].wait()
        loads[1].wait()

        def prepare(s, place_of):
            off_z, off_y = place_of(s)
            z, y = plane_place("y", off_y, off_z)
            info = tok_v[z, y, :, :, pl.ds(features, 128)].reshape(tok, 128)
            info32 = info.astype(f32)
            place = matmul(lower, info, ((1,), (0,))) - 1.0
            place = jnp.where(info32 > 0.5, place, -1.0)
            place_rows = place.T
            info_rows = info32.T
            row_picks, col_places = [], []
            shares = []
            for e in (0, 1):
                at = first + e
                row = jnp.sum(jnp.where(down_rows == at, place_rows, 0.0), axis=0, keepdims=True)
                gate = jnp.sum(
                    jnp.where(
                        (down_rows == experts_all + at) | (down_rows == 2 * experts_all + at),
                        info_rows,
                        0.0,
                    ),
                    axis=0,
                    keepdims=True,
                )
                slot = lax.broadcasted_iota(jnp.int32, (capacity, tok), 0).astype(f32)
                hit = slot == row
                row_picks.append(jnp.where(hit, 1.0, 0.0))
                shares.append(jnp.sum(jnp.where(hit, gate, 0.0), axis=1, keepdims=True))
                col_places.append(
                    jnp.sum(jnp.where(lane == at, place, 0.0), axis=1, keepdims=True)
                )
            pick = jnp.concatenate(row_picks, axis=0).astype(b16)
            lane_f = lane.astype(f32)
            pick_t[s] = (
                jnp.where(lane_f == col_places[0], 1.0, 0.0) * jnp.where(lane < capacity, 1.0, 0.0)
                + jnp.where(lane_f - float(capacity) == col_places[1], 1.0, 0.0)
                * jnp.where(lane >= capacity, 1.0, 0.0)
            ).astype(b16)
            share_v[s] = jnp.concatenate(shares, axis=0)
            rows = matmul(
                pick, tok_v[z, y, :, :, pl.ds(0, features)].reshape(tok, features), ((1,), (0,))
            ).astype(b16)
            c, i = s // group, s % group
            x_v[0, c, i] = rows[:capacity]
            x_v[1, c, i] = rows[capacity:]
            cots = matmul(pick, cot_v[z, y], ((1,), (0,))).astype(b16)
            deo_v[0, c, i] = cots[:capacity]
            deo_v[1, c, i] = cots[capacity:]

        def prepare_all(low, high, place_of):
            def step(s, carry):
                prepare(s, place_of)
                return carry

            lax.fori_loop(low, high, step, 0)

        def forward(c):
            weighted = []
            for e in (0, 1):
                x = x_v[e, c].reshape(chunk_rows, features)
                gate_val = matmul(x, gate_v[e], ((1,), (0,)))
                up_val = matmul(x, up_v[e], ((1,), (0,)))
                sigma = 1.0 / (1.0 + jnp.exp(-gate_val))
                act = gate_val * sigma
                inner = (act * up_val).astype(b16)
                inner_v[e, c] = inner
                act_v[e, c] = act.astype(b16)
                slope_v[e, c] = (up_val * (sigma * (1.0 + gate_val * (1.0 - sigma)))).astype(b16)
                made = matmul(inner, down_v[e], ((1,), (0,))).astype(b16).astype(f32)
                share = jnp.concatenate(
                    [share_v[c * group + i, pl.ds(e * capacity, capacity)] for i in range(group)],
                    axis=0,
                )
                mix_grad = residual_multiplier * deo_v[e, c].reshape(chunk_rows, features).astype(f32)
                dgate_v[e, c] = jnp.sum(made * mix_grad, axis=1, keepdims=True)
                deo_v[e, c] = (share * mix_grad).astype(b16).reshape(group, capacity, features)
                weighted.append((share * made).astype(b16))
            for i in range(group):
                both = jnp.concatenate(
                    [w[i * capacity : (i + 1) * capacity] for w in weighted], axis=0
                )
                off_z, off_y = near_place(c * group + i)
                z, y = plane_place("y", off_y, off_z)
                mix_v[z, y] = matmul(pick_t[c * group + i], both, ((1,), (0,))).astype(b16)

        prepare_all(0, 9, near_place)
        advance(gather)
        for item in loads[2:]:
            item.wait()
        forward(0)
        finish(gather)
        prepare_all(9, sources, far_place)
        forward(1)
        stores = [pltpu.make_async_copy(mix_v, mix_hbm, out_sem.at[0])]
        stores[0].start()
        lane_rows = lax.broadcasted_iota(jnp.int32, (chunk_rows, 128), 1)

        def backward(c):
            made = []
            for e in (0, 1):
                deo = deo_v[e, c].reshape(chunk_rows, features)
                d_inner = matmul(deo, down_v[e], ((1,), (1,)))
                d_gate = (d_inner * slope_v[e, c].astype(f32)).astype(b16)
                d_up = (d_inner * act_v[e, c].astype(f32)).astype(b16)
                slope_v[e, c] = d_gate
                act_v[e, c] = d_up
                d_rows = (
                    matmul(d_gate, gate_v[e], ((1,), (1,))) + matmul(d_up, up_v[e], ((1,), (1,)))
                ).astype(b16)
                coarse = dgate_v[e, c].astype(b16).astype(f32)
                fine = dgate_v[e, c] - coarse
                columns = jnp.where(lane_rows == first + e, coarse, 0.0) + jnp.where(
                    lane_rows == experts_all + first + e, fine, 0.0
                )
                made.append(jnp.concatenate([d_rows, columns.astype(b16)], axis=1))
            for i in range(group):
                both = jnp.concatenate(
                    [m[i * capacity : (i + 1) * capacity] for m in made], axis=0
                )
                off_z, off_y = near_place(c * group + i)
                z, y = plane_place("y", off_y, off_z)
                rows_v[z, y] = (
                    matmul(pick_t[c * group + i], both, ((1,), (0,)))
                    .astype(b16)
                    .reshape(4, quarter, wide)
                )

        def store(low, total):
            back_ref[pl.ds(low, 2)] = total

        reduce = plane_reduce(
            rows_v, far, near, far_last, near_last, r_send, r_recv, store
        )
        backward(1)
        advance(reduce)
        backward(0)
        advance(reduce)
        rows_all = chunks * chunk_rows

        def whole(ref, e, columns):
            return ref[e].reshape(rows_all, columns)

        for e in (0, 1):
            x = whole(x_v, e, features)
            for i, source, target in (
                (e, slope_v, ggate_hbm),
                (2 + e, act_v, gup_hbm),
            ):
                grad_v[i] = matmul(x, whole(source, e, hidden_units), ((0,), (0,))).astype(b16)
                stores.append(
                    pltpu.make_async_copy(grad_v.at[i], target.at[e], out_sem.at[1 + i])
                )
                stores[-1].start()
            advance(reduce)
        for e in (0, 1):
            grad = matmul(
                whole(inner_v, e, hidden_units), whole(deo_v, e, features), ((0,), (0,))
            ).astype(b16)
            cot_v[e] = grad.reshape(4, 128, features)
            stores.append(
                pltpu.make_async_copy(cot_v.at[e], gdown_hbm.at[e], out_sem.at[5 + e])
            )
            stores[-1].start()
            if e == 0:
                advance(reduce)
        finish(reduce)
        for item in stores:
            item.wait()

    anywhere = pl.BlockSpec(memory_space=pl.ANY)
    local = gate_full.shape[0]
    outs = pl.pallas_call(
        kernel,
        out_shape=(
            jax.ShapeDtypeStruct((SIDE, SIDE, tok, features), b16),
            jax.ShapeDtypeStruct((4, quarter, wide), f32),
            jax.ShapeDtypeStruct((local, features, hidden_units), b16),
            jax.ShapeDtypeStruct((local, features, hidden_units), b16),
            jax.ShapeDtypeStruct((local, 4, hidden_units // 4, features), b16),
        ),
        in_specs=[anywhere] * 5,
        out_specs=(anywhere, pl.BlockSpec(memory_space=pltpu.VMEM)) + (anywhere,) * 3,
        scratch_shapes=[
            pltpu.VMEM((SIDE, SIDE, 4, quarter, wide), b16),
            pltpu.VMEM((SIDE, SIDE, tok, features), b16),
            pltpu.VMEM(gate_full.shape, b16),
            pltpu.VMEM(up_full.shape, b16),
            pltpu.VMEM(down_full.shape, b16),
            pltpu.VMEM((SIDE, SIDE, tok, features), b16),
            pltpu.VMEM((4, features, hidden_units), b16),
            pltpu.VMEM((2, chunks, group, capacity, features), b16),
            pltpu.VMEM((2, chunks, group, capacity, features), b16),
            pltpu.VMEM((2, chunks, chunk_rows, hidden_units), b16),
            pltpu.VMEM((2, chunks, chunk_rows, hidden_units), b16),
            pltpu.VMEM((2, chunks, chunk_rows, hidden_units), b16),
            pltpu.VMEM((sources, tok, 2 * capacity), b16),
            pltpu.VMEM((sources, 2 * capacity, 1), f32),
            pltpu.VMEM((2, chunks, chunk_rows, 1), f32),
            pltpu.SemaphoreType.DMA((5,)),
            pltpu.SemaphoreType.DMA((7,)),
            pltpu.SemaphoreType.DMA((2, 20)),
            pltpu.SemaphoreType.DMA((2, 20)),
        ]
        + reduce_scratch(quarter, wide),
        compiler_params=comm_params(number, 60),
        name="expert_layer",
    )(
        tokens_own.reshape(4, quarter, wide),
        cot_all.reshape(SIDE, SIDE, tok, features),
        gate_full,
        up_full,
        down_full,
    )
    return (
        outs[0].reshape(sources, tok, features),
        outs[1].reshape(tok, wide),
        outs[2],
        outs[3],
        outs[4].reshape(local, hidden_units, features),
    )


def norm_backward(grad_normed, values, scale, gain_full):
    grad_gain = jnp.sum(grad_normed * values * scale, axis=0)
    grad_hat = grad_normed * gain_full
    grad_values = scale * grad_hat - values * (scale * scale * scale) * jnp.mean(
        grad_hat * values, axis=1, keepdims=True
    )
    return (grad_values, grad_gain)


def local(
    tokens,
    weight_qkv,
    weight_out,
    router,
    gain_attn,
    gain_ffn,
    expert_gate,
    expert_up,
    expert_down,
    expert_ids,
    cotangent,
):
    tok_dev = tokens.shape[1]
    features = tokens.shape[2]
    seq_parts = lax.axis_size("seq")
    owners = lax.axis_size("wshard")
    local_experts = expert_gate.shape[0]
    experts_all = local_experts * owners
    top_count = expert_ids.shape[2]
    capacity = 2 * tok_dev * top_count // experts_all
    heads_dev = HEADS // seq_parts
    key_heads = KV_HEADS // seq_parts
    query_cols = heads_dev * HEAD_DIM
    key_cols = key_heads * HEAD_DIM
    query_width = HEADS * HEAD_DIM
    key_width = KV_HEADS * HEAD_DIM
    length = tok_dev * seq_parts
    qkv_width = weight_qkv.shape[1]
    smalls = jnp.concatenate(
        [
            router,
            gain_attn[:, None],
            gain_ffn[:, None],
            jnp.zeros((router.shape[0], 128 - experts_all - 2), jnp.bfloat16),
        ],
        axis=1,
    )
    weights_full, gate_full, up_full, down_full = weights_gather(
        weight_qkv, [weight_out, smalls], [expert_gate, expert_up, expert_down], 0
    )
    qkv_full = weights_full[:, :qkv_width]
    out_full = weights_full[:, qkv_width : qkv_width + features]
    smalls_full = weights_full[:, qkv_width + features :]
    router_full = smalls_full[:, :experts_all]
    gain_one = smalls_full[:, experts_all].astype(jnp.float32)
    gain_two = smalls_full[:, experts_all + 1].astype(jnp.float32)
    inputs = tokens[0].astype(jnp.float32)
    chosen_ids = expert_ids[0]
    scale_one = rms_scale(inputs)
    normed_one = (inputs * scale_one * gain_one).astype(jnp.bfloat16)
    cosine, sine = (jnp.asarray(table) for table in rope_tables(length))
    attended, heads_all, cot_all = attention_forward(
        normed_one, weights_full, qkv_width, cosine, sine, cotangent[0], 5
    )
    branch = jnp.dot(attended, out_full, preferred_element_type=jnp.float32)
    hidden = inputs + residual_multiplier * branch
    scale_two = rms_scale(hidden)
    normed_two = (hidden * scale_two * gain_two).astype(jnp.bfloat16)
    logits = jnp.dot(normed_two, router_full, preferred_element_type=jnp.float32)
    gates_own, gate_info = gate_columns(logits, chosen_ids, experts_all)
    mix_part, back, grad_gate, grad_up, grad_down = expert_layer(
        jnp.concatenate([normed_two, gate_info], axis=1),
        cot_all,
        gate_full,
        up_full,
        down_full,
        experts_all,
        capacity,
        1,
    )
    grad_output = cotangent[0].astype(jnp.float32)
    grad_back = back[:, :features]
    grad_gates = (
        back[:, features : features + experts_all]
        + back[:, features + experts_all : features + 2 * experts_all]
    )
    grad_logits = (
        gates_own
        * (grad_gates - jnp.sum(gates_own * grad_gates, axis=1, keepdims=True))
    ).astype(jnp.bfloat16)
    grad_normed_two = jnp.dot(grad_logits, router_full.T, preferred_element_type=jnp.float32)
    grad_normed_two = grad_normed_two + grad_back
    grad_hidden_norm, grad_gain_ffn = norm_backward(grad_normed_two, hidden, scale_two, gain_two)
    grad_hidden = grad_output + grad_hidden_norm
    grad_branch = (residual_multiplier * grad_hidden).astype(jnp.bfloat16)
    grad_out = jnp.dot(attended.T, grad_branch, preferred_element_type=jnp.float32)
    grad_attended = jnp.dot(grad_branch, out_full.T, preferred_element_type=jnp.float32).astype(
        jnp.bfloat16
    )
    grad_proj, mixture, own_gate, own_up = attention_backward(
        grad_attended, heads_all, cosine, sine, mix_part, [grad_gate, grad_up], 6
    )
    output = hidden + residual_multiplier * mixture
    grad_qkv = jnp.dot(normed_one.T, grad_proj, preferred_element_type=jnp.float32)
    grad_normed_one = jnp.dot(grad_proj, qkv_full.T, preferred_element_type=jnp.float32)
    grad_input_norm, grad_gain_attn = norm_backward(grad_normed_one, inputs, scale_one, gain_one)
    grad_input = grad_hidden + grad_input_norm
    column = jnp.arange(128, dtype=jnp.int32)[None, :]
    grad_smalls = (
        jnp.dot(
            normed_two.T,
            jnp.pad(grad_logits, ((0, 0), (0, 128 - experts_all))),
            preferred_element_type=jnp.float32,
        )
        + jnp.where(column == experts_all, grad_gain_attn[:, None], 0.0)
        + jnp.where(column == experts_all + 1, grad_gain_ffn[:, None], 0.0)
    ).astype(jnp.bfloat16)
    own_qkv, own_out, own_smalls, own_down = weights_reduce(
        [grad_qkv.astype(jnp.bfloat16), grad_out.astype(jnp.bfloat16), grad_smalls],
        [grad_down],
        4,
    )
    shares = (
        own_qkv,
        own_out,
        own_smalls[:, :experts_all],
        own_smalls[:, experts_all],
        own_smalls[:, experts_all + 1],
    )
    expert_shares = (own_gate, own_up, own_down)
    return (
        output.astype(jnp.bfloat16)[None],
        grad_input.astype(jnp.bfloat16)[None],
        shares[0],
        shares[1],
        shares[2],
        shares[3],
        shares[4],
        expert_shares[0],
        expert_shares[1],
        expert_shares[2],
    )


def solution(mesh):
    placed = (
        P("wshard", "seq", None),
        P(("seq", "wshard"), None),
        P(("seq", "wshard"), None),
        P(("seq", "wshard"), None),
        P(("seq", "wshard")),
        P(("seq", "wshard")),
        P("wshard", "seq", None),
        P("wshard", "seq", None),
        P("wshard", "seq", None),
        P("wshard", "seq", None),
        P("wshard", "seq", None),
    )
    return jax.shard_map(
        local,
        mesh=mesh,
        in_specs=placed,
        out_specs=(
            P("wshard", "seq", None),
            P("wshard", "seq", None),
            P(("seq", "wshard"), None),
            P(("seq", "wshard"), None),
            P(("seq", "wshard"), None),
            P(("seq", "wshard")),
            P(("seq", "wshard")),
            P("wshard", "seq", None),
            P("wshard", "seq", None),
            P("wshard", "seq", None),
        ),
        check_vma=False,
    )
```

```python
import jax
import jax.numpy as jnp
import numpy as np
from jax import lax
from jax.experimental import pallas as pl
from jax.experimental.pallas import tpu as pltpu
from jax.sharding import PartitionSpec as P

HEADS = 16
KV_HEADS = 8
HEAD_DIM = 64


epsilon = 1e-06
attention_multiplier = 0.015625
residual_multiplier = 0.22
rope_theta = 10000.0


MESH = pl.DeviceIdType.MESH
SIDE = 4


def plane_place(first, offset_first, offset_second):
    mine = lax.axis_index("wshard")
    z, y = mine // SIDE, mine % SIDE
    if first == "y":
        return ((z + offset_second + SIDE) % SIDE, (y + offset_first + SIDE) % SIDE)
    return ((z + offset_first + SIDE) % SIDE, (y + offset_second + SIDE) % SIDE)


def plane_peer(first, offset_first, offset_second):
    z, y = plane_place(first, offset_first, offset_second)
    return {"wshard": z * SIDE + y}


def plane_neighbours():
    return [plane_peer("y", step, 0) for step in (1, -1)] + [
        plane_peer("y", 0, step) for step in (1, -1)
    ]


def seq_peer(offset_x, flip):
    mine = lax.axis_index("seq")
    x, core = mine // 2, mine % 2
    if flip:
        core = 1 - core
    return {"seq": ((x + offset_x) % SIDE) * 2 + core}


def greet(peers):
    barrier = pltpu.get_barrier_semaphore()
    for peer in peers:
        pl.semaphore_signal(barrier, inc=1, device_id=peer, device_id_type=MESH)
    pl.semaphore_wait(barrier, len(peers))


HALVES = (("y", 0), ("z", 2))
ORDER = (0, -1, 1, 2)


def plane_gather(own, view, send, recv, after_row):
    started = []

    def copy(half, kind, source, target, peer):
        return pltpu.make_async_remote_copy(
            src_ref=source,
            dst_ref=target,
            send_sem=send.at[half, kind],
            recv_sem=recv.at[half, kind],
            device_id=peer,
            device_id_type=MESH,
        )

    def push(half, kind, source, target, peer):
        item = copy(half, kind, source, target, peer)
        item.start()
        started.append(item)

    def arrived(half, kind, target):
        first, _ = HALVES[half]
        copy(half, kind, target, target, plane_peer(first, 1, 0)).wait_recv()

    def block(half, along_first, along_second, low, count):
        first, base = HALVES[half]
        z, y = plane_place(first, along_first, along_second)
        return view(z, y, base + low, count)

    def ring(half, slot, axis, along, source):
        first, base = HALVES[half]
        for kind, step in ((0, 1), (1, -1)):
            peer = plane_peer(first, step, 0) if axis == 0 else plane_peer(first, 0, step)
            push(half, 4 * slot + kind, source, block(half, along, 0, 0, 2), peer)

    def ring_relay(half, slot, axis, along):
        first, base = HALVES[half]
        for kind, step in ((0, 1), (1, -1)):
            where = (-step, 0) if axis == 0 else (along, -step)
            arrived(half, 4 * slot + kind, block(half, where[0], where[1], 0, 2))
            part = block(half, where[0], where[1], kind, 1)
            peer = plane_peer(first, step, 0) if axis == 0 else plane_peer(first, 0, step)
            push(half, 4 * slot + 2 + kind, part, part, peer)

    def ring_end(half, slot, axis, along):
        where = (2, 0) if axis == 0 else (along, 2)
        for kind in (0, 1):
            arrived(half, 4 * slot + 2 + kind, block(half, where[0], where[1], kind, 1))

    for half in (0, 1):
        ring(half, 0, 0, 0, own(HALVES[half][1], 2))
    for half in (0, 1):
        ring(half, 1, 1, 0, own(HALVES[half][1], 2))
    yield
    for half in (0, 1):
        ring_relay(half, 0, 0, 0)
        for slot in (1, 2):
            ring(half, 1 + slot, 1, ORDER[slot], block(half, ORDER[slot], 0, 0, 2))
    yield
    for half in (0, 1):
        ring_end(half, 0, 0, 0)
        ring(half, 4, 1, 2, block(half, 2, 0, 0, 2))
        after_row(half, 0)
    for slot in (0, 1, 2, 3):
        for half in (0, 1):
            ring_relay(half, 1 + slot, 1, ORDER[slot])
        yield
    for half in (0, 1):
        after_row(half, -1)
        after_row(half, 1)
    for half in (0, 1):
        for slot in (0, 1, 2, 3):
            ring_end(half, 1 + slot, 1, ORDER[slot])
        after_row(half, 2)
    for item in started:
        item.wait_send()


def plane_reduce(parts, far, near, far_last, near_last, send, recv, store):
    started = []

    def copy(half, kind, source, target, peer):
        return pltpu.make_async_remote_copy(
            src_ref=source,
            dst_ref=target,
            send_sem=send.at[half, kind],
            recv_sem=recv.at[half, kind],
            device_id=peer,
            device_id_type=MESH,
        )

    def push(half, kind, source, target, peer):
        item = copy(half, kind, source, target, peer)
        item.start()
        started.append(item)

    def arrived(half, kind, target):
        first, _ = HALVES[half]
        copy(half, kind, target, target, plane_peer(first, 1, 0)).wait_recv()

    def rows(half, offset, low, count):
        first, base = HALVES[half]
        z, y = plane_place(first, 0, offset)
        if first == "y":
            return parts.at[z, :, pl.ds(base + low, count)]
        return parts.at[:, y, pl.ds(base + low, count)]

    def one(half, offset, low, count):
        first, base = HALVES[half]
        z, y = plane_place(first, offset, 0)
        return parts.at[z, y, pl.ds(base + low, count)]

    def add(target, *others):
        if len(others) == 1:
            target[...] = target[...] + others[0][...]
            return
        total = target[...].astype(jnp.float32)
        for other in others:
            total = total + other[...].astype(jnp.float32)
        target[...] = total.astype(target.dtype)

    def add_rows(half, offset, low, count, *others):
        target = rows(half, offset, low, count)
        def step(at, carry):
            add(target.at[at], *[other.at[at] for other in others])
            return carry
        lax.fori_loop(0, SIDE, step, 0)

    def peer(half, axis, step):
        first, _ = HALVES[half]
        return plane_peer(first, 0, step) if axis == 1 else plane_peer(first, step, 0)

    for half in (0, 1):
        push(half, 0, rows(half, 2, 0, 1), far.at[half, 0], peer(half, 1, 1))
        push(half, 1, rows(half, 2, 1, 1), far.at[half, 1], peer(half, 1, -1))
    yield
    for half in (0, 1):
        push(half, 2, rows(half, 1, 1, 1), near.at[half, 0, :, pl.ds(1, 1)], peer(half, 1, 1))
        push(half, 3, rows(half, -1, 0, 1), near.at[half, 1, :, pl.ds(0, 1)], peer(half, 1, -1))
    yield
    for half in (0, 1):
        arrived(half, 0, far.at[half, 0])
        add_rows(half, 1, 0, 1, far.at[half, 0])
        push(half, 4, rows(half, 1, 0, 1), near.at[half, 0, :, pl.ds(0, 1)], peer(half, 1, 1))
        arrived(half, 1, far.at[half, 1])
        add_rows(half, -1, 1, 1, far.at[half, 1])
        push(half, 5, rows(half, -1, 1, 1), near.at[half, 1, :, pl.ds(1, 1)], peer(half, 1, -1))
    yield
    for half in (0, 1):
        arrived(half, 2, near.at[half, 0, :, pl.ds(1, 1)])
        arrived(half, 3, near.at[half, 1, :, pl.ds(0, 1)])
        arrived(half, 4, near.at[half, 0, :, pl.ds(0, 1)])
        arrived(half, 5, near.at[half, 1, :, pl.ds(1, 1)])
        add_rows(half, 0, 0, 2, near.at[half, 0], near.at[half, 1])
        push(half, 6, one(half, 2, 0, 1), far_last.at[half, 0], peer(half, 0, 1))
        push(half, 7, one(half, 2, 1, 1), far_last.at[half, 1], peer(half, 0, -1))
        push(half, 8, one(half, 1, 1, 1), near_last.at[half, 0, pl.ds(1, 1)], peer(half, 0, 1))
        push(half, 9, one(half, -1, 0, 1), near_last.at[half, 1, pl.ds(0, 1)], peer(half, 0, -1))
    yield
    for half in (0, 1):
        arrived(half, 6, far_last.at[half, 0])
        add(one(half, 1, 0, 1), far_last.at[half, 0])
        push(half, 10, one(half, 1, 0, 1), near_last.at[half, 0, pl.ds(0, 1)], peer(half, 0, 1))
        arrived(half, 7, far_last.at[half, 1])
        add(one(half, -1, 1, 1), far_last.at[half, 1])
        push(half, 11, one(half, -1, 1, 1), near_last.at[half, 1, pl.ds(1, 1)], peer(half, 0, -1))
    yield
    for half in (0, 1):
        arrived(half, 8, near_last.at[half, 0, pl.ds(1, 1)])
        arrived(half, 9, near_last.at[half, 1, pl.ds(0, 1)])
        arrived(half, 10, near_last.at[half, 0, pl.ds(0, 1)])
        arrived(half, 11, near_last.at[half, 1, pl.ds(1, 1)])
        total = one(half, 0, 0, 2)[...].astype(jnp.float32)
        for side in (0, 1):
            total = total + near_last[half, side].astype(jnp.float32)
        store(HALVES[half][1], total)
    for item in started:
        item.wait_send()


def reduce_scratch(quarter_rows, width):
    unit = (quarter_rows, width)
    return [
        pltpu.VMEM((SIDE, SIDE, 4) + unit, jnp.bfloat16),
        pltpu.VMEM((2, 2, SIDE, 1) + unit, jnp.bfloat16),
        pltpu.VMEM((2, 2, SIDE, 2) + unit, jnp.bfloat16),
        pltpu.VMEM((2, 2, 1) + unit, jnp.bfloat16),
        pltpu.VMEM((2, 2, 2) + unit, jnp.bfloat16),
        pltpu.SemaphoreType.DMA((2, 12)),
        pltpu.SemaphoreType.DMA((2, 12)),
    ]


def comm_params(number, limit_mb):
    return pltpu.CompilerParams(
        collective_id=number, has_side_effects=True, vmem_limit_bytes=limit_mb * 1024 * 1024
    )


def nothing(half, offset):
    return None


def advance(steps):
    next(steps, None)


def finish(steps):
    for _ in steps:
        pass


def pair_up(low, high, lane):
    return (
        jnp.where(lane < HEAD_DIM, low, pltpu.roll(high, HEAD_DIM, 1)),
        jnp.where(lane < HEAD_DIM, pltpu.roll(low, HEAD_DIM, 1), high),
    )


def by_group(rows):
    lane = lax.broadcasted_iota(jnp.int32, (rows.shape[0], 128), 1)
    tile = lambda at: rows[:, at * 128 : (at + 1) * 128]
    parts = []
    for j in range(4):
        low, high = tile(8 + j), tile(12 + j)
        first, second = pair_up(low, high, lane)
        parts += [tile(2 * j), first, tile(2 * j + 1), second]
    return jnp.concatenate(parts, axis=1)


def by_kind(rows):
    lane = lax.broadcasted_iota(jnp.int32, (rows.shape[0], 128), 1)
    tile = lambda at: rows[:, at * 128 : (at + 1) * 128]
    queries, keys, values = [], [], []
    for j in range(4):
        queries += [tile(4 * j), tile(4 * j + 2)]
        key, value = pair_up(tile(4 * j + 1), tile(4 * j + 3), lane)
        keys.append(key)
        values.append(value)
    return jnp.concatenate(queries + keys + values, axis=1)


def ring_gather(owns, outs, send, recv, core_send, core_recv, local):
    seq = lax.axis_index("seq")
    x, core = seq // 2, seq % 2
    other = seq_peer(0, True)
    started, swaps = [], []
    count = len(owns)

    def at(m, step, side):
        return outs[m].at[:, (x + step) % SIDE, side]

    def copy(m, kind, source, target, step):
        return pltpu.make_async_remote_copy(
            src_ref=source,
            dst_ref=target,
            send_sem=send.at[m, kind],
            recv_sem=recv.at[m, kind],
            device_id=seq_peer(step, False),
            device_id_type=MESH,
        )

    def push(m, kind, source, target, step):
        item = copy(m, kind, source, target, step)
        item.start()
        started.append(item)

    def arrived(m, kind, target):
        copy(m, kind, target, target, 1).wait_recv()

    def swap(m, kind, source, step):
        def across(out_of, into):
            return pltpu.make_async_remote_copy(
                src_ref=out_of,
                dst_ref=into,
                send_sem=core_send.at[m, kind],
                recv_sem=core_recv.at[m, kind],
                device_id=other,
                device_id_type=MESH,
            )

        item = across(source, at(m, step, core))
        item.start()
        started.append(item)
        swaps.append(across(at(m, step, 1 - core), at(m, step, 1 - core)))

    keeps = [pltpu.make_async_copy(owns[m], at(m, 0, core), local.at[m]) for m in range(count)]
    for m in range(count):
        push(m, 0, owns[m], at(m, 0, core), 1)
        push(m, 1, owns[m], at(m, 0, core), 3)
    for m in range(count):
        keeps[m].start()
        swap(m, 0, owns[m], 0)
    yield
    for m in range(count):
        for kind, expert, came, onward in ((0, 0, 3, 1), (1, 1, 1, 3)):
            arrived(m, kind, at(m, came, core))
            part = outs[m].at[expert, (x + came) % SIDE, core]
            push(m, 2 + kind, part, part, onward)
            swap(m, 1 + kind, at(m, came, core), came)
    yield
    for m in range(count):
        for kind in (0, 1):
            arrived(m, 2 + kind, outs[m].at[kind, (x + 2) % SIDE, core])
        swap(m, 3, at(m, 2, core), 2)
    for item in swaps:
        item.wait_recv()
    for item in keeps:
        item.wait()
    for item in started:
        item.wait_send()


def weights_gather(qkv, others, experts, number):
    rows, qkv_width = qkv.shape
    width = qkv_width + sum(other.shape[1] for other in others)
    kinds = len(experts)

    def kernel(*refs):
        refs = list(refs)
        take = lambda count: [refs.pop(0) for _ in range(count)]
        ins, ex_ins, (out_ref,), ex_outs = take(1 + len(others)), take(kinds), take(1), take(kinds)
        own_ref, send, recv, x_send, x_recv, core_send, core_recv, local_sem = take(8)
        ring_send, ring_recv, swap_send, swap_recv, ring_local = take(5)
        own_ref[:, pl.ds(0, qkv_width)] = by_group(ins[0][...].astype(jnp.float32)).astype(
            own_ref.dtype
        )
        at = qkv_width
        for other in ins[1:]:
            own_ref[:, pl.ds(at, other.shape[1])] = other[...]
            at += other.shape[1]
        seq = lax.axis_index("seq")
        x, core = seq // 2, seq % 2
        x_peers = [seq_peer(step, False) for step in (1, 3, 2)]
        other = seq_peer(0, True)
        greet(plane_neighbours() + x_peers + [other])
        z, y = plane_place("y", 0, 0)
        keep = pltpu.make_async_copy(own_ref, out_ref.at[x, core, z, y], local_sem)
        keep.start()
        sends = []
        for i, step in enumerate((1, 3, 2)):
            item = pltpu.make_async_remote_copy(
                src_ref=own_ref,
                dst_ref=out_ref.at[x, core, z, y],
                send_sem=x_send.at[i],
                recv_sem=x_recv.at[i],
                device_id=x_peers[i],
                device_id_type=MESH,
            )
            item.start()
            sends.append(item)
        keep.wait()
        for i, step in enumerate((1, 3, 2)):
            came = out_ref.at[(x + SIDE - step) % SIDE, core, z, y]
            pltpu.make_async_remote_copy(
                src_ref=came,
                dst_ref=came,
                send_sem=x_send.at[i],
                recv_sem=x_recv.at[i],
                device_id=x_peers[i],
                device_id_type=MESH,
            ).wait_recv()

        swaps = []

        def swap(half, offset):
            first, base = HALVES[half]
            z, y = plane_place(first, 0, offset)
            mine = (
                out_ref.at[pl.ds(base, 2), core, z]
                if first == "y"
                else out_ref.at[pl.ds(base, 2), core, :, y]
            )
            theirs = (
                out_ref.at[pl.ds(base, 2), 1 - core, z]
                if first == "y"
                else out_ref.at[pl.ds(base, 2), 1 - core, :, y]
            )
            kind = ORDER.index(offset)
            item = pltpu.make_async_remote_copy(
                src_ref=mine,
                dst_ref=mine,
                send_sem=core_send.at[half, kind],
                recv_sem=core_recv.at[half, kind],
                device_id=other,
                device_id_type=MESH,
            )
            item.start()
            sends.append(item)
            swaps.append(
                pltpu.make_async_remote_copy(
                    src_ref=theirs,
                    dst_ref=theirs,
                    send_sem=core_send.at[half, kind],
                    recv_sem=core_recv.at[half, kind],
                    device_id=other,
                    device_id_type=MESH,
                )
            )

        plane = plane_gather(
            lambda low, count: out_ref.at[pl.ds(low, count), core, z, y],
            lambda z, y, low, count: out_ref.at[pl.ds(low, count), core, z, y],
            send,
            recv,
            swap,
        )
        ring = ring_gather(
            ex_ins, ex_outs, ring_send, ring_recv, swap_send, swap_recv, ring_local
        )
        advance(plane)
        advance(ring)
        for _ in range(5):
            advance(plane)
        advance(ring)
        finish(plane)
        finish(ring)
        for item in swaps:
            item.wait_recv()
        for item in sends:
            item.wait_send()

    out = pl.pallas_call(
        kernel,
        out_shape=(jax.ShapeDtypeStruct((4, 2, SIDE, SIDE, rows, width), qkv.dtype),)
        + tuple(
            jax.ShapeDtypeStruct((2, 4, 2) + expert.shape[1:], expert.dtype) for expert in experts
        ),
        in_specs=[pl.BlockSpec(memory_space=pltpu.VMEM)] * (1 + len(others))
        + [pl.BlockSpec(memory_space=pl.ANY)] * kinds,
        out_specs=(pl.BlockSpec(memory_space=pl.ANY),) * (1 + kinds),
        scratch_shapes=[
            pltpu.VMEM((rows, width), qkv.dtype),
            pltpu.SemaphoreType.DMA((2, 20)),
            pltpu.SemaphoreType.DMA((2, 20)),
            pltpu.SemaphoreType.DMA((3,)),
            pltpu.SemaphoreType.DMA((3,)),
            pltpu.SemaphoreType.DMA((2, 4)),
            pltpu.SemaphoreType.DMA((2, 4)),
            pltpu.SemaphoreType.DMA,
        ]
        + [pltpu.SemaphoreType.DMA((kinds, 4))] * 4
        + [pltpu.SemaphoreType.DMA((kinds,))],
        compiler_params=comm_params(number, 8),
        name="weights_gather",
    )(qkv, *others, *experts)
    return (out[0].reshape(4 * 2 * SIDE * SIDE * rows, width),) + tuple(
        full.reshape(2, 8 * expert.shape[1], expert.shape[2])
        for full, expert in zip(out[1:], experts)
    )


def expert_shares_of(experts):
    return [(2, 4, 2, expert.shape[1] // 8, expert.shape[2]) for expert in experts]


def ring_reduce_scratch(experts):
    units = [share[3:] for share in expert_shares_of(experts)]
    count = len(units)
    return (
        [pltpu.VMEM((2, 4) + unit, jnp.bfloat16) for unit in units]
        + [pltpu.VMEM((2, 4) + unit, jnp.bfloat16) for unit in units]
        + [pltpu.VMEM((2,) + unit, jnp.bfloat16) for unit in units]
        + [pltpu.VMEM((2, 2) + unit, jnp.bfloat16) for unit in units]
        + [pltpu.SemaphoreType.DMA((count,))] * 3
        + [pltpu.SemaphoreType.DMA((count, 6))] * 2
    )


def ring_reduce(ins, outs, refs):
    count = len(ins)
    sums, twins = refs[:count], refs[count : 2 * count]
    far, near = refs[2 * count : 3 * count], refs[3 * count : 4 * count]
    load, core_send, core_recv, send, recv = refs[4 * count :]
    core = lax.axis_index("seq") % 2
    loads, swaps = [], []
    for m in range(count):
        loads.append(pltpu.make_async_copy(ins[m].at[:, :, core], sums[m], load.at[m]))
        loads[m].start()
        swaps.append(
            pltpu.make_async_remote_copy(
                src_ref=ins[m].at[:, :, 1 - core],
                dst_ref=twins[m],
                send_sem=core_send.at[m],
                recv_sem=core_recv.at[m],
                device_id=seq_peer(0, True),
                device_id_type=MESH,
            )
        )
        swaps[m].start()
    yield
    x = lax.axis_index("seq") // 2
    started = []

    def copy(m, kind, source, target, step):
        return pltpu.make_async_remote_copy(
            src_ref=source,
            dst_ref=target,
            send_sem=send.at[m, kind],
            recv_sem=recv.at[m, kind],
            device_id=seq_peer(step, False),
            device_id_type=MESH,
        )

    def push(m, kind, source, target, step):
        item = copy(m, kind, source, target, step)
        item.start()
        started.append(item)

    def arrived(m, kind, target):
        copy(m, kind, target, target, 1).wait_recv()

    def at(step):
        return (x + step) % SIDE

    for m in range(count):
        loads[m].wait()
        swaps[m].wait_recv()
        started.append(swaps[m])

        def add_pair(at, carry):
            sums[m][at // 4, at % 4] = sums[m][at // 4, at % 4] + twins[m][at // 4, at % 4]
            return carry

        lax.fori_loop(0, 8, add_pair, 0)
        push(m, 0, sums[m].at[0, at(2)], far[m].at[0], 1)
        push(m, 1, sums[m].at[1, at(2)], far[m].at[1], 3)
    for m in range(count):
        push(m, 2, sums[m].at[1, at(1)], near[m].at[0, 1], 1)
        push(m, 3, sums[m].at[0, at(3)], near[m].at[1, 0], 3)
    yield
    for m in range(count):
        for kind, expert, step in ((0, 0, 1), (1, 1, 3)):
            arrived(m, kind, far[m].at[kind])
            target = sums[m].at[expert, at(step)]
            target[...] = target[...] + far[m][kind]
            push(m, 4 + kind, target, near[m].at[kind, expert], step)
    yield
    for m in range(count):
        arrived(m, 2, near[m].at[0, 1])
        arrived(m, 3, near[m].at[1, 0])
        arrived(m, 4, near[m].at[0, 0])
        arrived(m, 5, near[m].at[1, 1])
        for expert in (0, 1):
            outs[m][expert] = (
                sums[m][expert, at(0)].astype(jnp.float32)
                + near[m][0, expert].astype(jnp.float32)
                + near[m][1, expert].astype(jnp.float32)
            )
    for item in started:
        item.wait_send()


def weights_reduce(pieces, experts, number):
    widths = [piece.shape[1] for piece in pieces]
    width = sum(widths)
    rows = pieces[0].shape[0] // (4 * 2 * SIDE * SIDE)
    kinds = len(experts)
    shares = expert_shares_of(experts)

    def kernel(*refs):
        refs = list(refs)
        take = lambda count: [refs.pop(0) for _ in range(count)]
        ins, ex_ins = take(len(widths)), take(kinds)
        qkv_ref, out_ref, small_ref = take(3)
        ex_outs = take(kinds)
        (parts, far, near, far_last, near_last, send, recv, twin, mine, from_x, load, core_send,
         core_recv, x_send, x_recv) = take(15)
        ring = ring_reduce(ex_ins, ex_outs, refs)
        seq = lax.axis_index("seq")
        x, core = seq // 2, seq % 2
        x_peers = [seq_peer(step, False) for step in (1, 3, 2)]
        other = seq_peer(0, True)
        loads = []
        for quarter in range(4):
            at = 0
            for i, one_width in enumerate(widths):
                item = pltpu.make_async_copy(
                    ins[i].at[quarter, core],
                    parts.at[:, :, quarter, :, pl.ds(at, one_width)],
                    load.at[quarter, i],
                )
                item.start()
                loads.append(item)
                at += one_width
        greet(plane_neighbours() + x_peers + [other])
        swaps = []
        for quarter in range(4):
            at = 0
            for i, one_width in enumerate(widths):
                item = pltpu.make_async_remote_copy(
                    src_ref=ins[i].at[quarter, 1 - core],
                    dst_ref=twin.at[quarter, :, :, :, pl.ds(at, one_width)],
                    send_sem=core_send.at[quarter, i],
                    recv_sem=core_recv.at[quarter, i],
                    device_id=other,
                    device_id_type=MESH,
                )
                item.start()
                swaps.append(item)
                at += one_width
        for quarter in range(4):
            for i in range(len(widths)):
                loads[quarter * len(widths) + i].wait()
                swaps[quarter * len(widths) + i].wait_recv()

            def add(at, carry):
                z, y = at // SIDE, at % SIDE
                parts[z, y, quarter] = parts[z, y, quarter] + twin[quarter, z, y]
                return carry

            lax.fori_loop(0, SIDE * SIDE, add, 0)

        def store(low, total):
            mine[pl.ds(low, 2)] = total.astype(mine.dtype)

        plane = plane_reduce(parts, far, near, far_last, near_last, send, recv, store)
        advance(plane)
        advance(plane)
        advance(ring)
        advance(plane)
        advance(ring)
        advance(plane)
        advance(ring)
        advance(plane)
        finish(ring)
        finish(plane)
        sends = []
        for i, step in enumerate((1, 3, 2)):
            item = pltpu.make_async_remote_copy(
                src_ref=mine.at[(x + step) % SIDE],
                dst_ref=from_x.at[i],
                send_sem=x_send.at[i],
                recv_sem=x_recv.at[i],
                device_id=x_peers[i],
                device_id_type=MESH,
            )
            item.start()
            sends.append(item)
        total = mine[x].astype(jnp.float32)
        for i in range(3):
            sends[i].wait_recv()
            total = total + from_x[i].astype(jnp.float32)
        qkv_ref[...] = by_kind(total[:, : widths[0]])
        out_ref[...] = total[:, widths[0] : widths[0] + widths[1]]
        small_ref[...] = total[:, widths[0] + widths[1] :]
        for item in sends + swaps:
            item.wait_send()

    unit = (rows, width)
    pairs = (4, len(widths))
    vmem = pl.BlockSpec(memory_space=pltpu.VMEM)
    return pl.pallas_call(
        kernel,
        out_shape=tuple(
            [jax.ShapeDtypeStruct((rows, one_width), jnp.float32) for one_width in widths]
            + [jax.ShapeDtypeStruct((2,) + share[3:], jnp.float32) for share in shares]
        ),
        in_specs=[pl.BlockSpec(memory_space=pl.ANY)] * (len(widths) + kinds),
        out_specs=(vmem,) * (len(widths) + kinds),
        scratch_shapes=reduce_scratch(rows, width)
        + [
            pltpu.VMEM((4, SIDE, SIDE) + unit, jnp.bfloat16),
            pltpu.VMEM((4,) + unit, jnp.bfloat16),
            pltpu.VMEM((3,) + unit, jnp.bfloat16),
            pltpu.SemaphoreType.DMA(pairs),
            pltpu.SemaphoreType.DMA(pairs),
            pltpu.SemaphoreType.DMA(pairs),
            pltpu.SemaphoreType.DMA((3,)),
            pltpu.SemaphoreType.DMA((3,)),
        ]
        + ring_reduce_scratch(experts),
        compiler_params=comm_params(number, 48),
        name="weights_reduce",
    )(
        *[piece.reshape(4, 2, SIDE, SIDE, rows, piece.shape[1]) for piece in pieces],
        *[expert.reshape(share) for expert, share in zip(experts, shares)],
    )


def rms_scale(values):
    return lax.rsqrt(jnp.mean(values * values, axis=-1, keepdims=True) + epsilon)


def rope_tables(length):
    half_dim = HEAD_DIM // 2
    frequency = np.float32(rope_theta) ** (
        -np.arange(half_dim, dtype=np.float32) / np.float32(half_dim)
    )
    angles = np.arange(length, dtype=np.float32)[:, None] * frequency[None, :].astype(np.float32)
    cosine = np.cos(angles.astype(np.float64)).astype(np.float32)
    sine = np.sin(angles.astype(np.float64)).astype(np.float32)
    one_cos = np.concatenate([cosine, cosine], axis=1)
    one_sin = np.concatenate([-sine, sine], axis=1)
    return (
        np.concatenate([one_cos, one_cos], axis=1),
        np.concatenate([one_sin, one_sin], axis=1),
    )


def group_tables(cosine, sine):
    lane = lax.broadcasted_iota(jnp.int32, cosine.shape, 1)
    return (
        jnp.concatenate([cosine, jnp.where(lane < HEAD_DIM, cosine, 1.0)], axis=1),
        jnp.concatenate([sine, jnp.where(lane < HEAD_DIM, sine, 0.0)], axis=1),
    )


def turn(values, cosine, sine):
    half_dim = HEAD_DIM // 2
    width = values.shape[1]
    lane = lax.broadcasted_iota(jnp.int32, values.shape, 1)
    ahead = pltpu.roll(values, width - half_dim, 1)
    behind = pltpu.roll(values, half_dim, 1)
    return values * cosine + jnp.where(lane % HEAD_DIM < half_dim, ahead, behind) * sine


SEQ_STEPS = (4, 5, 3, 2, 6, 1, 7)


def seq_exchange(source, target, send, recv):
    me = lax.axis_index("seq")
    count = 8

    def copy(step, peer, out_of, into):
        return pltpu.make_async_remote_copy(
            src_ref=out_of,
            dst_ref=into,
            send_sem=send.at[step - 1],
            recv_sem=recv.at[step - 1],
            device_id={"seq": peer},
            device_id_type=MESH,
        )

    def start(steps):
        items = []
        for step in steps:
            peer = (me + step) % count
            item = copy(step, peer, source(peer), target(me))
            item.start()
            items.append(item)
        return items

    def wait(step):
        peer = (me + count - step) % count
        copy(step, peer, target(peer), target(peer)).wait_recv()

    return (start, wait)


def seq_plane_greet():
    me = lax.axis_index("seq")
    greet(plane_neighbours() + [{"seq": (me + step) % 8} for step in range(1, 8)])


def twice(pair, lane):
    swapped = pltpu.roll(pair.astype(jnp.float32), HEAD_DIM, 1).astype(pair.dtype)
    return (
        jnp.where(lane < HEAD_DIM, pair, swapped),
        jnp.where(lane < HEAD_DIM, swapped, pair),
    )


def apart(pair, lane):
    zero = jnp.zeros_like(pair)
    return jnp.concatenate(
        [jnp.where(lane < HEAD_DIM, pair, zero), jnp.where(lane < HEAD_DIM, zero, pair)], axis=0
    )


def matmul(a, b, dims):
    return lax.dot_general(a, b, (dims, ((), ())), preferred_element_type=jnp.float32)


BLOCK = 256


def block_probs(queries, keys, at):
    scores = matmul(queries, keys, ((1,), (1,)))
    row = lax.broadcasted_iota(jnp.int32, scores.shape, 0) % BLOCK + at * BLOCK
    column = lax.broadcasted_iota(jnp.int32, scores.shape, 1)
    scores = jnp.where(column <= row, scores, -1e30)
    exponent = jnp.exp(scores - jnp.max(scores, axis=1, keepdims=True))
    return exponent * (1.0 / jnp.sum(exponent, axis=1, keepdims=True))


def attention_forward(normed, weights, width, cosine, sine, beside, number):
    tok, depth = normed.shape
    features = beside.shape[1]
    seq_parts = 8
    group = width // seq_parts
    pair = 2 * HEAD_DIM
    length = tok * seq_parts
    per_block = BLOCK // tok

    def kernel(
        normed_ref, weights_ref, cos_hbm, sin_hbm, beside_ref, out_ref, heads_ref, all_ref,
        packed, mixed, proj_w, cos_ref, sin_ref,
        send, recv, o_send, o_recv, p_send, p_recv, local_sem, load,
    ):
        me = lax.axis_index("seq")
        here = pl.ds(pl.multiple_of(me * tok, tok), tok)
        loads = [
            pltpu.make_async_copy(weights_ref.at[:, pl.ds(0, width)], proj_w, load.at[0]),
            pltpu.make_async_copy(cos_hbm.at[here], cos_ref, load.at[1]),
            pltpu.make_async_copy(sin_hbm.at[here], sin_ref, load.at[2]),
        ]
        for item in loads:
            item.start()
        z, y = plane_place("y", 0, 0)
        keep = pltpu.make_async_copy(beside_ref, all_ref.at[z, y], local_sem)
        keep.start()
        seq_plane_greet()
        steps = plane_gather(
            lambda low, count: beside_ref.at[pl.ds(low, count)],
            lambda z, y, low, count: all_ref.at[z, y, pl.ds(low, count)],
            p_send,
            p_recv,
            nothing,
        )
        advance(steps)
        for item in loads:
            item.wait()
        cosines, sines = group_tables(cos_ref[...], sin_ref[...])
        for d in range(seq_parts):
            projected = matmul(
                normed_ref[...], proj_w[:, d * group : (d + 1) * group], ((1,), (0,))
            )
            packed[d] = turn(projected, cosines, sines).astype(packed.dtype)
        start, wait = seq_exchange(
            lambda d: packed.at[d], lambda d: heads_ref.at[d], send, recv
        )
        items = start(SEQ_STEPS)
        heads_ref[me] = packed[me]
        advance(steps)
        for step in SEQ_STEPS:
            wait(step)
        advance(steps)
        lane = lax.broadcasted_iota(jnp.int32, (length, pair), 1)
        heads = heads_ref[...].reshape(length, group)
        keys, values = twice(heads[:, pair:], lane)
        lane_block = lane[:BLOCK]
        back, back_wait = seq_exchange(
            lambda d: mixed.at[d],
            lambda d: out_ref.at[:, pl.ds(pl.multiple_of(d * pair, pair), pair)],
            o_send,
            o_recv,
        )
        for at in range(length // BLOCK):
            block = heads[at * BLOCK : (at + 1) * BLOCK, :pair]
            queries = apart(block * jnp.asarray(attention_multiplier, block.dtype), lane_block)
            upto = (at + 1) * BLOCK
            probs = block_probs(queries, keys[:upto], at).astype(jnp.bfloat16)
            both = matmul(probs, values[:upto], ((1,), (0,)))
            made = jnp.where(lane_block < HEAD_DIM, both[:BLOCK], both[BLOCK:]).astype(mixed.dtype)
            mixed[at * per_block : (at + 1) * per_block] = made.reshape(per_block, tok, pair)
            if at % 2:
                advance(steps)
        items += back(SEQ_STEPS)
        out_ref[:, pl.ds(pl.multiple_of(me * pair, pair), pair)] = mixed[me]
        advance(steps)
        for step in SEQ_STEPS:
            back_wait(step)
        finish(steps)
        keep.wait()
        for item in items:
            item.wait_send()

    vmem = pl.BlockSpec(memory_space=pltpu.VMEM)
    anywhere = pl.BlockSpec(memory_space=pl.ANY)
    attended, heads, gathered = pl.pallas_call(
        kernel,
        out_shape=(
            jax.ShapeDtypeStruct((tok, seq_parts * pair), jnp.bfloat16),
            jax.ShapeDtypeStruct((seq_parts, tok, group), jnp.bfloat16),
            jax.ShapeDtypeStruct((SIDE, SIDE, 4, tok // 4, features), beside.dtype),
        ),
        in_specs=[vmem] + [anywhere] * 4,
        out_specs=(vmem, vmem, anywhere),
        scratch_shapes=[
            pltpu.VMEM((seq_parts, tok, group), jnp.bfloat16),
            pltpu.VMEM((seq_parts, tok, pair), jnp.bfloat16),
            pltpu.VMEM((depth, width), jnp.bfloat16),
            pltpu.VMEM((tok, pair), jnp.float32),
            pltpu.VMEM((tok, pair), jnp.float32),
        ]
        + [pltpu.SemaphoreType.DMA((7,))] * 4
        + [pltpu.SemaphoreType.DMA((2, 20))] * 2
        + [pltpu.SemaphoreType.DMA, pltpu.SemaphoreType.DMA((3,))],
        compiler_params=comm_params(number, 48),
        name="attention_forward",
    )(normed, weights, cosine, sine, beside.reshape(4, tok // 4, features))
    return (attended, heads, gathered.reshape(SIDE * SIDE, tok, features))


def attention_backward(grad_attended, heads_in, cosine, sine, beside, experts, number):
    kinds = len(experts)
    shares = expert_shares_of(experts)
    seq_parts, tok, group = heads_in.shape
    features = beside.shape[2]
    pair = 2 * HEAD_DIM
    length = tok * seq_parts
    per_block = BLOCK // tok

    def kernel(*refs):
        refs = list(refs)
        take = lambda count: [refs.pop(0) for _ in range(count)]
        grad_ref, heads_ref, cos_ref, sin_ref, beside_ref = take(5)
        ex_ins = take(kinds)
        out_ref, sum_ref = take(2)
        ex_outs = take(kinds)
        came, packed, d_queries, d_keys, d_values, send, recv, o_send, o_recv = take(9)
        parts, far, near, far_last, near_last, p_send, p_recv, load = take(8)
        ring = ring_reduce(ex_ins, ex_outs, refs)
        me = lax.axis_index("seq")
        loaded = pltpu.make_async_copy(beside_ref, parts, load)
        loaded.start()
        seq_plane_greet()

        def store(low, total):
            sum_ref[pl.ds(low, 2)] = total

        steps = plane_reduce(parts, far, near, far_last, near_last, p_send, p_recv, store)
        columns = lambda d: grad_ref.at[:, pl.ds(pl.multiple_of(d * pair, pair), pair)]
        start, wait = seq_exchange(columns, lambda d: came.at[d], send, recv)
        items = start(SEQ_STEPS)
        loaded.wait()
        advance(steps)
        advance(steps)
        advance(ring)
        came[me] = grad_ref[:, pl.ds(pl.multiple_of(me * pair, pair), pair)]
        lane = lax.broadcasted_iota(jnp.int32, (length, pair), 1)
        lane_block = lane[:BLOCK]
        heads = heads_ref[...].reshape(length, group)
        keys, values = twice(heads[:, pair:], lane)
        for step in SEQ_STEPS:
            wait(step)
        advance(ring)
        cosines, sines = group_tables(cos_ref[...], sin_ref[...])
        lane_group = lane_block

        def back_copy(step, peer, out_of, into):
            return pltpu.make_async_remote_copy(
                src_ref=out_of,
                dst_ref=into,
                send_sem=o_send.at[step - 1],
                recv_sem=o_recv.at[step - 1],
                device_id={"seq": peer},
                device_id_type=MESH,
            )

        def columns_of(d):
            return out_ref.at[:, pl.ds(pl.multiple_of(d * group, group), group)]

        last = length // BLOCK - 1
        for at in reversed(range(length // BLOCK)):
            if at == 1:
                advance(ring)
            upto = (at + 1) * BLOCK
            block = heads[at * BLOCK : upto, :pair]
            queries = apart(block * jnp.asarray(attention_multiplier, block.dtype), lane_block)
            grads = apart(
                came[at * per_block : (at + 1) * per_block].reshape(BLOCK, pair), lane_block
            )
            probs = block_probs(queries, keys[:upto], at)
            d_probs = matmul(grads, values[:upto], ((1,), (1,)))
            center = jnp.sum(probs * d_probs, axis=1, keepdims=True)
            d_scores = (probs * (d_probs - center)).astype(jnp.bfloat16)
            both = matmul(d_scores, keys[:upto], ((1,), (0,))) * attention_multiplier
            d_queries[at * BLOCK : upto] = jnp.where(
                lane_block < HEAD_DIM, both[:BLOCK], both[BLOCK:]
            )
            more_keys = matmul(d_scores, queries, ((0,), (0,)))
            more_values = matmul(probs.astype(jnp.bfloat16), grads, ((0,), (0,)))
            before = at * BLOCK
            if at == last:
                d_keys[...] = more_keys
                d_values[...] = more_values
            else:
                d_keys[:upto] += more_keys
                d_values[:upto] += more_values
            keys_here, values_here = d_keys[before:upto], d_values[before:upto]
            rest = jnp.where(
                lane_group < HEAD_DIM,
                keys_here + pltpu.roll(keys_here, HEAD_DIM, 1),
                values_here + pltpu.roll(values_here, HEAD_DIM, 1),
            )
            done = jnp.concatenate([d_queries[before:upto], rest], axis=1)
            packed[at * per_block : (at + 1) * per_block] = (
                turn(done, cosines[before:upto], -sines[before:upto])
                .astype(packed.dtype)
                .reshape(per_block, tok, group)
            )
            for d in range(at * per_block, (at + 1) * per_block):

                @pl.when(me != d)
                def _():
                    step = (d - me + seq_parts) % seq_parts
                    back_copy(step, d, packed.at[d], columns_of(me)).start()

            if at in (last, 0):
                advance(steps)
        out_ref[:, pl.ds(pl.multiple_of(me * group, group), group)] = packed[me]
        advance(steps)
        for step in SEQ_STEPS:
            came_from = (me + seq_parts - step) % seq_parts
            back_copy(step, came_from, columns_of(came_from), columns_of(came_from)).wait_recv()
        finish(ring)
        finish(steps)
        for item in items:
            item.wait_send()
        for step in SEQ_STEPS:
            went_to = (me + step) % seq_parts
            back_copy(step, went_to, packed.at[went_to], columns_of(me)).wait_send()

    vmem = pl.BlockSpec(memory_space=pltpu.VMEM)
    outs = pl.pallas_call(
        kernel,
        out_shape=(
            jax.ShapeDtypeStruct((tok, seq_parts * group), jnp.bfloat16),
            jax.ShapeDtypeStruct((4, tok // 4, features), jnp.float32),
        )
        + tuple(jax.ShapeDtypeStruct((2,) + share[3:], jnp.float32) for share in shares),
        in_specs=[vmem] * 4 + [pl.BlockSpec(memory_space=pl.ANY)] * (1 + kinds),
        out_specs=(vmem,) * (2 + kinds),
        scratch_shapes=[
            pltpu.VMEM((seq_parts, tok, pair), jnp.bfloat16),
            pltpu.VMEM((seq_parts, tok, group), jnp.bfloat16),
            pltpu.VMEM((length, pair), jnp.float32),
            pltpu.VMEM((length, pair), jnp.float32),
            pltpu.VMEM((length, pair), jnp.float32),
        ]
        + [pltpu.SemaphoreType.DMA((7,))] * 4
        + reduce_scratch(tok // 4, features)
        + [pltpu.SemaphoreType.DMA]
        + ring_reduce_scratch(experts),
        compiler_params=comm_params(number, 56),
        name="attention_backward",
    )(
        grad_attended,
        heads_in,
        cosine,
        sine,
        beside.reshape(SIDE, SIDE, 4, tok // 4, features),
        *[expert.reshape(share) for expert, share in zip(experts, shares)],
    )
    return (outs[0], outs[1].reshape(tok, features)) + tuple(outs[2:])


def gate_columns(logits, chosen_ids, experts_all):
    named = jnp.any(
        chosen_ids[..., None] == jnp.arange(experts_all, dtype=jnp.int32), axis=-2
    )
    peak = jnp.max(jnp.where(named, logits, -jnp.inf), axis=-1, keepdims=True)
    exponent = jnp.where(named, jnp.exp(logits - peak), 0.0)
    gates = exponent / jnp.sum(exponent, axis=-1, keepdims=True)
    coarse = lax.reduce_precision(gates, 8, 7)
    columns = jnp.concatenate(
        [named.astype(jnp.float32), coarse, gates - coarse, jnp.zeros_like(gates)], axis=-1
    ).astype(jnp.bfloat16)
    return (gates, columns)


def near_place(at):
    if isinstance(at, int) and at >= 9:
        return far_place(at)
    return (at // 3 - 1, at % 3 - 1)


def far_place(at):
    beyond = at - 9
    turn_over = beyond // 4
    return (
        2 * (1 - turn_over) + turn_over * (beyond - 5),
        (1 - turn_over) * (beyond - 1) + turn_over * 2,
    )


def expert_layer(
    tokens_own, cot_all, gate_full, up_full, down_full, experts_all, capacity, number
):
    tok, wide = tokens_own.shape
    sources = SIDE * SIDE
    quarter = tok // 4
    features = wide - 128
    hidden_units = gate_full.shape[2]
    group = 8
    chunks = sources // group
    chunk_rows = group * capacity
    f32, b16 = jnp.float32, jnp.bfloat16

    def kernel(
        tok_hbm, cot_hbm, gate_hbm, up_hbm, down_hbm,
        mix_hbm, back_ref, ggate_hbm, gup_hbm, gdown_hbm,
        tok_v, cot_v, gate_v, up_v, down_v, mix_v, grad_v,
        x_v, deo_v, slope_v, act_v, inner_v, pick_t, share_v, dgate_v,
        in_sem, out_sem, g_send, g_recv,
        rows_v, far, near, far_last, near_last, r_send, r_recv,
    ):
        first = lax.axis_index("wshard") * 2
        home_z, home_y = plane_place("y", 0, 0)
        loads = [
            pltpu.make_async_copy(source, target, in_sem.at[i])
            for i, (source, target) in enumerate(
                [(tok_hbm, tok_v.at[home_z, home_y]), (cot_hbm, cot_v), (gate_hbm, gate_v), (up_hbm, up_v),
                 (down_hbm, down_v)]
            )
        ]
        for item in loads:
            item.start()
        lane = lax.broadcasted_iota(jnp.int32, (tok, 128), 1)
        down_rows = lax.broadcasted_iota(jnp.int32, (tok, 128), 0)
        lower = jnp.where(down_rows >= lane, 1.0, 0.0).astype(b16)
        greet(plane_neighbours())
        gather = plane_gather(
            lambda low, count: tok_hbm.at[pl.ds(low, count)],
            lambda z, y, low, count: tok_v.at[z, y, pl.ds(low, count)],
            g_send,
            g_recv,
            nothing,
        )
        advance(gather)
        advance(gather)
        advance(gather)
        advance(gather)
        advance(gather)
        loads[0].wait()
        loads[1].wait()

        def prepare(s, place_of):
            off_z, off_y = place_of(s)
            z, y = plane_place("y", off_y, off_z)
            info = tok_v[z, y, :, :, pl.ds(features, 128)].reshape(tok, 128)
            info32 = info.astype(f32)
            place = matmul(lower, info, ((1,), (0,))) - 1.0
            place = jnp.where(info32 > 0.5, place, -1.0)
            place_rows = place.T
            info_rows = info32.T
            row_picks, col_places = [], []
            shares = []
            for e in (0, 1):
                at = first + e
                row = jnp.sum(jnp.where(down_rows == at, place_rows, 0.0), axis=0, keepdims=True)
                gate = jnp.sum(
                    jnp.where(
                        (down_rows == experts_all + at) | (down_rows == 2 * experts_all + at),
                        info_rows,
                        0.0,
                    ),
                    axis=0,
                    keepdims=True,
                )
                slot = lax.broadcasted_iota(jnp.int32, (capacity, tok), 0).astype(f32)
                hit = slot == row
                row_picks.append(jnp.where(hit, 1.0, 0.0))
                shares.append(jnp.sum(jnp.where(hit, gate, 0.0), axis=1, keepdims=True))
                col_places.append(
                    jnp.sum(jnp.where(lane == at, place, 0.0), axis=1, keepdims=True)
                )
            pick = jnp.concatenate(row_picks, axis=0).astype(b16)
            lane_f = lane.astype(f32)
            pick_t[s] = (
                jnp.where(lane_f == col_places[0], 1.0, 0.0) * jnp.where(lane < capacity, 1.0, 0.0)
                + jnp.where(lane_f - float(capacity) == col_places[1], 1.0, 0.0)
                * jnp.where(lane >= capacity, 1.0, 0.0)
            ).astype(b16)
            share_v[s] = jnp.concatenate(shares, axis=0)
            rows = matmul(
                pick, tok_v[z, y, :, :, pl.ds(0, features)].reshape(tok, features), ((1,), (0,))
            ).astype(b16)
            c, i = s // group, s % group
            x_v[0, c, i] = rows[:capacity]
            x_v[1, c, i] = rows[capacity:]
            cots = matmul(pick, cot_v[z, y], ((1,), (0,))).astype(b16)
            deo_v[0, c, i] = cots[:capacity]
            deo_v[1, c, i] = cots[capacity:]

        def prepare_all(low, high, place_of):
            def step(s, carry):
                prepare(s, place_of)
                return carry

            lax.fori_loop(low, high, step, 0)

        def forward(c):
            weighted = []
            for e in (0, 1):
                x = x_v[e, c].reshape(chunk_rows, features)
                gate_val = matmul(x, gate_v[e], ((1,), (0,)))
                up_val = matmul(x, up_v[e], ((1,), (0,)))
                sigma = 1.0 / (1.0 + jnp.exp(-gate_val))
                act = gate_val * sigma
                inner = (act * up_val).astype(b16)
                inner_v[e, c] = inner
                act_v[e, c] = act.astype(b16)
                slope_v[e, c] = (up_val * (sigma * (1.0 + gate_val * (1.0 - sigma)))).astype(b16)
                made = matmul(inner, down_v[e], ((1,), (0,))).astype(b16).astype(f32)
                share = jnp.concatenate(
                    [share_v[c * group + i, pl.ds(e * capacity, capacity)] for i in range(group)],
                    axis=0,
                )
                mix_grad = residual_multiplier * deo_v[e, c].reshape(chunk_rows, features).astype(f32)
                dgate_v[e, c] = jnp.sum(made * mix_grad, axis=1, keepdims=True)
                deo_v[e, c] = (share * mix_grad).astype(b16).reshape(group, capacity, features)
                weighted.append((share * made).astype(b16))
            for i in range(group):
                both = jnp.concatenate(
                    [w[i * capacity : (i + 1) * capacity] for w in weighted], axis=0
                )
                off_z, off_y = near_place(c * group + i)
                z, y = plane_place("y", off_y, off_z)
                mix_v[z, y] = matmul(pick_t[c * group + i], both, ((1,), (0,))).astype(b16)

        prepare_all(0, 9, near_place)
        advance(gather)
        for item in loads[2:]:
            item.wait()
        forward(0)
        finish(gather)
        prepare_all(9, sources, far_place)
        forward(1)
        stores = [pltpu.make_async_copy(mix_v, mix_hbm, out_sem.at[0])]
        stores[0].start()
        lane_rows = lax.broadcasted_iota(jnp.int32, (chunk_rows, 128), 1)

        def backward(c):
            made = []
            for e in (0, 1):
                deo = deo_v[e, c].reshape(chunk_rows, features)
                d_inner = matmul(deo, down_v[e], ((1,), (1,)))
                d_gate = (d_inner * slope_v[e, c].astype(f32)).astype(b16)
                d_up = (d_inner * act_v[e, c].astype(f32)).astype(b16)
                slope_v[e, c] = d_gate
                act_v[e, c] = d_up
                d_rows = (
                    matmul(d_gate, gate_v[e], ((1,), (1,))) + matmul(d_up, up_v[e], ((1,), (1,)))
                ).astype(b16)
                coarse = dgate_v[e, c].astype(b16).astype(f32)
                fine = dgate_v[e, c] - coarse
                columns = jnp.where(lane_rows == first + e, coarse, 0.0) + jnp.where(
                    lane_rows == experts_all + first + e, fine, 0.0
                )
                made.append(jnp.concatenate([d_rows, columns.astype(b16)], axis=1))
            for i in range(group):
                both = jnp.concatenate(
                    [m[i * capacity : (i + 1) * capacity] for m in made], axis=0
                )
                off_z, off_y = near_place(c * group + i)
                z, y = plane_place("y", off_y, off_z)
                rows_v[z, y] = (
                    matmul(pick_t[c * group + i], both, ((1,), (0,)))
                    .astype(b16)
                    .reshape(4, quarter, wide)
                )

        def store(low, total):
            back_ref[pl.ds(low, 2)] = total

        reduce = plane_reduce(
            rows_v, far, near, far_last, near_last, r_send, r_recv, store
        )
        backward(1)
        advance(reduce)
        backward(0)
        advance(reduce)
        rows_all = chunks * chunk_rows

        def whole(ref, e, columns):
            return ref[e].reshape(rows_all, columns)

        for e in (0, 1):
            x = whole(x_v, e, features)
            for i, source, target in (
                (e, slope_v, ggate_hbm),
                (2 + e, act_v, gup_hbm),
            ):
                grad_v[i] = matmul(x, whole(source, e, hidden_units), ((0,), (0,))).astype(b16)
                stores.append(
                    pltpu.make_async_copy(grad_v.at[i], target.at[e], out_sem.at[1 + i])
                )
                stores[-1].start()
            advance(reduce)
        for e in (0, 1):
            grad = matmul(
                whole(inner_v, e, hidden_units), whole(deo_v, e, features), ((0,), (0,))
            ).astype(b16)
            cot_v[e] = grad.reshape(4, 128, features)
            stores.append(
                pltpu.make_async_copy(cot_v.at[e], gdown_hbm.at[e], out_sem.at[5 + e])
            )
            stores[-1].start()
            if e == 0:
                advance(reduce)
        finish(reduce)
        for item in stores:
            item.wait()

    anywhere = pl.BlockSpec(memory_space=pl.ANY)
    local = gate_full.shape[0]
    outs = pl.pallas_call(
        kernel,
        out_shape=(
            jax.ShapeDtypeStruct((SIDE, SIDE, tok, features), b16),
            jax.ShapeDtypeStruct((4, quarter, wide), f32),
            jax.ShapeDtypeStruct((local, features, hidden_units), b16),
            jax.ShapeDtypeStruct((local, features, hidden_units), b16),
            jax.ShapeDtypeStruct((local, 4, hidden_units // 4, features), b16),
        ),
        in_specs=[anywhere] * 5,
        out_specs=(anywhere, pl.BlockSpec(memory_space=pltpu.VMEM)) + (anywhere,) * 3,
        scratch_shapes=[
            pltpu.VMEM((SIDE, SIDE, 4, quarter, wide), b16),
            pltpu.VMEM((SIDE, SIDE, tok, features), b16),
            pltpu.VMEM(gate_full.shape, b16),
            pltpu.VMEM(up_full.shape, b16),
            pltpu.VMEM(down_full.shape, b16),
            pltpu.VMEM((SIDE, SIDE, tok, features), b16),
            pltpu.VMEM((4, features, hidden_units), b16),
            pltpu.VMEM((2, chunks, group, capacity, features), b16),
            pltpu.VMEM((2, chunks, group, capacity, features), b16),
            pltpu.VMEM((2, chunks, chunk_rows, hidden_units), b16),
            pltpu.VMEM((2, chunks, chunk_rows, hidden_units), b16),
            pltpu.VMEM((2, chunks, chunk_rows, hidden_units), b16),
            pltpu.VMEM((sources, tok, 2 * capacity), b16),
            pltpu.VMEM((sources, 2 * capacity, 1), f32),
            pltpu.VMEM((2, chunks, chunk_rows, 1), f32),
            pltpu.SemaphoreType.DMA((5,)),
            pltpu.SemaphoreType.DMA((7,)),
            pltpu.SemaphoreType.DMA((2, 20)),
            pltpu.SemaphoreType.DMA((2, 20)),
        ]
        + reduce_scratch(quarter, wide),
        compiler_params=comm_params(number, 60),
        name="expert_layer",
    )(
        tokens_own.reshape(4, quarter, wide),
        cot_all.reshape(SIDE, SIDE, tok, features),
        gate_full,
        up_full,
        down_full,
    )
    return (
        outs[0].reshape(sources, tok, features),
        outs[1].reshape(tok, wide),
        outs[2],
        outs[3],
        outs[4].reshape(local, hidden_units, features),
    )


def norm_backward(grad_normed, values, scale, gain_full):
    grad_gain = jnp.sum(grad_normed * values * scale, axis=0)
    grad_hat = grad_normed * gain_full
    grad_values = scale * grad_hat - values * (scale * scale * scale) * jnp.mean(
        grad_hat * values, axis=1, keepdims=True
    )
    return (grad_values, grad_gain)


def local(
    tokens,
    weight_qkv,
    weight_out,
    router,
    gain_attn,
    gain_ffn,
    expert_gate,
    expert_up,
    expert_down,
    expert_ids,
    cotangent,
):
    tok_dev = tokens.shape[1]
    features = tokens.shape[2]
    seq_parts = lax.axis_size("seq")
    owners = lax.axis_size("wshard")
    local_experts = expert_gate.shape[0]
    experts_all = local_experts * owners
    top_count = expert_ids.shape[2]
    capacity = 2 * tok_dev * top_count // experts_all
    heads_dev = HEADS // seq_parts
    key_heads = KV_HEADS // seq_parts
    query_cols = heads_dev * HEAD_DIM
    key_cols = key_heads * HEAD_DIM
    query_width = HEADS * HEAD_DIM
    key_width = KV_HEADS * HEAD_DIM
    length = tok_dev * seq_parts
    qkv_width = weight_qkv.shape[1]
    smalls = jnp.concatenate(
        [
            router,
            gain_attn[:, None],
            gain_ffn[:, None],
            jnp.zeros((router.shape[0], 128 - experts_all - 2), jnp.bfloat16),
        ],
        axis=1,
    )
    weights_full, gate_full, up_full, down_full = weights_gather(
        weight_qkv, [weight_out, smalls], [expert_gate, expert_up, expert_down], 0
    )
    qkv_full = weights_full[:, :qkv_width]
    out_full = weights_full[:, qkv_width : qkv_width + features]
    smalls_full = weights_full[:, qkv_width + features :]
    router_full = smalls_full[:, :experts_all]
    gain_one = smalls_full[:, experts_all].astype(jnp.float32)
    gain_two = smalls_full[:, experts_all + 1].astype(jnp.float32)
    inputs = tokens[0].astype(jnp.float32)
    chosen_ids = expert_ids[0]
    scale_one = rms_scale(inputs)
    normed_one = (inputs * scale_one * gain_one).astype(jnp.bfloat16)
    cosine, sine = (jnp.asarray(table) for table in rope_tables(length))
    attended, heads_all, cot_all = attention_forward(
        normed_one, weights_full, qkv_width, cosine, sine, cotangent[0], 5
    )
    branch = jnp.dot(attended, out_full, preferred_element_type=jnp.float32)
    hidden = inputs + residual_multiplier * branch
    scale_two = rms_scale(hidden)
    normed_two = (hidden * scale_two * gain_two).astype(jnp.bfloat16)
    logits = jnp.dot(normed_two, router_full, preferred_element_type=jnp.float32)
    gates_own, gate_info = gate_columns(logits, chosen_ids, experts_all)
    mix_part, back, grad_gate, grad_up, grad_down = expert_layer(
        jnp.concatenate([normed_two, gate_info], axis=1),
        cot_all,
        gate_full,
        up_full,
        down_full,
        experts_all,
        capacity,
        1,
    )
    grad_output = cotangent[0].astype(jnp.float32)
    grad_back = back[:, :features]
    grad_gates = (
        back[:, features : features + experts_all]
        + back[:, features + experts_all : features + 2 * experts_all]
    )
    grad_logits = (
        gates_own
        * (grad_gates - jnp.sum(gates_own * grad_gates, axis=1, keepdims=True))
    ).astype(jnp.bfloat16)
    grad_normed_two = jnp.dot(grad_logits, router_full.T, preferred_element_type=jnp.float32)
    grad_normed_two = grad_normed_two + grad_back
    grad_hidden_norm, grad_gain_ffn = norm_backward(grad_normed_two, hidden, scale_two, gain_two)
    grad_hidden = grad_output + grad_hidden_norm
    grad_branch = (residual_multiplier * grad_hidden).astype(jnp.bfloat16)
    grad_out = jnp.dot(attended.T, grad_branch, preferred_element_type=jnp.float32)
    grad_attended = jnp.dot(grad_branch, out_full.T, preferred_element_type=jnp.float32).astype(
        jnp.bfloat16
    )
    grad_proj, mixture, own_gate, own_up = attention_backward(
        grad_attended, heads_all, cosine, sine, mix_part, [grad_gate, grad_up], 6
    )
    output = hidden + residual_multiplier * mixture
    grad_qkv = jnp.dot(normed_one.T, grad_proj, preferred_element_type=jnp.float32)
    grad_normed_one = jnp.dot(grad_proj, qkv_full.T, preferred_element_type=jnp.float32)
    grad_input_norm, grad_gain_attn = norm_backward(grad_normed_one, inputs, scale_one, gain_one)
    grad_input = grad_hidden + grad_input_norm
    column = jnp.arange(128, dtype=jnp.int32)[None, :]
    grad_smalls = (
        jnp.dot(
            normed_two.T,
            jnp.pad(grad_logits, ((0, 0), (0, 128 - experts_all))),
            preferred_element_type=jnp.float32,
        )
        + jnp.where(column == experts_all, grad_gain_attn[:, None], 0.0)
        + jnp.where(column == experts_all + 1, grad_gain_ffn[:, None], 0.0)
    ).astype(jnp.bfloat16)
    own_qkv, own_out, own_smalls, own_down = weights_reduce(
        [grad_qkv.astype(jnp.bfloat16), grad_out.astype(jnp.bfloat16), grad_smalls],
        [grad_down],
        4,
    )
    shares = (
        own_qkv,
        own_out,
        own_smalls[:, :experts_all],
        own_smalls[:, experts_all],
        own_smalls[:, experts_all + 1],
    )
    expert_shares = (own_gate, own_up, own_down)
    return (
        output.astype(jnp.bfloat16)[None],
        grad_input.astype(jnp.bfloat16)[None],
        shares[0],
        shares[1],
        shares[2],
        shares[3],
        shares[4],
        expert_shares[0],
        expert_shares[1],
        expert_shares[2],
    )


def solution(mesh):
    placed = (
        P("wshard", "seq", None),
        P(("seq", "wshard"), None),
        P(("seq", "wshard"), None),
        P(("seq", "wshard"), None),
        P(("seq", "wshard")),
        P(("seq", "wshard")),
        P("wshard", "seq", None),
        P("wshard", "seq", None),
        P("wshard", "seq", None),
        P("wshard", "seq", None),
        P("wshard", "seq", None),
    )
    return jax.shard_map(
        local,
        mesh=mesh,
        in_specs=placed,
        out_specs=(
            P("wshard", "seq", None),
            P("wshard", "seq", None),
            P(("seq", "wshard"), None),
            P(("seq", "wshard"), None),
            P(("seq", "wshard"), None),
            P(("seq", "wshard")),
            P(("seq", "wshard")),
            P("wshard", "seq", None),
            P("wshard", "seq", None),
            P("wshard", "seq", None),
        ),
        check_vma=False,
    )
```
